32 devices in a mesh: dp: 16 (over z, y, x), mp: 2 (over core).
Axes of the slice: x: 2, y: 2, z: 4, core: 2. Of those that a mesh axis runs over, the one named last changes fastest.
Arguments:
- pixels: bfloat16 [2, 18816, 128], P('mp', 'dp')
- labels: int32 [2, 16], P('mp', 'dp'), may hold values from 0 to 999
- stem: float32 [1167136], P(('dp', 'mp'))
- stem_first: float32 [1167136], P(('dp', 'mp')), may hold values from -0.00021362305 to 0.00021362305
- stem_second: float32 [1167136], P(('dp', 'mp')), may hold values from 5.4471976e-11 to 8.715516e-10
- small: float32 [166048], P(('dp', 'mp'))
- small_first: float32 [166048], P(('dp', 'mp')), may hold values from -0.00021362305 to 0.00021362305
- small_second: float32 [166048], P(('dp', 'mp')), may hold values from 5.4471976e-11 to 8.715516e-10
- block: float32 [3, 768, 3072], P(None, 'dp', 'mp')
- block_first: float32 [3, 768, 3072], P(None, 'dp', 'mp'), may hold values from -0.00021362305 to 0.00021362305
- block_second: float32 [3, 768, 3072], P(None, 'dp', 'mp'), may hold values from 5.4471976e-11 to 8.715516e-10
- head: float32 [768, 1000], P('dp', 'mp'), may hold values from -0.21875 to 0.21875
- head_first: float32 [768, 1000], P('dp', 'mp'), may hold values from -0.00021362305 to 0.00021362305
- head_second: float32 [768, 1000], P('dp', 'mp'), may hold values from 5.4471976e-11 to 8.715516e-10
Outputs:
- stem_new: float32 [1167136], P(('dp', 'mp'))
- stem_first_new: float32 [1167136], P(('dp', 'mp'))
- stem_second_new: float32 [1167136], P(('dp', 'mp'))
- small_new: float32 [166048], P(('dp', 'mp'))
- small_first_new: float32 [166048], P(('dp', 'mp'))
- small_second_new: float32 [166048], P(('dp', 'mp'))
- block_new: float32 [3, 768, 3072], P(None, 'dp', 'mp')
- block_first_new: float32 [3, 768, 3072], P(None, 'dp', 'mp')
- block_second_new: float32 [3, 768, 3072], P(None, 'dp', 'mp')
- head_new: float32 [768, 1000], P('dp', 'mp')
- head_first_new: float32 [768, 1000], P('dp', 'mp')
- head_second_new: float32 [768, 1000], P('dp', 'mp')
- loss_sum: float32 [], replicated
- grad_norm: float32 [], replicated
The draws below stay inside these ranges and needn't reach their ends.
All inputs are finite; a program needn't handle non-finite values.
Results may differ from the reference program's by a relative error of at most 0.03.
Values may be sent and summed in bfloat16 or wider, within the bound.
No kernel may reach another device: no remote copies, remote signals or barrier semaphores. Data moves between devices by JAX's collectives and lax.ppermute only.
A program may use at most 192 MiB of HBM per device.

```python
import math
import jax
import jax.numpy as jnp
from jax import lax

D = 768
HEADS = 12
HEAD_DIM = 64
FF = 3072
CLASSES = 1000
C1 = 48
C2 = 96
C3 = 192
C4 = 384
IMG = 224
STEP = 10
BATCH = 2
CANVAS = 3584
NP = 196
TOK = 197
STEM_LEN = 1167136
SMALL_LEN = 166048
PARAMS = 9179032
N_DP = 16


def small_layout_drawn(width, hidden, chans, tokens, classes):
    names = (('bn_gain', sum(chans)), ('bn_bias', sum(chans)), ('proj_bias', width), ('class_token', width), ('position', tokens * width), ('norm1_gain', width), ('norm1_bias', width), ('query_bias', width), ('value_bias', width), ('out_bias', width), ('norm2_gain', width), ('norm2_bias', width), ('hidden_bias', hidden), ('mlp_bias', width), ('final_gain', width), ('final_bias', width), ('head_bias', classes))
    layout = []
    offset = 0
    for name, length in names:
        layout.append((name, offset, length))
        offset = offset + length
    return layout


def stem_layout_drawn(chans, width):
    layout = []
    offset = 0
    for level in range(4):
        layout.append((offset, 9 * chans[level], chans[level + 1]))
        offset = offset + 9 * chans[level] * chans[level + 1]
    layout.append((offset, chans[4], width))
    return layout


def ramp(length, top):
    return 1.0 + (top - 1.0) * jnp.arange(length, dtype=jnp.float32) / max(length - 1, 1)


def draw_pixels(key, part):
    key = jax.random.fold_in(key, 1)
    shape = (BATCH, CANVAS, IMG, 3)
    base = jax.random.truncated_normal(key, -4.0, 4.0, shape, jnp.float32)
    top = 3.0
    rising = ramp(CANVAS, top)[None, :, None, None] * ramp(BATCH, top)[:, None, None, None]
    return (base * jnp.sqrt(rising)).reshape(BATCH, CANVAS * IMG * 3 // 128, 128).astype(jnp.bfloat16)


def draw_stem(key, part):
    key = jax.random.fold_in(key, 2)
    noise = jax.random.normal(key, (STEM_LEN,), jnp.float32)
    scales = []
    used = 0
    for start, fan_in, chan_out in stem_layout_drawn((3, C1, C2, C3, C4), D):
        scales.append(jnp.full((fan_in * chan_out,), fan_in ** (-0.5), jnp.float32))
        used = used + fan_in * chan_out
    scales.append(jnp.full((STEM_LEN - used,), 0.05, jnp.float32))
    return noise * jnp.concatenate(scales)


def draw_small(key, part):
    key = jax.random.fold_in(key, 3)
    pieces = []
    used = 0
    for name, start, length in small_layout_drawn(D, FF, (C1, C2, C3, C4), TOK, CLASSES):
        noise = jax.random.normal(jax.random.fold_in(key, start + 7), (length,), jnp.float32)
        if name in ('norm1_gain', 'norm2_gain', 'final_gain'):
            pieces.append(jnp.linspace(0.6, 1.8, length, dtype=jnp.float32) * (1.0 + 0.1 * noise))
        elif name == 'bn_gain':
            pieces.append(1.0 + 0.15 * noise)
        elif name == 'class_token':
            pieces.append(noise)
        elif name == 'position':
            pieces.append(0.5 * noise)
        else:
            pieces.append(0.2 * noise)
        used = used + length
    pieces.append(0.2 * jax.random.normal(jax.random.fold_in(key, 5), (SMALL_LEN - used,), jnp.float32))
    return jnp.concatenate(pieces)


def draw_block(key, part):
    key = jax.random.fold_in(key, 4)
    noise = jax.random.normal(key, (3, D, FF), jnp.float32)
    slot = jax.lax.broadcasted_iota(jnp.int32, (3, D, FF), 0)
    column = jax.lax.broadcasted_iota(jnp.int32, (3, D, FF), 2)
    first = jnp.where(column < 3 * D, D ** (-0.5), 4.0 * D ** (-0.5))
    scale = jnp.where(slot == 0, first, jnp.where(slot == 1, D ** (-0.5), FF ** (-0.5)))
    return noise * scale


def touch_ends(array, stream_key, least, top_value):
    longest = array.shape.index(max(array.shape))
    spots = []
    for shift in (0, 1):
        where = [jax.random.randint(jax.random.fold_in(stream_key, axis), (), 0, length) for axis, length in enumerate(array.shape)]
        where[longest] = (where[longest] + shift) % array.shape[longest]
        spots.append(tuple(where))
    return array.at[spots[0]].set(least).at[spots[1]].set(top_value)


def steps_of(stream_key, dims, cuts, low, top_value):
    def one(dim, shards_of):
        steps = jax.random.uniform(jax.random.fold_in(jax.random.fold_in(stream_key, 6), dim), (shards_of,), jnp.float32, low / len(cuts), top_value / len(cuts))
        return jnp.repeat(jnp.exp(steps), dims[dim] // shards_of).reshape((-1,) + (1,) * (len(dims) - dim - 1))

    loudness = one(*cuts[0])
    for cut in cuts[1:]:
        loudness = loudness * one(*cut)
    return loudness


def centred(key, extent, spread, reach, cuts=(), kind=jnp.bfloat16):
    array = spread * jax.random.normal(key, extent, jnp.float32)
    if cuts:
        array = array * steps_of(key, extent, cuts, -0.22, 0.18)
    return jnp.clip(array, -reach, reach).astype(kind)


def setup_inputs(seed: int = 0) -> dict:
    keys = jax.random.split(jax.random.key(seed), 15)
    pixels = draw_pixels(jax.random.fold_in(keys[14], 71), 0)
    labels = touch_ends(jax.random.randint(keys[1], (BATCH, N_DP), 0, CLASSES), jax.random.fold_in(keys[1], 1), 0, CLASSES - 1).astype(jnp.int32)
    stem = draw_stem(jax.random.fold_in(keys[14], 71), 0)
    stem_first = centred(keys[3], (STEM_LEN,), (0.111 / PARAMS ** 0.5), 0.00021362305, ((0, 32),), jnp.float32)
    stem_second = jnp.clip(jnp.exp(math.log(8.715516086610364e-10) - 2.7725887 * jax.random.uniform(keys[4], (STEM_LEN,), jnp.float32) ** steps_of(keys[4], (STEM_LEN,), ((0, 32),), -0.2, 0.2)), 5.4471975541314777e-11, 8.715516086610364e-10)
    small = draw_small(jax.random.fold_in(keys[14], 71), 0)
    small_first = centred(keys[6], (SMALL_LEN,), (0.111 / PARAMS ** 0.5), 0.00021362305, ((0, 32),), jnp.float32)
    small_second = jnp.clip(jnp.exp(math.log(8.715516086610364e-10) - 2.7725887 * jax.random.uniform(keys[7], (SMALL_LEN,), jnp.float32) ** steps_of(keys[7], (SMALL_LEN,), ((0, 32),), -0.2, 0.2)), 5.4471975541314777e-11, 8.715516086610364e-10)
    block = draw_block(jax.random.fold_in(keys[14], 71), 0)
    block_first = centred(keys[9], (3, D, FF), (0.111 / PARAMS ** 0.5), 0.00021362305, ((1, 16), (2, 2)), jnp.float32)
    block_second = jnp.clip(jnp.exp(math.log(8.715516086610364e-10) - 2.7725887 * jax.random.uniform(keys[10], (3, D, FF), jnp.float32) ** steps_of(keys[10], (3, D, FF), ((1, 16), (2, 2)), -0.2, 0.2)), 5.4471975541314777e-11, 8.715516086610364e-10)
    head = centred(keys[11], (D, CLASSES), D ** -0.5, 0.21875, ((0, 16), (1, 2)), jnp.float32)
    head_first = centred(keys[12], (D, CLASSES), (0.111 / PARAMS ** 0.5), 0.00021362305, ((0, 16), (1, 2)), jnp.float32)
    head_second = jnp.clip(jnp.exp(math.log(8.715516086610364e-10) - 2.7725887 * jax.random.uniform(keys[13], (D, CLASSES), jnp.float32) ** steps_of(keys[13], (D, CLASSES), ((0, 16), (1, 2)), -0.2, 0.2)), 5.4471975541314777e-11, 8.715516086610364e-10)
    return {"pixels": pixels, "labels": labels, "stem": stem, "stem_first": stem_first, "stem_second": stem_second, "small": small, "small_first": small_first, "small_second": small_second, "block": block, "block_first": block_first, "block_second": block_second, "head": head, "head_first": head_first, "head_second": head_second}


beta_one = 0.9
beta_two = 0.999
adam_epsilon = 1e-08
decay_rate = 0.05
clip_norm = 1.0
rate_stem = 0.05
rate_small = 0.5
rate_block = 0.05
rate_head = 0.05
batch_epsilon = 1e-05
layer_epsilon = 1e-06
smoothing = 0.1
highest = lax.Precision.HIGHEST

@jax.custom_vjp
def low(v):
    return lax.optimization_barrier(v.astype(jnp.bfloat16)).astype(jnp.float32)

@jax.custom_vjp
def low_back(v):
    return v

def low_keep(v):
    return (low(v), None)

def low_pass(kept, grad):
    return (grad,)

def back_keep(v):
    return (v, None)

def back_low(kept, grad):
    return (low(grad),)
low.defvjp(low_keep, low_pass)
low_back.defvjp(back_keep, back_low)

def small_layout(width, hidden, chans, tokens, classes):
    names = (('bn_gain', sum(chans)), ('bn_bias', sum(chans)), ('proj_bias', width), ('class_token', width), ('position', tokens * width), ('norm1_gain', width), ('norm1_bias', width), ('query_bias', width), ('value_bias', width), ('out_bias', width), ('norm2_gain', width), ('norm2_bias', width), ('hidden_bias', hidden), ('mlp_bias', width), ('final_gain', width), ('final_bias', width), ('head_bias', classes))
    layout = []
    offset = 0
    for name, length in names:
        layout.append((name, offset, length))
        offset = offset + length
    return layout

def stem_layout(chans, width):
    layout = []
    offset = 0
    for level in range(4):
        layout.append((offset, 9 * chans[level], chans[level + 1]))
        offset = offset + 9 * chans[level] * chans[level + 1]
    layout.append((offset, chans[4], width))
    return layout

def layer_norm(values, gain, bias):
    mean = lax.optimization_barrier(jnp.mean(values, -1, keepdims=True))
    variance = lax.optimization_barrier(jnp.mean(jnp.square(values - mean), -1, keepdims=True))
    return (values - mean) * lax.rsqrt(variance + layer_epsilon) * gain + bias

def forward(stem, small, block, head, images, targets):
    stem, small, block, head = (low(stem), low(small), low(block), low(head))
    chans = (3, C1, C2, C3, C4)
    table = {}
    for name, start, length in small_layout(D, FF, chans[1:], TOK, CLASSES):
        table[name] = (start, length)

    def part(name):
        return small[table[name][0]:table[name][0] + table[name][1]]
    layout = stem_layout(chans, D)
    activation = images
    first = 0
    for level in range(4):
        start, fan_in, chan_out = layout[level]
        kernel = stem[start:start + fan_in * chan_out].reshape(3, 3, chans[level], chan_out)
        conv = low_back(lax.conv_general_dilated(activation, kernel, (2, 2), ((1, 0), (1, 0)), dimension_numbers=('NHWC', 'HWIO', 'NHWC'), precision=highest))
        mean = lax.optimization_barrier(jnp.mean(conv, (0, 1, 2)))
        variance = lax.optimization_barrier(jnp.mean(jnp.square(conv - mean), (0, 1, 2)))
        normed = (conv - mean) * lax.rsqrt(variance + batch_epsilon) * part('bn_gain')[first:first + chan_out] + part('bn_bias')[first:first + chan_out]
        activation = low(jax.nn.gelu(normed))
        first = first + chan_out
    count = activation.shape[0]
    start, fan_in, width = layout[4]
    projection = stem[start:start + fan_in * width].reshape(fan_in, width)
    patch = low_back(jnp.einsum('npc,cd->npd', activation.reshape(count, NP, C4), projection, precision=highest) + part('proj_bias'))
    class_rows = jnp.broadcast_to(part('class_token'), (count, 1, D))
    residual = jnp.concatenate([class_rows, patch], 1) + part('position').reshape(TOK, D)
    normed = low(layer_norm(residual, part('norm1_gain'), part('norm1_bias')))
    mixing = block[0]
    bias = jnp.concatenate([part('query_bias'), jnp.zeros((D,), jnp.float32), part('value_bias')])
    projected = jnp.einsum('ntd,dk->ntk', normed, mixing[:, :3 * D], precision=highest) + bias
    projected = low(low_back(projected)).reshape(count, TOK, 3, HEADS, HEAD_DIM)
    scale = HEAD_DIM ** (-0.5)
    scores = low_back(jnp.einsum('bqhd,bkhd->bhqk', projected[:, :, 0], projected[:, :, 1], precision=highest) * scale)
    probs = low(jax.nn.softmax(scores, -1))
    mixed = jnp.einsum('bhqk,bkhd->bqhd', probs, projected[:, :, 2], precision=highest).reshape(count, TOK, D)
    mixed = low(low_back(mixed))
    residual = residual + low_back(jnp.einsum('nti,oi->nto', mixed, mixing[:, 3 * D:], precision=highest) + part('out_bias'))
    normed = low(layer_norm(residual, part('norm2_gain'), part('norm2_bias')))
    hidden_in = low_back(jnp.einsum('ntd,df->ntf', normed, block[1], precision=highest) + part('hidden_bias'))
    hidden = low(jax.nn.gelu(hidden_in))
    residual = residual + low_back(jnp.einsum('ntf,df->ntd', hidden, block[2], precision=highest) + part('mlp_bias'))
    pooled = lax.optimization_barrier(jnp.mean(residual, 1))
    final = low(layer_norm(pooled, part('final_gain'), part('final_bias')))
    logits = low_back(jnp.dot(final, head, precision=highest) + part('head_bias'))
    log_probs = jax.nn.log_softmax(logits, -1)
    picked = jnp.take_along_axis(log_probs, targets[:, None], 1)[:, 0]
    return -jnp.sum((1.0 - smoothing) * picked + smoothing * lax.optimization_barrier(jnp.mean(log_probs, -1)))

def adam_step(weight, first, second, grad, factor, rate):
    grad = grad * factor
    first = beta_one * first + (1.0 - beta_one) * grad
    second = beta_two * second + (1.0 - beta_two) * grad * grad
    first_fixed = first / (1.0 - beta_one ** STEP)
    second_fixed = second / (1.0 - beta_two ** STEP)
    return (weight - rate * (first_fixed / (jnp.sqrt(second_fixed) + adam_epsilon) + decay_rate * weight), first, second)

def reference(pixels, labels, stem, stem_first, stem_second, small, small_first, small_second, block, block_first, block_second, head, head_first, head_second):
    canvas = jnp.roll(pixels.astype(jnp.float32).reshape(BATCH, CANVAS, IMG, 3), -(IMG // 2), axis=1)
    images = canvas.reshape(BATCH * N_DP, IMG, IMG, 3)
    targets = labels.reshape(-1).astype(jnp.int32)

    def loss_of(stem_w, small_w, block_w, head_w):
        return forward(stem_w, small_w, block_w, head_w, images, targets)
    loss, pull = jax.vjp(loss_of, stem, small, block, head)
    grad_stem, grad_small, grad_block, grad_head = pull(jnp.ones((), jnp.float32))
    squares = jnp.sum(grad_stem * grad_stem) + jnp.sum(grad_small * grad_small) + jnp.sum(grad_block * grad_block) + jnp.sum(grad_head * grad_head)
    grad_norm = jnp.sqrt(squares)
    factor = jnp.minimum(1.0, clip_norm / grad_norm)
    stem_new = adam_step(stem, stem_first, stem_second, grad_stem, factor, rate_stem)
    small_new = adam_step(small, small_first, small_second, grad_small, factor, rate_small)
    block_new = adam_step(block, block_first, block_second, grad_block, factor, rate_block)
    head_new = adam_step(head, head_first, head_second, grad_head, factor, rate_head)
    return (stem_new[0], stem_new[1], stem_new[2], small_new[0], small_new[1], small_new[2], block_new[0], block_new[1], block_new[2], head_new[0], head_new[1], head_new[2], loss, grad_norm)
```

```python
import functools

import jax
import jax.numpy as jnp
from jax import lax
from jax.experimental import pallas as pl
from jax.experimental.pallas import tpu as pltpu
from jax.sharding import PartitionSpec as P

D = 768
HEADS = 12
HEAD_DIM = 64
FF = 3072
CLASSES = 1000
C1 = 48
C2 = 96
C3 = 192
C4 = 384
STEP = 10
TOK = 197
SIDE = 14
T = 16 * SIDE
W = 384
CHANS = (3, C1, C2, C3, C4)

beta_one = 0.9
beta_two = 0.999
adam_epsilon = 1e-08
decay_rate = 0.05
clip_norm = 1.0
rate_stem = 0.05
rate_small = 0.5
rate_block = 0.05
rate_head = 0.05
batch_epsilon = 1e-05
layer_epsilon = 1e-06
smoothing = 0.1

bf16 = jnp.bfloat16
f32 = jnp.float32

STEM_SHIFT = 112
SMALL_SHIFT = 96
ROW_W2 = 11
ROW_W3 = ROW_W2 + 9 * C1 * C2 // 128
ROW_W4 = ROW_W3 + 9 * C2 * C3 // 128
ROW_WP = ROW_W4 + 9 * C3 * C4 // 128
STEM_ROWS = ROW_WP + C4 * D // 128
SMALL_NAMES = (
    ("proj_bias", 6),
    ("class_token", 6),
    ("position", 6 * TOK),
    ("norm1_gain", 6),
    ("norm1_bias", 6),
    ("query_bias", 6),
    ("value_bias", 6),
    ("out_bias", 6),
    ("norm2_gain", 6),
    ("norm2_bias", 6),
    ("hidden_bias", 24),
    ("mlp_bias", 6),
    ("final_gain", 6),
    ("final_bias", 6),
    ("head_bias", 8),
)
SMALL_AT = {}
_row = 12
for _name, _rows in SMALL_NAMES:
    SMALL_AT[_name] = _row
    _row += _rows
SMALL_ROWS = _row
VEC_NAMES = (
    "proj_bias",
    "norm1_gain",
    "norm1_bias",
    "query_bias",
    "value_bias",
    "out_bias",
    "norm2_gain",
    "norm2_bias",
    "mlp_bias",
    "final_gain",
    "final_bias",
)
VEC = {name: index for index, name in enumerate(VEC_NAMES)}
VEC_HIDDEN = 12


def dot(a, b):
    return jnp.dot(a, b, preferred_element_type=f32)


def dot_nt(a, b):
    return lax.dot_general(a, b, (((1,), (1,)), ((), ())), preferred_element_type=f32)


def dot_tn(a, b):
    return lax.dot_general(a, b, (((0,), (0,)), ((), ())), preferred_element_type=f32)


GELU_A = 0.7978845608028654
GELU_B = 0.044715


def gelu(x):
    return 0.5 * x * (1.0 + jnp.tanh(GELU_A * (x + GELU_B * x * x * x)))


def gelu_slope(x):
    t = jnp.tanh(GELU_A * (x + GELU_B * x * x * x))
    return 0.5 * (1.0 + t) + 0.5 * x * (1.0 - t * t) * GELU_A * (1.0 + 3.0 * GELU_B * x * x)


def up16(n):
    return -(-n // 16) * 16


def slot_index():
    return lax.broadcasted_iota(jnp.int32, (T, 1), 0)


def patch_mask():
    return ((slot_index() & 15) < SIDE).astype(f32)


def token_mask():
    p = slot_index()
    return (((p & 15) < SIDE) | (p == SIDE)).astype(f32)


def fold_phases(x, chan):
    step = W // 2
    while step >= chan:
        x = x + jnp.concatenate([x[:, step:], x[:, :step]], 1)
        step //= 2
    return x


def bn_stats(st_ref, count, chan):
    tot = fold_phases(jnp.sum(st_ref[:, 0:2, :], 0), chan)
    mean = tot[0:1] / count
    inv = lax.rsqrt(tot[1:2] / count - mean * mean + batch_epsilon)
    return mean, inv


def shift_lanes(x, s):
    lane = lax.broadcasted_iota(jnp.int32, x.shape, 1)
    row = lax.broadcasted_iota(jnp.int32, x.shape, 0)
    moved = pltpu.roll(x, s, 1)
    before = jnp.where(row == 0, 0.0, pltpu.roll(moved, 1, 0))
    return jnp.where(lane >= s, moved, before)


def pack_kernel(at_ref, stem_ref, small_ref, out_ref):
    rows = stem_ref.shape[0]
    out_ref[0:rows, :] = shift_lanes(stem_ref[...], at_ref[0]).astype(bf16)
    out_ref[rows:, :] = shift_lanes(small_ref[...], at_ref[1]).astype(bf16)


def flat_lanes(ref, row, count):
    return jnp.concatenate([ref[row + k : row + k + 1, :] for k in range(count)], 1)


def assemble_kernel(parts, mp, stem_len, small_len, rows_stem, rows_small, at_ref, *refs):
    pieces = refs[:parts]
    t1_ref, t2_ref, t3_ref, t4_ref, wp_ref, bn_ref, vec_ref, hb_ref, pos_ref = refs[parts : parts + 9]
    frame, table, s1, s2, s3a, s3b, u1, u2, u3 = refs[parts + 9 :]
    frame[...] = jnp.zeros_like(frame)
    table[...] = jnp.zeros_like(table)
    for index, ref in enumerate(pieces):
        mv = at_ref[index]

        def put(d, carry):
            owner = d * mp + mv
            a = (owner * stem_len + STEM_SHIFT) // 128
            frame[pl.ds(a, rows_stem), :] += ref[d, 0:rows_stem, :].astype(f32)
            b = (owner * small_len + SMALL_SHIFT) // 128
            table[pl.ds(b, rows_small), :] += ref[d, rows_stem : rows_stem + rows_small, :].astype(f32)
            return carry

        lax.fori_loop(0, ref.shape[0], put, 0)
    s1[...] = jnp.zeros_like(s1)
    flat = flat_lanes(frame, 0, ROW_W2)
    for k in range(27):
        s1[k : k + 1, 0:C1] = flat[:, STEM_SHIFT + 48 * k : STEM_SHIFT + 48 * k + 48]
    u1[...] = jnp.zeros_like(u1)
    for tap in range(3):
        for j in range(8):
            cols = slice(j * C1, (j + 1) * C1)
            if j == 0:
                u1[tap * 64 + 48 : tap * 64 + 51, cols] = s1[tap * 9 : tap * 9 + 3, 0:C1]
                u1[tap * 64 : tap * 64 + 6, cols] = s1[tap * 9 + 3 : tap * 9 + 9, 0:C1]
            else:
                at = tap * 64 + 6 * j - 3
                u1[at : at + 9, cols] = s1[tap * 9 : tap * 9 + 9, 0:C1]
    t1_ref[...] = u1[...].astype(bf16)
    q = 9 * C1 // 4
    wide = jnp.concatenate([frame[pl.ds(ROW_W2 + k, q, stride=3), :] for k in range(3)], 1)
    for k in range(4):
        s2[pl.ds(k, q, stride=4), 0:C2] = wide[:, k * C2 : (k + 1) * C2]
    q = 9 * C2 // 2
    wide = jnp.concatenate([frame[pl.ds(ROW_W3 + k, q, stride=3), :] for k in range(3)], 1)
    for k in range(2):
        part = wide[:, k * C3 : (k + 1) * C3]
        s3a[pl.ds(k, q, stride=2), :] = part[:, 0:128]
        s3b[pl.ds(k, q, stride=2), 0 : C3 - 128] = part[:, 128:C3]
    for ref, chan_in, chan_out, src, u in (
        (t2_ref, C1, C2, (s2,), u2),
        (t3_ref, C2, C3, (s3a, s3b), u3),
    ):
        for tap in range(3):
            u[...] = jnp.zeros_like(u)
            base = tap * 3 * chan_in
            for j in range(W // chan_out):
                for k, s in enumerate(src):
                    width = min(128, chan_out - 128 * k)
                    cols = slice(j * chan_out + 128 * k, j * chan_out + 128 * k + width)
                    if j == 0:
                        u[W : W + chan_in, cols] = s[base : base + chan_in, 0:width]
                        u[0 : 2 * chan_in, cols] = s[base + chan_in : base + 3 * chan_in, 0:width]
                    else:
                        at = (2 * j - 1) * chan_in
                        u[at : at + 3 * chan_in, cols] = s[base : base + 3 * chan_in, 0:width]
            ref[tap] = u[...].astype(bf16)
    for tap in range(3):
        rows = 3 * C3
        for k in range(3):
            lanes = slice(k * 128, (k + 1) * 128)
            at = ROW_W4 + k + 3 * tap * rows
            t4_ref[tap, 0 : 2 * C3, lanes] = frame[pl.ds(at + 3 * C3, 2 * C3, stride=3), :].astype(bf16)
            t4_ref[tap, 2 * C3 : 3 * C3, lanes] = frame[pl.ds(at, C3, stride=3), :].astype(bf16)
    for k in range(6):
        lanes = slice(k * 128, (k + 1) * 128)
        wp_ref[:, lanes] = frame[pl.ds(ROW_WP + k, C4, stride=6), :].astype(bf16)
    flat = flat_lanes(table, 0, 12)
    first = SMALL_SHIFT
    for level in range(4):
        chan = CHANS[level + 1]
        for which in range(2):
            at = first + which * (C1 + C2 + C3 + C4)
            part = flat[:, at : at + chan]
            row = 2 * level + which
            for j in range(W // chan):
                bn_ref[row : row + 1, j * chan : (j + 1) * chan] = part
        first += chan
    vec_ref[...] = jnp.zeros_like(vec_ref)
    for name, index in VEC.items():
        vec_ref[index : index + 1, :] = flat_lanes(table, SMALL_AT[name], 6)
    for k in range(4):
        row = VEC_HIDDEN + k
        vec_ref[row : row + 1, :] = flat_lanes(table, SMALL_AT["hidden_bias"] + 6 * k, 6)
    flat = flat_lanes(table, SMALL_AT["head_bias"], 8)
    hb_ref[...] = jnp.zeros_like(hb_ref)
    hb_ref[:, 0:500] = flat[:, 0:500]
    hb_ref[:, 512:1012] = flat[:, 500:1000]
    pos_ref[...] = jnp.zeros_like(pos_ref)
    at = SMALL_AT["position"]
    for k in range(6):
        lanes = slice(k * 128, (k + 1) * 128)
        for r in range(SIDE):
            rows = table[pl.ds(at + k + 6 * (1 + SIDE * r), SIDE, stride=6), :]
            pos_ref[16 * r : 16 * r + SIDE, lanes] = rows
        mark = SMALL_AT["class_token"] + k
        pos_ref[SIDE : SIDE + 1, lanes] = table[mark : mark + 1, :] + table[at + k : at + k + 1, :]


def conv1_kernel(own_ref, next_ref, t1_ref, xk_ref, out_ref, st_ref, flat, chunks, xe):
    half = own_ref.shape[0]
    flat[0:half, :] = own_ref[...].astype(f32)
    flat[half : 2 * half, :] = next_ref[...].astype(f32)
    n = 2 * half // 3
    wide = jnp.concatenate([flat[pl.ds(k, n, stride=3), :] for k in range(3)], 1)
    for j in range(8):
        chunks[pl.ds(j, n, stride=8), 0:48] = wide[:, 48 * j : 48 * j + 48]
    mask = patch_mask()
    lane = lax.broadcasted_iota(jnp.int32, (T, 64), 1)

    def spread(i, carry):
        rows = [chunks[pl.ds(16 * SIDE * r + SIDE * i, 16), 0:64] for r in range(SIDE)]
        x = jnp.where(lane < 48, jnp.concatenate(rows, 0), 0.0) * mask
        left = pltpu.roll(jnp.concatenate([x, x], 1), 3, 1)[:, 0:64]
        left = jnp.where((lane >= 48) & (lane < 51), pltpu.roll(left, 1, 0), 0.0)
        xe[i + 1] = (x + left).astype(bf16)
        return carry

    chunks[pl.ds(n * 8, 16), :] = jnp.zeros((16, 128), f32)
    lax.fori_loop(0, 16, spread, 0)
    last = xe[16]
    xe[0] = jnp.concatenate([jnp.zeros((16, 64), bf16), last[: T - 16]], 0)
    weights = t1_ref[...]

    def step(i, carry):
        first, second = carry
        x = jnp.concatenate([xe[2 * i], xe[2 * i + 1], xe[2 * i + 2]], 1)
        xk_ref[i] = x
        y = dot(x, weights)
        out_ref[i] = y
        ym = y * mask
        return first + jnp.sum(ym, 0, keepdims=True), second + jnp.sum(ym * y, 0, keepdims=True)

    zero = jnp.zeros((1, W), f32)
    first, second = lax.fori_loop(0, 8, step, (zero, zero))
    st = jnp.concatenate([first, second], 0)
    st_ref[...] = jnp.broadcast_to(st[None], st_ref.shape)


def conv_kernel(level, count, c_ref, stin_ref, bn_ref, t_ref, ax_ref, out_ref, st_ref):
    chan = CHANS[level]
    rows = c_ref.shape[0]
    mean, inv = bn_stats(stin_ref, count, chan)
    gain = bn_ref[2 * level - 2 : 2 * level - 1, :]
    bias = bn_ref[2 * level - 1 : 2 * level, :]
    mask = patch_mask()

    def activate(i, carry):
        a = gelu((c_ref[i] - mean) * inv * gain + bias) * mask
        left = pltpu.roll(a[:, W - chan :], 1, 0)
        ax_ref[i + 1, :, 0:W] = a.astype(bf16)
        ax_ref[i + 1, :, W:] = left.astype(bf16)
        return carry

    lax.fori_loop(0, rows, activate, 0)
    last = ax_ref[rows]
    ax_ref[0] = jnp.concatenate([jnp.zeros((16, W + chan), bf16), last[: T - 16]], 0)

    def step(i, carry):
        first, second = carry
        y = dot(ax_ref[2 * i], t_ref[0])
        y = y + dot(ax_ref[2 * i + 1], t_ref[1])
        y = y + dot(ax_ref[2 * i + 2], t_ref[2])
        out_ref[i] = y
        ym = y * mask
        return first + jnp.sum(ym, 0, keepdims=True), second + jnp.sum(ym * y, 0, keepdims=True)

    zero = jnp.zeros((1, W), f32)
    first, second = lax.fori_loop(0, rows // 2, step, (zero, zero))
    st = jnp.concatenate([first, second], 0)
    st_ref[...] = jnp.broadcast_to(st[None], st_ref.shape)


def layer_norm(x):
    centered = x - jnp.mean(x, -1, keepdims=True)
    inv = lax.rsqrt(jnp.mean(centered * centered, -1, keepdims=True) + layer_epsilon)
    return centered * inv, inv


def layer_norm_back(dy, s, inv, gain):
    scaled = dy * gain
    inner = scaled - jnp.mean(scaled, -1, keepdims=True)
    return inv * (inner - s * jnp.mean(scaled * s, -1, keepdims=True))


def colsum(x):
    return jnp.sum(x, 0, keepdims=True)


def block_kernel(
    count,
    label_ref,
    c_ref,
    st_ref,
    bn_ref,
    wp_ref,
    pos_ref,
    vec_ref,
    hb_ref,
    g_ref,
    gr_ref,
    bn4_ref,
    sums_ref,
    gv_ref,
    gpos_ref,
    dwp_ref,
    ghb_ref,
    bo_ref,
    fin_ref,
    hs_ref,
    bl_ref,
    loss_ref,
    wa,
    wu,
    wd,
    wh,
    sems,
    a4,
    x0,
    n1,
    qkv,
    probs,
    mixed,
    n2t,
    pre,
    acc,
    bqkv,
):
    copies = []
    for m in range(2):
        for k, (ref, at, size) in enumerate(
            ((wa, 0, 1536), (wu, 1536, 1536), (wd, 3072, 1536), (wh, 4608, 512))
        ):
            copy = pltpu.make_async_copy(
                g_ref.at[:, m, :, at : at + size], ref.at[m], sems.at[4 * m + k]
            )
            copy.start()
            copies.append(copy)

    def vec(name):
        return vec_ref[VEC[name] : VEC[name] + 1, :]

    mask = patch_mask()
    valid = token_mask()
    key = lax.broadcasted_iota(jnp.int32, (1, T), 1)
    key_bias = jnp.where(((key & 15) < SIDE) | (key == SIDE), 0.0, -1e30)

    def normed4():
        mean, inv = bn_stats(st_ref, count, C4)
        s = (c_ref[0] - mean) * inv
        return s, s * bn_ref[6:7, :] + bn_ref[7:8, :]

    s4, y4 = normed4()
    a4[...] = (gelu(y4) * mask).astype(bf16)
    x0[...] = (dot(a4[...], wp_ref[...]) + vec("proj_bias")) * mask + pos_ref[...]
    s1, i1 = layer_norm(x0[...])
    n1[...] = (s1 * vec("norm1_gain") + vec("norm1_bias")).astype(bf16)
    copies[0].wait()
    copies[4].wait()

    def tile(ref, m, at, size=256):
        return ref[m, :, :, pl.ds(at, size)].reshape(D, size)

    for part in range(9):
        y = dot(n1[...], tile(wa, part // 6, 256 * (part % 6)))
        lanes = slice(256 * (part % 3), 256 * (part % 3) + 256)
        if part < 3:
            y = y + vec("query_bias")[:, lanes]
        elif part >= 6:
            y = y + vec("value_bias")[:, lanes]
        qkv[:, 256 * part : 256 * part + 256] = y.astype(bf16)
    scale = HEAD_DIM**-0.5

    def attend(pair, carry):
        at = pl.multiple_of(pair * 128, 128)
        q = qkv[:, pl.ds(at, 128)]
        k = qkv[:, pl.ds(at + D, 128)]
        v = qkv[:, pl.ds(at + 2 * D, 128)]
        out = []
        for h in range(2):
            lanes = slice(64 * h, 64 * h + 64)
            scores = dot_nt(q[:, lanes], k[:, lanes]) * scale + key_bias
            e = jnp.exp(scores - jnp.max(scores, -1, keepdims=True))
            p = e / jnp.sum(e, -1, keepdims=True)
            probs[2 * pair + h] = p
            out.append(dot(p.astype(bf16), v[:, lanes]))
        mixed[:, pl.ds(at, 128)] = jnp.concatenate(out, 1).astype(bf16)
        return carry

    lax.fori_loop(0, HEADS // 2, attend, 0)
    att = [dot_nt(mixed[...], wa[1, :, :, D : 2 * D].reshape(D, D))]
    x1 = x0[...] + att[0] + vec("out_bias")
    mean_x1 = colsum(x1 * valid) / TOK
    s2, i2 = layer_norm(x1)
    n2 = (s2 * vec("norm2_gain") + vec("norm2_bias")).astype(bf16)
    n2t[...] = n2.T
    copies[1].wait()
    copies[5].wait()
    for m in range(2):

        def up(k, carry):
            at = pl.multiple_of(k * 256, 256)
            y = dot(n2, tile(wu, m, at))
            pre[m, :, pl.ds(at, 256)] = y
            return carry

        lax.fori_loop(0, 6, up, 0)
        for k in range(6):
            f = 1536 * m + 256 * k
            lanes = slice(256 * k, 256 * k + 256)
            row = VEC_HIDDEN + f // D
            y = pre[m, :, lanes] + vec_ref[row : row + 1, f % D : f % D + 256]
            pre[m, :, lanes] = y
            h = gelu(y).astype(bf16).astype(f32) * valid
            hs_ref[:, f : f + 256] = colsum(h)
    copies[2].wait()
    copies[6].wait()
    hs = hs_ref[...] / TOK
    high = hs.astype(bf16)
    low = (hs - high.astype(f32)).astype(bf16)
    out = jnp.zeros((1, D), f32)
    for m in range(2):
        lanes = slice(1536 * m, 1536 * m + 1536)
        both = jnp.concatenate(
            [jnp.broadcast_to(high[:, lanes], (8, 1536)), jnp.broadcast_to(low[:, lanes], (8, 1536))], 0
        )
        y = dot_nt(both, wd[m].reshape(D, 1536))
        out = out + y[0:1] + y[8:9]
    pooled = mean_x1 + out + vec("mlp_bias")
    s3, i3 = layer_norm(pooled)
    final = (s3 * vec("final_gain") + vec("final_bias")).astype(bf16)
    copies[3].wait()
    copies[7].wait()
    wide = jnp.broadcast_to(final, (16, D))
    logits = jnp.concatenate([dot(wide, wh[m].reshape(D, 512))[0:1] for m in range(2)], 1)
    lane = lax.broadcasted_iota(jnp.int32, (1, 1024), 1)
    real = (lane & 511) < CLASSES // 2
    logits = jnp.where(real, logits + hb_ref[...], -1e30)
    top = jnp.max(logits, -1, keepdims=True)
    log_probs = logits - top - jnp.log(jnp.sum(jnp.exp(logits - top), -1, keepdims=True))
    chosen = jnp.where(lane < 512, lane, lane - 512 + CLASSES // 2) == label_ref[0, 0]
    aim = jnp.where(chosen, 1.0 - smoothing, 0.0) + smoothing / CLASSES
    aim = jnp.where(real, aim, 0.0)
    loss = -jnp.sum(jnp.where(real, aim * log_probs, 0.0), keepdims=True)
    loss_ref[...] = jnp.broadcast_to(loss, loss_ref.shape)
    back_logits = jnp.where(real, jnp.exp(log_probs) - aim, 0.0).astype(bf16)
    bl_ref[...] = back_logits.astype(f32)
    ghb_ref[...] = back_logits.astype(f32)
    fin_ref[...] = final.astype(f32)
    wide = jnp.broadcast_to(back_logits, (16, 1024))
    back_final = (
        dot_nt(wide[:, 0:512], wh[0].reshape(D, 512)) + dot_nt(wide[:, 512:], wh[1].reshape(D, 512))
    )[0:1]
    gv_ref[...] = jnp.zeros_like(gv_ref)

    def put(name, value):
        gv_ref[VEC[name] : VEC[name] + 1, :] = value

    put("final_gain", back_final * s3)
    put("final_bias", back_final)
    back2 = layer_norm_back(back_final, s3, i3, vec("final_gain")) / TOK
    back_out = back2.astype(bf16)
    bo_ref[...] = back_out.astype(f32)
    put("mlp_bias", back_out.astype(f32) * TOK)
    wide = jnp.broadcast_to(back_out, (16, D))
    acc[...] = jnp.zeros_like(acc)
    for m in range(2):

        def down(k, carry):
            at = pl.multiple_of(k * 256, 256)
            back = dot(wide, tile(wd, m, at))[0:1]
            bp = (back * gelu_slope(pre[m, :, pl.ds(at, 256)]) * valid).astype(bf16)
            ghid = colsum(bp.astype(f32))
            pre[m, 0:1, pl.ds(at, 256)] = ghid
            grad = dot(n2t[...], bp)
            gr_ref[:, m, :, pl.ds(1536 + at, 256)] = grad.astype(bf16).reshape(16, 48, 256)
            acc[...] += dot_nt(bp, tile(wu, m, at))
            return carry

        lax.fori_loop(0, 6, down, 0)
        for k in range(2):
            row = VEC_HIDDEN + 2 * m + k
            gv_ref[row : row + 1, :] = pre[m, 0:1, D * k : D * k + D]
    back_n2 = acc[...]
    put("norm2_gain", colsum(back_n2 * s2))
    put("norm2_bias", colsum(back_n2))
    back1 = back2 * valid + layer_norm_back(back_n2, s2, i2, vec("norm2_gain"))
    back_att = back1.astype(bf16)
    put("out_bias", colsum(back_att.astype(f32)))
    back_att_t = back_att.T
    for k in range(3):
        lanes = slice(256 * k, 256 * k + 256)
        grad = dot(back_att_t, mixed[:, lanes])
        gr_ref[:, 1, :, D + 256 * k : D + 256 * k + 256] = grad.astype(bf16).reshape(16, 48, 256)
    acc[...] = dot(back_att, wa[1, :, :, D : 2 * D].reshape(D, D))

    def attend_back(pair, carry):
        at = pl.multiple_of(pair * 128, 128)
        q = qkv[:, pl.ds(at, 128)]
        k = qkv[:, pl.ds(at + D, 128)]
        v = qkv[:, pl.ds(at + 2 * D, 128)]
        bm = acc[:, pl.ds(at, 128)].astype(bf16)
        bq, bk, bv = [], [], []
        for h in range(2):
            lanes = slice(64 * h, 64 * h + 64)
            p = probs[2 * pair + h]
            bp = dot_nt(bm[:, lanes], v[:, lanes])
            bv.append(dot_tn(p.astype(bf16), bm[:, lanes]))
            inner = jnp.sum(bp * p, -1, keepdims=True)
            bs = (p * (bp - inner)).astype(bf16)
            bq.append(dot(bs, k[:, lanes]) * scale)
            bk.append(dot_tn(bs, q[:, lanes]) * scale)
        bqkv[:, pl.ds(at, 128)] = jnp.concatenate(bq, 1).astype(bf16)
        bqkv[:, pl.ds(at + D, 128)] = jnp.concatenate(bk, 1).astype(bf16)
        bqkv[:, pl.ds(at + 2 * D, 128)] = jnp.concatenate(bv, 1).astype(bf16)
        return carry

    lax.fori_loop(0, HEADS // 2, attend_back, 0)
    put("query_bias", colsum(bqkv[:, 0:D].astype(f32)))
    put("value_bias", colsum(bqkv[:, 2 * D :].astype(f32)))
    n1t = n1[...].T
    acc[...] = jnp.zeros_like(acc)
    for part in range(9):
        m, at = part // 6, 256 * (part % 6)
        b = bqkv[:, 256 * part : 256 * part + 256]
        gr_ref[:, m, :, at : at + 256] = dot(n1t, b).astype(bf16).reshape(16, 48, 256)
        acc[...] += dot_nt(b, tile(wa, m, at))
    back_n1 = acc[...]
    s1, i1 = layer_norm(x0[...])
    put("norm1_gain", colsum(back_n1 * s1))
    put("norm1_bias", colsum(back_n1))
    back0 = back1 + layer_norm_back(back_n1, s1, i1, vec("norm1_gain"))
    gpos_ref[...] = back0
    back_patch = (back0 * mask).astype(bf16)
    put("proj_bias", colsum(back_patch.astype(f32)))
    dwp_ref[...] = dot_tn(a4[...], back_patch)
    s4, y4 = normed4()
    bn4 = dot_nt(back_patch, wp_ref[...]) * gelu_slope(y4) * mask
    bn4_ref[0] = bn4
    sums_ref[...] = jnp.concatenate([colsum(bn4), colsum(bn4 * s4)], 0)


def conv_back_kernel(
    level,
    count,
    count_in,
    back_ref,
    tot_ref,
    c_ref,
    st_ref,
    ax_ref,
    t_ref,
    cin_ref,
    stin_ref,
    bn_ref,
    dw_ref,
    backin_ref,
    so_ref,
    ss_ref,
    g,
    dt,
):
    chan, chan_in = CHANS[level], CHANS[level - 1]
    rows = back_ref.shape[0]
    mask = patch_mask()
    mean, inv = bn_stats(st_ref, count, chan)
    gain = bn_ref[2 * level - 2 : 2 * level - 1, :]
    tot = fold_phases(jnp.sum(tot_ref[:, 0:2, :], 0), chan) / count

    def finish(i, carry):
        s = (c_ref[i] - mean) * inv
        g[i] = (inv * gain * (back_ref[i] - tot[0:1] - s * tot[1:2]) * mask).astype(bf16)
        return carry

    lax.fori_loop(0, rows, finish, 0)
    head = g[0]
    g[rows] = jnp.concatenate([head[16:], jnp.zeros((16, W), bf16)], 0)
    dt[...] = jnp.zeros_like(dt)

    def weights(i, carry):
        for tap in range(3):
            dt[tap] += dot_tn(ax_ref[2 * i + tap], g[i])
        return carry

    lax.fori_loop(0, rows, weights, 0)
    for tap in range(3):
        base = tap * 3 * chan_in
        for j in range(W // chan):
            for k in range(dw_ref.shape[0]):
                width = min(128, chan - 128 * k)
                cols = slice(j * chan + 128 * k, j * chan + 128 * k + width)
                if j == 0:
                    dw_ref[k, base : base + chan_in, 0:width] = dt[tap, W : W + chan_in, cols]
                    dw_ref[k, base + chan_in : base + 3 * chan_in, 0:width] = dt[
                        tap, 0 : 2 * chan_in, cols
                    ]
                else:
                    at = (2 * j - 1) * chan_in
                    dw_ref[k, base : base + 3 * chan_in, 0:width] += dt[
                        tap, at : at + 3 * chan_in, cols
                    ]
    mean, inv = bn_stats(stin_ref, count_in, chan_in)
    gain = bn_ref[2 * level - 4 : 2 * level - 3, :]
    bias = bn_ref[2 * level - 3 : 2 * level - 2, :]

    def through(q, p, carry):
        first, second = carry
        left = pltpu.roll(p[:, W:], T - 1, 0)
        p = jnp.concatenate([p[:, 0 : W - chan_in], p[:, W - chan_in : W] + left], 1)
        s = (cin_ref[q] - mean) * inv
        y = p * gelu_slope(s * gain + bias) * mask
        backin_ref[q] = y
        return first + colsum(y), second + colsum(y * s)

    def back(i, carry):
        carry = through(2 * i, dot_nt(g[i], t_ref[1]), carry)
        p = dot_nt(g[i], t_ref[2]) + dot_nt(g[i + 1], t_ref[0])
        return through(2 * i + 1, p, carry)

    zero = jnp.zeros((1, W), f32)
    first, second = lax.fori_loop(0, rows, back, (zero, zero))
    st = jnp.concatenate([first, second], 0)
    ss_ref[...] = st
    so_ref[...] = jnp.broadcast_to(st[None], so_ref.shape)


def grads_kernel(
    count,
    parts,
    mp,
    stem_len,
    small_len,
    rows_stem,
    rows_small,
    at_ref,
    back_ref,
    tot_ref,
    c_ref,
    st_ref,
    xk_ref,
    bn_ref,
    dw2_ref,
    dw3_ref,
    dw4_ref,
    dwp_ref,
    ss1_ref,
    ss2_ref,
    ss3_ref,
    ss4_ref,
    gv_ref,
    gpos_ref,
    ghb_ref,
    *refs,
):
    outs = refs[:parts]
    frame, table, dt, s1 = refs[parts:]
    mask = patch_mask()
    mean, inv = bn_stats(st_ref, count, C1)
    gain = bn_ref[0:1, :]
    tot = fold_phases(jnp.sum(tot_ref[:, 0:2, :], 0), C1) / count
    dt[...] = jnp.zeros_like(dt)

    def weights(i, carry):
        s = (c_ref[i] - mean) * inv
        g = (inv * gain * (back_ref[i] - tot[0:1] - s * tot[1:2]) * mask).astype(bf16)
        dt[...] += dot_tn(xk_ref[i], g)
        return carry

    lax.fori_loop(0, 8, weights, 0)
    s1[...] = jnp.zeros_like(s1)
    for tap in range(3):
        for j in range(8):
            cols = slice(j * C1, (j + 1) * C1)
            if j == 0:
                s1[9 * tap : 9 * tap + 3, 0:C1] += dt[tap * 64 + 48 : tap * 64 + 51, cols]
                s1[9 * tap + 3 : 9 * tap + 9, 0:C1] += dt[tap * 64 : tap * 64 + 6, cols]
            else:
                at = tap * 64 + 6 * j - 3
                s1[9 * tap : 9 * tap + 9, 0:C1] += dt[at : at + 9, cols]
    frame[ROW_W2 + 9 * C1 * C2 // 128 - 1 :, :] = jnp.zeros(
        (frame.shape[0] - (ROW_W2 + 9 * C1 * C2 // 128 - 1), 128), f32
    )
    line = [jnp.zeros((1, STEM_SHIFT), f32)] + [s1[k : k + 1, 0:C1] for k in range(27)]
    line = jnp.concatenate(line, 1)
    for k in range(ROW_W2):
        frame[k : k + 1, :] = line[:, 128 * k : 128 * k + 128]
    q = 9 * C1 // 4
    wide = jnp.concatenate([dw2_ref[0, pl.ds(k, q, stride=4), :][:, 0:C2] for k in range(4)], 1)
    for k in range(3):
        frame[pl.ds(ROW_W2 + k, q, stride=3), :] = wide[:, 128 * k : 128 * k + 128]
    q = 9 * C2 // 2
    wide = jnp.concatenate(
        [
            jnp.concatenate(
                [
                    dw3_ref[0, pl.ds(k, q, stride=2), :],
                    dw3_ref[1, pl.ds(k, q, stride=2), :][:, 0 : C3 - 128],
                ],
                1,
            )
            for k in range(2)
        ],
        1,
    )
    for k in range(3):
        frame[pl.ds(ROW_W3 + k, q, stride=3), :] = wide[:, 128 * k : 128 * k + 128]
    for k in range(3):
        frame[pl.ds(ROW_W4 + k, 9 * C3, stride=3), :] = dw4_ref[k]
    for k in range(6):
        frame[pl.ds(ROW_WP + k, C4, stride=6), :] = dwp_ref[:, 128 * k : 128 * k + 128]
    table[...] = jnp.zeros_like(table)
    line = [jnp.zeros((1, SMALL_SHIFT), f32)]
    for which in (1, 0):
        for ss_ref, chan in ((ss1_ref, C1), (ss2_ref, C2), (ss3_ref, C3), (ss4_ref, C4)):
            line.append(fold_phases(ss_ref[...], chan)[which : which + 1, 0:chan])
    line = jnp.concatenate(line, 1)
    for k in range(12):
        table[k : k + 1, :] = line[:, 128 * k : 128 * k + 128]
    for k in range(6):
        lanes = slice(128 * k, 128 * k + 128)
        for name, index in VEC.items():
            row = SMALL_AT[name] + k
            table[row : row + 1, :] = gv_ref[index : index + 1, lanes]
        for h in range(4):
            row = SMALL_AT["hidden_bias"] + 6 * h + k
            table[row : row + 1, :] = gv_ref[VEC_HIDDEN + h : VEC_HIDDEN + h + 1, lanes]
        at = SMALL_AT["position"] + k
        for r in range(SIDE):
            table[pl.ds(at + 6 * (1 + SIDE * r), SIDE, stride=6), :] = gpos_ref[
                16 * r : 16 * r + SIDE, lanes
            ]
        table[at : at + 1, :] = gpos_ref[SIDE : SIDE + 1, lanes]
        row = SMALL_AT["class_token"] + k
        table[row : row + 1, :] = gpos_ref[SIDE : SIDE + 1, lanes]
    line = jnp.concatenate(
        [ghb_ref[:, 0:500], ghb_ref[:, 512:1012], jnp.zeros((1, 24), f32)], 1
    )
    row = SMALL_AT["head_bias"]
    for k in range(8):
        table[row + k : row + k + 1, :] = line[:, 128 * k : 128 * k + 128]
    for index, ref in enumerate(outs):
        mv = at_ref[index]

        def take(d, carry):
            owner = d * mp + mv
            a = (owner * stem_len + STEM_SHIFT) // 128
            ref[d, 0:rows_stem, :] = frame[pl.ds(a, rows_stem), :].astype(bf16)
            b = (owner * small_len + SMALL_SHIFT) // 128
            ref[d, rows_stem : rows_stem + rows_small, :] = table[pl.ds(b, rows_small), :].astype(bf16)
            return carry

        lax.fori_loop(0, ref.shape[0], take, 0)


def unpack_kernel(stem_len, small_len, at_ref, x_ref, stem_ref, small_ref, sq_ref):
    rows = stem_ref.shape[0]
    total = jnp.sum(x_ref[...].astype(f32), 0)
    squares = jnp.zeros((1, 128), f32)
    for ref, part, s, length in (
        (stem_ref, total[0:rows], at_ref[0], stem_len),
        (small_ref, total[rows:], at_ref[1], small_len),
    ):
        lane = lax.broadcasted_iota(jnp.int32, part.shape, 1)
        row = lax.broadcasted_iota(jnp.int32, part.shape, 0)
        moved = pltpu.roll(part, 128 - s, 1)
        after = pltpu.roll(moved, part.shape[0] - 1, 0)
        y = jnp.where(lane < 128 - s, moved, after)
        y = jnp.where(row * 128 + lane < length, y, 0.0)
        ref[...] = y
        squares = squares + colsum(y * y)
    sq_ref[...] = squares


def call(kernel, outs, *args, scratch=(), smem=0, hbm=(), limit=48):
    specs = []
    for index, arg in enumerate(args):
        if index < smem:
            specs.append(pl.BlockSpec(memory_space=pltpu.SMEM))
        elif index in hbm:
            specs.append(pl.BlockSpec(memory_space=pl.ANY))
        else:
            specs.append(pl.BlockSpec(memory_space=pltpu.VMEM))
    return pl.pallas_call(
        kernel,
        out_shape=[jax.ShapeDtypeStruct(shape, dtype) for shape, dtype in outs],
        in_specs=specs,
        out_specs=[pl.BlockSpec(memory_space=pltpu.VMEM)] * len(outs),
        scratch_shapes=list(scratch),
        compiler_params=pltpu.CompilerParams(vmem_limit_bytes=limit * 1024 * 1024),
    )(*args)


def adam_step(weight, first, second, grad, factor, rate):
    grad = grad * factor
    first = beta_one * first + (1.0 - beta_one) * grad
    second = beta_two * second + (1.0 - beta_two) * grad * grad
    first_fixed = first / (1.0 - beta_one**STEP)
    second_fixed = second / (1.0 - beta_two**STEP)
    return (
        weight
        - rate * (first_fixed / (jnp.sqrt(second_fixed) + adam_epsilon) + decay_rate * weight),
        first,
        second,
    )


def local(
    pixels,
    labels,
    stem,
    stem_first,
    stem_second,
    small,
    small_first,
    small_second,
    block,
    block_first,
    block_second,
    head,
    head_first,
    head_second,
):
    dp, mp = lax.axis_size("dp"), lax.axis_size("mp")
    n = dp * mp
    me, mine = lax.axis_index("dp"), lax.axis_index("mp")
    owner = me * mp + mine
    stem_len, small_len = stem.shape[0], small.shape[0]
    rows_stem = up16(-(-(stem_len + 127) // 128))
    rows_small = up16(-(-(small_len + 127) // 128))
    rows = rows_stem + rows_small
    everyone = ("dp", "mp")

    def share(x):
        return lax.all_to_all(x, everyone, 0, 0)

    part = FF // mp
    cls = CLASSES // mp
    cls_pad = 512 // (mp // 2)
    packed = jnp.concatenate(
        [block[0], block[1], block[2], jnp.pad(head, ((0, 0), (0, cls_pad - cls)))], 1
    ).astype(bf16)
    gathered = lax.all_gather(packed, everyone, axis=0)
    if (dp, mp) == (16, 2):
        gathered = gathered.reshape(16, 2, 48, packed.shape[1])
    else:
        g = gathered.reshape(dp, mp, D // dp, packed.shape[1])
        g = jnp.transpose(g, (0, 2, 1, 3)).reshape(D, mp, -1)
        slots = [g[:, :, k * part : (k + 1) * part].reshape(D, 2, FF // 2) for k in range(3)]
        top = g[:, :, 3 * part : 3 * part + cls].reshape(D, 2, CLASSES // 2)
        slots.append(jnp.pad(top, ((0, 0), (0, 0), (0, 12))))
        g = jnp.concatenate(slots, 2).reshape(16, 48, 2, -1)
        gathered = jnp.transpose(g, (0, 2, 1, 3))

    strip = pixels.reshape(pixels.shape[1], 128)
    half = strip.shape[0] // 2
    pairs = [(source, (source + dp - 1) % dp) for source in range(dp)]
    lower = lax.ppermute(strip[:half], "dp", pairs)

    at = jnp.stack(
        [(owner * stem_len + STEM_SHIFT) % 128, (owner * small_len + SMALL_SHIFT) % 128]
    ).astype(jnp.int32)
    (piece,) = call(
        pack_kernel,
        [((rows, 128), bf16)],
        at,
        jnp.pad(stem, (0, rows_stem * 128 - stem_len)).reshape(rows_stem, 128),
        jnp.pad(small, (0, rows_small * 128 - small_len)).reshape(rows_small, 128),
        smem=1,
    )
    column = lax.all_to_all(jnp.broadcast_to(piece[None], (dp, rows, 128)), "dp", 0, 0)
    if mp == 2:
        swap = [(0, 1), (1, 0)]
        pieces = [column, lax.ppermute(column, "mp", swap)]
        which = jnp.stack([mine, 1 - mine]).astype(jnp.int32)
    else:
        columns = lax.all_gather(column, "mp", axis=0)
        pieces = [columns[k] for k in range(mp)]
        which = jnp.arange(mp, dtype=jnp.int32)
    frame_rows = (stem_len * n + STEM_SHIFT) // 128 + rows_stem + 16
    table_rows = (small_len * n + SMALL_SHIFT) // 128 + rows_small + 16
    frames = [pltpu.VMEM((frame_rows, 128), f32), pltpu.VMEM((table_rows, 128), f32)]
    t1, t2, t3, t4, wp, bn, vec, hb, pos = call(
        functools.partial(assemble_kernel, len(pieces), mp, stem_len, small_len, rows_stem, rows_small),
        [
            ((192, W), bf16),
            ((3, W + C1, W), bf16),
            ((3, W + C2, W), bf16),
            ((3, W + C3, W), bf16),
            ((C4, D), bf16),
            ((8, W), f32),
            ((16, D), f32),
            ((1, 1024), f32),
            ((T, D), f32),
        ],
        which,
        *pieces,
        smem=1,
        scratch=frames
        + [
            pltpu.VMEM((32, 128), f32),
            pltpu.VMEM((9 * C1, 128), f32),
            pltpu.VMEM((9 * C2, 128), f32),
            pltpu.VMEM((9 * C2, 128), f32),
            pltpu.VMEM((192, W), f32),
            pltpu.VMEM((W + C1, W), f32),
            pltpu.VMEM((W + C2, W), f32),
        ],
    )

    positions = SIDE * SIDE * n
    counts = [None, 64.0 * positions, 16.0 * positions, 4.0 * positions, 1.0 * positions]
    xk, conv, st = call(
        conv1_kernel,
        [((8, T, 192), bf16), ((8, T, W), f32), ((n, 2, W), f32)],
        strip[half:],
        lower,
        t1,
        scratch=[
            pltpu.VMEM((2 * half, 128), f32),
            pltpu.VMEM((16 * half // 3 + 16, 128), f32),
            pltpu.VMEM((17, T, 64), bf16),
        ],
    )
    convs = [None, conv]
    stats = [None, share(st)]
    inputs = [None, None]
    kernels = [None, t1, t2, t3, t4]
    for level in (2, 3, 4):
        r = 2 ** (4 - level)
        ax, conv, st = call(
            functools.partial(conv_kernel, level - 1, counts[level - 1]),
            [((2 * r + 1, T, W + CHANS[level - 1]), bf16), ((r, T, W), f32), ((n, 2, W), f32)],
            convs[level - 1],
            stats[level - 1],
            bn,
            kernels[level],
        )
        inputs.append(ax)
        convs.append(conv)
        stats.append(share(st))

    outs = call(
        functools.partial(block_kernel, counts[4]),
        [
            ((16, 2, 48, FF), bf16),
            ((1, T, W), f32),
            ((2, W), f32),
            ((16, D), f32),
            ((T, D), f32),
            ((C4, D), f32),
            ((1, 1024), f32),
            ((1, D), f32),
            ((1, D), f32),
            ((1, FF), f32),
            ((1, 1024), f32),
            ((1, 128), f32),
        ],
        labels,
        convs[4],
        stats[4],
        bn,
        wp,
        pos,
        vec,
        hb,
        gathered,
        smem=1,
        hbm=(8,),
        limit=60,
        scratch=[
            pltpu.VMEM((2, 16, 48, 1536), bf16),
            pltpu.VMEM((2, 16, 48, 1536), bf16),
            pltpu.VMEM((2, 16, 48, 1536), bf16),
            pltpu.VMEM((2, 16, 48, 512), bf16),
            pltpu.SemaphoreType.DMA((8,)),
            pltpu.VMEM((T, W), bf16),
            pltpu.VMEM((T, D), f32),
            pltpu.VMEM((T, D), bf16),
            pltpu.VMEM((T, 3 * D), bf16),
            pltpu.VMEM((HEADS, T, T), f32),
            pltpu.VMEM((T, D), bf16),
            pltpu.VMEM((D, T), bf16),
            pltpu.VMEM((2, T, 1536), f32),
            pltpu.VMEM((T, D), f32),
            pltpu.VMEM((T, 3 * D), bf16),
        ],
    )
    grads, back, sums4, gvec, gpos, dwp, ghb, bo, fin, hs, bl, loss = outs
    if (dp, mp) == (16, 2):
        grads = grads.reshape(n * 48, FF)
    else:
        g = jnp.transpose(grads, (0, 2, 1, 3)).reshape(D, 2, 2, FF // 2)
        g = jnp.transpose(g, (0, 2, 1, 3)).reshape(dp, D // dp, 2, mp, part)
        grads = jnp.transpose(g, (0, 3, 1, 2, 4)).reshape(n * (D // dp), 2 * part)
    owned = lax.psum_scatter(grads, everyone, scatter_dimension=0, tiled=True)
    grad_block01 = jnp.stack([owned[:, :part], owned[:, part:]], 0).astype(f32)

    rows_d = D // dp
    head_line = jnp.concatenate([bl[:, :500], bl[:, 512:1012]], 1).reshape(1, mp, cls)
    line = jnp.concatenate(
        [
            jnp.broadcast_to(bo.reshape(dp, 1, rows_d), (dp, mp, rows_d)),
            jnp.broadcast_to(fin.reshape(dp, 1, rows_d), (dp, mp, rows_d)),
            jnp.broadcast_to(hs.reshape(1, mp, part), (dp, mp, part)),
            jnp.broadcast_to(head_line, (dp, mp, cls)),
        ],
        2,
    ).reshape(n, -1)
    tail = -(-line.shape[1] // W)
    line = jnp.pad(line, ((0, 0), (0, tail * W - line.shape[1]))).reshape(n, tail, W)
    tot = share(jnp.concatenate([jnp.broadcast_to(sums4[None], (n, 2, W)), line], 1))
    line = tot[:, 2:].reshape(n, tail * W)
    bo_all, fin_all = line[:, :rows_d], line[:, rows_d : 2 * rows_d]
    hs_all, bl_all = line[:, 2 * rows_d : 2 * rows_d + part], line[:, 2 * rows_d + part : 2 * rows_d + part + cls]
    grad_down = lax.dot_general(
        bo_all, hs_all, (((0,), (0,)), ((), ())), precision=lax.Precision.HIGHEST
    )
    grad_head = lax.dot_general(
        fin_all, bl_all, (((0,), (0,)), ((), ())), precision=lax.Precision.HIGHEST
    )
    sums = [None, None, None, None, sums4]
    kernel_grads = [None] * 5
    for level in (4, 3, 2):
        r = 2 ** (4 - level)
        chan_in = CHANS[level - 1]
        dw, back, so, sums[level - 1] = call(
            functools.partial(conv_back_kernel, level, counts[level], counts[level - 1]),
            [
                ((-(-CHANS[level] // 128), 9 * chan_in, 128), f32),
                ((2 * r, T, W), f32),
                ((n, 2, W), f32),
                ((2, W), f32),
            ],
            back,
            tot,
            convs[level],
            stats[level],
            inputs[level],
            kernels[level],
            convs[level - 1],
            stats[level - 1],
            bn,
            scratch=[pltpu.VMEM((r + 1, T, W), bf16), pltpu.VMEM((3, W + chan_in, W), f32)],
        )
        kernel_grads[level] = dw
        tot = share(so)
    outs = call(
        functools.partial(
            grads_kernel, counts[1], len(pieces), mp, stem_len, small_len, rows_stem, rows_small
        ),
        [((dp, rows, 128), bf16)] * len(pieces),
        which,
        back,
        tot,
        convs[1],
        stats[1],
        xk,
        bn,
        kernel_grads[2],
        kernel_grads[3],
        kernel_grads[4],
        dwp,
        *sums[1:],
        gvec,
        gpos,
        ghb,
        smem=1,
        scratch=frames + [pltpu.VMEM((192, W), f32), pltpu.VMEM((32, 128), f32)],
    )
    if mp == 2:
        column = outs[0] + lax.ppermute(outs[1], "mp", swap)
    else:
        column = lax.psum_scatter(jnp.stack(outs, 0), "mp", scatter_dimension=0)
    column = lax.all_to_all(column, "dp", 0, 0)
    grad_stem, grad_small, squares = call(
        functools.partial(unpack_kernel, stem_len, small_len),
        [((rows_stem, 128), f32), ((rows_small, 128), f32), ((1, 128), f32)],
        at,
        column,
        smem=1,
    )
    grad_stem = grad_stem.reshape(-1)[:stem_len]
    grad_small = grad_small.reshape(-1)[:small_len]

    squares = (
        jnp.sum(squares)
        + jnp.sum(grad_block01 * grad_block01)
        + jnp.sum(grad_down * grad_down)
        + jnp.sum(grad_head * grad_head)
    )
    pair = jnp.concatenate([loss, jnp.broadcast_to(squares, (1, 128))], 0)
    pair = jnp.sum(share(jnp.broadcast_to(pair[None], (n, 2, 128))), 0)
    loss_sum, grad_norm = pair[0, 0], jnp.sqrt(pair[1, 0])
    factor = jnp.minimum(1.0, clip_norm / grad_norm)
    grad_block = jnp.concatenate([grad_block01, grad_down[None]], 0)
    stem_new = adam_step(stem, stem_first, stem_second, grad_stem, factor, rate_stem)
    small_new = adam_step(small, small_first, small_second, grad_small, factor, rate_small)
    block_new = adam_step(block, block_first, block_second, grad_block, factor, rate_block)
    head_new = adam_step(head, head_first, head_second, grad_head, factor, rate_head)
    return (*stem_new, *small_new, *block_new, *head_new, loss_sum, grad_norm)


def solution(mesh):
    flat = P(("dp", "mp"))
    matrix = P(None, "dp", "mp")
    head = P("dp", "mp")
    states = (flat,) * 6 + (matrix,) * 3 + (head,) * 3
    return jax.shard_map(
        local,
        mesh=mesh,
        in_specs=(P("mp", "dp", None), P("mp", "dp")) + states,
        out_specs=states + (P(), P()),
        check_vma=False,
    )
```

```python
import functools

import jax
import jax.numpy as jnp
from jax import lax
from jax.experimental import pallas as pl
from jax.experimental.pallas import tpu as pltpu
from jax.sharding import PartitionSpec as P

D = 768
HEADS = 12
HEAD_DIM = 64
FF = 3072
CLASSES = 1000
C1 = 48
C2 = 96
C3 = 192
C4 = 384
STEP = 10
TOK = 197
SIDE = 14
T = 16 * SIDE
W = 384
CHANS = (3, C1, C2, C3, C4)

beta_one = 0.9
beta_two = 0.999
adam_epsilon = 1e-08
decay_rate = 0.05
clip_norm = 1.0
rate_stem = 0.05
rate_small = 0.5
rate_block = 0.05
rate_head = 0.05
batch_epsilon = 1e-05
layer_epsilon = 1e-06
smoothing = 0.1

bf16 = jnp.bfloat16
f32 = jnp.float32

STEM_SHIFT = 112
SMALL_SHIFT = 96
ROW_W2 = 11
ROW_W3 = ROW_W2 + 9 * C1 * C2 // 128
ROW_W4 = ROW_W3 + 9 * C2 * C3 // 128
ROW_WP = ROW_W4 + 9 * C3 * C4 // 128
STEM_ROWS = ROW_WP + C4 * D // 128
SMALL_NAMES = (
    ("proj_bias", 6),
    ("class_token", 6),
    ("position", 6 * TOK),
    ("norm1_gain", 6),
    ("norm1_bias", 6),
    ("query_bias", 6),
    ("value_bias", 6),
    ("out_bias", 6),
    ("norm2_gain", 6),
    ("norm2_bias", 6),
    ("hidden_bias", 24),
    ("mlp_bias", 6),
    ("final_gain", 6),
    ("final_bias", 6),
    ("head_bias", 8),
)
SMALL_AT = {}
_row = 12
for _name, _rows in SMALL_NAMES:
    SMALL_AT[_name] = _row
    _row += _rows
SMALL_ROWS = _row
VEC_NAMES = (
    "proj_bias",
    "norm1_gain",
    "norm1_bias",
    "query_bias",
    "value_bias",
    "out_bias",
    "norm2_gain",
    "norm2_bias",
    "mlp_bias",
    "final_gain",
    "final_bias",
)
VEC = {name: index for index, name in enumerate(VEC_NAMES)}
VEC_HIDDEN = 12
VEC_HEAD = 16
VEC_AIM = 18
OUT_BACK = 16
OUT_FINAL = 17
OUT_HIDDEN = 18
OUT_HEAD = 22
OUT_SUMS = 24
OUT_LOSS = 25


def dot(a, b):
    return jnp.dot(a, b, preferred_element_type=f32)


def dot_nt(a, b):
    return lax.dot_general(a, b, (((1,), (1,)), ((), ())), preferred_element_type=f32)


def dot_tn(a, b):
    return lax.dot_general(a, b, (((0,), (0,)), ((), ())), preferred_element_type=f32)


GELU_A = 0.7978845608028654
GELU_B = 0.044715


def gelu(x):
    return 0.5 * x * (1.0 + jnp.tanh(GELU_A * (x + GELU_B * x * x * x)))


def gelu_slope(x):
    t = jnp.tanh(GELU_A * (x + GELU_B * x * x * x))
    return 0.5 * (1.0 + t) + 0.5 * x * (1.0 - t * t) * GELU_A * (1.0 + 3.0 * GELU_B * x * x)


def dot_f32(a, b):
    return jnp.dot(a, b, preferred_element_type=f32, precision=lax.Precision.HIGHEST)


def up16(n):
    return -(-n // 16) * 16


def colsum(x):
    return jnp.sum(x, 0, keepdims=True)


def slot_index():
    return lax.broadcasted_iota(jnp.int32, (T, 1), 0)


def patch_mask():
    return ((slot_index() & 15) < SIDE).astype(f32)


def token_mask():
    p = slot_index()
    return (((p & 15) < SIDE) | (p == SIDE)).astype(f32)


def fold_phases(x, chan):
    step = W // 2
    while step >= chan:
        x = x + jnp.concatenate([x[:, step:], x[:, :step]], 1)
        step //= 2
    return x


def bn_stats(st_ref, count, chan):
    tot = fold_phases(jnp.sum(st_ref[:, 0:2, :], 0), chan)
    mean = tot[0:1] / count
    inv = lax.rsqrt(tot[1:2] / count - mean * mean + batch_epsilon)
    return mean, inv


def shift_lanes(x, s):
    lane = lax.broadcasted_iota(jnp.int32, x.shape, 1)
    row = lax.broadcasted_iota(jnp.int32, x.shape, 0)
    moved = pltpu.roll(x, s, 1)
    before = jnp.where(row == 0, 0.0, pltpu.roll(moved, 1, 0))
    return jnp.where(lane >= s, moved, before)


def pack_kernel(at_ref, stem_ref, small_ref, out_ref):
    rows = stem_ref.shape[0]
    out_ref[0:rows, :] = shift_lanes(stem_ref[...], at_ref[0]).astype(bf16)
    out_ref[rows:, :] = shift_lanes(small_ref[...], at_ref[1]).astype(bf16)


def flat_lanes(ref, row, count):
    return jnp.concatenate([ref[row + k : row + k + 1, :] for k in range(count)], 1)


def assemble_kernel(parts, mp, stem_len, small_len, rows_stem, rows_small, at_ref, *refs):
    pieces = refs[:parts]
    s1, t1_ref, t2_ref, t3_ref, t4_ref, wp_ref, bn_ref, vec_ref, pos_ref = refs[parts : parts + 9]
    frame, table, s2, s3a, s3b, u1, u2, u3 = refs[parts + 9 :]
    frame[...] = jnp.zeros_like(frame)
    table[...] = jnp.zeros_like(table)
    for index, ref in enumerate(pieces):
        mv = at_ref[index]

        def put(d, carry):
            owner = d * mp + mv
            a = (owner * stem_len + STEM_SHIFT) // 128
            frame[pl.ds(a, rows_stem), :] += ref[d, 0:rows_stem, :].astype(f32)
            b = (owner * small_len + SMALL_SHIFT) // 128
            table[pl.ds(b, rows_small), :] += ref[d, rows_stem : rows_stem + rows_small, :].astype(f32)
            return carry

        lax.fori_loop(0, ref.shape[0], put, 0)
    s1[...] = jnp.zeros_like(s1)
    flat = flat_lanes(frame, 0, ROW_W2)
    for k in range(27):
        s1[k : k + 1, 0:C1] = flat[:, STEM_SHIFT + 48 * k : STEM_SHIFT + 48 * k + 48]
    u1[...] = jnp.zeros_like(u1)
    for tap in range(3):
        for j in range(8):
            cols = slice(j * C1, (j + 1) * C1)
            if j == 0:
                u1[tap * 64 + 48 : tap * 64 + 51, cols] = s1[tap * 9 : tap * 9 + 3, 0:C1]
                u1[tap * 64 : tap * 64 + 6, cols] = s1[tap * 9 + 3 : tap * 9 + 9, 0:C1]
            else:
                at = tap * 64 + 6 * j - 3
                u1[at : at + 9, cols] = s1[tap * 9 : tap * 9 + 9, 0:C1]
    t1_ref[...] = u1[...].astype(bf16)
    q = 9 * C1 // 4
    wide = jnp.concatenate([frame[pl.ds(ROW_W2 + k, q, stride=3), :] for k in range(3)], 1)
    for k in range(4):
        s2[pl.ds(k, q, stride=4), 0:C2] = wide[:, k * C2 : (k + 1) * C2]
    q = 9 * C2 // 2
    wide = jnp.concatenate([frame[pl.ds(ROW_W3 + k, q, stride=3), :] for k in range(3)], 1)
    for k in range(2):
        part = wide[:, k * C3 : (k + 1) * C3]
        s3a[pl.ds(k, q, stride=2), :] = part[:, 0:128]
        s3b[pl.ds(k, q, stride=2), 0 : C3 - 128] = part[:, 128:C3]
    for ref, chan_in, chan_out, src, u in (
        (t2_ref, C1, C2, (s2,), u2),
        (t3_ref, C2, C3, (s3a, s3b), u3),
    ):
        for tap in range(3):
            u[...] = jnp.zeros_like(u)
            base = tap * 3 * chan_in
            for j in range(W // chan_out):
                for k, s in enumerate(src):
                    width = min(128, chan_out - 128 * k)
                    cols = slice(j * chan_out + 128 * k, j * chan_out + 128 * k + width)
                    if j == 0:
                        u[W : W + chan_in, cols] = s[base : base + chan_in, 0:width]
                        u[0 : 2 * chan_in, cols] = s[base + chan_in : base + 3 * chan_in, 0:width]
                    else:
                        at = (2 * j - 1) * chan_in
                        u[at : at + 3 * chan_in, cols] = s[base : base + 3 * chan_in, 0:width]
            ref[tap] = u[...].astype(bf16)
    for tap in range(3):
        rows = 3 * C3
        for k in range(3):
            lanes = slice(k * 128, (k + 1) * 128)
            at = ROW_W4 + k + 3 * tap * rows
            t4_ref[tap, 0 : 2 * C3, lanes] = frame[pl.ds(at + 3 * C3, 2 * C3, stride=3), :].astype(bf16)
            t4_ref[tap, 2 * C3 : 3 * C3, lanes] = frame[pl.ds(at, C3, stride=3), :].astype(bf16)
    for k in range(6):
        lanes = slice(k * 128, (k + 1) * 128)
        wp_ref[:, lanes] = frame[pl.ds(ROW_WP + k, C4, stride=6), :].astype(bf16)
    flat = flat_lanes(table, 0, 12)
    first = SMALL_SHIFT
    for level in range(4):
        chan = CHANS[level + 1]
        for which in range(2):
            at = first + which * (C1 + C2 + C3 + C4)
            part = flat[:, at : at + chan]
            row = 2 * level + which
            for j in range(W // chan):
                bn_ref[row : row + 1, j * chan : (j + 1) * chan] = part
        first += chan
    vec_ref[...] = jnp.zeros_like(vec_ref)
    for name, index in VEC.items():
        vec_ref[index : index + 1, :] = flat_lanes(table, SMALL_AT[name], 6)
    for k in range(4):
        row = VEC_HIDDEN + k
        vec_ref[row : row + 1, :] = flat_lanes(table, SMALL_AT["hidden_bias"] + 6 * k, 6)
    flat = flat_lanes(table, SMALL_AT["head_bias"], 8)
    lane = lax.broadcasted_iota(jnp.int32, (1, 512), 1)
    for m in range(2):
        vec_ref[VEC_HEAD + m : VEC_HEAD + m + 1, 0:500] = flat[:, 500 * m : 500 * m + 500]
        aim = jnp.where(lane + 500 * m == at_ref[parts], 1.0 - smoothing, 0.0) + smoothing / CLASSES
        vec_ref[VEC_AIM + m : VEC_AIM + m + 1, 0:512] = jnp.where(lane < 500, aim, 0.0)
    pos_ref[...] = jnp.zeros_like(pos_ref)
    at = SMALL_AT["position"]
    for k in range(6):
        lanes = slice(k * 128, (k + 1) * 128)
        for r in range(SIDE):
            rows = table[pl.ds(at + k + 6 * (1 + SIDE * r), SIDE, stride=6), :]
            pos_ref[16 * r : 16 * r + SIDE, lanes] = rows
        mark = SMALL_AT["class_token"] + k
        pos_ref[SIDE : SIDE + 1, lanes] = table[mark : mark + 1, :] + table[at + k : at + k + 1, :]


def image_kernel(own_ref, next_ref, xk_ref, gram_ref, flat, chunks, xe):
    half = own_ref.shape[0]
    flat[0:half, :] = own_ref[...].astype(f32)
    flat[half : 2 * half, :] = next_ref[...].astype(f32)
    n = 2 * half // 3
    wide = jnp.concatenate([flat[pl.ds(k, n, stride=3), :] for k in range(3)], 1)
    for j in range(8):
        chunks[pl.ds(j, n, stride=8), 0:48] = wide[:, 48 * j : 48 * j + 48]
    mask = patch_mask()
    lane = lax.broadcasted_iota(jnp.int32, (T, 64), 1)

    def spread(i, carry):
        rows = [chunks[pl.ds(16 * SIDE * r + SIDE * i, 16), 0:64] for r in range(SIDE)]
        x = jnp.where(lane < 48, jnp.concatenate(rows, 0), 0.0) * mask
        left = pltpu.roll(jnp.concatenate([x, x], 1), 3, 1)[:, 0:64]
        left = jnp.where((lane >= 48) & (lane < 51), pltpu.roll(left, 1, 0), 0.0)
        xe[i + 1] = ((x + left) * mask).astype(bf16)
        return carry

    chunks[pl.ds(n * 8, 16), :] = jnp.zeros((16, 128), f32)
    lax.fori_loop(0, 16, spread, 0)
    last = xe[16]
    xe[0] = jnp.concatenate([jnp.zeros((16, 64), bf16), last[: T - 16]], 0)

    def step(i, carry):
        gram, ones = carry
        x = jnp.concatenate([xe[2 * i], xe[2 * i + 1], xe[2 * i + 2]], 1)
        xk_ref[i] = x
        return gram + dot_tn(x, x), ones + colsum(x.astype(f32))

    gram, ones = lax.fori_loop(0, 8, step, (jnp.zeros((192, 192), f32), jnp.zeros((1, 192), f32)))
    row = lax.broadcasted_iota(jnp.int32, (192, 256), 0)
    col = lax.broadcasted_iota(jnp.int32, (192, 256), 1)
    j, k = col >> 5, col & 31
    tap = (k >= 9).astype(jnp.int32) + (k >= 18).astype(jnp.int32)
    u = k - 9 * tap
    at = 64 * tap + jnp.where(j == 0, jnp.where(u < 3, 48 + u, u - 3), 6 * j - 3 + u)
    pick = ((row == at) & (k < 27)).astype(f32)
    both = lax.dot_general(
        pick,
        dot_f32(gram, pick),
        (((0,), (0,)), ((), ())),
        preferred_element_type=f32,
        precision=lax.Precision.HIGHEST,
    )
    ones = dot_f32(jnp.broadcast_to(ones, (8, 192)), pick)[0:1]
    total = jnp.zeros((32, 32), f32)
    line = jnp.zeros((1, 32), f32)
    for q in range(8):
        lanes = slice(32 * q, 32 * q + 32)
        total = total + both[lanes, lanes]
        line = line + ones[:, lanes]
    r32 = lax.broadcasted_iota(jnp.int32, (32, 32), 0)
    c32 = lax.broadcasted_iota(jnp.int32, (32, 32), 1)
    total = total + jnp.where(r32 == 27, line, 0.0)
    column = jnp.sum(jnp.where(r32 == c32, line, 0.0), 1, keepdims=True)
    total = total + jnp.where(c32 == 27, column, 0.0)
    flat8 = jnp.concatenate([total[8 * q : 8 * q + 8] for q in range(4)], 1)
    gram_ref[...] = jnp.broadcast_to(flat8[None], gram_ref.shape)


def level1_stats(gram_ref, w1_ref, count):
    flat8 = jnp.sum(gram_ref[...], 0)
    gram = jnp.concatenate([flat8[:, 32 * q : 32 * q + 32] for q in range(4)], 0)
    cross = dot_f32(gram, w1_ref[...])
    mean = cross[27:28] / count
    squares = colsum(w1_ref[...] * cross) / count
    inv = lax.rsqrt(squares - mean * mean + batch_epsilon)
    return gram, cross, mean, inv


def tile_lanes(x, chan):
    return jnp.concatenate([x[:, 0:chan]] * (W // chan), 1)


def conv12_kernel(count, xk_ref, gram_ref, w1_ref, t1_ref, bn_ref, t_ref, ax_ref, out_ref, st_ref):
    gram, cross, mean, inv = level1_stats(gram_ref, w1_ref, count)
    mean, inv = tile_lanes(mean, C1), tile_lanes(inv, C1)
    gain, bias = bn_ref[0:1, :], bn_ref[1:2, :]
    mask = patch_mask()
    weights = t1_ref[...]

    def activate(i, carry):
        a = gelu((dot(xk_ref[i], weights) - mean) * inv * gain + bias) * mask
        put_input(ax_ref, i, a, C1)
        return carry

    lax.fori_loop(0, 8, activate, 0)
    convolve(8, ax_ref, t_ref, out_ref, st_ref, mask, C1)


def put_input(ax_ref, i, a, chan):
    left = pltpu.roll(a[:, W - chan :], 1, 0)
    ax_ref[i + 1, :, 0:W] = a.astype(bf16)
    ax_ref[i + 1, :, W:] = left.astype(bf16)


def convolve(rows, ax_ref, t_ref, out_ref, st_ref, mask, chan):
    last = ax_ref[rows]
    ax_ref[0] = jnp.concatenate([jnp.zeros((16, W + chan), bf16), last[: T - 16]], 0)

    def step(i, carry):
        first, second = carry
        y = dot(ax_ref[2 * i], t_ref[0])
        y = y + dot(ax_ref[2 * i + 1], t_ref[1])
        y = y + dot(ax_ref[2 * i + 2], t_ref[2])
        out_ref[i] = y
        ym = y * mask
        return first + colsum(ym), second + colsum(ym * y)

    zero = jnp.zeros((1, W), f32)
    first, second = lax.fori_loop(0, rows // 2, step, (zero, zero))
    st = jnp.concatenate([first, second], 0)
    st_ref[...] = jnp.broadcast_to(st[None], st_ref.shape)


def conv_kernel(level, count, c_ref, stin_ref, bn_ref, t_ref, ax_ref, out_ref, st_ref):
    chan = CHANS[level]
    rows = c_ref.shape[0]
    mean, inv = bn_stats(stin_ref, count, chan)
    gain = bn_ref[2 * level - 2 : 2 * level - 1, :]
    bias = bn_ref[2 * level - 1 : 2 * level, :]
    mask = patch_mask()

    def activate(i, carry):
        put_input(ax_ref, i, gelu((c_ref[i] - mean) * inv * gain + bias) * mask, chan)
        return carry

    lax.fori_loop(0, rows, activate, 0)
    convolve(rows, ax_ref, t_ref, out_ref, st_ref, mask, chan)


def layer_norm(x):
    centered = x - jnp.mean(x, -1, keepdims=True)
    inv = lax.rsqrt(jnp.mean(centered * centered, -1, keepdims=True) + layer_epsilon)
    return centered * inv, inv


def layer_norm_back(dy, s, inv, gain):
    scaled = dy * gain
    inner = scaled - jnp.mean(scaled, -1, keepdims=True)
    return inv * (inner - s * jnp.mean(scaled * s, -1, keepdims=True))


def block_kernel(
    count,
    st_ref,
    bn_ref,
    c_hbm,
    wp_hbm,
    pos_hbm,
    vec_hbm,
    g_ref,
    gr_ref,
    bn4_hbm,
    so_hbm,
    out_hbm,
    gpos_hbm,
    dwp_hbm,
    c_ref,
    wp_ref,
    pos_ref,
    vec_ref,
    bn4_ref,
    so_ref,
    out_ref,
    gpos_ref,
    dwp_ref,
    wa,
    wu,
    wd,
    wh,
    sems,
    a4,
    x0,
    n1,
    qkv,
    probs,
    mixed,
    n2t,
    pre,
    acc,
    bqkv,
):
    gr0, gr1 = wu, wd
    fetched = []
    for k, (source, ref) in enumerate(
        ((c_hbm, c_ref), (wp_hbm, wp_ref), (pos_hbm, pos_ref), (vec_hbm, vec_ref))
    ):
        fetched.append(pltpu.make_async_copy(source, ref, sems.at[24 + k]))
        fetched[-1].start()
    copies = []
    for m in range(2):
        for k, (ref, at, size) in enumerate(
            ((wa, 0, 1536), (wu, 1536, 1536), (wd, 3072, 1536), (wh, 4608, 512))
        ):
            copy = pltpu.make_async_copy(
                g_ref.at[:, m, :, at : at + size], ref.at[m], sems.at[4 * m + k]
            )
            copy.start()
            copies.append(copy)

    def send_out(grad, slot):
        out = []
        lanes = slice(1536 * slot, 1536 * slot + 1536)
        for m in range(2):
            for z in range(4):
                copy = pltpu.make_async_copy(
                    grad.at[m, 4 * z : 4 * z + 4],
                    gr_ref.at[:, m, z, :, lanes],
                    sems.at[8 + 8 * slot + 4 * m + z],
                )
                copy.start()
                out.append(copy)
        return out

    def write(ref, target, k):
        copy = pltpu.make_async_copy(ref, target, sems.at[28 + k])
        copy.start()
        moving.append(copy)

    def vec(name):
        return vec_ref[VEC[name] : VEC[name] + 1, :]

    mask = patch_mask()
    valid = token_mask()
    out_row = lax.broadcasted_iota(jnp.int32, (32, 1), 0)
    out_ref[...] = jnp.zeros_like(out_ref)
    key = lax.broadcasted_iota(jnp.int32, (1, T), 1)
    key_bias = jnp.where(((key & 15) < SIDE) | (key == SIDE), 0.0, -1e30)

    def normed4():
        mean, inv = bn_stats(st_ref, count, C4)
        s = (c_ref[0] - mean) * inv
        return s, s * bn_ref[6:7, :] + bn_ref[7:8, :]

    for copy in fetched:
        copy.wait()
    s4, y4 = normed4()
    a4[...] = (gelu(y4) * mask).astype(bf16)
    x0[...] = (dot(a4[...], wp_ref[...]) + vec("proj_bias")) * mask + pos_ref[...]
    s1, i1 = layer_norm(x0[...])
    n1[...] = (s1 * vec("norm1_gain") + vec("norm1_bias")).astype(bf16)
    copies[0].wait()
    copies[4].wait()

    def tile(ref, m, at, size=256):
        return ref[m, :, :, pl.ds(at, size)].reshape(D, size)

    for part in range(9):
        y = dot(n1[...], tile(wa, part // 6, 256 * (part % 6)))
        lanes = slice(256 * (part % 3), 256 * (part % 3) + 256)
        if part < 3:
            y = y + vec("query_bias")[:, lanes]
        elif part >= 6:
            y = y + vec("value_bias")[:, lanes]
        qkv[:, 256 * part : 256 * part + 256] = y.astype(bf16)
    scale = HEAD_DIM**-0.5

    def attend(pair, carry):
        at = pl.multiple_of(pair * 128, 128)
        q = qkv[:, pl.ds(at, 128)]
        k = qkv[:, pl.ds(at + D, 128)]
        v = qkv[:, pl.ds(at + 2 * D, 128)]
        out = []
        for h in range(2):
            lanes = slice(64 * h, 64 * h + 64)
            scores = dot_nt(q[:, lanes], k[:, lanes]) * scale + key_bias
            e = jnp.exp(scores - jnp.max(scores, -1, keepdims=True))
            p = e / jnp.sum(e, -1, keepdims=True)
            probs[2 * pair + h] = p
            out.append(dot(p.astype(bf16), v[:, lanes]))
        mixed[:, pl.ds(at, 128)] = jnp.concatenate(out, 1).astype(bf16)
        return carry

    lax.fori_loop(0, HEADS // 2, attend, 0)
    att = [dot_nt(mixed[...], wa[1, :, :, D : 2 * D].reshape(D, D))]
    x1 = x0[...] + att[0] + vec("out_bias")
    mean_x1 = colsum(x1 * valid) / TOK
    s2, i2 = layer_norm(x1)
    n2 = (s2 * vec("norm2_gain") + vec("norm2_bias")).astype(bf16)
    n2t[...] = n2.T
    copies[1].wait()
    copies[5].wait()
    for m in range(2):

        def up(k, carry):
            at = pl.multiple_of(k * 256, 256)
            y = dot(n2, tile(wu, m, at))
            pre[m, :, pl.ds(at, 256)] = y
            return carry

        lax.fori_loop(0, 6, up, 0)
        for k in range(6):
            f = 1536 * m + 256 * k
            lanes = slice(256 * k, 256 * k + 256)
            row = VEC_HIDDEN + f // D
            y = pre[m, :, lanes] + vec_ref[row : row + 1, f % D : f % D + 256]
            pre[m, :, lanes] = y
            h = gelu(y).astype(bf16).astype(f32) * valid
            row = OUT_HIDDEN + f // D
            out_ref[row : row + 1, f % D : f % D + 256] = colsum(h)
    copies[2].wait()
    copies[6].wait()
    hs = jnp.concatenate([out_ref[OUT_HIDDEN + k : OUT_HIDDEN + k + 1, :] for k in range(4)], 1) / TOK
    high = hs.astype(bf16)
    low = (hs - high.astype(f32)).astype(bf16)
    out = jnp.zeros((1, D), f32)
    for m in range(2):
        lanes = slice(1536 * m, 1536 * m + 1536)
        both = jnp.concatenate(
            [jnp.broadcast_to(high[:, lanes], (8, 1536)), jnp.broadcast_to(low[:, lanes], (8, 1536))], 0
        )
        y = dot_nt(both, wd[m].reshape(D, 1536))
        out = out + y[0:1] + y[8:9]
    pooled = mean_x1 + out + vec("mlp_bias")
    s3, i3 = layer_norm(pooled)
    final = (s3 * vec("final_gain") + vec("final_bias")).astype(bf16)
    copies[3].wait()
    copies[7].wait()
    wide = jnp.broadcast_to(final, (16, D))
    logits = jnp.concatenate([dot(wide, wh[m].reshape(D, 512))[0:1] for m in range(2)], 1)
    lane = lax.broadcasted_iota(jnp.int32, (1, 1024), 1)
    real = (lane & 511) < CLASSES // 2
    def pair(row):
        return jnp.concatenate([vec_ref[row : row + 1, 0:512], vec_ref[row + 1 : row + 2, 0:512]], 1)

    logits = jnp.where(real, logits + pair(VEC_HEAD), -1e30)
    top = jnp.max(logits, -1, keepdims=True)
    log_probs = logits - top - jnp.log(jnp.sum(jnp.exp(logits - top), -1, keepdims=True))
    aim = pair(VEC_AIM)
    loss = -jnp.sum(jnp.where(real, aim * log_probs, 0.0), keepdims=True)
    out_ref[...] = jnp.where(out_row >= OUT_LOSS, jnp.broadcast_to(loss, out_ref.shape), out_ref[...])
    back_logits = jnp.where(real, jnp.exp(log_probs) - aim, 0.0).astype(bf16)
    for m in range(2):
        row = OUT_HEAD + m
        out_ref[row : row + 1, 0:512] = back_logits[:, 512 * m : 512 * m + 512].astype(f32)
    out_ref[OUT_FINAL : OUT_FINAL + 1, :] = final.astype(f32)
    wide = jnp.broadcast_to(back_logits, (16, 1024))
    back_final = (
        dot_nt(wide[:, 0:512], wh[0].reshape(D, 512)) + dot_nt(wide[:, 512:], wh[1].reshape(D, 512))
    )[0:1]
    def put(name, value):
        out_ref[VEC[name] : VEC[name] + 1, :] = value

    put("final_gain", back_final * s3)
    put("final_bias", back_final)
    back2 = layer_norm_back(back_final, s3, i3, vec("final_gain")) / TOK
    back_out = back2.astype(bf16)
    out_ref[OUT_BACK : OUT_BACK + 1, :] = back_out.astype(f32)
    put("mlp_bias", back_out.astype(f32) * TOK)
    wide = jnp.broadcast_to(back_out, (16, D))
    acc[...] = jnp.zeros_like(acc)
    for m in range(2):

        def down(k, carry):
            at = pl.multiple_of(k * 256, 256)
            back = dot(wide, tile(wd, m, at))[0:1]
            bp = (back * gelu_slope(pre[m, :, pl.ds(at, 256)]) * valid).astype(bf16)
            ghid = colsum(bp.astype(f32))
            pre[m, 0:1, pl.ds(at, 256)] = ghid
            grad = dot(n2t[...], bp)
            gr1[m, :, :, pl.ds(at, 256)] = grad.astype(bf16).reshape(16, 48, 256)
            acc[...] += dot_nt(bp, tile(wu, m, at))
            return carry

        lax.fori_loop(0, 6, down, 0)
        for k in range(2):
            row = VEC_HIDDEN + 2 * m + k
            out_ref[row : row + 1, :] = pre[m, 0:1, D * k : D * k + D]
    moving = send_out(gr1, 1)
    back_n2 = acc[...]
    put("norm2_gain", colsum(back_n2 * s2))
    put("norm2_bias", colsum(back_n2))
    back1 = back2 * valid + layer_norm_back(back_n2, s2, i2, vec("norm2_gain"))
    back_att = back1.astype(bf16)
    put("out_bias", colsum(back_att.astype(f32)))
    back_att_t = back_att.T
    for k in range(3):
        lanes = slice(256 * k, 256 * k + 256)
        grad = dot(back_att_t, mixed[:, lanes])
        gr0[1, :, :, D + 256 * k : D + 256 * k + 256] = grad.astype(bf16).reshape(16, 48, 256)
    acc[...] = dot(back_att, wa[1, :, :, D : 2 * D].reshape(D, D))

    def attend_back(pair, carry):
        at = pl.multiple_of(pair * 128, 128)
        q = qkv[:, pl.ds(at, 128)]
        k = qkv[:, pl.ds(at + D, 128)]
        v = qkv[:, pl.ds(at + 2 * D, 128)]
        bm = acc[:, pl.ds(at, 128)].astype(bf16)
        bq, bk, bv = [], [], []
        for h in range(2):
            lanes = slice(64 * h, 64 * h + 64)
            p = probs[2 * pair + h]
            bp = dot_nt(bm[:, lanes], v[:, lanes])
            bv.append(dot_tn(p.astype(bf16), bm[:, lanes]))
            inner = jnp.sum(bp * p, -1, keepdims=True)
            bs = (p * (bp - inner)).astype(bf16)
            bq.append(dot(bs, k[:, lanes]) * scale)
            bk.append(dot_tn(bs, q[:, lanes]) * scale)
        bqkv[:, pl.ds(at, 128)] = jnp.concatenate(bq, 1).astype(bf16)
        bqkv[:, pl.ds(at + D, 128)] = jnp.concatenate(bk, 1).astype(bf16)
        bqkv[:, pl.ds(at + 2 * D, 128)] = jnp.concatenate(bv, 1).astype(bf16)
        return carry

    lax.fori_loop(0, HEADS // 2, attend_back, 0)
    put("query_bias", colsum(bqkv[:, 0:D].astype(f32)))
    put("value_bias", colsum(bqkv[:, 2 * D :].astype(f32)))
    n1t = n1[...].T
    acc[...] = jnp.zeros_like(acc)
    for part in range(9):
        m, at = part // 6, 256 * (part % 6)
        b = bqkv[:, 256 * part : 256 * part + 256]
        gr0[m, :, :, at : at + 256] = dot(n1t, b).astype(bf16).reshape(16, 48, 256)
        acc[...] += dot_nt(b, tile(wa, m, at))
    moving += send_out(gr0, 0)
    back_n1 = acc[...]
    s1, i1 = layer_norm(x0[...])
    put("norm1_gain", colsum(back_n1 * s1))
    put("norm1_bias", colsum(back_n1))
    back0 = back1 + layer_norm_back(back_n1, s1, i1, vec("norm1_gain"))
    gpos_ref[...] = back0
    write(gpos_ref, gpos_hbm, 0)
    back_patch = (back0 * mask).astype(bf16)
    put("proj_bias", colsum(back_patch.astype(f32)))
    dwp_ref[...] = dot_tn(a4[...], back_patch)
    write(dwp_ref, dwp_hbm, 1)
    s4, y4 = normed4()
    bn4 = dot_nt(back_patch, wp_ref[...]) * gelu_slope(y4) * mask
    bn4_ref[0] = bn4
    write(bn4_ref, bn4_hbm, 2)
    st = jnp.concatenate([colsum(bn4), colsum(bn4 * s4)], 0)
    so_ref[...] = jnp.broadcast_to(st[None], so_ref.shape)
    write(so_ref, so_hbm, 3)
    out_ref[OUT_SUMS : OUT_SUMS + 1, :] = jnp.concatenate([st[0:1], st[1:2]], 1)
    write(out_ref, out_hbm, 4)
    for copy in moving:
        copy.wait()


def conv_back_kernel(
    level,
    count,
    count_in,
    back_ref,
    tot_ref,
    c_ref,
    st_ref,
    t_ref,
    cin_ref,
    stin_ref,
    bn_ref,
    g,
    backin_ref,
    so_ref,
    ss_ref,
):
    finish_level(level, count, back_ref, tot_ref, c_ref, st_ref, bn_ref, g)
    mean, inv = bn_stats(stin_ref, count_in, CHANS[level - 1])

    def normed(q):
        return (cin_ref[q] - mean) * inv

    def keep(q, y):
        backin_ref[q] = y

    st = back_through(level, g, t_ref, bn_ref, normed, keep)
    ss_ref[...] = st
    so_ref[...] = jnp.broadcast_to(st[None], so_ref.shape)


def finish_level(level, count, back_ref, tot_ref, c_ref, st_ref, bn_ref, g):
    chan = CHANS[level]
    rows = back_ref.shape[0]
    mask = patch_mask()
    mean, inv = bn_stats(st_ref, count, chan)
    gain = bn_ref[2 * level - 2 : 2 * level - 1, :]
    tot = fold_phases(jnp.sum(tot_ref[:, 0:2, :], 0), chan) / count

    def finish(i, carry):
        s = (c_ref[i] - mean) * inv
        g[i] = (inv * gain * (back_ref[i] - tot[0:1] - s * tot[1:2]) * mask).astype(bf16)
        return carry

    lax.fori_loop(0, rows, finish, 0)
    head = g[0]
    g[rows] = jnp.concatenate([head[16:], jnp.zeros((16, W), bf16)], 0)


def kernel_grad(level, ax_ref, g, dw_ref, dt):
    chan, chan_in = CHANS[level], CHANS[level - 1]
    rows = g.shape[0] - 1
    dt[...] = jnp.zeros_like(dt)

    def weights(i, carry):
        for tap in range(3):
            dt[tap] += dot_tn(ax_ref[2 * i + tap], g[i])
        return carry

    lax.fori_loop(0, rows, weights, 0)
    for tap in range(3):
        base = tap * 3 * chan_in
        for j in range(W // chan):
            for k in range(dw_ref.shape[0]):
                width = min(128, chan - 128 * k)
                cols = slice(j * chan + 128 * k, j * chan + 128 * k + width)
                if j == 0:
                    dw_ref[k, base : base + chan_in, 0:width] = dt[tap, W : W + chan_in, cols]
                    dw_ref[k, base + chan_in : base + 3 * chan_in, 0:width] = dt[
                        tap, 0 : 2 * chan_in, cols
                    ]
                else:
                    at = (2 * j - 1) * chan_in
                    dw_ref[k, base : base + 3 * chan_in, 0:width] += dt[
                        tap, at : at + 3 * chan_in, cols
                    ]


def back_through(level, g, t_ref, bn_ref, normed, keep):
    chan_in = CHANS[level - 1]
    rows = g.shape[0] - 1
    mask = patch_mask()
    gain = bn_ref[2 * level - 4 : 2 * level - 3, :]
    bias = bn_ref[2 * level - 3 : 2 * level - 2, :]

    def through(q, p, carry):
        first, second = carry
        left = pltpu.roll(p[:, W:], T - 1, 0)
        p = jnp.concatenate([p[:, 0 : W - chan_in], p[:, W - chan_in : W] + left], 1)
        s = normed(q)
        y = p * gelu_slope(s * gain + bias) * mask
        keep(q, y)
        return first + colsum(y), second + colsum(y * s)

    def back(i, carry):
        carry = through(2 * i, dot_nt(g[i], t_ref[1]), carry)
        p = dot_nt(g[i], t_ref[2]) + dot_nt(g[i + 1], t_ref[0])
        return through(2 * i + 1, p, carry)

    zero = jnp.zeros((1, W), f32)
    first, second = lax.fori_loop(0, rows, back, (zero, zero))
    return jnp.concatenate([first, second], 0)


LATE_W1 = 9 * C1 * C2 // 128
LATE_SUMS = LATE_W1 + 32
LATE_ROWS = LATE_SUMS + 4 * 6


def conv2_back_kernel(
    count,
    count_in,
    back_ref,
    tot_ref,
    c_ref,
    st_ref,
    ax_ref,
    t_ref,
    xk_ref,
    gram_ref,
    w1_ref,
    t1_ref,
    bn_ref,
    ss2_ref,
    ss3_ref,
    ss4_ref,
    late_ref,
    dw,
    g,
    dt,
    dt1,
    late,
):
    finish_level(2, count, back_ref, tot_ref, c_ref, st_ref, bn_ref, g)
    kernel_grad(2, ax_ref, g, dw, dt)
    gram, cross, mean, inv = level1_stats(gram_ref, w1_ref, count_in)
    mean, inv = tile_lanes(mean, C1), tile_lanes(inv, C1)
    weights = t1_ref[...]
    dt1[...] = jnp.zeros_like(dt1)

    def normed(q):
        return (dot(xk_ref[q], weights) - mean) * inv

    def keep(q, y):
        dt1[...] += dot_tn(xk_ref[q], y.astype(bf16))

    st = back_through(2, g, t_ref, bn_ref, normed, keep)
    late[...] = jnp.zeros_like(late)
    q = 9 * C1 // 4
    wide = jnp.concatenate([dw[0, pl.ds(k, q, stride=4), :][:, 0:C2] for k in range(4)], 1)
    for k in range(3):
        late[pl.ds(k, q, stride=3), :] = wide[:, 128 * k : 128 * k + 128]
    for tap in range(3):
        base = LATE_W1 + 9 * tap
        for j in range(8):
            cols = slice(j * C1, (j + 1) * C1)
            if j == 0:
                late[base : base + 3, 0:C1] = dt1[tap * 64 + 48 : tap * 64 + 51, cols]
                late[base + 3 : base + 9, 0:C1] = dt1[tap * 64 : tap * 64 + 6, cols]
            else:
                at = tap * 64 + 6 * j - 3
                late[base : base + 9, 0:C1] += dt1[at : at + 9, cols]
    ss4 = jnp.concatenate(
        [ss4_ref[OUT_SUMS : OUT_SUMS + 1, 0:W], ss4_ref[OUT_SUMS : OUT_SUMS + 1, W:]], 0
    )
    for level, ss in enumerate((st, ss2_ref[...], ss3_ref[...], ss4)):
        for which in range(2):
            for k in range(3):
                row = LATE_SUMS + 6 * level + 3 * which + k
                late[row : row + 1, :] = ss[which : which + 1, 128 * k : 128 * k + 128]
    each = late_ref.shape[1]
    for d in range(late_ref.shape[0]):
        late_ref[d] = late[each * d : each * d + each, :]


def early_kernel(
    parts,
    mp,
    stem_len,
    small_len,
    rows_stem,
    rows_small,
    at_ref,
    dw3_ref,
    dw4_ref,
    dwp_ref,
    gv_ref,
    gpos_ref,
    *refs,
):
    outs = refs[:parts]
    frame, table, vecs = refs[parts:]
    if outs[0].shape[1] > rows_stem + rows_small:
        vecs[...] = jnp.zeros_like(vecs)
        base = pl.multiple_of(24 * at_ref[0], 8)
        for index, ref in enumerate(outs):
            first = at_ref[index] == 0
            hs = [gv_ref[OUT_HIDDEN + k : OUT_HIDDEN + k + 1, :] for k in range(4)]
            hs = jnp.concatenate([jnp.where(first, hs[0], hs[2]), jnp.where(first, hs[1], hs[3])], 1)
            bl = [gv_ref[OUT_HEAD + k : OUT_HEAD + k + 1, 0:512] for k in range(2)]
            bl = jnp.where(first, bl[0], bl[1])
            rows = [hs[:, 128 * k : 128 * k + 128] for k in range(12)]
            rows += [bl[:, 128 * k : 128 * k + 128] for k in range(4)]
            vecs[pl.ds(base, 16), :] = jnp.concatenate(rows, 0)
            for d in range(16):
                lanes = slice(48 * d, 48 * d + 48)
                fill = jnp.zeros((1, 16), f32)
                row = jnp.concatenate(
                    [
                        gv_ref[OUT_BACK : OUT_BACK + 1, lanes],
                        fill,
                        gv_ref[OUT_FINAL : OUT_FINAL + 1, lanes],
                        fill,
                    ],
                    1,
                )
                vecs[pl.ds(base + 16, 8), :] = jnp.broadcast_to(row, (8, 128))
                ref[d, rows_stem + rows_small :, :] = vecs[...].astype(bf16)
    frame[0:ROW_W3, :] = jnp.zeros((ROW_W3, 128), f32)
    frame[STEM_ROWS:, :] = jnp.zeros((frame.shape[0] - STEM_ROWS, 128), f32)
    q = 9 * C2 // 2
    wide = jnp.concatenate(
        [
            jnp.concatenate(
                [
                    dw3_ref[0, pl.ds(k, q, stride=2), :],
                    dw3_ref[1, pl.ds(k, q, stride=2), :][:, 0 : C3 - 128],
                ],
                1,
            )
            for k in range(2)
        ],
        1,
    )
    for k in range(3):
        frame[pl.ds(ROW_W3 + k, q, stride=3), :] = wide[:, 128 * k : 128 * k + 128]
    for k in range(3):
        frame[pl.ds(ROW_W4 + k, 9 * C3, stride=3), :] = dw4_ref[k]
    for k in range(6):
        frame[pl.ds(ROW_WP + k, C4, stride=6), :] = dwp_ref[:, 128 * k : 128 * k + 128]
    table[0:12, :] = jnp.zeros((12, 128), f32)
    table[SMALL_ROWS:, :] = jnp.zeros((table.shape[0] - SMALL_ROWS, 128), f32)
    for k in range(6):
        lanes = slice(128 * k, 128 * k + 128)
        for name, index in VEC.items():
            row = SMALL_AT[name] + k
            table[row : row + 1, :] = gv_ref[index : index + 1, lanes]
        for h in range(4):
            row = SMALL_AT["hidden_bias"] + 6 * h + k
            table[row : row + 1, :] = gv_ref[VEC_HIDDEN + h : VEC_HIDDEN + h + 1, lanes]
        at = SMALL_AT["position"] + k
        for r in range(SIDE):
            table[pl.ds(at + 6 * (1 + SIDE * r), SIDE, stride=6), :] = gpos_ref[
                16 * r : 16 * r + SIDE, lanes
            ]
        table[at : at + 1, :] = gpos_ref[SIDE : SIDE + 1, lanes]
        row = SMALL_AT["class_token"] + k
        table[row : row + 1, :] = gpos_ref[SIDE : SIDE + 1, lanes]
    line = jnp.concatenate(
        [
            gv_ref[OUT_HEAD : OUT_HEAD + 1, 0:500],
            gv_ref[OUT_HEAD + 1 : OUT_HEAD + 2, 0:500],
            jnp.zeros((1, 24), f32),
        ],
        1,
    )
    row = SMALL_AT["head_bias"]
    for k in range(8):
        table[row + k : row + k + 1, :] = line[:, 128 * k : 128 * k + 128]
    for index, ref in enumerate(outs):
        mv = at_ref[index]

        def take(d, carry):
            owner = d * mp + mv
            a = (owner * stem_len + STEM_SHIFT) // 128
            ref[d, 0:rows_stem, :] = frame[pl.ds(a, rows_stem), :].astype(bf16)
            b = (owner * small_len + SMALL_SHIFT) // 128
            ref[d, rows_stem : rows_stem + rows_small, :] = table[pl.ds(b, rows_small), :].astype(bf16)
            return carry

        lax.fori_loop(0, ref.shape[0], take, 0)


def unshift_lanes(x, s, length):
    lane = lax.broadcasted_iota(jnp.int32, x.shape, 1)
    row = lax.broadcasted_iota(jnp.int32, x.shape, 0)
    moved = pltpu.roll(x, 128 - s, 1)
    after = pltpu.roll(moved, x.shape[0] - 1, 0)
    y = jnp.where(lane < 128 - s, moved, after)
    return jnp.where(row * 128 + lane < length, y, 0.0)


def unpack_kernel(stem_len, small_len, at_ref, x_ref, stem_ref, small_ref, sq_ref):
    rows = stem_ref.shape[0]
    end = rows + small_ref.shape[0]
    total = jnp.sum(x_ref[:, 0:end, :].astype(f32), 0)
    stem = unshift_lanes(total[0:rows], at_ref[0], stem_len)
    small = unshift_lanes(total[rows:], at_ref[1], small_len)
    stem_ref[...] = stem
    small_ref[...] = small
    sq_ref[...] = colsum(stem * stem) + colsum(small * small)


def sum_kernel(parts, *refs):
    late_ref, sq_ref, down_ref, head_ref, loss_ref, g0_ref, g1_ref, out_ref = refs[parts:]
    total = sum(ref[...].astype(f32) for ref in refs[:parts])
    half = g0_ref.shape[1]
    g0, g1 = total[:, 0:half], total[:, half:]
    g0_ref[...] = g0
    g1_ref[...] = g1
    squares = jnp.sum(g0 * g0 + g1 * g1 + down_ref[...] * down_ref[...], keepdims=True)
    squares = squares + jnp.sum(head_ref[...] * head_ref[...], keepdims=True)
    squares = squares + jnp.sum(sq_ref[...], keepdims=True)
    late = jnp.sum(late_ref[...], 0)
    each = late.shape[0]
    out_ref[:, 0:each, :] = jnp.broadcast_to(late[None], (out_ref.shape[0], each, 128))
    out_ref[:, each : each + 1, :] = jnp.broadcast_to(squares[None], (out_ref.shape[0], 1, 128))
    out_ref[:, each + 1 : each + 2, :] = jnp.broadcast_to(
        loss_ref[OUT_LOSS : OUT_LOSS + 1, 0:128][None], (out_ref.shape[0], 1, 128)
    )


def last_kernel(
    counts,
    stem_len,
    small_len,
    at_ref,
    x_ref,
    gram_ref,
    w1_ref,
    bn_ref,
    stem_ref,
    small_ref,
    stem_out,
    small_out,
    facts_ref,
    late,
    frame,
    table,
):
    devices, each = x_ref.shape[0], x_ref.shape[1] - 2
    for d in range(devices):
        late[each * d : each * d + each, :] = x_ref[d, 0:each, :]
    ends = jnp.sum(x_ref[:, each : each + 2, :], 0)
    frame[...] = jnp.zeros_like(frame)
    table[...] = jnp.zeros_like(table)
    frame[ROW_W2:ROW_W3, :] = late[0:LATE_W1, :]
    line = [[jnp.zeros((1, SMALL_SHIFT), f32)], []]
    for level in range(4):
        chan = CHANS[level + 1]
        rows = []
        for which in range(2):
            row = LATE_SUMS + 6 * level + 3 * which
            rows.append(jnp.concatenate([late[row + k : row + k + 1, :] for k in range(3)], 1))
        both = fold_phases(jnp.concatenate(rows, 0), chan)
        line[0].append(both[1:2, 0:chan])
        line[1].append(both[0:1, 0:chan])
        if level == 0:
            tot = both[:, 0:128] / counts
    line = jnp.concatenate(line[0] + line[1], 1)
    for k in range(12):
        table[k : k + 1, :] = line[:, 128 * k : 128 * k + 128]
    gram, cross, mean, inv = level1_stats(gram_ref, w1_ref, counts)
    ones = gram[:, 27:28]
    grad = late[LATE_W1:LATE_SUMS, :] - ones * tot[0:1] - (cross - ones * mean) * inv * tot[1:2]
    grad = grad * (inv * bn_ref[0:1, 0:128])
    line = [jnp.zeros((1, STEM_SHIFT), f32)] + [grad[k : k + 1, 0:C1] for k in range(27)]
    line = jnp.concatenate(line, 1)
    for k in range(ROW_W2):
        frame[k : k + 1, :] = line[:, 128 * k : 128 * k + 128]
    squares = ends[0:1] + jnp.sum(frame[0:ROW_W3, :] * frame[0:ROW_W3, :], keepdims=True)
    squares = squares + jnp.sum(table[0:12, :] * table[0:12, :], keepdims=True)
    norm = jnp.sqrt(squares)
    facts_ref[0:1, :] = ends[1:2]
    facts_ref[1:2, :] = norm
    facts_ref[2:3, :] = jnp.minimum(1.0, clip_norm / norm)
    part = frame[pl.ds(at_ref[2], stem_ref.shape[0]), :]
    stem_out[...] = stem_ref[...] + unshift_lanes(part, at_ref[0], stem_len)
    part = table[pl.ds(at_ref[3], small_ref.shape[0]), :]
    small_out[...] = small_ref[...] + unshift_lanes(part, at_ref[1], small_len)


def call(kernel, outs, *args, scratch=(), smem=0, hbm=(), load=(), store=(), hbm_out=(), limit=32):
    def space(index, free):
        if index in free:
            return pl.BlockSpec(memory_space=pltpu.HBM)
        return pl.BlockSpec(memory_space=pltpu.VMEM)

    def shape(index):
        where = pltpu.HBM if index in (*hbm_out, *store) else jax.ShapeDtypeStruct
        return where(*outs[index])

    args = [
        pltpu.with_memory_space_constraint(arg, pltpu.HBM) if index in (*hbm, *load) else arg
        for index, arg in enumerate(args)
    ]
    count = len(args)
    moved = [jax.ShapeDtypeStruct(args[k].shape, args[k].dtype) for k in load]
    moved += [jax.ShapeDtypeStruct(*outs[k]) for k in store]

    def body(*refs):
        refs = list(refs)
        if not moved:
            return kernel(*refs)
        buffers, sems = refs[-1 - len(moved) : -1], refs[-1]
        refs = refs[: -1 - len(moved)]
        copies = []
        for k, index in enumerate(load):
            copies.append(pltpu.make_async_copy(refs[index], buffers[k], sems.at[k]))
            copies[-1].start()
            refs[index] = buffers[k]
        for copy in copies:
            copy.wait()
        targets = []
        for k, index in enumerate(store):
            targets.append((buffers[len(load) + k], refs[count + index], sems.at[len(load) + k]))
            refs[count + index] = buffers[len(load) + k]
        kernel(*refs)
        copies = [pltpu.make_async_copy(*target) for target in targets]
        for copy in copies:
            copy.start()
        for copy in copies:
            copy.wait()

    extra = [pltpu.VMEM(x.shape, x.dtype) for x in moved]
    if moved:
        extra.append(pltpu.SemaphoreType.DMA((len(moved),)))
    specs = [pl.BlockSpec(memory_space=pltpu.SMEM)] * smem
    specs += [space(index, (*hbm, *load)) for index in range(smem, count)]
    return pl.pallas_call(
        body,
        out_shape=[shape(index) for index in range(len(outs))],
        in_specs=specs,
        out_specs=[space(index, (*hbm_out, *store)) for index in range(len(outs))],
        scratch_shapes=[*scratch, *extra],
        compiler_params=pltpu.CompilerParams(vmem_limit_bytes=limit * 1024 * 1024),
    )(*args)


def adam_step(weight, first, second, grad, factor, rate):
    grad = grad * factor
    first = beta_one * first + (1.0 - beta_one) * grad
    second = beta_two * second + (1.0 - beta_two) * grad * grad
    first_fixed = first / (1.0 - beta_one**STEP)
    second_fixed = second / (1.0 - beta_two**STEP)
    return (
        weight
        - rate * (first_fixed / (jnp.sqrt(second_fixed) + adam_epsilon) + decay_rate * weight),
        first,
        second,
    )


def local(
    pixels,
    labels,
    stem,
    stem_first,
    stem_second,
    small,
    small_first,
    small_second,
    block,
    block_first,
    block_second,
    head,
    head_first,
    head_second,
):
    dp, mp = lax.axis_size("dp"), lax.axis_size("mp")
    n = dp * mp
    me, mine = lax.axis_index("dp"), lax.axis_index("mp")
    owner = me * mp + mine
    stem_len, small_len = stem.shape[0], small.shape[0]
    rows_stem = up16(-(-(stem_len + 127) // 128))
    rows_small = up16(-(-(small_len + 127) // 128))
    rows = rows_stem + rows_small
    everyone = ("dp", "mp")

    def share(x):
        return lax.all_to_all(x, everyone, 0, 0)

    part = FF // mp
    cls = CLASSES // mp
    cls_pad = 512 // (mp // 2)
    packed = jnp.concatenate(
        [block[0], block[1], block[2], jnp.pad(head, ((0, 0), (0, cls_pad - cls)))], 1
    ).astype(bf16)
    stem_at, small_at = owner * stem_len + STEM_SHIFT, owner * small_len + SMALL_SHIFT
    at = jnp.stack(
        [
            stem_at % 128,
            small_at % 128,
            jnp.minimum(stem_at // 128, ROW_W3),
            jnp.minimum(small_at // 128, 16),
        ]
    ).astype(jnp.int32)
    (piece,) = call(
        pack_kernel,
        [((rows, 128), bf16)],
        at,
        jnp.pad(stem, (0, rows_stem * 128 - stem_len)).reshape(rows_stem, 128),
        jnp.pad(small, (0, rows_small * 128 - small_len)).reshape(rows_small, 128),
        smem=1,
        limit=4,
    )

    strip = pixels.reshape(pixels.shape[1], 128)
    strip, piece, packed, at = lax.optimization_barrier((strip, piece, packed, at))
    gathered = lax.all_gather(packed, everyone, axis=0)
    half = strip.shape[0] // 2
    pairs = [(source, (source + dp - 1) % dp) for source in range(dp)]
    lower = lax.ppermute(strip[:half], "dp", pairs)

    if (dp, mp) == (16, 2):
        gathered = gathered.reshape(16, 2, 48, packed.shape[1])
    else:
        g = gathered.reshape(dp, mp, D // dp, packed.shape[1])
        g = jnp.transpose(g, (0, 2, 1, 3)).reshape(D, mp, -1)
        slots = [g[:, :, k * part : (k + 1) * part].reshape(D, 2, FF // 2) for k in range(3)]
        top = g[:, :, 3 * part : 3 * part + cls].reshape(D, 2, CLASSES // 2)
        slots.append(jnp.pad(top, ((0, 0), (0, 0), (0, 12))))
        g = jnp.concatenate(slots, 2).reshape(16, 48, 2, -1)
        gathered = jnp.transpose(g, (0, 2, 1, 3))

    xk, gram = call(
        image_kernel,
        [((8, T, 192), bf16), ((n, 8, 128), f32)],
        strip[half:],
        lower,
        scratch=[
            pltpu.VMEM((2 * half, 128), f32),
            pltpu.VMEM((16 * half // 3 + 16, 128), f32),
            pltpu.VMEM((17, T, 64), bf16),
        ],
        limit=12,
    )
    column = lax.all_to_all(jnp.broadcast_to(piece[None], (dp, rows, 128)), "dp", 0, 0)
    gram, xk, column = lax.optimization_barrier((gram, xk, column))
    gram = share(gram)
    if mp == 2:
        swap = [(0, 1), (1, 0)]
        pieces = [column, lax.ppermute(column, "mp", swap)]
        which = jnp.stack([mine, 1 - mine]).astype(jnp.int32)
    else:
        columns = lax.all_gather(column, "mp", axis=0)
        pieces = [columns[k] for k in range(mp)]
        which = jnp.arange(mp, dtype=jnp.int32)
    frame_rows = (stem_len * n + STEM_SHIFT) // 128 + rows_stem + 16
    table_rows = (small_len * n + SMALL_SHIFT) // 128 + rows_small + 16
    frames = [pltpu.VMEM((frame_rows, 128), f32), pltpu.VMEM((table_rows, 128), f32)]
    w1, t1, t2, t3, t4, wp, bn, vec, pos = call(
        functools.partial(assemble_kernel, len(pieces), mp, stem_len, small_len, rows_stem, rows_small),
        [
            ((32, 128), f32),
            ((192, W), bf16),
            ((3, W + C1, W), bf16),
            ((3, W + C2, W), bf16),
            ((3, W + C3, W), bf16),
            ((C4, D), bf16),
            ((8, W), f32),
            ((24, D), f32),
            ((T, D), f32),
        ],
        jnp.concatenate([which, labels.reshape(1)]),
        *pieces,
        smem=1,
        store=(1, 2, 3, 4, 5, 7, 8),
        scratch=frames
        + [
            pltpu.VMEM((9 * C1, 128), f32),
            pltpu.VMEM((9 * C2, 128), f32),
            pltpu.VMEM((9 * C2, 128), f32),
            pltpu.VMEM((192, W), f32),
            pltpu.VMEM((W + C1, W), f32),
            pltpu.VMEM((W + C2, W), f32),
        ],
        limit=20,
    )

    positions = SIDE * SIDE * n
    counts = [None, 64.0 * positions, 16.0 * positions, 4.0 * positions, 1.0 * positions]
    ax, conv, st = call(
        functools.partial(conv12_kernel, counts[1]),
        [((9, T, W + C1), bf16), ((4, T, W), f32), ((n, 2, W), f32)],
        xk,
        gram,
        w1,
        t1,
        bn,
        t2,
        load=(3, 5),
        limit=14,
    )
    convs = [None, None, conv]
    stats = [None, None, share(st)]
    inputs = [None, None, ax]
    kernels = [None, t1, t2, t3, t4]
    for level in (3, 4):
        r = 2 ** (4 - level)
        ax, conv, st = call(
            functools.partial(conv_kernel, level - 1, counts[level - 1]),
            [((2 * r + 1, T, W + CHANS[level - 1]), bf16), ((r, T, W), f32), ((n, 2, W), f32)],
            convs[level - 1],
            stats[level - 1],
            bn,
            kernels[level],
            load=(3,),
            store=(1, 2) if level == 4 else (),
            limit=10,
        )
        inputs.append(ax)
        convs.append(conv)
        stats.append(share(st))

    stats[4], gathered = lax.optimization_barrier((stats[4], gathered))
    fast = (dp, mp) == (16, 2)
    outs = call(
        functools.partial(block_kernel, counts[4]),
        [
            ((4, 2, 4, 48, FF), bf16),
            ((1, T, W), f32),
            ((n, 2, W), f32),
            ((32, D), f32),
            ((T, D), f32),
            ((C4, D), f32),
        ],
        stats[4],
        bn,
        convs[4],
        wp,
        pos,
        vec,
        gathered,
        hbm=(2, 3, 4, 5, 6),
        hbm_out=(0, 1, 2, 3, 4, 5),
        limit=40,
        scratch=[
            pltpu.VMEM((1, T, W), f32),
            pltpu.VMEM((C4, D), bf16),
            pltpu.VMEM((T, D), f32),
            pltpu.VMEM((24, D), f32),
            pltpu.VMEM((1, T, W), f32),
            pltpu.VMEM((n, 2, W), f32),
            pltpu.VMEM((32, D), f32),
            pltpu.VMEM((T, D), f32),
            pltpu.VMEM((C4, D), f32),
            pltpu.VMEM((2, 16, 48, 1536), bf16),
            pltpu.VMEM((2, 16, 48, 1536), bf16),
            pltpu.VMEM((2, 16, 48, 1536), bf16),
            pltpu.VMEM((2, 16, 48, 512), bf16),
            pltpu.SemaphoreType.DMA((33,)),
            pltpu.VMEM((T, W), bf16),
            pltpu.VMEM((T, D), f32),
            pltpu.VMEM((T, D), bf16),
            pltpu.VMEM((T, 3 * D), bf16),
            pltpu.VMEM((HEADS, T, T), f32),
            pltpu.VMEM((T, D), bf16),
            pltpu.VMEM((D, T), bf16),
            pltpu.VMEM((2, T, 1536), f32),
            pltpu.VMEM((T, D), f32),
            pltpu.VMEM((T, 3 * D), bf16),
        ],
    )
    grads, back, tot, facts, gpos, dwp = outs
    tot = share(tot)
    if fast:
        planes = [[8 * z + k for k in range(8)] for z in range(4)]
        owned = lax.psum_scatter(
            grads.reshape(8 * 4 * 48, FF),
            everyone,
            scatter_dimension=0,
            tiled=True,
            axis_index_groups=planes,
        )
        lines = [[8 * z + k for z in range(4)] for k in range(8)]
        owned = [
            lax.psum_scatter(
                owned, everyone, scatter_dimension=0, tiled=True, axis_index_groups=lines
            )
        ]
    else:
        g = jnp.transpose(grads, (2, 0, 3, 1, 4)).reshape(D, 2, 2, FF // 2)
        g = jnp.transpose(g, (0, 2, 1, 3)).reshape(dp, D // dp, 2, mp, part)
        g = jnp.transpose(g, (0, 3, 1, 2, 4)).reshape(n * (D // dp), 2 * part)
        owned = [lax.psum_scatter(g, everyone, scatter_dimension=0, tiled=True)]

    rows_d = D // dp
    rows_vec = 48 if fast else 0

    def outer(bo_all, fin_all, hs_all, bl_all):
        return dot_tn(bo_all, hs_all), dot_tn(fin_all, bl_all)

    if not fast:
        bo, fin = facts[OUT_BACK : OUT_BACK + 1], facts[OUT_FINAL : OUT_FINAL + 1]
        hs, bl = facts[OUT_HIDDEN:OUT_HEAD].reshape(1, FF), facts[OUT_HEAD:OUT_SUMS, 0:512].reshape(1, 1024)
        head_line = jnp.concatenate([bl[:, :500], bl[:, 512:1012]], 1).reshape(1, mp, cls)
        line = jnp.concatenate(
            [
                jnp.broadcast_to(bo.reshape(dp, 1, rows_d), (dp, mp, rows_d)),
                jnp.broadcast_to(fin.reshape(dp, 1, rows_d), (dp, mp, rows_d)),
                jnp.broadcast_to(hs.reshape(1, mp, part), (dp, mp, part)),
                jnp.broadcast_to(head_line, (dp, mp, cls)),
            ],
            2,
        ).reshape(n, -1)
        width = -(-line.shape[1] // 1024) * 1024
        line = jnp.pad(line, ((0, 0), (0, width - line.shape[1]))).astype(bf16)
        line = share(line.reshape(n, width // 128, 128)).reshape(n, width)
        cuts = [0, rows_d, 2 * rows_d, 2 * rows_d + part, 2 * rows_d + part + cls]
        grad_down, grad_head = outer(*[line[:, a:b] for a, b in zip(cuts[:-1], cuts[1:])])

    sums = [None] * 5
    kernel_grads = [None] * 5
    for level in (4, 3):
        r = 2 ** (4 - level)
        chan_in = CHANS[level - 1]
        g, back, so, sums[level - 1] = call(
            functools.partial(conv_back_kernel, level, counts[level], counts[level - 1]),
            [
                ((r + 1, T, W), bf16),
                ((2 * r, T, W), f32),
                ((n, 2, W), f32),
                ((2, W), f32),
            ],
            back,
            tot,
            convs[level],
            stats[level],
            kernels[level],
            convs[level - 1],
            stats[level - 1],
            bn,
            load=(0, 2, 4) if level == 4 else (4,),
            limit=12,
        )
        (kernel_grads[level],) = call(
            functools.partial(kernel_grad, level),
            [((-(-CHANS[level] // 128), 9 * chan_in, 128), f32)],
            inputs[level],
            g,
            scratch=[pltpu.VMEM((3, W + chan_in, W), f32)],
            limit=12,
        )
        if level == 4:
            so, kernel_grads[4] = lax.optimization_barrier((so, kernel_grads[4]))
            tot = share(so)
    outs = call(
        functools.partial(early_kernel, len(pieces), mp, stem_len, small_len, rows_stem, rows_small),
        [((dp, rows + rows_vec, 128), bf16)] * len(pieces),
        which,
        kernel_grads[3],
        kernel_grads[4],
        dwp,
        facts,
        gpos,
        smem=1,
        load=(3, 4, 5),
        scratch=frames + [pltpu.VMEM((48, 128), f32)],
        limit=18,
    )
    if mp == 2:
        column = outs[0] + lax.ppermute(outs[1], "mp", swap)
    else:
        column = lax.psum_scatter(jnp.stack(outs, 0), "mp", scatter_dimension=0)
    so, column = lax.optimization_barrier((so, column))
    tot = share(so)
    tot, column = lax.optimization_barrier((tot, column))
    column = lax.all_to_all(column, "dp", 0, 0)
    each = -(-LATE_ROWS // n)
    (late,) = call(
        functools.partial(conv2_back_kernel, counts[2], counts[1]),
        [((n, each, 128), f32)],
        back,
        tot,
        convs[2],
        stats[2],
        inputs[2],
        t2,
        xk,
        gram,
        w1,
        t1,
        bn,
        *sums[2:4],
        facts,
        load=(5, 9, 13),
        scratch=[
            pltpu.VMEM((1, 9 * C1, 128), f32),
            pltpu.VMEM((5, T, W), bf16),
            pltpu.VMEM((3, W + C1, W), f32),
            pltpu.VMEM((192, W), f32),
            pltpu.VMEM((n * each, 128), f32),
        ],
        limit=20,
    )
    late, column = lax.optimization_barrier((late, column))
    late = share(late)
    if fast:
        line = column[:, rows:].reshape(2 * dp, 24, 128)
        grad_down, grad_head = outer(
            line[:, 16, 0:48],
            line[:, 16, 64:112],
            line[:, 0:12].reshape(2 * dp, part),
            line[:, 12:16].reshape(2 * dp, 512)[:, :cls],
        )
    grad_stem, grad_small, squares = call(
        functools.partial(unpack_kernel, stem_len, small_len),
        [((rows_stem, 128), f32), ((rows_small, 128), f32), ((1, 128), f32)],
        at,
        column,
        smem=1,
        limit=8,
    )

    g0, g1, ends = call(
        functools.partial(sum_kernel, len(owned)),
        [((rows_d, part), f32), ((rows_d, part), f32), ((n, each + 2, 128), f32)],
        *owned,
        late,
        squares,
        grad_down,
        grad_head,
        facts,
        limit=8,
    )
    grad_stem, grad_small, facts = call(
        functools.partial(last_kernel, counts[1], stem_len, small_len),
        [((rows_stem, 128), f32), ((rows_small, 128), f32), ((3, 128), f32)],
        at,
        share(ends),
        gram,
        w1,
        bn,
        grad_stem,
        grad_small,
        smem=1,
        scratch=[
            pltpu.VMEM((n * each, 128), f32),
            pltpu.VMEM((ROW_W3 + rows_stem, 128), f32),
            pltpu.VMEM((16 + rows_small, 128), f32),
        ],
        limit=8,
    )
    grad_stem = grad_stem.reshape(-1)[:stem_len]
    grad_small = grad_small.reshape(-1)[:small_len]
    loss_sum, grad_norm, factor = facts[0, 0], facts[1, 0], facts[2, 0]
    grad_block = jnp.stack([g0, g1, grad_down], 0)
    stem_new = adam_step(stem, stem_first, stem_second, grad_stem, factor, rate_stem)
    small_new = adam_step(small, small_first, small_second, grad_small, factor, rate_small)
    block_new = adam_step(block, block_first, block_second, grad_block, factor, rate_block)
    head_new = adam_step(head, head_first, head_second, grad_head, factor, rate_head)
    return (*stem_new, *small_new, *block_new, *head_new, loss_sum, grad_norm)


def solution(mesh):
    flat = P(("dp", "mp"))
    matrix = P(None, "dp", "mp")
    head = P("dp", "mp")
    states = (flat,) * 6 + (matrix,) * 3 + (head,) * 3
    return jax.shard_map(
        local,
        mesh=mesh,
        in_specs=(P("mp", "dp", None), P("mp", "dp")) + states,
        out_specs=states + (P(), P()),
        check_vma=False,
    )
```

```python
import functools

import jax
import jax.numpy as jnp
from jax import lax
from jax.experimental import pallas as pl
from jax.experimental.pallas import tpu as pltpu
from jax.sharding import PartitionSpec as P

D = 768
HEADS = 12
HEAD_DIM = 64
FF = 3072
CLASSES = 1000
C1 = 48
C2 = 96
C3 = 192
C4 = 384
STEP = 10
TOK = 197
SIDE = 14
T = 16 * SIDE
W = 384
CHANS = (3, C1, C2, C3, C4)

beta_one = 0.9
beta_two = 0.999
adam_epsilon = 1e-08
decay_rate = 0.05
clip_norm = 1.0
rate_stem = 0.05
rate_small = 0.5
rate_block = 0.05
rate_head = 0.05
batch_epsilon = 1e-05
layer_epsilon = 1e-06
smoothing = 0.1

bf16 = jnp.bfloat16
f32 = jnp.float32

STEM_SHIFT = 112
SMALL_SHIFT = 96
ROW_W2 = 11
ROW_W3 = ROW_W2 + 9 * C1 * C2 // 128
ROW_W4 = ROW_W3 + 9 * C2 * C3 // 128
ROW_WP = ROW_W4 + 9 * C3 * C4 // 128
STEM_ROWS = ROW_WP + C4 * D // 128
SMALL_NAMES = (
    ("proj_bias", 6),
    ("class_token", 6),
    ("position", 6 * TOK),
    ("norm1_gain", 6),
    ("norm1_bias", 6),
    ("query_bias", 6),
    ("value_bias", 6),
    ("out_bias", 6),
    ("norm2_gain", 6),
    ("norm2_bias", 6),
    ("hidden_bias", 24),
    ("mlp_bias", 6),
    ("final_gain", 6),
    ("final_bias", 6),
    ("head_bias", 8),
)
SMALL_AT = {}
_row = 12
for _name, _rows in SMALL_NAMES:
    SMALL_AT[_name] = _row
    _row += _rows
SMALL_ROWS = _row
VEC_NAMES = (
    "proj_bias",
    "norm1_gain",
    "norm1_bias",
    "query_bias",
    "value_bias",
    "out_bias",
    "norm2_gain",
    "norm2_bias",
    "mlp_bias",
    "final_gain",
    "final_bias",
)
VEC = {name: index for index, name in enumerate(VEC_NAMES)}
VEC_HIDDEN = 12
VEC_HEAD = 16
VEC_AIM = 18
OUT_BACK = 16
OUT_FINAL = 17
OUT_HIDDEN = 18
OUT_HEAD = 22
OUT_SUMS = 24
OUT_LOSS = 25


def dot(a, b):
    return jnp.dot(a, b, preferred_element_type=f32)


def dot_nt(a, b):
    return lax.dot_general(a, b, (((1,), (1,)), ((), ())), preferred_element_type=f32)


def dot_tn(a, b):
    return lax.dot_general(a, b, (((0,), (0,)), ((), ())), preferred_element_type=f32)


GELU_A = 0.7978845608028654
GELU_B = 0.044715


def gelu(x):
    return 0.5 * x * (1.0 + jnp.tanh(GELU_A * (x + GELU_B * x * x * x)))


def gelu_slope(x):
    t = jnp.tanh(GELU_A * (x + GELU_B * x * x * x))
    return 0.5 * (1.0 + t) + 0.5 * x * (1.0 - t * t) * GELU_A * (1.0 + 3.0 * GELU_B * x * x)


def dot_f32(a, b):
    return jnp.dot(a, b, preferred_element_type=f32, precision=lax.Precision.HIGHEST)


def up16(n):
    return -(-n // 16) * 16


def colsum(x):
    return jnp.sum(x, 0, keepdims=True)


def slot_index():
    return lax.broadcasted_iota(jnp.int32, (T, 1), 0)


def patch_mask():
    return ((slot_index() & 15) < SIDE).astype(f32)


def token_mask():
    p = slot_index()
    return (((p & 15) < SIDE) | (p == SIDE)).astype(f32)


def fold_phases(x, chan):
    step = W // 2
    while step >= chan:
        x = x + jnp.concatenate([x[:, step:], x[:, :step]], 1)
        step //= 2
    return x


def bn_stats(st_ref, count, chan):
    tot = fold_phases(jnp.sum(st_ref[:, 0:2, :], 0), chan)
    mean = tot[0:1] / count
    inv = lax.rsqrt(tot[1:2] / count - mean * mean + batch_epsilon)
    return mean, inv


def shift_lanes(x, s):
    lane = lax.broadcasted_iota(jnp.int32, x.shape, 1)
    row = lax.broadcasted_iota(jnp.int32, x.shape, 0)
    moved = pltpu.roll(x, s, 1)
    before = jnp.where(row == 0, 0.0, pltpu.roll(moved, 1, 0))
    return jnp.where(lane >= s, moved, before)


def pack_kernel(at_ref, stem_ref, small_ref, out_ref):
    rows = stem_ref.shape[0]
    out_ref[0:rows, :] = shift_lanes(stem_ref[...], at_ref[0]).astype(bf16)
    out_ref[rows:, :] = shift_lanes(small_ref[...], at_ref[1]).astype(bf16)


def flat_lanes(ref, row, count):
    return jnp.concatenate([ref[row + k : row + k + 1, :] for k in range(count)], 1)


def assemble_kernel(parts, mp, stem_len, small_len, rows_stem, rows_small, at_ref, *refs):
    pieces = refs[:parts]
    s1, t1_ref, t2_ref, t3_ref, t4_ref, wp_ref, bn_ref, vec_ref, pos_ref = refs[parts : parts + 9]
    frame, table, s2, s3a, s3b, u1, u2, u3 = refs[parts + 9 :]
    frame[...] = jnp.zeros_like(frame)
    table[...] = jnp.zeros_like(table)
    for index, ref in enumerate(pieces):
        mv = at_ref[index]

        def put(d, carry):
            owner = d * mp + mv
            a = (owner * stem_len + STEM_SHIFT) // 128
            frame[pl.ds(a, rows_stem), :] += ref[d, 0:rows_stem, :].astype(f32)
            b = (owner * small_len + SMALL_SHIFT) // 128
            table[pl.ds(b, rows_small), :] += ref[d, rows_stem : rows_stem + rows_small, :].astype(f32)
            return carry

        lax.fori_loop(0, ref.shape[0], put, 0)
    s1[...] = jnp.zeros_like(s1)
    flat = flat_lanes(frame, 0, ROW_W2)
    for k in range(27):
        s1[k : k + 1, 0:C1] = flat[:, STEM_SHIFT + 48 * k : STEM_SHIFT + 48 * k + 48]
    u1[...] = jnp.zeros_like(u1)
    for tap in range(3):
        for j in range(8):
            cols = slice(j * C1, (j + 1) * C1)
            if j == 0:
                u1[tap * 64 + 48 : tap * 64 + 51, cols] = s1[tap * 9 : tap * 9 + 3, 0:C1]
                u1[tap * 64 : tap * 64 + 6, cols] = s1[tap * 9 + 3 : tap * 9 + 9, 0:C1]
            else:
                at = tap * 64 + 6 * j - 3
                u1[at : at + 9, cols] = s1[tap * 9 : tap * 9 + 9, 0:C1]
    t1_ref[...] = u1[...].astype(bf16)
    q = 9 * C1 // 4
    wide = jnp.concatenate([frame[pl.ds(ROW_W2 + k, q, stride=3), :] for k in range(3)], 1)
    for k in range(4):
        s2[pl.ds(k, q, stride=4), 0:C2] = wide[:, k * C2 : (k + 1) * C2]
    q = 9 * C2 // 2
    wide = jnp.concatenate([frame[pl.ds(ROW_W3 + k, q, stride=3), :] for k in range(3)], 1)
    for k in range(2):
        part = wide[:, k * C3 : (k + 1) * C3]
        s3a[pl.ds(k, q, stride=2), :] = part[:, 0:128]
        s3b[pl.ds(k, q, stride=2), 0 : C3 - 128] = part[:, 128:C3]
    for ref, chan_in, chan_out, src, u in (
        (t2_ref, C1, C2, (s2,), u2),
        (t3_ref, C2, C3, (s3a, s3b), u3),
    ):
        for tap in range(3):
            u[...] = jnp.zeros_like(u)
            base = tap * 3 * chan_in
            for j in range(W // chan_out):
                for k, s in enumerate(src):
                    width = min(128, chan_out - 128 * k)
                    cols = slice(j * chan_out + 128 * k, j * chan_out + 128 * k + width)
                    if j == 0:
                        u[W : W + chan_in, cols] = s[base : base + chan_in, 0:width]
                        u[0 : 2 * chan_in, cols] = s[base + chan_in : base + 3 * chan_in, 0:width]
                    else:
                        at = (2 * j - 1) * chan_in
                        u[at : at + 3 * chan_in, cols] = s[base : base + 3 * chan_in, 0:width]
            ref[tap] = u[...].astype(bf16)
    for tap in range(3):
        rows = 3 * C3
        for k in range(3):
            lanes = slice(k * 128, (k + 1) * 128)
            at = ROW_W4 + k + 3 * tap * rows
            t4_ref[tap, 0 : 2 * C3, lanes] = frame[pl.ds(at + 3 * C3, 2 * C3, stride=3), :].astype(bf16)
            t4_ref[tap, 2 * C3 : 3 * C3, lanes] = frame[pl.ds(at, C3, stride=3), :].astype(bf16)
    for k in range(6):
        lanes = slice(k * 128, (k + 1) * 128)
        wp_ref[:, lanes] = frame[pl.ds(ROW_WP + k, C4, stride=6), :].astype(bf16)
    flat = flat_lanes(table, 0, 12)
    first = SMALL_SHIFT
    for level in range(4):
        chan = CHANS[level + 1]
        for which in range(2):
            at = first + which * (C1 + C2 + C3 + C4)
            part = flat[:, at : at + chan]
            row = 2 * level + which
            for j in range(W // chan):
                bn_ref[row : row + 1, j * chan : (j + 1) * chan] = part
        first += chan
    vec_ref[...] = jnp.zeros_like(vec_ref)
    for name, index in VEC.items():
        vec_ref[index : index + 1, :] = flat_lanes(table, SMALL_AT[name], 6)
    for k in range(4):
        row = VEC_HIDDEN + k
        vec_ref[row : row + 1, :] = flat_lanes(table, SMALL_AT["hidden_bias"] + 6 * k, 6)
    flat = flat_lanes(table, SMALL_AT["head_bias"], 8)
    lane = lax.broadcasted_iota(jnp.int32, (1, 512), 1)
    for m in range(2):
        vec_ref[VEC_HEAD + m : VEC_HEAD + m + 1, 0:500] = flat[:, 500 * m : 500 * m + 500]
        aim = jnp.where(lane + 500 * m == at_ref[parts], 1.0 - smoothing, 0.0) + smoothing / CLASSES
        vec_ref[VEC_AIM + m : VEC_AIM + m + 1, 0:512] = jnp.where(lane < 500, aim, 0.0)
    pos_ref[...] = jnp.zeros_like(pos_ref)
    at = SMALL_AT["position"]
    for k in range(6):
        lanes = slice(k * 128, (k + 1) * 128)
        for r in range(SIDE):
            rows = table[pl.ds(at + k + 6 * (1 + SIDE * r), SIDE, stride=6), :]
            pos_ref[16 * r : 16 * r + SIDE, lanes] = rows
        mark = SMALL_AT["class_token"] + k
        pos_ref[SIDE : SIDE + 1, lanes] = table[mark : mark + 1, :] + table[at + k : at + k + 1, :]


def image_kernel(own_ref, next_ref, xk_ref, gram_ref, flat, chunks, xe):
    half = own_ref.shape[0]
    flat[0:half, :] = own_ref[...].astype(f32)
    flat[half : 2 * half, :] = next_ref[...].astype(f32)
    n = 2 * half // 3
    wide = jnp.concatenate([flat[pl.ds(k, n, stride=3), :] for k in range(3)], 1)
    for j in range(8):
        chunks[pl.ds(j, n, stride=8), 0:48] = wide[:, 48 * j : 48 * j + 48]
    mask = patch_mask()
    lane = lax.broadcasted_iota(jnp.int32, (T, 64), 1)

    def spread(i, carry):
        rows = [chunks[pl.ds(16 * SIDE * r + SIDE * i, 16), 0:64] for r in range(SIDE)]
        x = jnp.where(lane < 48, jnp.concatenate(rows, 0), 0.0) * mask
        left = pltpu.roll(jnp.concatenate([x, x], 1), 3, 1)[:, 0:64]
        left = jnp.where((lane >= 48) & (lane < 51), pltpu.roll(left, 1, 0), 0.0)
        xe[i + 1] = ((x + left) * mask).astype(bf16)
        return carry

    chunks[pl.ds(n * 8, 16), :] = jnp.zeros((16, 128), f32)
    lax.fori_loop(0, 16, spread, 0)
    last = xe[16]
    xe[0] = jnp.concatenate([jnp.zeros((16, 64), bf16), last[: T - 16]], 0)

    def step(i, carry):
        gram, ones = carry
        x = jnp.concatenate([xe[2 * i], xe[2 * i + 1], xe[2 * i + 2]], 1)
        xk_ref[i] = x
        return gram + dot_tn(x, x), ones + colsum(x.astype(f32))

    gram, ones = lax.fori_loop(0, 8, step, (jnp.zeros((192, 192), f32), jnp.zeros((1, 192), f32)))
    row = lax.broadcasted_iota(jnp.int32, (192, 256), 0)
    col = lax.broadcasted_iota(jnp.int32, (192, 256), 1)
    j, k = col >> 5, col & 31
    tap = (k >= 9).astype(jnp.int32) + (k >= 18).astype(jnp.int32)
    u = k - 9 * tap
    at = 64 * tap + jnp.where(j == 0, jnp.where(u < 3, 48 + u, u - 3), 6 * j - 3 + u)
    pick = ((row == at) & (k < 27)).astype(f32)
    both = lax.dot_general(
        pick,
        dot_f32(gram, pick),
        (((0,), (0,)), ((), ())),
        preferred_element_type=f32,
        precision=lax.Precision.HIGHEST,
    )
    ones = dot_f32(jnp.broadcast_to(ones, (8, 192)), pick)[0:1]
    total = jnp.zeros((32, 32), f32)
    line = jnp.zeros((1, 32), f32)
    for q in range(8):
        lanes = slice(32 * q, 32 * q + 32)
        total = total + both[lanes, lanes]
        line = line + ones[:, lanes]
    r32 = lax.broadcasted_iota(jnp.int32, (32, 32), 0)
    c32 = lax.broadcasted_iota(jnp.int32, (32, 32), 1)
    total = total + jnp.where(r32 == 27, line, 0.0)
    column = jnp.sum(jnp.where(r32 == c32, line, 0.0), 1, keepdims=True)
    total = total + jnp.where(c32 == 27, column, 0.0)
    flat8 = jnp.concatenate([total[8 * q : 8 * q + 8] for q in range(4)], 1)
    gram_ref[...] = jnp.broadcast_to(flat8[None], gram_ref.shape)


def level1_stats(gram_ref, w1_ref, count):
    flat8 = jnp.sum(gram_ref[...], 0)
    gram = jnp.concatenate([flat8[:, 32 * q : 32 * q + 32] for q in range(4)], 0)
    cross = dot_f32(gram, w1_ref[...])
    mean = cross[27:28] / count
    squares = colsum(w1_ref[...] * cross) / count
    inv = lax.rsqrt(squares - mean * mean + batch_epsilon)
    return gram, cross, mean, inv


def tile_lanes(x, chan):
    return jnp.concatenate([x[:, 0:chan]] * (W // chan), 1)


def conv12_kernel(count, xk_ref, gram_ref, w1_ref, t1_ref, bn_ref, t_ref, ax_ref, out_ref, st_ref):
    gram, cross, mean, inv = level1_stats(gram_ref, w1_ref, count)
    mean, inv = tile_lanes(mean, C1), tile_lanes(inv, C1)
    gain, bias = bn_ref[0:1, :], bn_ref[1:2, :]
    mask = patch_mask()
    weights = t1_ref[...]

    def activate(i, carry):
        a = gelu((dot(xk_ref[i], weights) - mean) * inv * gain + bias) * mask
        put_input(ax_ref, i, a, C1)
        return carry

    lax.fori_loop(0, 8, activate, 0)
    convolve(8, ax_ref, t_ref, out_ref, st_ref, mask, C1)


def put_input(ax_ref, i, a, chan):
    left = pltpu.roll(a[:, W - chan :], 1, 0)
    ax_ref[i + 1, :, 0:W] = a.astype(bf16)
    ax_ref[i + 1, :, W:] = left.astype(bf16)


def convolve(rows, ax_ref, t_ref, out_ref, st_ref, mask, chan):
    last = ax_ref[rows]
    ax_ref[0] = jnp.concatenate([jnp.zeros((16, W + chan), bf16), last[: T - 16]], 0)

    def step(i, carry):
        first, second = carry
        y = dot(ax_ref[2 * i], t_ref[0])
        y = y + dot(ax_ref[2 * i + 1], t_ref[1])
        y = y + dot(ax_ref[2 * i + 2], t_ref[2])
        out_ref[i] = y
        ym = y * mask
        return first + colsum(ym), second + colsum(ym * y)

    zero = jnp.zeros((1, W), f32)
    first, second = lax.fori_loop(0, rows // 2, step, (zero, zero))
    st = jnp.concatenate([first, second], 0)
    st_ref[...] = jnp.broadcast_to(st[None], st_ref.shape)


def conv_kernel(level, count, c_ref, stin_ref, bn_ref, t_ref, ax_ref, out_ref, st_ref):
    chan = CHANS[level]
    rows = c_ref.shape[0]
    mean, inv = bn_stats(stin_ref, count, chan)
    gain = bn_ref[2 * level - 2 : 2 * level - 1, :]
    bias = bn_ref[2 * level - 1 : 2 * level, :]
    mask = patch_mask()

    def activate(i, carry):
        put_input(ax_ref, i, gelu((c_ref[i] - mean) * inv * gain + bias) * mask, chan)
        return carry

    lax.fori_loop(0, rows, activate, 0)
    convolve(rows, ax_ref, t_ref, out_ref, st_ref, mask, chan)


def layer_norm(x):
    centered = x - jnp.mean(x, -1, keepdims=True)
    inv = lax.rsqrt(jnp.mean(centered * centered, -1, keepdims=True) + layer_epsilon)
    return centered * inv, inv


def layer_norm_back(dy, s, inv, gain):
    scaled = dy * gain
    inner = scaled - jnp.mean(scaled, -1, keepdims=True)
    return inv * (inner - s * jnp.mean(scaled * s, -1, keepdims=True))


def normed4(count, st_ref, bn_ref, c_ref):
    mean, inv = bn_stats(st_ref, count, C4)
    s = (c_ref[0] - mean) * inv
    return s, s * bn_ref[6:7, :] + bn_ref[7:8, :]


def embed_kernel(count, st_ref, bn_ref, c_ref, wp_ref, pos_ref, vec_ref, a4_ref, x0_ref, n1_ref):
    def vec(name):
        return vec_ref[VEC[name] : VEC[name] + 1, :]

    mask = patch_mask()
    _, y4 = normed4(count, st_ref, bn_ref, c_ref)
    a4_ref[...] = (gelu(y4) * mask).astype(bf16)
    x0 = (dot(a4_ref[...], wp_ref[...]) + vec("proj_bias")) * mask + pos_ref[...]
    x0_ref[...] = x0
    s1, _ = layer_norm(x0)
    n1_ref[...] = (s1 * vec("norm1_gain") + vec("norm1_bias")).astype(bf16)


def block_kernel(
    count,
    st_ref,
    bn_ref,
    n1_hbm,
    vec_hbm,
    x0_hbm,
    a4_hbm,
    wp_hbm,
    c_hbm,
    g_ref,
    gr_ref,
    bn4_hbm,
    so_hbm,
    out_hbm,
    gpos_hbm,
    dwp_hbm,
    c_ref,
    wp_ref,
    vec_ref,
    bn4_ref,
    so_ref,
    out_ref,
    gpos_ref,
    dwp_ref,
    wa,
    wu,
    wd,
    wh,
    sems,
    a4,
    x0,
    n1,
    qkv,
    probs,
    mixed,
    n2t,
    pre,
    acc,
    bqkv,
    mixed_f,
    bpre,
    rowbuf,
):
    gr0, gr1 = wu, wd
    fetched = []
    for k, (source, ref) in enumerate(
        ((n1_hbm, n1), (vec_hbm, vec_ref), (x0_hbm, x0), (a4_hbm, a4), (wp_hbm, wp_ref), (c_hbm, c_ref))
    ):
        fetched.append(pltpu.make_async_copy(source, ref, sems.at[24 + k]))
        if k < 2:
            fetched[-1].start()
    copies = []
    for k, (ref, at, size) in enumerate(
        ((wa, 0, 1536), (wu, 1536, 1536), (wd, 3072, 1536), (wh, 4608, 512))
    ):
        for m in range(2):
            copy = pltpu.make_async_copy(
                g_ref.at[:, m, :, at : at + size], ref.at[m], sems.at[2 * k + m]
            )
            copy.start()
            copies.append(copy)
        if k == 0:
            for copy in fetched[2:]:
                copy.start()

    def send_out(grad, slot):
        out = []
        lanes = slice(1536 * slot, 1536 * slot + 1536)
        for m in range(2):
            for z in range(4):
                copy = pltpu.make_async_copy(
                    grad.at[m, 4 * z : 4 * z + 4],
                    gr_ref.at[:, m, z, :, lanes],
                    sems.at[8 + 8 * slot + 4 * m + z],
                )
                copy.start()
                out.append(copy)
        return out

    def write(ref, target, k):
        copy = pltpu.make_async_copy(ref, target, sems.at[30 + k])
        copy.start()
        moving.append(copy)

    def vec(name):
        return vec_ref[VEC[name] : VEC[name] + 1, :]

    mask = patch_mask()
    valid = token_mask()
    out_row = lax.broadcasted_iota(jnp.int32, (32, 1), 0)
    out_ref[...] = jnp.zeros_like(out_ref)
    key = lax.broadcasted_iota(jnp.int32, (1, T), 1)
    key_bias = jnp.where(((key & 15) < SIDE) | (key == SIDE), 0.0, -1e30)

    for copy in fetched[:2]:
        copy.wait()
    copies[0].wait()
    copies[1].wait()

    def tile(ref, m, at, size=256):
        return ref[m, :, :, pl.ds(at, size)].reshape(D, size)

    for part in range(9):
        y = dot(n1[...], tile(wa, part // 6, 256 * (part % 6)))
        lanes = slice(256 * (part % 3), 256 * (part % 3) + 256)
        if part < 3:
            y = y + vec("query_bias")[:, lanes]
        elif part >= 6:
            y = y + vec("value_bias")[:, lanes]
        qkv[:, 256 * part : 256 * part + 256] = y.astype(bf16)
    scale = HEAD_DIM**-0.5

    def attend(pair, carry):
        at = pl.multiple_of(pair * 128, 128)
        q = qkv[:, pl.ds(at, 128)] * bf16(scale)
        k = qkv[:, pl.ds(at + D, 128)]
        v = qkv[:, pl.ds(at + 2 * D, 128)]
        out = []
        for h in range(2):
            lanes = slice(64 * h, 64 * h + 64)
            scores = dot_nt(q[:, lanes], k[:, lanes]) + key_bias
            e = jnp.exp(scores - jnp.max(scores, -1, keepdims=True))
            p = e * (1.0 / jnp.sum(e, -1, keepdims=True))
            probs[2 * pair + h] = p
            out.append(dot(p.astype(bf16), v[:, lanes]))
        out = jnp.concatenate(out, 1)
        mixed[:, pl.ds(at, 128)] = out.astype(bf16)
        mixed_f[:, pl.ds(at, 128)] = out
        return carry

    lax.fori_loop(0, HEADS // 2, attend, 0, unroll=3)
    for copy in fetched[2:]:
        copy.wait()
    att = [dot_nt(mixed[...], wa[1, :, :, D : 2 * D].reshape(D, D))]
    x1 = x0[...] + att[0] + vec("out_bias")
    mean_x1 = colsum(x1 * valid) / TOK
    s2, i2 = layer_norm(x1)
    n2 = (s2 * vec("norm2_gain") + vec("norm2_bias")).astype(bf16)
    n2t[...] = n2.T
    copies[2].wait()
    copies[3].wait()
    bias = [jnp.concatenate([vec_ref[r : r + 1, :], vec_ref[r + 1 : r + 2, :]], 1) for r in (12, 14)]
    rowbuf[0:1, :] = bias[0]
    rowbuf[8:9, :] = bias[1]
    for m in range(2):

        def up(k, carry):
            at = pl.multiple_of(k * 256, 256)
            y = dot(n2, tile(wu, m, at)) + rowbuf[8 * m : 8 * m + 1, pl.ds(at, 256)]
            t = jnp.tanh(GELU_A * (y + GELU_B * y * y * y))
            half = 0.5 + 0.5 * t
            h = (y * half).astype(bf16).astype(f32) * valid
            rowbuf[16 + 8 * m : 17 + 8 * m, pl.ds(at, 256)] = colsum(h)
            inner = GELU_A + (3.0 * GELU_A * GELU_B) * y * y
            pre[m, :, pl.ds(at, 256)] = (half + 0.5 * y * (1.0 - t * t) * inner) * valid
            return carry

        lax.fori_loop(0, 6, up, 0, unroll=3)
        for k in range(2):
            row = OUT_HIDDEN + 2 * m + k
            out_ref[row : row + 1, :] = rowbuf[16 + 8 * m : 17 + 8 * m, D * k : D * k + D]
    copies[4].wait()
    copies[5].wait()
    hs = jnp.concatenate([out_ref[OUT_HIDDEN + k : OUT_HIDDEN + k + 1, :] for k in range(4)], 1) / TOK
    high = hs.astype(bf16)
    low = (hs - high.astype(f32)).astype(bf16)
    out = jnp.zeros((1, D), f32)
    for m in range(2):
        lanes = slice(1536 * m, 1536 * m + 1536)
        both = jnp.concatenate(
            [jnp.broadcast_to(high[:, lanes], (8, 1536)), jnp.broadcast_to(low[:, lanes], (8, 1536))], 0
        )
        y = dot_nt(both, wd[m].reshape(D, 1536))
        out = out + y[0:1] + y[8:9]
    pooled = mean_x1 + out + vec("mlp_bias")
    s3, i3 = layer_norm(pooled)
    final = (s3 * vec("final_gain") + vec("final_bias")).astype(bf16)
    copies[6].wait()
    copies[7].wait()
    wide = jnp.broadcast_to(final, (16, D))
    logits = jnp.concatenate([dot(wide, wh[m].reshape(D, 512))[0:1] for m in range(2)], 1)
    lane = lax.broadcasted_iota(jnp.int32, (1, 1024), 1)
    real = (lane & 511) < CLASSES // 2
    def pair(row):
        return jnp.concatenate([vec_ref[row : row + 1, 0:512], vec_ref[row + 1 : row + 2, 0:512]], 1)

    logits = jnp.where(real, logits + pair(VEC_HEAD), -1e30)
    top = jnp.max(logits, -1, keepdims=True)
    log_probs = logits - top - jnp.log(jnp.sum(jnp.exp(logits - top), -1, keepdims=True))
    aim = pair(VEC_AIM)
    loss = -jnp.sum(jnp.where(real, aim * log_probs, 0.0), keepdims=True)
    out_ref[...] = jnp.where(out_row >= OUT_LOSS, jnp.broadcast_to(loss, out_ref.shape), out_ref[...])
    back_logits = jnp.where(real, jnp.exp(log_probs) - aim, 0.0).astype(bf16)
    for m in range(2):
        row = OUT_HEAD + m
        out_ref[row : row + 1, 0:512] = back_logits[:, 512 * m : 512 * m + 512].astype(f32)
    out_ref[OUT_FINAL : OUT_FINAL + 1, :] = final.astype(f32)
    wide = jnp.broadcast_to(back_logits, (16, 1024))
    back_final = (
        dot_nt(wide[:, 0:512], wh[0].reshape(D, 512)) + dot_nt(wide[:, 512:], wh[1].reshape(D, 512))
    )[0:1]
    def put(name, value):
        out_ref[VEC[name] : VEC[name] + 1, :] = value

    put("final_gain", back_final * s3)
    put("final_bias", back_final)
    back2 = layer_norm_back(back_final, s3, i3, vec("final_gain")) / TOK
    back_out = back2.astype(bf16)
    out_ref[OUT_BACK : OUT_BACK + 1, :] = back_out.astype(f32)
    put("mlp_bias", back_out.astype(f32) * TOK)
    wide = jnp.broadcast_to(back_out, (16, D))
    for m in range(2):
        for k in range(6):
            at = 256 * k
            rowbuf[8 * m : 8 * m + 1, at : at + 256] = dot(wide, tile(wd, m, at))[0:1]
    for m in range(2):

        def down(k, carry):
            at = pl.multiple_of(k * 256, 256)
            bp = (rowbuf[8 * m : 8 * m + 1, pl.ds(at, 256)] * pre[m, :, pl.ds(at, 256)]).astype(bf16)
            rowbuf[16 + 8 * m : 17 + 8 * m, pl.ds(at, 256)] = colsum(bp.astype(f32))
            bpre[m, :, pl.ds(at, 256)] = bp
            grad = dot(n2t[...], bp)
            gr1[m, :, :, pl.ds(at, 256)] = grad.astype(bf16).reshape(16, 48, 256)
            return carry

        lax.fori_loop(0, 6, down, 0, unroll=2)
        for k in range(2):
            row = VEC_HIDDEN + 2 * m + k
            out_ref[row : row + 1, :] = rowbuf[16 + 8 * m : 17 + 8 * m, D * k : D * k + D]
    moving = send_out(gr1, 1)
    back_n2 = dot_nt(bpre[0], wu[0].reshape(D, 1536)) + dot_nt(bpre[1], wu[1].reshape(D, 1536))
    put("norm2_gain", colsum(back_n2 * s2))
    put("norm2_bias", colsum(back_n2))
    back1 = back2 * valid + layer_norm_back(back_n2, s2, i2, vec("norm2_gain"))
    back_att = back1.astype(bf16)
    put("out_bias", colsum(back_att.astype(f32)))
    back_att_t = back_att.T
    for k in range(3):
        lanes = slice(256 * k, 256 * k + 256)
        grad = dot(back_att_t, mixed[:, lanes])
        gr0[1, :, :, D + 256 * k : D + 256 * k + 256] = grad.astype(bf16).reshape(16, 48, 256)
    acc[...] = dot(back_att, wa[1, :, :, D : 2 * D].reshape(D, D))

    def attend_back(pair, carry):
        at = pl.multiple_of(pair * 128, 128)
        q = qkv[:, pl.ds(at, 128)]
        k = qkv[:, pl.ds(at + D, 128)]
        v = qkv[:, pl.ds(at + 2 * D, 128)]
        bm = acc[:, pl.ds(at, 128)].astype(bf16)
        bm_mixed = bm.astype(f32) * mixed_f[:, pl.ds(at, 128)]
        bq, bk, bv = [], [], []
        for h in range(2):
            lanes = slice(64 * h, 64 * h + 64)
            p = probs[2 * pair + h]
            bp = dot_nt(bm[:, lanes], v[:, lanes])
            bv.append(dot_tn(p.astype(bf16), bm[:, lanes]))
            inner = jnp.sum(bm_mixed[:, lanes], -1, keepdims=True)
            bs = (p * (bp - inner)).astype(bf16)
            bq.append(dot(bs, k[:, lanes]) * scale)
            bk.append(dot_tn(bs, q[:, lanes]) * scale)
        bqkv[:, pl.ds(at, 128)] = jnp.concatenate(bq, 1).astype(bf16)
        bqkv[:, pl.ds(at + D, 128)] = jnp.concatenate(bk, 1).astype(bf16)
        bqkv[:, pl.ds(at + 2 * D, 128)] = jnp.concatenate(bv, 1).astype(bf16)
        return carry

    lax.fori_loop(0, HEADS // 2, attend_back, 0, unroll=2)
    put("query_bias", colsum(bqkv[:, 0:D].astype(f32)))
    put("value_bias", colsum(bqkv[:, 2 * D :].astype(f32)))
    n1t = n1[...].T
    for part in range(9):
        m, at = part // 6, 256 * (part % 6)
        b = bqkv[:, 256 * part : 256 * part + 256]
        gr0[m, :, :, at : at + 256] = dot(n1t, b).astype(bf16).reshape(16, 48, 256)
    moving += send_out(gr0, 0)
    back_n1 = dot_nt(bqkv[:, 0:1536], wa[0].reshape(D, 1536))
    back_n1 = back_n1 + dot_nt(bqkv[:, 1536:], wa[1, :, :, 0:D].reshape(D, D))
    s1, i1 = layer_norm(x0[...])
    put("norm1_gain", colsum(back_n1 * s1))
    put("norm1_bias", colsum(back_n1))
    back0 = back1 + layer_norm_back(back_n1, s1, i1, vec("norm1_gain"))
    gpos_ref[...] = back0
    write(gpos_ref, gpos_hbm, 0)
    back_patch = (back0 * mask).astype(bf16)
    put("proj_bias", colsum(back_patch.astype(f32)))
    dwp_ref[...] = dot_tn(a4[...], back_patch)
    write(dwp_ref, dwp_hbm, 1)
    s4, y4 = normed4(count, st_ref, bn_ref, c_ref)
    bn4 = dot_nt(back_patch, wp_ref[...]) * gelu_slope(y4) * mask
    bn4_ref[0] = bn4
    write(bn4_ref, bn4_hbm, 2)
    st = jnp.concatenate([colsum(bn4), colsum(bn4 * s4)], 0)
    so_ref[...] = jnp.broadcast_to(st[None], so_ref.shape)
    write(so_ref, so_hbm, 3)
    out_ref[OUT_SUMS : OUT_SUMS + 1, :] = jnp.concatenate([st[0:1], st[1:2]], 1)
    write(out_ref, out_hbm, 4)
    for copy in moving:
        copy.wait()


def conv_back_kernel(
    level,
    count,
    count_in,
    back_ref,
    tot_ref,
    c_ref,
    st_ref,
    t_ref,
    cin_ref,
    stin_ref,
    bn_ref,
    g,
    backin_ref,
    so_ref,
    ss_ref,
):
    finish_level(level, count, back_ref, tot_ref, c_ref, st_ref, bn_ref, g)
    mean, inv = bn_stats(stin_ref, count_in, CHANS[level - 1])

    def normed(q):
        return (cin_ref[q] - mean) * inv

    def keep(q, y):
        backin_ref[q] = y

    st = back_through(level, g, t_ref, bn_ref, normed, keep)
    ss_ref[...] = st
    so_ref[...] = jnp.broadcast_to(st[None], so_ref.shape)


def finish_level(level, count, back_ref, tot_ref, c_ref, st_ref, bn_ref, g):
    chan = CHANS[level]
    rows = back_ref.shape[0]
    mask = patch_mask()
    mean, inv = bn_stats(st_ref, count, chan)
    gain = bn_ref[2 * level - 2 : 2 * level - 1, :]
    tot = fold_phases(jnp.sum(tot_ref[:, 0:2, :], 0), chan) / count

    def finish(i, carry):
        s = (c_ref[i] - mean) * inv
        g[i] = (inv * gain * (back_ref[i] - tot[0:1] - s * tot[1:2]) * mask).astype(bf16)
        return carry

    lax.fori_loop(0, rows, finish, 0)
    head = g[0]
    g[rows] = jnp.concatenate([head[16:], jnp.zeros((16, W), bf16)], 0)


def kernel_grad(level, ax_ref, g, dw_ref, dt):
    chan, chan_in = CHANS[level], CHANS[level - 1]
    rows = g.shape[0] - 1
    dt[...] = jnp.zeros_like(dt)

    def weights(i, carry):
        for tap in range(3):
            dt[tap] += dot_tn(ax_ref[2 * i + tap], g[i])
        return carry

    lax.fori_loop(0, rows, weights, 0)
    for tap in range(3):
        base = tap * 3 * chan_in
        for j in range(W // chan):
            for k in range(dw_ref.shape[0]):
                width = min(128, chan - 128 * k)
                cols = slice(j * chan + 128 * k, j * chan + 128 * k + width)
                if j == 0:
                    dw_ref[k, base : base + chan_in, 0:width] = dt[tap, W : W + chan_in, cols]
                    dw_ref[k, base + chan_in : base + 3 * chan_in, 0:width] = dt[
                        tap, 0 : 2 * chan_in, cols
                    ]
                else:
                    at = (2 * j - 1) * chan_in
                    dw_ref[k, base : base + 3 * chan_in, 0:width] += dt[
                        tap, at : at + 3 * chan_in, cols
                    ]


def back_through(level, g, t_ref, bn_ref, normed, keep):
    chan_in = CHANS[level - 1]
    rows = g.shape[0] - 1
    mask = patch_mask()
    gain = bn_ref[2 * level - 4 : 2 * level - 3, :]
    bias = bn_ref[2 * level - 3 : 2 * level - 2, :]

    def through(q, p, carry):
        first, second = carry
        left = pltpu.roll(p[:, W:], T - 1, 0)
        p = jnp.concatenate([p[:, 0 : W - chan_in], p[:, W - chan_in : W] + left], 1)
        s = normed(q)
        y = p * gelu_slope(s * gain + bias) * mask
        keep(q, y)
        return first + colsum(y), second + colsum(y * s)

    def back(i, carry):
        carry = through(2 * i, dot_nt(g[i], t_ref[1]), carry)
        p = dot_nt(g[i], t_ref[2]) + dot_nt(g[i + 1], t_ref[0])
        return through(2 * i + 1, p, carry)

    zero = jnp.zeros((1, W), f32)
    first, second = lax.fori_loop(0, rows, back, (zero, zero))
    return jnp.concatenate([first, second], 0)


LATE_W1 = 9 * C1 * C2 // 128
LATE_SUMS = LATE_W1 + 32
LATE_ROWS = LATE_SUMS + 4 * 6


def conv2_back_kernel(
    count,
    count_in,
    back_ref,
    tot_ref,
    c_ref,
    st_ref,
    ax_ref,
    t_ref,
    xk_ref,
    gram_ref,
    w1_ref,
    t1_ref,
    bn_ref,
    ss2_ref,
    ss3_ref,
    ss4_ref,
    late_ref,
    dw,
    g,
    dt,
    dt1,
    late,
):
    finish_level(2, count, back_ref, tot_ref, c_ref, st_ref, bn_ref, g)
    kernel_grad(2, ax_ref, g, dw, dt)
    gram, cross, mean, inv = level1_stats(gram_ref, w1_ref, count_in)
    mean, inv = tile_lanes(mean, C1), tile_lanes(inv, C1)
    weights = t1_ref[...]
    dt1[...] = jnp.zeros_like(dt1)

    def normed(q):
        return (dot(xk_ref[q], weights) - mean) * inv

    def keep(q, y):
        dt1[...] += dot_tn(xk_ref[q], y.astype(bf16))

    st = back_through(2, g, t_ref, bn_ref, normed, keep)
    late[...] = jnp.zeros_like(late)
    q = 9 * C1 // 4
    wide = jnp.concatenate([dw[0, pl.ds(k, q, stride=4), :][:, 0:C2] for k in range(4)], 1)
    for k in range(3):
        late[pl.ds(k, q, stride=3), :] = wide[:, 128 * k : 128 * k + 128]
    for tap in range(3):
        base = LATE_W1 + 9 * tap
        for j in range(8):
            cols = slice(j * C1, (j + 1) * C1)
            if j == 0:
                late[base : base + 3, 0:C1] = dt1[tap * 64 + 48 : tap * 64 + 51, cols]
                late[base + 3 : base + 9, 0:C1] = dt1[tap * 64 : tap * 64 + 6, cols]
            else:
                at = tap * 64 + 6 * j - 3
                late[base : base + 9, 0:C1] += dt1[at : at + 9, cols]
    ss4 = jnp.concatenate(
        [ss4_ref[OUT_SUMS : OUT_SUMS + 1, 0:W], ss4_ref[OUT_SUMS : OUT_SUMS + 1, W:]], 0
    )
    for level, ss in enumerate((st, ss2_ref[...], ss3_ref[...], ss4)):
        for which in range(2):
            for k in range(3):
                row = LATE_SUMS + 6 * level + 3 * which + k
                late[row : row + 1, :] = ss[which : which + 1, 128 * k : 128 * k + 128]
    each = late_ref.shape[1]
    for d in range(late_ref.shape[0]):
        late_ref[d] = late[each * d : each * d + each, :]


def early_kernel(
    parts,
    mp,
    stem_len,
    small_len,
    rows_stem,
    rows_small,
    at_ref,
    dw3_ref,
    dw4_ref,
    dwp_ref,
    gv_ref,
    gpos_ref,
    *refs,
):
    outs = refs[:parts]
    frame, table, vecs = refs[parts:]
    if outs[0].shape[1] > rows_stem + rows_small:
        vecs[...] = jnp.zeros_like(vecs)
        base = pl.multiple_of(24 * at_ref[0], 8)
        for index, ref in enumerate(outs):
            first = at_ref[index] == 0
            hs = [gv_ref[OUT_HIDDEN + k : OUT_HIDDEN + k + 1, :] for k in range(4)]
            hs = jnp.concatenate([jnp.where(first, hs[0], hs[2]), jnp.where(first, hs[1], hs[3])], 1)
            bl = [gv_ref[OUT_HEAD + k : OUT_HEAD + k + 1, 0:512] for k in range(2)]
            bl = jnp.where(first, bl[0], bl[1])
            rows = [hs[:, 128 * k : 128 * k + 128] for k in range(12)]
            rows += [bl[:, 128 * k : 128 * k + 128] for k in range(4)]
            vecs[pl.ds(base, 16), :] = jnp.concatenate(rows, 0)
            for d in range(16):
                lanes = slice(48 * d, 48 * d + 48)
                fill = jnp.zeros((1, 16), f32)
                row = jnp.concatenate(
                    [
                        gv_ref[OUT_BACK : OUT_BACK + 1, lanes],
                        fill,
                        gv_ref[OUT_FINAL : OUT_FINAL + 1, lanes],
                        fill,
                    ],
                    1,
                )
                vecs[pl.ds(base + 16, 8), :] = jnp.broadcast_to(row, (8, 128))
                ref[d, rows_stem + rows_small :, :] = vecs[...].astype(bf16)
    frame[0:ROW_W3, :] = jnp.zeros((ROW_W3, 128), f32)
    frame[STEM_ROWS:, :] = jnp.zeros((frame.shape[0] - STEM_ROWS, 128), f32)
    q = 9 * C2 // 2
    wide = jnp.concatenate(
        [
            jnp.concatenate(
                [
                    dw3_ref[0, pl.ds(k, q, stride=2), :],
                    dw3_ref[1, pl.ds(k, q, stride=2), :][:, 0 : C3 - 128],
                ],
                1,
            )
            for k in range(2)
        ],
        1,
    )
    for k in range(3):
        frame[pl.ds(ROW_W3 + k, q, stride=3), :] = wide[:, 128 * k : 128 * k + 128]
    for k in range(3):
        frame[pl.ds(ROW_W4 + k, 9 * C3, stride=3), :] = dw4_ref[k]
    for k in range(6):
        frame[pl.ds(ROW_WP + k, C4, stride=6), :] = dwp_ref[:, 128 * k : 128 * k + 128]
    table[0:12, :] = jnp.zeros((12, 128), f32)
    table[SMALL_ROWS:, :] = jnp.zeros((table.shape[0] - SMALL_ROWS, 128), f32)
    for k in range(6):
        lanes = slice(128 * k, 128 * k + 128)
        for name, index in VEC.items():
            row = SMALL_AT[name] + k
            table[row : row + 1, :] = gv_ref[index : index + 1, lanes]
        for h in range(4):
            row = SMALL_AT["hidden_bias"] + 6 * h + k
            table[row : row + 1, :] = gv_ref[VEC_HIDDEN + h : VEC_HIDDEN + h + 1, lanes]
        at = SMALL_AT["position"] + k
        for r in range(SIDE):
            table[pl.ds(at + 6 * (1 + SIDE * r), SIDE, stride=6), :] = gpos_ref[
                16 * r : 16 * r + SIDE, lanes
            ]
        table[at : at + 1, :] = gpos_ref[SIDE : SIDE + 1, lanes]
        row = SMALL_AT["class_token"] + k
        table[row : row + 1, :] = gpos_ref[SIDE : SIDE + 1, lanes]
    line = jnp.concatenate(
        [
            gv_ref[OUT_HEAD : OUT_HEAD + 1, 0:500],
            gv_ref[OUT_HEAD + 1 : OUT_HEAD + 2, 0:500],
            jnp.zeros((1, 24), f32),
        ],
        1,
    )
    row = SMALL_AT["head_bias"]
    for k in range(8):
        table[row + k : row + k + 1, :] = line[:, 128 * k : 128 * k + 128]
    for index, ref in enumerate(outs):
        mv = at_ref[index]

        def take(d, carry):
            owner = d * mp + mv
            a = (owner * stem_len + STEM_SHIFT) // 128
            ref[d, 0:rows_stem, :] = frame[pl.ds(a, rows_stem), :].astype(bf16)
            b = (owner * small_len + SMALL_SHIFT) // 128
            ref[d, rows_stem : rows_stem + rows_small, :] = table[pl.ds(b, rows_small), :].astype(bf16)
            return carry

        lax.fori_loop(0, ref.shape[0], take, 0)


def unshift_lanes(x, s, length):
    lane = lax.broadcasted_iota(jnp.int32, x.shape, 1)
    row = lax.broadcasted_iota(jnp.int32, x.shape, 0)
    moved = pltpu.roll(x, 128 - s, 1)
    after = pltpu.roll(moved, x.shape[0] - 1, 0)
    y = jnp.where(lane < 128 - s, moved, after)
    return jnp.where(row * 128 + lane < length, y, 0.0)


def unpack_kernel(stem_len, small_len, at_ref, x_ref, stem_ref, small_ref, sq_ref):
    rows = stem_ref.shape[0]
    end = rows + small_ref.shape[0]
    total = jnp.sum(x_ref[:, 0:end, :].astype(f32), 0)
    stem = unshift_lanes(total[0:rows], at_ref[0], stem_len)
    small = unshift_lanes(total[rows:], at_ref[1], small_len)
    stem_ref[...] = stem
    small_ref[...] = small
    sq_ref[...] = colsum(stem * stem) + colsum(small * small)


def norm_kernel(parts, *refs):
    sq_ref, sq1_ref, down_ref, head_ref, loss_ref, g0_ref, g1_ref, out_ref = refs[parts:]
    total = sum(ref[...].astype(f32) for ref in refs[:parts])
    half = g0_ref.shape[1]
    g0, g1 = total[:, 0:half], total[:, half:]
    g0_ref[...] = g0
    g1_ref[...] = g1
    squares = jnp.sum(g0 * g0 + g1 * g1 + down_ref[...] * down_ref[...], keepdims=True)
    squares = squares + jnp.sum(head_ref[...] * head_ref[...], keepdims=True)
    squares = squares + jnp.sum(sq_ref[...], keepdims=True)
    squares = squares + sq1_ref[0:1, 0:1] * (1.0 / out_ref.shape[0])
    lane = lax.broadcasted_iota(jnp.int32, (1, 128), 1)
    line = jnp.where(lane == 0, squares, loss_ref[OUT_LOSS : OUT_LOSS + 1, 0:128])
    out_ref[...] = jnp.broadcast_to(line[None], out_ref.shape)


def late_kernel(x_ref, out_ref):
    out_ref[...] = jnp.broadcast_to(jnp.sum(x_ref[...], 0)[None], out_ref.shape)


def last_kernel(
    counts,
    stem_len,
    small_len,
    at_ref,
    x_ref,
    gram_ref,
    w1_ref,
    bn_ref,
    stem_ref,
    small_ref,
    stem_out,
    small_out,
    sq_ref,
    late,
    frame,
    table,
):
    devices, each = x_ref.shape[0], x_ref.shape[1]
    for d in range(devices):
        late[each * d : each * d + each, :] = x_ref[d, 0:each, :]
    frame[...] = jnp.zeros_like(frame)
    table[...] = jnp.zeros_like(table)
    frame[ROW_W2:ROW_W3, :] = late[0:LATE_W1, :]
    line = [[jnp.zeros((1, SMALL_SHIFT), f32)], []]
    for level in range(4):
        chan = CHANS[level + 1]
        rows = []
        for which in range(2):
            row = LATE_SUMS + 6 * level + 3 * which
            rows.append(jnp.concatenate([late[row + k : row + k + 1, :] for k in range(3)], 1))
        both = fold_phases(jnp.concatenate(rows, 0), chan)
        line[0].append(both[1:2, 0:chan])
        line[1].append(both[0:1, 0:chan])
        if level == 0:
            tot = both[:, 0:128] / counts
    line = jnp.concatenate(line[0] + line[1], 1)
    for k in range(12):
        table[k : k + 1, :] = line[:, 128 * k : 128 * k + 128]
    gram, cross, mean, inv = level1_stats(gram_ref, w1_ref, counts)
    ones = gram[:, 27:28]
    grad = late[LATE_W1:LATE_SUMS, :] - ones * tot[0:1] - (cross - ones * mean) * inv * tot[1:2]
    grad = grad * (inv * bn_ref[0:1, 0:128])
    line = [jnp.zeros((1, STEM_SHIFT), f32)] + [grad[k : k + 1, 0:C1] for k in range(27)]
    line = jnp.concatenate(line, 1)
    for k in range(ROW_W2):
        frame[k : k + 1, :] = line[:, 128 * k : 128 * k + 128]
    squares = jnp.sum(frame[0:ROW_W3, :] * frame[0:ROW_W3, :], keepdims=True)
    squares = squares + jnp.sum(table[0:12, :] * table[0:12, :], keepdims=True)
    sq_ref[...] = jnp.broadcast_to(squares, sq_ref.shape)
    part = frame[pl.ds(at_ref[2], stem_ref.shape[0]), :]
    stem_out[...] = stem_ref[...] + unshift_lanes(part, at_ref[0], stem_len)
    part = table[pl.ds(at_ref[3], small_ref.shape[0]), :]
    small_out[...] = small_ref[...] + unshift_lanes(part, at_ref[1], small_len)


def call(kernel, outs, *args, scratch=(), smem=0, hbm=(), load=(), store=(), hbm_out=(), limit=32):
    def space(index, free):
        if index in free:
            return pl.BlockSpec(memory_space=pltpu.HBM)
        return pl.BlockSpec(memory_space=pltpu.VMEM)

    def shape(index):
        where = pltpu.HBM if index in (*hbm_out, *store) else jax.ShapeDtypeStruct
        return where(*outs[index])

    args = [
        pltpu.with_memory_space_constraint(arg, pltpu.HBM) if index in (*hbm, *load) else arg
        for index, arg in enumerate(args)
    ]
    count = len(args)
    moved = [jax.ShapeDtypeStruct(args[k].shape, args[k].dtype) for k in load]
    moved += [jax.ShapeDtypeStruct(*outs[k]) for k in store]

    def body(*refs):
        refs = list(refs)
        if not moved:
            return kernel(*refs)
        buffers, sems = refs[-1 - len(moved) : -1], refs[-1]
        refs = refs[: -1 - len(moved)]
        copies = []
        for k, index in enumerate(load):
            copies.append(pltpu.make_async_copy(refs[index], buffers[k], sems.at[k]))
            copies[-1].start()
            refs[index] = buffers[k]
        for copy in copies:
            copy.wait()
        targets = []
        for k, index in enumerate(store):
            targets.append((buffers[len(load) + k], refs[count + index], sems.at[len(load) + k]))
            refs[count + index] = buffers[len(load) + k]
        kernel(*refs)
        copies = [pltpu.make_async_copy(*target) for target in targets]
        for copy in copies:
            copy.start()
        for copy in copies:
            copy.wait()

    extra = [pltpu.VMEM(x.shape, x.dtype) for x in moved]
    if moved:
        extra.append(pltpu.SemaphoreType.DMA((len(moved),)))
    specs = [pl.BlockSpec(memory_space=pltpu.SMEM)] * smem
    specs += [space(index, (*hbm, *load)) for index in range(smem, count)]
    return pl.pallas_call(
        body,
        out_shape=[shape(index) for index in range(len(outs))],
        in_specs=specs,
        out_specs=[space(index, (*hbm_out, *store)) for index in range(len(outs))],
        scratch_shapes=[*scratch, *extra],
        compiler_params=pltpu.CompilerParams(vmem_limit_bytes=limit * 1024 * 1024),
    )(*args)


def adam_step(weight, first, second, grad, factor, rate):
    grad = grad * factor
    first = beta_one * first + (1.0 - beta_one) * grad
    second = beta_two * second + (1.0 - beta_two) * grad * grad
    first_fixed = first / (1.0 - beta_one**STEP)
    second_fixed = second / (1.0 - beta_two**STEP)
    return (
        weight
        - rate * (first_fixed / (jnp.sqrt(second_fixed) + adam_epsilon) + decay_rate * weight),
        first,
        second,
    )


def local(
    pixels,
    labels,
    stem,
    stem_first,
    stem_second,
    small,
    small_first,
    small_second,
    block,
    block_first,
    block_second,
    head,
    head_first,
    head_second,
):
    dp, mp = lax.axis_size("dp"), lax.axis_size("mp")
    n = dp * mp
    me, mine = lax.axis_index("dp"), lax.axis_index("mp")
    owner = me * mp + mine
    stem_len, small_len = stem.shape[0], small.shape[0]
    rows_stem = up16(-(-(stem_len + 127) // 128))
    rows_small = up16(-(-(small_len + 127) // 128))
    rows = rows_stem + rows_small
    everyone = ("dp", "mp")

    def share(x):
        return lax.all_to_all(x, everyone, 0, 0)

    part = FF // mp
    cls = CLASSES // mp
    cls_pad = 512 // (mp // 2)
    packed = jnp.concatenate(
        [block[0], block[1], block[2], jnp.pad(head, ((0, 0), (0, cls_pad - cls)))], 1
    ).astype(bf16)
    packed, stem, small = lax.optimization_barrier((packed, stem, small))
    stem_at, small_at = owner * stem_len + STEM_SHIFT, owner * small_len + SMALL_SHIFT
    at = jnp.stack(
        [
            stem_at % 128,
            small_at % 128,
            jnp.minimum(stem_at // 128, ROW_W3),
            jnp.minimum(small_at // 128, 16),
        ]
    ).astype(jnp.int32)
    (piece,) = call(
        pack_kernel,
        [((rows, 128), bf16)],
        at,
        jnp.pad(stem, (0, rows_stem * 128 - stem_len)).reshape(rows_stem, 128),
        jnp.pad(small, (0, rows_small * 128 - small_len)).reshape(rows_small, 128),
        smem=1,
        limit=4,
    )

    strip = pixels.reshape(pixels.shape[1], 128)
    strip, piece, packed, at = lax.optimization_barrier((strip, piece, packed, at))
    gathered = lax.all_gather(packed, everyone, axis=0)
    half = strip.shape[0] // 2
    pairs = [(source, (source + dp - 1) % dp) for source in range(dp)]
    lower = lax.ppermute(strip[:half], "dp", pairs)

    if (dp, mp) == (16, 2):
        gathered = gathered.reshape(16, 2, 48, packed.shape[1])
    else:
        g = gathered.reshape(dp, mp, D // dp, packed.shape[1])
        g = jnp.transpose(g, (0, 2, 1, 3)).reshape(D, mp, -1)
        slots = [g[:, :, k * part : (k + 1) * part].reshape(D, 2, FF // 2) for k in range(3)]
        top = g[:, :, 3 * part : 3 * part + cls].reshape(D, 2, CLASSES // 2)
        slots.append(jnp.pad(top, ((0, 0), (0, 0), (0, 12))))
        g = jnp.concatenate(slots, 2).reshape(16, 48, 2, -1)
        gathered = jnp.transpose(g, (0, 2, 1, 3))

    xk, gram = call(
        image_kernel,
        [((8, T, 192), bf16), ((n, 8, 128), f32)],
        strip[half:],
        lower,
        scratch=[
            pltpu.VMEM((2 * half, 128), f32),
            pltpu.VMEM((16 * half // 3 + 16, 128), f32),
            pltpu.VMEM((17, T, 64), bf16),
        ],
        limit=12,
    )
    column = lax.all_to_all(jnp.broadcast_to(piece[None], (dp, rows, 128)), "dp", 0, 0)
    gram, xk, column = lax.optimization_barrier((gram, xk, column))
    gram = share(gram)
    if mp == 2:
        swap = [(0, 1), (1, 0)]
        pieces = [column, lax.ppermute(column, "mp", swap)]
        which = jnp.stack([mine, 1 - mine]).astype(jnp.int32)
    else:
        columns = lax.all_gather(column, "mp", axis=0)
        pieces = [columns[k] for k in range(mp)]
        which = jnp.arange(mp, dtype=jnp.int32)
    which = jnp.concatenate([which, labels.reshape(1)])
    frame_rows = (stem_len * n + STEM_SHIFT) // 128 + rows_stem + 16
    table_rows = (small_len * n + SMALL_SHIFT) // 128 + rows_small + 16
    frames = [pltpu.VMEM((frame_rows, 128), f32), pltpu.VMEM((table_rows, 128), f32)]
    w1, t1, t2, t3, t4, wp, bn, vec, pos = call(
        functools.partial(assemble_kernel, len(pieces), mp, stem_len, small_len, rows_stem, rows_small),
        [
            ((32, 128), f32),
            ((192, W), bf16),
            ((3, W + C1, W), bf16),
            ((3, W + C2, W), bf16),
            ((3, W + C3, W), bf16),
            ((C4, D), bf16),
            ((8, W), f32),
            ((24, D), f32),
            ((T, D), f32),
        ],
        which,
        *pieces,
        smem=1,
        store=(1, 2, 3, 4, 5, 7, 8),
        scratch=frames
        + [
            pltpu.VMEM((9 * C1, 128), f32),
            pltpu.VMEM((9 * C2, 128), f32),
            pltpu.VMEM((9 * C2, 128), f32),
            pltpu.VMEM((192, W), f32),
            pltpu.VMEM((W + C1, W), f32),
            pltpu.VMEM((W + C2, W), f32),
        ],
        limit=20,
    )

    positions = SIDE * SIDE * n
    counts = [None, 64.0 * positions, 16.0 * positions, 4.0 * positions, 1.0 * positions]
    ax, conv, st = call(
        functools.partial(conv12_kernel, counts[1]),
        [((9, T, W + C1), bf16), ((4, T, W), f32), ((n, 2, W), f32)],
        xk,
        gram,
        w1,
        t1,
        bn,
        t2,
        load=(3, 5),
        limit=14,
    )
    convs = [None, None, conv]
    stats = [None, None, share(st)]
    inputs = [None, None, ax]
    kernels = [None, t1, t2, t3, t4]
    for level in (3, 4):
        r = 2 ** (4 - level)
        ax, conv, st = call(
            functools.partial(conv_kernel, level - 1, counts[level - 1]),
            [((2 * r + 1, T, W + CHANS[level - 1]), bf16), ((r, T, W), f32), ((n, 2, W), f32)],
            convs[level - 1],
            stats[level - 1],
            bn,
            kernels[level],
            load=(3,),
            store=(1, 2) if level == 4 else (),
            limit=10,
        )
        inputs.append(ax)
        convs.append(conv)
        stats.append(share(st))

    a4, x0, n1 = call(
        functools.partial(embed_kernel, counts[4]),
        [((T, C4), bf16), ((T, D), f32), ((T, D), bf16)],
        stats[4],
        bn,
        convs[4],
        wp,
        pos,
        vec,
        load=(2, 3, 4, 5),
        store=(0, 1, 2),
        limit=12,
    )
    fast = (dp, mp) == (16, 2)
    outs = call(
        functools.partial(block_kernel, counts[4]),
        [
            ((4, 2, 4, 48, FF), bf16),
            ((1, T, W), f32),
            ((n, 2, W), f32),
            ((32, D), f32),
            ((T, D), f32),
            ((C4, D), f32),
        ],
        stats[4],
        bn,
        n1,
        vec,
        x0,
        a4,
        wp,
        convs[4],
        gathered,
        hbm=(2, 3, 4, 5, 6, 7, 8),
        hbm_out=(0, 1, 2, 3, 4, 5),
        limit=44,
        scratch=[
            pltpu.VMEM((1, T, W), f32),
            pltpu.VMEM((C4, D), bf16),
            pltpu.VMEM((24, D), f32),
            pltpu.VMEM((1, T, W), f32),
            pltpu.VMEM((n, 2, W), f32),
            pltpu.VMEM((32, D), f32),
            pltpu.VMEM((T, D), f32),
            pltpu.VMEM((C4, D), f32),
            pltpu.VMEM((2, 16, 48, 1536), bf16),
            pltpu.VMEM((2, 16, 48, 1536), bf16),
            pltpu.VMEM((2, 16, 48, 1536), bf16),
            pltpu.VMEM((2, 16, 48, 512), bf16),
            pltpu.SemaphoreType.DMA((35,)),
            pltpu.VMEM((T, W), bf16),
            pltpu.VMEM((T, D), f32),
            pltpu.VMEM((T, D), bf16),
            pltpu.VMEM((T, 3 * D), bf16),
            pltpu.VMEM((HEADS, T, T), f32),
            pltpu.VMEM((T, D), bf16),
            pltpu.VMEM((D, T), bf16),
            pltpu.VMEM((2, T, 1536), f32),
            pltpu.VMEM((T, D), f32),
            pltpu.VMEM((T, 3 * D), bf16),
            pltpu.VMEM((T, D), f32),
            pltpu.VMEM((2, T, 1536), bf16),
            pltpu.VMEM((32, 1536), f32),
        ],
    )
    grads, back, tot, facts, gpos, dwp = outs
    tot = share(tot)
    if fast:
        planes = [[8 * z + k for k in range(8)] for z in range(4)]
        owned = lax.psum_scatter(
            grads.reshape(8 * 4 * 48, FF),
            everyone,
            scatter_dimension=0,
            tiled=True,
            axis_index_groups=planes,
        )
        owned = [owned]
    else:
        g = jnp.transpose(grads, (2, 0, 3, 1, 4)).reshape(D, 2, 2, FF // 2)
        g = jnp.transpose(g, (0, 2, 1, 3)).reshape(dp, D // dp, 2, mp, part)
        g = jnp.transpose(g, (0, 3, 1, 2, 4)).reshape(n * (D // dp), 2 * part)
        owned = [lax.psum_scatter(g, everyone, scatter_dimension=0, tiled=True)]

    rows_d = D // dp
    rows_vec = 48 if fast else 0

    def outer(bo_all, fin_all, hs_all, bl_all):
        return dot_tn(bo_all, hs_all), dot_tn(fin_all, bl_all)

    if not fast:
        bo, fin = facts[OUT_BACK : OUT_BACK + 1], facts[OUT_FINAL : OUT_FINAL + 1]
        hs, bl = facts[OUT_HIDDEN:OUT_HEAD].reshape(1, FF), facts[OUT_HEAD:OUT_SUMS, 0:512].reshape(1, 1024)
        head_line = jnp.concatenate([bl[:, :500], bl[:, 512:1012]], 1).reshape(1, mp, cls)
        line = jnp.concatenate(
            [
                jnp.broadcast_to(bo.reshape(dp, 1, rows_d), (dp, mp, rows_d)),
                jnp.broadcast_to(fin.reshape(dp, 1, rows_d), (dp, mp, rows_d)),
                jnp.broadcast_to(hs.reshape(1, mp, part), (dp, mp, part)),
                jnp.broadcast_to(head_line, (dp, mp, cls)),
            ],
            2,
        ).reshape(n, -1)
        width = -(-line.shape[1] // 1024) * 1024
        line = jnp.pad(line, ((0, 0), (0, width - line.shape[1]))).astype(bf16)
        line = share(line.reshape(n, width // 128, 128)).reshape(n, width)
        cuts = [0, rows_d, 2 * rows_d, 2 * rows_d + part, 2 * rows_d + part + cls]
        grad_down, grad_head = outer(*[line[:, a:b] for a, b in zip(cuts[:-1], cuts[1:])])

    sums = [None] * 5
    kernel_grads = [None] * 5
    for level in (4, 3):
        r = 2 ** (4 - level)
        chan_in = CHANS[level - 1]
        g, back, so, sums[level - 1] = call(
            functools.partial(conv_back_kernel, level, counts[level], counts[level - 1]),
            [
                ((r + 1, T, W), bf16),
                ((2 * r, T, W), f32),
                ((n, 2, W), f32),
                ((2, W), f32),
            ],
            back,
            tot,
            convs[level],
            stats[level],
            kernels[level],
            convs[level - 1],
            stats[level - 1],
            bn,
            load=(0, 2, 4) if level == 4 else (4,),
            limit=12,
        )
        (kernel_grads[level],) = call(
            functools.partial(kernel_grad, level),
            [((-(-CHANS[level] // 128), 9 * chan_in, 128), f32)],
            inputs[level],
            g,
            scratch=[pltpu.VMEM((3, W + chan_in, W), f32)],
            limit=12,
        )
        if level == 4:
            so, kernel_grads[4] = lax.optimization_barrier((so, kernel_grads[4]))
            tot = share(so)
    outs = call(
        functools.partial(early_kernel, len(pieces), mp, stem_len, small_len, rows_stem, rows_small),
        [((dp, rows + rows_vec, 128), bf16)] * len(pieces),
        which,
        kernel_grads[3],
        kernel_grads[4],
        dwp,
        facts,
        gpos,
        smem=1,
        load=(3, 4, 5),
        scratch=frames + [pltpu.VMEM((48, 128), f32)],
        limit=18,
    )
    if mp == 2:
        column = outs[0] + lax.ppermute(outs[1], "mp", swap)
    else:
        column = lax.psum_scatter(jnp.stack(outs, 0), "mp", scatter_dimension=0)
    so, column = lax.optimization_barrier((so, column))
    tot = share(so)
    tot, column = lax.optimization_barrier((tot, column))
    column = lax.all_to_all(column, "dp", 0, 0)
    each = -(-LATE_ROWS // n)
    (late,) = call(
        functools.partial(conv2_back_kernel, counts[2], counts[1]),
        [((n, each, 128), f32)],
        back,
        tot,
        convs[2],
        stats[2],
        inputs[2],
        t2,
        xk,
        gram,
        w1,
        t1,
        bn,
        *sums[2:4],
        facts,
        load=(0, 4, 5, 6, 9, 13),
        scratch=[
            pltpu.VMEM((1, 9 * C1, 128), f32),
            pltpu.VMEM((5, T, W), bf16),
            pltpu.VMEM((3, W + C1, W), f32),
            pltpu.VMEM((192, W), f32),
            pltpu.VMEM((n * each, 128), f32),
        ],
        limit=20,
    )
    if fast:
        late, owned[0] = lax.optimization_barrier((late, owned[0]))
        lines = [[8 * z + k for z in range(4)] for k in range(8)]
        owned[0] = lax.psum_scatter(
            owned[0], everyone, scatter_dimension=0, tiled=True, axis_index_groups=lines
        )
    late, column = lax.optimization_barrier((late, column))
    late = share(late)
    (late,) = call(late_kernel, [((n, each, 128), f32)], late, limit=8)
    late = share(late)
    if fast:
        line = column[:, rows:].reshape(2 * dp, 24, 128)
        grad_down, grad_head = outer(
            line[:, 16, 0:48],
            line[:, 16, 64:112],
            line[:, 0:12].reshape(2 * dp, part),
            line[:, 12:16].reshape(2 * dp, 512)[:, :cls],
        )
    grad_stem, grad_small, squares = call(
        functools.partial(unpack_kernel, stem_len, small_len),
        [((rows_stem, 128), f32), ((rows_small, 128), f32), ((1, 128), f32)],
        at,
        column,
        smem=1,
        limit=8,
    )

    grad_stem, grad_small, squares1 = call(
        functools.partial(last_kernel, counts[1], stem_len, small_len),
        [((rows_stem, 128), f32), ((rows_small, 128), f32), ((1, 128), f32)],
        at,
        late,
        gram,
        w1,
        bn,
        grad_stem,
        grad_small,
        smem=1,
        scratch=[
            pltpu.VMEM((n * each, 128), f32),
            pltpu.VMEM((ROW_W3 + rows_stem, 128), f32),
            pltpu.VMEM((16 + rows_small, 128), f32),
        ],
        limit=8,
    )

    g0, g1, ends = call(
        functools.partial(norm_kernel, len(owned)),
        [((rows_d, part), f32), ((rows_d, part), f32), ((n, 1, 128), f32)],
        *owned,
        squares,
        squares1,
        grad_down,
        grad_head,
        facts,
        limit=8,
    )
    ends = jnp.sum(share(ends), 0)
    loss_sum, grad_norm = ends[0, 1], jnp.sqrt(ends[0, 0])
    factor = jnp.minimum(1.0, clip_norm / grad_norm)
    grad_stem = grad_stem.reshape(-1)[:stem_len]
    grad_small = grad_small.reshape(-1)[:small_len]
    grad_block = jnp.stack([g0, g1, grad_down], 0)
    stem_new = adam_step(stem, stem_first, stem_second, grad_stem, factor, rate_stem)
    small_new = adam_step(small, small_first, small_second, grad_small, factor, rate_small)
    block_new = adam_step(block, block_first, block_second, grad_block, factor, rate_block)
    head_new = adam_step(head, head_first, head_second, grad_head, factor, rate_head)
    return (*stem_new, *small_new, *block_new, *head_new, loss_sum, grad_norm)


def solution(mesh):
    flat = P(("dp", "mp"))
    matrix = P(None, "dp", "mp")
    head = P("dp", "mp")
    states = (flat,) * 6 + (matrix,) * 3 + (head,) * 3
    return jax.shard_map(
        local,
        mesh=mesh,
        in_specs=(P("mp", "dp", None), P("mp", "dp")) + states,
        out_specs=states + (P(), P()),
        check_vma=False,
    )
```

```python
import functools

import jax
import jax.numpy as jnp
from jax import lax
from jax.experimental import pallas as pl
from jax.experimental.pallas import tpu as pltpu
from jax.sharding import PartitionSpec as P

D = 768
HEADS = 12
HEAD_DIM = 64
FF = 3072
CLASSES = 1000
C1 = 48
C2 = 96
C3 = 192
C4 = 384
STEP = 10
TOK = 197
SIDE = 14
T = 16 * SIDE
W = 384
CHANS = (3, C1, C2, C3, C4)

beta_one = 0.9
beta_two = 0.999
adam_epsilon = 1e-08
decay_rate = 0.05
clip_norm = 1.0
rate_stem = 0.05
rate_small = 0.5
rate_block = 0.05
rate_head = 0.05
batch_epsilon = 1e-05
layer_epsilon = 1e-06
smoothing = 0.1

bf16 = jnp.bfloat16
f32 = jnp.float32

STEM_SHIFT = 112
SMALL_SHIFT = 96
ROW_W2 = 11
ROW_W3 = ROW_W2 + 9 * C1 * C2 // 128
ROW_W4 = ROW_W3 + 9 * C2 * C3 // 128
ROW_WP = ROW_W4 + 9 * C3 * C4 // 128
STEM_ROWS = ROW_WP + C4 * D // 128
SMALL_NAMES = (
    ("proj_bias", 6),
    ("class_token", 6),
    ("position", 6 * TOK),
    ("norm1_gain", 6),
    ("norm1_bias", 6),
    ("query_bias", 6),
    ("value_bias", 6),
    ("out_bias", 6),
    ("norm2_gain", 6),
    ("norm2_bias", 6),
    ("hidden_bias", 24),
    ("mlp_bias", 6),
    ("final_gain", 6),
    ("final_bias", 6),
    ("head_bias", 8),
)
SMALL_AT = {}
_row = 12
for _name, _rows in SMALL_NAMES:
    SMALL_AT[_name] = _row
    _row += _rows
SMALL_ROWS = _row
VEC_NAMES = (
    "proj_bias",
    "norm1_gain",
    "norm1_bias",
    "query_bias",
    "value_bias",
    "out_bias",
    "norm2_gain",
    "norm2_bias",
    "mlp_bias",
    "final_gain",
    "final_bias",
)
VEC = {name: index for index, name in enumerate(VEC_NAMES)}
VEC_HIDDEN = 12
VEC_HEAD = 16
VEC_AIM = 18
OUT_BACK = 16
OUT_FINAL = 17
OUT_HIDDEN = 18
OUT_HEAD = 22
OUT_SUMS = 24
OUT_LOSS = 25


def dot(a, b):
    return jnp.dot(a, b, preferred_element_type=f32)


def dot_nt(a, b):
    return lax.dot_general(a, b, (((1,), (1,)), ((), ())), preferred_element_type=f32)


def dot_tn(a, b):
    return lax.dot_general(a, b, (((0,), (0,)), ((), ())), preferred_element_type=f32)


GELU_A = 0.7978845608028654
GELU_B = 0.044715


def gelu(x):
    return 0.5 * x * (1.0 + jnp.tanh(GELU_A * (x + GELU_B * x * x * x)))


def gelu_slope(x):
    t = jnp.tanh(GELU_A * (x + GELU_B * x * x * x))
    return 0.5 * (1.0 + t) + 0.5 * x * (1.0 - t * t) * GELU_A * (1.0 + 3.0 * GELU_B * x * x)


def dot_f32(a, b):
    return jnp.dot(a, b, preferred_element_type=f32, precision=lax.Precision.HIGHEST)


def up16(n):
    return -(-n // 16) * 16


def colsum(x):
    return jnp.sum(x, 0, keepdims=True)


def slot_index():
    return lax.broadcasted_iota(jnp.int32, (T, 1), 0)


def patch_mask():
    return ((slot_index() & 15) < SIDE).astype(f32)


def token_mask():
    p = slot_index()
    return (((p & 15) < SIDE) | (p == SIDE)).astype(f32)


def fold_phases(x, chan):
    step = W // 2
    while step >= chan:
        x = x + jnp.concatenate([x[:, step:], x[:, :step]], 1)
        step //= 2
    return x


def bn_stats(st_ref, count, chan):
    tot = fold_phases(jnp.sum(st_ref[:, 0:2, :], 0), chan)
    mean = tot[0:1] / count
    inv = lax.rsqrt(tot[1:2] / count - mean * mean + batch_epsilon)
    return mean, inv


def shift_lanes(x, s):
    lane = lax.broadcasted_iota(jnp.int32, x.shape, 1)
    row = lax.broadcasted_iota(jnp.int32, x.shape, 0)
    moved = pltpu.roll(x, s, 1)
    before = jnp.where(row == 0, 0.0, pltpu.roll(moved, 1, 0))
    return jnp.where(lane >= s, moved, before)


def pack_kernel(at_ref, stem_ref, small_ref, out_ref):
    rows = stem_ref.shape[0]
    out_ref[0:rows, :] = shift_lanes(stem_ref[...], at_ref[0]).astype(bf16)
    out_ref[rows:, :] = shift_lanes(small_ref[...], at_ref[1]).astype(bf16)


def flat_lanes(ref, row, count):
    return jnp.concatenate([ref[row + k : row + k + 1, :] for k in range(count)], 1)


def assemble_kernel(by_plane, parts, mp, stem_len, small_len, rows_stem, rows_small, at_ref, *refs):
    pieces = refs[:parts]
    s1, t1_ref, t2_ref, t3_ref, t4_ref, wp_ref, bn_ref, vec_ref, pos_ref = refs[parts : parts + 9]
    frame, table, s2, s3a, s3b, u1, u2, u3 = refs[parts + 9 :]
    frame[...] = jnp.zeros_like(frame)
    table[...] = jnp.zeros_like(table)
    for index, ref in enumerate(pieces):
        mv = at_ref[index]

        def put(d, carry):
            owner = ((at_ref[parts + 1] ^ (d & 3)) * 4 + (d >> 2) if by_plane else d) * mp + mv
            a = (owner * stem_len + STEM_SHIFT) // 128
            frame[pl.ds(a, rows_stem), :] += ref[d, 0:rows_stem, :].astype(f32)
            b = (owner * small_len + SMALL_SHIFT) // 128
            table[pl.ds(b, rows_small), :] += ref[d, rows_stem : rows_stem + rows_small, :].astype(f32)
            return carry

        lax.fori_loop(0, ref.shape[0], put, 0)
    s1[...] = jnp.zeros_like(s1)
    flat = flat_lanes(frame, 0, ROW_W2)
    for k in range(27):
        s1[k : k + 1, 0:C1] = flat[:, STEM_SHIFT + 48 * k : STEM_SHIFT + 48 * k + 48]
    u1[...] = jnp.zeros_like(u1)
    for tap in range(3):
        for j in range(8):
            cols = slice(j * C1, (j + 1) * C1)
            if j == 0:
                u1[tap * 64 + 48 : tap * 64 + 51, cols] = s1[tap * 9 : tap * 9 + 3, 0:C1]
                u1[tap * 64 : tap * 64 + 6, cols] = s1[tap * 9 + 3 : tap * 9 + 9, 0:C1]
            else:
                at = tap * 64 + 6 * j - 3
                u1[at : at + 9, cols] = s1[tap * 9 : tap * 9 + 9, 0:C1]
    t1_ref[...] = u1[...].astype(bf16)
    q = 9 * C1 // 4
    wide = jnp.concatenate([frame[pl.ds(ROW_W2 + k, q, stride=3), :] for k in range(3)], 1)
    for k in range(4):
        s2[pl.ds(k, q, stride=4), 0:C2] = wide[:, k * C2 : (k + 1) * C2]
    q = 9 * C2 // 2
    wide = jnp.concatenate([frame[pl.ds(ROW_W3 + k, q, stride=3), :] for k in range(3)], 1)
    for k in range(2):
        part = wide[:, k * C3 : (k + 1) * C3]
        s3a[pl.ds(k, q, stride=2), :] = part[:, 0:128]
        s3b[pl.ds(k, q, stride=2), 0 : C3 - 128] = part[:, 128:C3]
    for ref, chan_in, chan_out, src, u in (
        (t2_ref, C1, C2, (s2,), u2),
        (t3_ref, C2, C3, (s3a, s3b), u3),
    ):
        for tap in range(3):
            u[...] = jnp.zeros_like(u)
            base = tap * 3 * chan_in
            for j in range(W // chan_out):
                for k, s in enumerate(src):
                    width = min(128, chan_out - 128 * k)
                    cols = slice(j * chan_out + 128 * k, j * chan_out + 128 * k + width)
                    if j == 0:
                        u[W : W + chan_in, cols] = s[base : base + chan_in, 0:width]
                        u[0 : 2 * chan_in, cols] = s[base + chan_in : base + 3 * chan_in, 0:width]
                    else:
                        at = (2 * j - 1) * chan_in
                        u[at : at + 3 * chan_in, cols] = s[base : base + 3 * chan_in, 0:width]
            ref[tap] = u[...].astype(bf16)
    for tap in range(3):
        rows = 3 * C3
        for k in range(3):
            lanes = slice(k * 128, (k + 1) * 128)
            at = ROW_W4 + k + 3 * tap * rows
            t4_ref[tap, 0 : 2 * C3, lanes] = frame[pl.ds(at + 3 * C3, 2 * C3, stride=3), :].astype(bf16)
            t4_ref[tap, 2 * C3 : 3 * C3, lanes] = frame[pl.ds(at, C3, stride=3), :].astype(bf16)
    for k in range(6):
        lanes = slice(k * 128, (k + 1) * 128)
        wp_ref[:, lanes] = frame[pl.ds(ROW_WP + k, C4, stride=6), :].astype(bf16)
    flat = flat_lanes(table, 0, 12)
    first = SMALL_SHIFT
    for level in range(4):
        chan = CHANS[level + 1]
        for which in range(2):
            at = first + which * (C1 + C2 + C3 + C4)
            part = flat[:, at : at + chan]
            row = 2 * level + which
            for j in range(W // chan):
                bn_ref[row : row + 1, j * chan : (j + 1) * chan] = part
        first += chan
    vec_ref[...] = jnp.zeros_like(vec_ref)
    for name, index in VEC.items():
        vec_ref[index : index + 1, :] = flat_lanes(table, SMALL_AT[name], 6)
    for k in range(4):
        row = VEC_HIDDEN + k
        vec_ref[row : row + 1, :] = flat_lanes(table, SMALL_AT["hidden_bias"] + 6 * k, 6)
    flat = flat_lanes(table, SMALL_AT["head_bias"], 8)
    lane = lax.broadcasted_iota(jnp.int32, (1, 512), 1)
    for m in range(2):
        vec_ref[VEC_HEAD + m : VEC_HEAD + m + 1, 0:500] = flat[:, 500 * m : 500 * m + 500]
        aim = jnp.where(lane + 500 * m == at_ref[parts], 1.0 - smoothing, 0.0) + smoothing / CLASSES
        vec_ref[VEC_AIM + m : VEC_AIM + m + 1, 0:512] = jnp.where(lane < 500, aim, 0.0)
    pos_ref[...] = jnp.zeros_like(pos_ref)
    at = SMALL_AT["position"]
    for k in range(6):
        lanes = slice(k * 128, (k + 1) * 128)
        for r in range(SIDE):
            rows = table[pl.ds(at + k + 6 * (1 + SIDE * r), SIDE, stride=6), :]
            pos_ref[16 * r : 16 * r + SIDE, lanes] = rows
        mark = SMALL_AT["class_token"] + k
        pos_ref[SIDE : SIDE + 1, lanes] = table[mark : mark + 1, :] + table[at + k : at + k + 1, :]


def image_kernel(own_ref, next_ref, xk_ref, gram_ref, flat, chunks, xe):
    half = own_ref.shape[0]
    flat[0:half, :] = own_ref[...].astype(f32)
    flat[half : 2 * half, :] = next_ref[...].astype(f32)
    n = 2 * half // 3
    wide = jnp.concatenate([flat[pl.ds(k, n, stride=3), :] for k in range(3)], 1)
    for j in range(8):
        chunks[pl.ds(j, n, stride=8), 0:48] = wide[:, 48 * j : 48 * j + 48]
    mask = patch_mask()
    lane = lax.broadcasted_iota(jnp.int32, (T, 64), 1)

    def spread(i, carry):
        rows = [chunks[pl.ds(16 * SIDE * r + SIDE * i, 16), 0:64] for r in range(SIDE)]
        x = jnp.where(lane < 48, jnp.concatenate(rows, 0), 0.0) * mask
        left = pltpu.roll(jnp.concatenate([x, x], 1), 3, 1)[:, 0:64]
        left = jnp.where((lane >= 48) & (lane < 51), pltpu.roll(left, 1, 0), 0.0)
        xe[i + 1] = ((x + left) * mask).astype(bf16)
        return carry

    chunks[pl.ds(n * 8, 16), :] = jnp.zeros((16, 128), f32)
    lax.fori_loop(0, 16, spread, 0)
    last = xe[16]
    xe[0] = jnp.concatenate([jnp.zeros((16, 64), bf16), last[: T - 16]], 0)

    def step(i, carry):
        gram, ones = carry
        x = jnp.concatenate([xe[2 * i], xe[2 * i + 1], xe[2 * i + 2]], 1)
        xk_ref[i] = x
        return gram + dot_tn(x, x), ones + colsum(x.astype(f32))

    gram, ones = lax.fori_loop(0, 8, step, (jnp.zeros((192, 192), f32), jnp.zeros((1, 192), f32)))
    row = lax.broadcasted_iota(jnp.int32, (192, 256), 0)
    col = lax.broadcasted_iota(jnp.int32, (192, 256), 1)
    j, k = col >> 5, col & 31
    tap = (k >= 9).astype(jnp.int32) + (k >= 18).astype(jnp.int32)
    u = k - 9 * tap
    at = 64 * tap + jnp.where(j == 0, jnp.where(u < 3, 48 + u, u - 3), 6 * j - 3 + u)
    pick = ((row == at) & (k < 27)).astype(f32)
    both = lax.dot_general(
        pick,
        dot_f32(gram, pick),
        (((0,), (0,)), ((), ())),
        preferred_element_type=f32,
        precision=lax.Precision.HIGHEST,
    )
    ones = dot_f32(jnp.broadcast_to(ones, (8, 192)), pick)[0:1]
    total = jnp.zeros((32, 32), f32)
    line = jnp.zeros((1, 32), f32)
    for q in range(8):
        lanes = slice(32 * q, 32 * q + 32)
        total = total + both[lanes, lanes]
        line = line + ones[:, lanes]
    r32 = lax.broadcasted_iota(jnp.int32, (32, 32), 0)
    c32 = lax.broadcasted_iota(jnp.int32, (32, 32), 1)
    total = total + jnp.where(r32 == 27, line, 0.0)
    column = jnp.sum(jnp.where(r32 == c32, line, 0.0), 1, keepdims=True)
    total = total + jnp.where(c32 == 27, column, 0.0)
    flat8 = jnp.concatenate([total[8 * q : 8 * q + 8] for q in range(4)], 1)
    gram_ref[...] = jnp.broadcast_to(flat8[None], gram_ref.shape)


def level1_stats(gram_ref, w1_ref, count):
    flat8 = jnp.sum(gram_ref[...], 0)
    gram = jnp.concatenate([flat8[:, 32 * q : 32 * q + 32] for q in range(4)], 0)
    cross = dot_f32(gram, w1_ref[...])
    mean = cross[27:28] / count
    squares = colsum(w1_ref[...] * cross) / count
    inv = lax.rsqrt(squares - mean * mean + batch_epsilon)
    return gram, cross, mean, inv


def tile_lanes(x, chan):
    return jnp.concatenate([x[:, 0:chan]] * (W // chan), 1)


def conv12_kernel(count, xk_ref, gram_ref, w1_ref, t1_ref, bn_ref, t_ref, ax_ref, out_ref, st_ref):
    gram, cross, mean, inv = level1_stats(gram_ref, w1_ref, count)
    mean, inv = tile_lanes(mean, C1), tile_lanes(inv, C1)
    gain, bias = bn_ref[0:1, :], bn_ref[1:2, :]
    mask = patch_mask()
    weights = t1_ref[...]

    def activate(i, carry):
        a = gelu((dot(xk_ref[i], weights) - mean) * inv * gain + bias) * mask
        put_input(ax_ref, i, a, C1)
        return carry

    lax.fori_loop(0, 8, activate, 0)
    convolve(8, ax_ref, t_ref, out_ref, st_ref, mask, C1)


def put_input(ax_ref, i, a, chan):
    left = pltpu.roll(a[:, W - chan :], 1, 0)
    ax_ref[i + 1, :, 0:W] = a.astype(bf16)
    ax_ref[i + 1, :, W:] = left.astype(bf16)


def convolve(rows, ax_ref, t_ref, out_ref, st_ref, mask, chan):
    last = ax_ref[rows]
    ax_ref[0] = jnp.concatenate([jnp.zeros((16, W + chan), bf16), last[: T - 16]], 0)

    def step(i, carry):
        first, second = carry
        y = dot(ax_ref[2 * i], t_ref[0])
        y = y + dot(ax_ref[2 * i + 1], t_ref[1])
        y = y + dot(ax_ref[2 * i + 2], t_ref[2])
        out_ref[i] = y
        ym = y * mask
        return first + colsum(ym), second + colsum(ym * y)

    zero = jnp.zeros((1, W), f32)
    first, second = lax.fori_loop(0, rows // 2, step, (zero, zero))
    st = jnp.concatenate([first, second], 0)
    st_ref[...] = jnp.broadcast_to(st[None], st_ref.shape)


def conv_kernel(level, count, c_ref, stin_ref, bn_ref, t_ref, ax_ref, out_ref, st_ref):
    chan = CHANS[level]
    rows = c_ref.shape[0]
    mean, inv = bn_stats(stin_ref, count, chan)
    gain = bn_ref[2 * level - 2 : 2 * level - 1, :]
    bias = bn_ref[2 * level - 1 : 2 * level, :]
    mask = patch_mask()

    def activate(i, carry):
        put_input(ax_ref, i, gelu((c_ref[i] - mean) * inv * gain + bias) * mask, chan)
        return carry

    lax.fori_loop(0, rows, activate, 0)
    convolve(rows, ax_ref, t_ref, out_ref, st_ref, mask, chan)


def layer_norm(x):
    centered = x - jnp.mean(x, -1, keepdims=True)
    inv = lax.rsqrt(jnp.mean(centered * centered, -1, keepdims=True) + layer_epsilon)
    return centered * inv, inv


def layer_norm_back(dy, s, inv, gain):
    scaled = dy * gain
    inner = scaled - jnp.mean(scaled, -1, keepdims=True)
    return inv * (inner - s * jnp.mean(scaled * s, -1, keepdims=True))


def normed4(count, st_ref, bn_ref, c_ref):
    mean, inv = bn_stats(st_ref, count, C4)
    s = (c_ref[0] - mean) * inv
    return s, s * bn_ref[6:7, :] + bn_ref[7:8, :]


def embed_kernel(count, st_ref, bn_ref, c_ref, wp_ref, pos_ref, vec_ref, a4_ref, x0_ref, n1_ref):
    def vec(name):
        return vec_ref[VEC[name] : VEC[name] + 1, :]

    mask = patch_mask()
    _, y4 = normed4(count, st_ref, bn_ref, c_ref)
    a4_ref[...] = (gelu(y4) * mask).astype(bf16)
    x0 = (dot(a4_ref[...], wp_ref[...]) + vec("proj_bias")) * mask + pos_ref[...]
    x0_ref[...] = x0
    s1, _ = layer_norm(x0)
    n1_ref[...] = (s1 * vec("norm1_gain") + vec("norm1_bias")).astype(bf16)


def block_kernel(
    count,
    st_ref,
    bn_ref,
    n1_hbm,
    vec_hbm,
    x0_hbm,
    a4_hbm,
    wp_hbm,
    c_hbm,
    g_ref,
    gr_ref,
    bn4_hbm,
    so_hbm,
    out_hbm,
    gpos_hbm,
    dwp_hbm,
    c_ref,
    wp_ref,
    vec_ref,
    bn4_ref,
    so_ref,
    out_ref,
    gpos_ref,
    dwp_ref,
    wa,
    wu,
    wd,
    wh,
    sems,
    a4,
    x0,
    n1,
    qkv,
    probs,
    mixed,
    n2t,
    pre,
    acc,
    bqkv,
    mixed_f,
    bpre,
    rowbuf,
):
    gr0, gr1 = wu, wd
    fetched = []
    for k, (source, ref) in enumerate(
        ((n1_hbm, n1), (vec_hbm, vec_ref), (x0_hbm, x0), (a4_hbm, a4), (wp_hbm, wp_ref), (c_hbm, c_ref))
    ):
        fetched.append(pltpu.make_async_copy(source, ref, sems.at[24 + k]))
        if k < 2:
            fetched[-1].start()
    copies = []
    for k, (ref, at, size) in enumerate(
        ((wa, 0, 1536), (wu, 1536, 1536), (wd, 3072, 1536), (wh, 4608, 512))
    ):
        for m in range(2):
            copy = pltpu.make_async_copy(
                g_ref.at[:, m, :, at : at + size], ref.at[m], sems.at[2 * k + m]
            )
            copy.start()
            copies.append(copy)
        if k == 0:
            for copy in fetched[2:]:
                copy.start()

    def send_out(grad, slot):
        out = []
        lanes = slice(1536 * slot, 1536 * slot + 1536)
        for m in range(2):
            for z in range(4):
                copy = pltpu.make_async_copy(
                    grad.at[m, 4 * z : 4 * z + 4],
                    gr_ref.at[:, m, z, :, lanes],
                    sems.at[8 + 8 * slot + 4 * m + z],
                )
                copy.start()
                out.append(copy)
        return out

    def write(ref, target, k):
        copy = pltpu.make_async_copy(ref, target, sems.at[30 + k])
        copy.start()
        moving.append(copy)

    def vec(name):
        return vec_ref[VEC[name] : VEC[name] + 1, :]

    mask = patch_mask()
    valid = token_mask()
    out_row = lax.broadcasted_iota(jnp.int32, (32, 1), 0)
    out_ref[...] = jnp.zeros_like(out_ref)
    key = lax.broadcasted_iota(jnp.int32, (1, T), 1)
    key_bias = jnp.where(((key & 15) < SIDE) | (key == SIDE), 0.0, -1e30)

    for copy in fetched[:2]:
        copy.wait()
    copies[0].wait()
    copies[1].wait()

    def tile(ref, m, at, size=256):
        return ref[m, :, :, pl.ds(at, size)].reshape(D, size)

    for part in range(9):
        y = dot(n1[...], tile(wa, part // 6, 256 * (part % 6)))
        lanes = slice(256 * (part % 3), 256 * (part % 3) + 256)
        if part < 3:
            y = y + vec("query_bias")[:, lanes]
        elif part >= 6:
            y = y + vec("value_bias")[:, lanes]
        qkv[:, 256 * part : 256 * part + 256] = y.astype(bf16)
    scale = HEAD_DIM**-0.5

    def attend(pair, carry):
        at = pl.multiple_of(pair * 128, 128)
        q = qkv[:, pl.ds(at, 128)] * bf16(scale)
        k = qkv[:, pl.ds(at + D, 128)]
        v = qkv[:, pl.ds(at + 2 * D, 128)]
        out = []
        for h in range(2):
            lanes = slice(64 * h, 64 * h + 64)
            scores = dot_nt(q[:, lanes], k[:, lanes]) + key_bias
            e = jnp.exp(scores - jnp.max(scores, -1, keepdims=True))
            p = e * (1.0 / jnp.sum(e, -1, keepdims=True))
            probs[2 * pair + h] = p
            out.append(dot(p.astype(bf16), v[:, lanes]))
        out = jnp.concatenate(out, 1)
        mixed[:, pl.ds(at, 128)] = out.astype(bf16)
        mixed_f[:, pl.ds(at, 128)] = out
        return carry

    lax.fori_loop(0, HEADS // 2, attend, 0, unroll=6)
    for copy in fetched[2:]:
        copy.wait()
    att = [dot_nt(mixed[...], wa[1, :, :, D : 2 * D].reshape(D, D))]
    x1 = x0[...] + att[0] + vec("out_bias")
    mean_x1 = colsum(x1 * valid) / TOK
    s2, i2 = layer_norm(x1)
    n2 = (s2 * vec("norm2_gain") + vec("norm2_bias")).astype(bf16)
    n2t[...] = n2.T
    copies[2].wait()
    copies[3].wait()
    bias = [jnp.concatenate([vec_ref[r : r + 1, :], vec_ref[r + 1 : r + 2, :]], 1) for r in (12, 14)]
    rowbuf[0:1, :] = bias[0]
    rowbuf[8:9, :] = bias[1]
    for m in range(2):

        def up(k, carry):
            at = pl.multiple_of(k * 256, 256)
            y = dot(n2, tile(wu, m, at)) + rowbuf[8 * m : 8 * m + 1, pl.ds(at, 256)]
            t = jnp.tanh(GELU_A * (y + GELU_B * y * y * y))
            half = 0.5 + 0.5 * t
            h = (y * half).astype(bf16).astype(f32) * valid
            rowbuf[16 + 8 * m : 17 + 8 * m, pl.ds(at, 256)] = colsum(h)
            inner = GELU_A + (3.0 * GELU_A * GELU_B) * y * y
            pre[m, :, pl.ds(at, 256)] = (half + 0.5 * y * (1.0 - t * t) * inner) * valid
            return carry

        lax.fori_loop(0, 6, up, 0, unroll=6)
        for k in range(2):
            row = OUT_HIDDEN + 2 * m + k
            out_ref[row : row + 1, :] = rowbuf[16 + 8 * m : 17 + 8 * m, D * k : D * k + D]
    copies[4].wait()
    copies[5].wait()
    hs = jnp.concatenate([out_ref[OUT_HIDDEN + k : OUT_HIDDEN + k + 1, :] for k in range(4)], 1) / TOK
    high = hs.astype(bf16)
    low = (hs - high.astype(f32)).astype(bf16)
    out = jnp.zeros((1, D), f32)
    for m in range(2):
        lanes = slice(1536 * m, 1536 * m + 1536)
        both = jnp.concatenate(
            [jnp.broadcast_to(high[:, lanes], (8, 1536)), jnp.broadcast_to(low[:, lanes], (8, 1536))], 0
        )
        y = dot_nt(both, wd[m].reshape(D, 1536))
        out = out + y[0:1] + y[8:9]
    pooled = mean_x1 + out + vec("mlp_bias")
    s3, i3 = layer_norm(pooled)
    final = (s3 * vec("final_gain") + vec("final_bias")).astype(bf16)
    copies[6].wait()
    copies[7].wait()
    wide = jnp.broadcast_to(final, (16, D))
    logits = jnp.concatenate([dot(wide, wh[m].reshape(D, 512))[0:1] for m in range(2)], 1)
    lane = lax.broadcasted_iota(jnp.int32, (1, 1024), 1)
    real = (lane & 511) < CLASSES // 2
    def pair(row):
        return jnp.concatenate([vec_ref[row : row + 1, 0:512], vec_ref[row + 1 : row + 2, 0:512]], 1)

    logits = jnp.where(real, logits + pair(VEC_HEAD), -1e30)
    top = jnp.max(logits, -1, keepdims=True)
    log_probs = logits - top - jnp.log(jnp.sum(jnp.exp(logits - top), -1, keepdims=True))
    aim = pair(VEC_AIM)
    loss = -jnp.sum(jnp.where(real, aim * log_probs, 0.0), keepdims=True)
    out_ref[...] = jnp.where(out_row >= OUT_LOSS, jnp.broadcast_to(loss, out_ref.shape), out_ref[...])
    back_logits = jnp.where(real, jnp.exp(log_probs) - aim, 0.0).astype(bf16)
    for m in range(2):
        row = OUT_HEAD + m
        out_ref[row : row + 1, 0:512] = back_logits[:, 512 * m : 512 * m + 512].astype(f32)
    out_ref[OUT_FINAL : OUT_FINAL + 1, :] = final.astype(f32)
    wide = jnp.broadcast_to(back_logits, (16, 1024))
    back_final = (
        dot_nt(wide[:, 0:512], wh[0].reshape(D, 512)) + dot_nt(wide[:, 512:], wh[1].reshape(D, 512))
    )[0:1]
    def put(name, value):
        out_ref[VEC[name] : VEC[name] + 1, :] = value

    put("final_gain", back_final * s3)
    put("final_bias", back_final)
    back2 = layer_norm_back(back_final, s3, i3, vec("final_gain")) / TOK
    back_out = back2.astype(bf16)
    out_ref[OUT_BACK : OUT_BACK + 1, :] = back_out.astype(f32)
    put("mlp_bias", back_out.astype(f32) * TOK)
    wide = jnp.broadcast_to(back_out, (16, D))
    for m in range(2):
        for k in range(6):
            at = 256 * k
            rowbuf[8 * m : 8 * m + 1, at : at + 256] = dot(wide, tile(wd, m, at))[0:1]
    for m in range(2):

        def down(k, carry):
            at = pl.multiple_of(k * 256, 256)
            bp = (rowbuf[8 * m : 8 * m + 1, pl.ds(at, 256)] * pre[m, :, pl.ds(at, 256)]).astype(bf16)
            rowbuf[16 + 8 * m : 17 + 8 * m, pl.ds(at, 256)] = colsum(bp.astype(f32))
            bpre[m, :, pl.ds(at, 256)] = bp
            grad = dot(n2t[...], bp)
            gr1[m, :, :, pl.ds(at, 256)] = grad.astype(bf16).reshape(16, 48, 256)
            return carry

        lax.fori_loop(0, 6, down, 0, unroll=6)
        for k in range(2):
            row = VEC_HIDDEN + 2 * m + k
            out_ref[row : row + 1, :] = rowbuf[16 + 8 * m : 17 + 8 * m, D * k : D * k + D]
    moving = send_out(gr1, 1)
    back_n2 = dot_nt(bpre[0], wu[0].reshape(D, 1536)) + dot_nt(bpre[1], wu[1].reshape(D, 1536))
    put("norm2_gain", colsum(back_n2 * s2))
    put("norm2_bias", colsum(back_n2))
    back1 = back2 * valid + layer_norm_back(back_n2, s2, i2, vec("norm2_gain"))
    back_att = back1.astype(bf16)
    put("out_bias", colsum(back_att.astype(f32)))
    back_att_t = back_att.T
    for k in range(3):
        lanes = slice(256 * k, 256 * k + 256)
        grad = dot(back_att_t, mixed[:, lanes])
        gr0[1, :, :, D + 256 * k : D + 256 * k + 256] = grad.astype(bf16).reshape(16, 48, 256)
    acc[...] = dot(back_att, wa[1, :, :, D : 2 * D].reshape(D, D))

    def attend_back(pair, carry):
        at = pl.multiple_of(pair * 128, 128)
        q = qkv[:, pl.ds(at, 128)]
        k = qkv[:, pl.ds(at + D, 128)]
        v = qkv[:, pl.ds(at + 2 * D, 128)]
        bm = acc[:, pl.ds(at, 128)].astype(bf16)
        bm_mixed = bm.astype(f32) * mixed_f[:, pl.ds(at, 128)]
        bq, bk, bv = [], [], []
        for h in range(2):
            lanes = slice(64 * h, 64 * h + 64)
            p = probs[2 * pair + h]
            bp = dot_nt(bm[:, lanes], v[:, lanes])
            bv.append(dot_tn(p.astype(bf16), bm[:, lanes]))
            inner = jnp.sum(bm_mixed[:, lanes], -1, keepdims=True)
            bs = (p * (bp - inner)).astype(bf16)
            bq.append(dot(bs, k[:, lanes]) * scale)
            bk.append(dot_tn(bs, q[:, lanes]) * scale)
        bqkv[:, pl.ds(at, 128)] = jnp.concatenate(bq, 1).astype(bf16)
        bqkv[:, pl.ds(at + D, 128)] = jnp.concatenate(bk, 1).astype(bf16)
        bqkv[:, pl.ds(at + 2 * D, 128)] = jnp.concatenate(bv, 1).astype(bf16)
        return carry

    lax.fori_loop(0, HEADS // 2, attend_back, 0, unroll=6)
    put("query_bias", colsum(bqkv[:, 0:D].astype(f32)))
    put("value_bias", colsum(bqkv[:, 2 * D :].astype(f32)))
    n1t = n1[...].T
    for part in range(9):
        m, at = part // 6, 256 * (part % 6)
        b = bqkv[:, 256 * part : 256 * part + 256]
        gr0[m, :, :, at : at + 256] = dot(n1t, b).astype(bf16).reshape(16, 48, 256)
    moving += send_out(gr0, 0)
    back_n1 = dot_nt(bqkv[:, 0:1536], wa[0].reshape(D, 1536))
    back_n1 = back_n1 + dot_nt(bqkv[:, 1536:], wa[1, :, :, 0:D].reshape(D, D))
    s1, i1 = layer_norm(x0[...])
    put("norm1_gain", colsum(back_n1 * s1))
    put("norm1_bias", colsum(back_n1))
    back0 = back1 + layer_norm_back(back_n1, s1, i1, vec("norm1_gain"))
    gpos_ref[...] = back0
    write(gpos_ref, gpos_hbm, 0)
    back_patch = (back0 * mask).astype(bf16)
    put("proj_bias", colsum(back_patch.astype(f32)))
    dwp_ref[...] = dot_tn(a4[...], back_patch)
    write(dwp_ref, dwp_hbm, 1)
    s4, y4 = normed4(count, st_ref, bn_ref, c_ref)
    bn4 = dot_nt(back_patch, wp_ref[...]) * gelu_slope(y4) * mask
    bn4_ref[0] = bn4
    write(bn4_ref, bn4_hbm, 2)
    st = jnp.concatenate([colsum(bn4), colsum(bn4 * s4)], 0)
    so_ref[...] = jnp.broadcast_to(st[None], so_ref.shape)
    write(so_ref, so_hbm, 3)
    out_ref[OUT_SUMS : OUT_SUMS + 1, :] = jnp.concatenate([st[0:1], st[1:2]], 1)
    write(out_ref, out_hbm, 4)
    for copy in moving:
        copy.wait()


def conv_back_kernel(
    level,
    count,
    count_in,
    back_ref,
    tot_ref,
    c_ref,
    st_ref,
    t_ref,
    cin_ref,
    stin_ref,
    bn_ref,
    g,
    backin_ref,
    so_ref,
    ss_ref,
):
    finish_level(level, count, back_ref, tot_ref, c_ref, st_ref, bn_ref, g)
    mean, inv = bn_stats(stin_ref, count_in, CHANS[level - 1])

    def normed(q):
        return (cin_ref[q] - mean) * inv

    def keep(q, y):
        backin_ref[q] = y

    st = back_through(level, g, t_ref, bn_ref, normed, keep)
    ss_ref[...] = st
    so_ref[...] = jnp.broadcast_to(st[None], so_ref.shape)


def finish_level(level, count, back_ref, tot_ref, c_ref, st_ref, bn_ref, g):
    chan = CHANS[level]
    rows = back_ref.shape[0]
    mask = patch_mask()
    mean, inv = bn_stats(st_ref, count, chan)
    gain = bn_ref[2 * level - 2 : 2 * level - 1, :]
    tot = fold_phases(jnp.sum(tot_ref[:, 0:2, :], 0), chan) / count

    def finish(i, carry):
        s = (c_ref[i] - mean) * inv
        g[i] = (inv * gain * (back_ref[i] - tot[0:1] - s * tot[1:2]) * mask).astype(bf16)
        return carry

    lax.fori_loop(0, rows, finish, 0)
    head = g[0]
    g[rows] = jnp.concatenate([head[16:], jnp.zeros((16, W), bf16)], 0)


def kernel_grad(level, ax_ref, g, dw_ref, dt):
    chan, chan_in = CHANS[level], CHANS[level - 1]
    rows = g.shape[0] - 1
    dt[...] = jnp.zeros_like(dt)

    def weights(i, carry):
        for tap in range(3):
            dt[tap] += dot_tn(ax_ref[2 * i + tap], g[i])
        return carry

    lax.fori_loop(0, rows, weights, 0)
    for tap in range(3):
        base = tap * 3 * chan_in
        for j in range(W // chan):
            for k in range(dw_ref.shape[0]):
                width = min(128, chan - 128 * k)
                cols = slice(j * chan + 128 * k, j * chan + 128 * k + width)
                if j == 0:
                    dw_ref[k, base : base + chan_in, 0:width] = dt[tap, W : W + chan_in, cols]
                    dw_ref[k, base + chan_in : base + 3 * chan_in, 0:width] = dt[
                        tap, 0 : 2 * chan_in, cols
                    ]
                else:
                    at = (2 * j - 1) * chan_in
                    dw_ref[k, base : base + 3 * chan_in, 0:width] += dt[
                        tap, at : at + 3 * chan_in, cols
                    ]


def back_through(level, g, t_ref, bn_ref, normed, keep):
    chan_in = CHANS[level - 1]
    rows = g.shape[0] - 1
    mask = patch_mask()
    gain = bn_ref[2 * level - 4 : 2 * level - 3, :]
    bias = bn_ref[2 * level - 3 : 2 * level - 2, :]

    def through(q, p, carry):
        first, second = carry
        left = pltpu.roll(p[:, W:], T - 1, 0)
        p = jnp.concatenate([p[:, 0 : W - chan_in], p[:, W - chan_in : W] + left], 1)
        s = normed(q)
        y = p * gelu_slope(s * gain + bias) * mask
        keep(q, y)
        return first + colsum(y), second + colsum(y * s)

    def back(i, carry):
        carry = through(2 * i, dot_nt(g[i], t_ref[1]), carry)
        p = dot_nt(g[i], t_ref[2]) + dot_nt(g[i + 1], t_ref[0])
        return through(2 * i + 1, p, carry)

    zero = jnp.zeros((1, W), f32)
    first, second = lax.fori_loop(0, rows, back, (zero, zero))
    return jnp.concatenate([first, second], 0)


LATE_W1 = 9 * C1 * C2 // 128
LATE_SUMS = LATE_W1 + 32
LATE_ROWS = LATE_SUMS + 4 * 6


def conv2_back_kernel(
    count,
    count_in,
    back_ref,
    tot_ref,
    c_ref,
    st_ref,
    ax_ref,
    t_ref,
    xk_ref,
    gram_ref,
    w1_ref,
    t1_ref,
    bn_ref,
    ss2_ref,
    ss3_ref,
    ss4_ref,
    late_ref,
    dw,
    g,
    dt,
    dt1,
    late,
):
    finish_level(2, count, back_ref, tot_ref, c_ref, st_ref, bn_ref, g)
    kernel_grad(2, ax_ref, g, dw, dt)
    gram, cross, mean, inv = level1_stats(gram_ref, w1_ref, count_in)
    mean, inv = tile_lanes(mean, C1), tile_lanes(inv, C1)
    weights = t1_ref[...]
    dt1[...] = jnp.zeros_like(dt1)

    def normed(q):
        return (dot(xk_ref[q], weights) - mean) * inv

    def keep(q, y):
        dt1[...] += dot_tn(xk_ref[q], y.astype(bf16))

    st = back_through(2, g, t_ref, bn_ref, normed, keep)
    late[...] = jnp.zeros_like(late)
    q = 9 * C1 // 4
    wide = jnp.concatenate([dw[0, pl.ds(k, q, stride=4), :][:, 0:C2] for k in range(4)], 1)
    for k in range(3):
        late[pl.ds(k, q, stride=3), :] = wide[:, 128 * k : 128 * k + 128]
    for tap in range(3):
        base = LATE_W1 + 9 * tap
        for j in range(8):
            cols = slice(j * C1, (j + 1) * C1)
            if j == 0:
                late[base : base + 3, 0:C1] = dt1[tap * 64 + 48 : tap * 64 + 51, cols]
                late[base + 3 : base + 9, 0:C1] = dt1[tap * 64 : tap * 64 + 6, cols]
            else:
                at = tap * 64 + 6 * j - 3
                late[base : base + 9, 0:C1] += dt1[at : at + 9, cols]
    ss4 = jnp.concatenate(
        [ss4_ref[OUT_SUMS : OUT_SUMS + 1, 0:W], ss4_ref[OUT_SUMS : OUT_SUMS + 1, W:]], 0
    )
    for level, ss in enumerate((st, ss2_ref[...], ss3_ref[...], ss4)):
        for which in range(2):
            for k in range(3):
                row = LATE_SUMS + 6 * level + 3 * which + k
                late[row : row + 1, :] = ss[which : which + 1, 128 * k : 128 * k + 128]
    each = late_ref.shape[1]
    for d in range(late_ref.shape[0]):
        late_ref[d] = late[each * d : each * d + each, :]


def early_kernel(
    parts,
    mp,
    stem_len,
    small_len,
    rows_stem,
    rows_small,
    at_ref,
    dw3_ref,
    dw4_ref,
    dwp_ref,
    gv_ref,
    gpos_ref,
    *refs,
):
    outs = refs[:parts]
    frame, table, vecs = refs[parts:]
    if outs[0].shape[1] > rows_stem + rows_small:
        vecs[...] = jnp.zeros_like(vecs)
        base = pl.multiple_of(24 * at_ref[0], 8)
        for index, ref in enumerate(outs):
            first = at_ref[index] == 0
            hs = [gv_ref[OUT_HIDDEN + k : OUT_HIDDEN + k + 1, :] for k in range(4)]
            hs = jnp.concatenate([jnp.where(first, hs[0], hs[2]), jnp.where(first, hs[1], hs[3])], 1)
            bl = [gv_ref[OUT_HEAD + k : OUT_HEAD + k + 1, 0:512] for k in range(2)]
            bl = jnp.where(first, bl[0], bl[1])
            rows = [hs[:, 128 * k : 128 * k + 128] for k in range(12)]
            rows += [bl[:, 128 * k : 128 * k + 128] for k in range(4)]
            vecs[pl.ds(base, 16), :] = jnp.concatenate(rows, 0)
            for d in range(16):
                lanes = slice(48 * d, 48 * d + 48)
                fill = jnp.zeros((1, 16), f32)
                row = jnp.concatenate(
                    [
                        gv_ref[OUT_BACK : OUT_BACK + 1, lanes],
                        fill,
                        gv_ref[OUT_FINAL : OUT_FINAL + 1, lanes],
                        fill,
                    ],
                    1,
                )
                vecs[pl.ds(base + 16, 8), :] = jnp.broadcast_to(row, (8, 128))
                ref[d, rows_stem + rows_small :, :] = vecs[...].astype(bf16)
    frame[0:ROW_W3, :] = jnp.zeros((ROW_W3, 128), f32)
    frame[STEM_ROWS:, :] = jnp.zeros((frame.shape[0] - STEM_ROWS, 128), f32)
    q = 9 * C2 // 2
    wide = jnp.concatenate(
        [
            jnp.concatenate(
                [
                    dw3_ref[0, pl.ds(k, q, stride=2), :],
                    dw3_ref[1, pl.ds(k, q, stride=2), :][:, 0 : C3 - 128],
                ],
                1,
            )
            for k in range(2)
        ],
        1,
    )
    for k in range(3):
        frame[pl.ds(ROW_W3 + k, q, stride=3), :] = wide[:, 128 * k : 128 * k + 128]
    for k in range(3):
        frame[pl.ds(ROW_W4 + k, 9 * C3, stride=3), :] = dw4_ref[k]
    for k in range(6):
        frame[pl.ds(ROW_WP + k, C4, stride=6), :] = dwp_ref[:, 128 * k : 128 * k + 128]
    table[0:12, :] = jnp.zeros((12, 128), f32)
    table[SMALL_ROWS:, :] = jnp.zeros((table.shape[0] - SMALL_ROWS, 128), f32)
    for k in range(6):
        lanes = slice(128 * k, 128 * k + 128)
        for name, index in VEC.items():
            row = SMALL_AT[name] + k
            table[row : row + 1, :] = gv_ref[index : index + 1, lanes]
        for h in range(4):
            row = SMALL_AT["hidden_bias"] + 6 * h + k
            table[row : row + 1, :] = gv_ref[VEC_HIDDEN + h : VEC_HIDDEN + h + 1, lanes]
        at = SMALL_AT["position"] + k
        for r in range(SIDE):
            table[pl.ds(at + 6 * (1 + SIDE * r), SIDE, stride=6), :] = gpos_ref[
                16 * r : 16 * r + SIDE, lanes
            ]
        table[at : at + 1, :] = gpos_ref[SIDE : SIDE + 1, lanes]
        row = SMALL_AT["class_token"] + k
        table[row : row + 1, :] = gpos_ref[SIDE : SIDE + 1, lanes]
    line = jnp.concatenate(
        [
            gv_ref[OUT_HEAD : OUT_HEAD + 1, 0:500],
            gv_ref[OUT_HEAD + 1 : OUT_HEAD + 2, 0:500],
            jnp.zeros((1, 24), f32),
        ],
        1,
    )
    row = SMALL_AT["head_bias"]
    for k in range(8):
        table[row + k : row + k + 1, :] = line[:, 128 * k : 128 * k + 128]
    for index, ref in enumerate(outs):
        mv = at_ref[index]

        def take(d, carry):
            owner = d * mp + mv
            a = (owner * stem_len + STEM_SHIFT) // 128
            ref[d, 0:rows_stem, :] = frame[pl.ds(a, rows_stem), :].astype(bf16)
            b = (owner * small_len + SMALL_SHIFT) // 128
            ref[d, rows_stem : rows_stem + rows_small, :] = table[pl.ds(b, rows_small), :].astype(bf16)
            return carry

        lax.fori_loop(0, ref.shape[0], take, 0)


def unshift_lanes(x, s, length):
    lane = lax.broadcasted_iota(jnp.int32, x.shape, 1)
    row = lax.broadcasted_iota(jnp.int32, x.shape, 0)
    moved = pltpu.roll(x, 128 - s, 1)
    after = pltpu.roll(moved, x.shape[0] - 1, 0)
    y = jnp.where(lane < 128 - s, moved, after)
    return jnp.where(row * 128 + lane < length, y, 0.0)


def unpack_kernel(stem_len, small_len, at_ref, x_ref, stem_ref, small_ref, sq_ref):
    rows = stem_ref.shape[0]
    end = rows + small_ref.shape[0]
    total = jnp.sum(x_ref[:, 0:end, :].astype(f32), 0)
    stem = unshift_lanes(total[0:rows], at_ref[0], stem_len)
    small = unshift_lanes(total[rows:], at_ref[1], small_len)
    stem_ref[...] = stem
    small_ref[...] = small
    sq_ref[...] = colsum(stem * stem) + colsum(small * small)


def norm_kernel(parts, *refs):
    late_ref, sq_ref, down_ref, head_ref, loss_ref, g0_ref, g1_ref, out_ref = refs[parts:]
    total = sum(ref[...].astype(f32) for ref in refs[:parts])
    half = g0_ref.shape[1]
    g0, g1 = total[:, 0:half], total[:, half:]
    g0_ref[...] = g0
    g1_ref[...] = g1
    squares = jnp.sum(g0 * g0 + g1 * g1 + down_ref[...] * down_ref[...], keepdims=True)
    squares = squares + jnp.sum(head_ref[...] * head_ref[...], keepdims=True)
    squares = squares + jnp.sum(sq_ref[...], keepdims=True)
    lane = lax.broadcasted_iota(jnp.int32, (1, 128), 1)
    line = jnp.where(lane == 0, squares, loss_ref[OUT_LOSS : OUT_LOSS + 1, 0:128])
    late = jnp.sum(late_ref[...], 0)
    each = late.shape[0]
    out_ref[:, 0:each, :] = jnp.broadcast_to(late[None], (out_ref.shape[0], each, 128))
    out_ref[:, each : each + 1, :] = jnp.broadcast_to(line[None], (out_ref.shape[0], 1, 128))


def last_kernel(
    counts,
    stem_len,
    small_len,
    at_ref,
    x_ref,
    gram_ref,
    w1_ref,
    bn_ref,
    stem_ref,
    small_ref,
    stem_out,
    small_out,
    facts_ref,
    late,
    frame,
    table,
):
    devices, each = x_ref.shape[0], x_ref.shape[1] - 1
    for d in range(devices):
        late[each * d : each * d + each, :] = x_ref[d, 0:each, :]
    frame[...] = jnp.zeros_like(frame)
    table[...] = jnp.zeros_like(table)
    frame[ROW_W2:ROW_W3, :] = late[0:LATE_W1, :]
    line = [[jnp.zeros((1, SMALL_SHIFT), f32)], []]
    for level in range(4):
        chan = CHANS[level + 1]
        rows = []
        for which in range(2):
            row = LATE_SUMS + 6 * level + 3 * which
            rows.append(jnp.concatenate([late[row + k : row + k + 1, :] for k in range(3)], 1))
        both = fold_phases(jnp.concatenate(rows, 0), chan)
        line[0].append(both[1:2, 0:chan])
        line[1].append(both[0:1, 0:chan])
        if level == 0:
            tot = both[:, 0:128] / counts
    line = jnp.concatenate(line[0] + line[1], 1)
    for k in range(12):
        table[k : k + 1, :] = line[:, 128 * k : 128 * k + 128]
    gram, cross, mean, inv = level1_stats(gram_ref, w1_ref, counts)
    ones = gram[:, 27:28]
    grad = late[LATE_W1:LATE_SUMS, :] - ones * tot[0:1] - (cross - ones * mean) * inv * tot[1:2]
    grad = grad * (inv * bn_ref[0:1, 0:128])
    line = [jnp.zeros((1, STEM_SHIFT), f32)] + [grad[k : k + 1, 0:C1] for k in range(27)]
    line = jnp.concatenate(line, 1)
    for k in range(ROW_W2):
        frame[k : k + 1, :] = line[:, 128 * k : 128 * k + 128]
    squares = jnp.sum(frame[0:ROW_W3, :] * frame[0:ROW_W3, :], keepdims=True)
    squares = squares + jnp.sum(table[0:12, :] * table[0:12, :], keepdims=True)
    ends = jnp.sum(x_ref[:, each : each + 1, :], 0)
    lane = lax.broadcasted_iota(jnp.int32, (1, 128), 1)
    norm = jnp.sqrt(squares + jnp.sum(jnp.where(lane == 0, ends, 0.0), keepdims=True))
    loss = jnp.sum(jnp.where(lane == 1, ends, 0.0), keepdims=True)
    row = lax.broadcasted_iota(jnp.int32, (8, 128), 0)
    factor = jnp.minimum(1.0, clip_norm / norm)
    facts_ref[...] = jnp.where(row == 0, loss, jnp.where(row == 1, norm, factor))
    part = frame[pl.ds(at_ref[2], stem_ref.shape[0]), :]
    stem_out[...] = stem_ref[...] + unshift_lanes(part, at_ref[0], stem_len)
    part = table[pl.ds(at_ref[3], small_ref.shape[0]), :]
    small_out[...] = small_ref[...] + unshift_lanes(part, at_ref[1], small_len)


def call(kernel, outs, *args, scratch=(), smem=0, hbm=(), load=(), store=(), hbm_out=(), limit=32):
    def space(index, free):
        if index in free:
            return pl.BlockSpec(memory_space=pltpu.HBM)
        return pl.BlockSpec(memory_space=pltpu.VMEM)

    def shape(index):
        where = pltpu.HBM if index in (*hbm_out, *store) else jax.ShapeDtypeStruct
        return where(*outs[index])

    args = [
        pltpu.with_memory_space_constraint(arg, pltpu.HBM) if index in (*hbm, *load) else arg
        for index, arg in enumerate(args)
    ]
    count = len(args)
    moved = [jax.ShapeDtypeStruct(args[k].shape, args[k].dtype) for k in load]
    moved += [jax.ShapeDtypeStruct(*outs[k]) for k in store]

    def body(*refs):
        refs = list(refs)
        if not moved:
            return kernel(*refs)
        buffers, sems = refs[-1 - len(moved) : -1], refs[-1]
        refs = refs[: -1 - len(moved)]
        copies = []
        for k, index in enumerate(load):
            copies.append(pltpu.make_async_copy(refs[index], buffers[k], sems.at[k]))
            copies[-1].start()
            refs[index] = buffers[k]
        for copy in copies:
            copy.wait()
        targets = []
        for k, index in enumerate(store):
            targets.append((buffers[len(load) + k], refs[count + index], sems.at[len(load) + k]))
            refs[count + index] = buffers[len(load) + k]
        kernel(*refs)
        copies = [pltpu.make_async_copy(*target) for target in targets]
        for copy in copies:
            copy.start()
        for copy in copies:
            copy.wait()

    extra = [pltpu.VMEM(x.shape, x.dtype) for x in moved]
    if moved:
        extra.append(pltpu.SemaphoreType.DMA((len(moved),)))
    specs = [pl.BlockSpec(memory_space=pltpu.SMEM)] * smem
    specs += [space(index, (*hbm, *load)) for index in range(smem, count)]
    return pl.pallas_call(
        body,
        out_shape=[shape(index) for index in range(len(outs))],
        in_specs=specs,
        out_specs=[space(index, (*hbm_out, *store)) for index in range(len(outs))],
        scratch_shapes=[*scratch, *extra],
        compiler_params=pltpu.CompilerParams(vmem_limit_bytes=limit * 1024 * 1024),
    )(*args)


def adam_step(weight, first, second, grad, factor, rate):
    grad = grad * factor
    first = beta_one * first + (1.0 - beta_one) * grad
    second = beta_two * second + (1.0 - beta_two) * grad * grad
    first_fixed = first / (1.0 - beta_one**STEP)
    second_fixed = second / (1.0 - beta_two**STEP)
    return (
        weight
        - rate * (first_fixed / (jnp.sqrt(second_fixed) + adam_epsilon) + decay_rate * weight),
        first,
        second,
    )


def local(
    pixels,
    labels,
    stem,
    stem_first,
    stem_second,
    small,
    small_first,
    small_second,
    block,
    block_first,
    block_second,
    head,
    head_first,
    head_second,
):
    dp, mp = lax.axis_size("dp"), lax.axis_size("mp")
    n = dp * mp
    me, mine = lax.axis_index("dp"), lax.axis_index("mp")
    owner = me * mp + mine
    stem_len, small_len = stem.shape[0], small.shape[0]
    rows_stem = up16(-(-(stem_len + 127) // 128))
    rows_small = up16(-(-(small_len + 127) // 128))
    rows = rows_stem + rows_small
    everyone = ("dp", "mp")
    fast = (dp, mp) == (16, 2)

    def share(x):
        return lax.all_to_all(x, everyone, 0, 0)

    part = FF // mp
    cls = CLASSES // mp
    cls_pad = 512 // (mp // 2)
    packed = jnp.concatenate(
        [block[0], block[1], block[2], jnp.pad(head, ((0, 0), (0, cls_pad - cls)))], 1
    ).astype(bf16)
    packed, stem, small = lax.optimization_barrier((packed, stem, small))
    stem_at, small_at = owner * stem_len + STEM_SHIFT, owner * small_len + SMALL_SHIFT
    at = jnp.stack(
        [
            stem_at % 128,
            small_at % 128,
            jnp.minimum(stem_at // 128, ROW_W3),
            jnp.minimum(small_at // 128, 16),
        ]
    ).astype(jnp.int32)
    (piece,) = call(
        pack_kernel,
        [((rows, 128), bf16)],
        at,
        jnp.pad(stem, (0, rows_stem * 128 - stem_len)).reshape(rows_stem, 128),
        jnp.pad(small, (0, rows_small * 128 - small_len)).reshape(rows_small, 128),
        smem=1,
        limit=4,
    )

    strip = pixels.reshape(pixels.shape[1], 128)
    strip, piece, packed, at = lax.optimization_barrier((strip, piece, packed, at))
    gathered = lax.all_gather(packed, everyone, axis=0)
    half = strip.shape[0] // 2
    pairs = [(source, (source + dp - 1) % dp) for source in range(dp)]
    lower = lax.ppermute(strip[:half], "dp", pairs)

    if fast:
        gathered = gathered.reshape(16, 2, 48, packed.shape[1])
    else:
        g = gathered.reshape(dp, mp, D // dp, packed.shape[1])
        g = jnp.transpose(g, (0, 2, 1, 3)).reshape(D, mp, -1)
        slots = [g[:, :, k * part : (k + 1) * part].reshape(D, 2, FF // 2) for k in range(3)]
        top = g[:, :, 3 * part : 3 * part + cls].reshape(D, 2, CLASSES // 2)
        slots.append(jnp.pad(top, ((0, 0), (0, 0), (0, 12))))
        g = jnp.concatenate(slots, 2).reshape(16, 48, 2, -1)
        gathered = jnp.transpose(g, (0, 2, 1, 3))

    if fast:
        planes = [[4 * z + k for k in range(4)] for z in range(4)]
        column = [piece]
        for k in (1, 2, 3):
            pairs = [(source, source ^ (4 * k)) for source in range(dp)]
            column.append(lax.ppermute(piece, "dp", pairs))
        *column, lower = lax.optimization_barrier((*column, lower))
        column = jnp.stack(column, 0)
        column = jnp.broadcast_to(column[None], (4, 4, rows, 128))
        column = lax.all_to_all(column, "dp", 0, 0, axis_index_groups=planes)
        column = column.reshape(dp, rows, 128)
    else:
        column = lax.all_to_all(jnp.broadcast_to(piece[None], (dp, rows, 128)), "dp", 0, 0)
    xk, gram = call(
        image_kernel,
        [((8, T, 192), bf16), ((n, 8, 128), f32)],
        strip[half:],
        lower,
        scratch=[
            pltpu.VMEM((2 * half, 128), f32),
            pltpu.VMEM((16 * half // 3 + 16, 128), f32),
            pltpu.VMEM((17, T, 64), bf16),
        ],
        limit=12,
    )
    gram, xk, column = lax.optimization_barrier((gram, xk, column))
    gram = share(gram)
    if mp == 2:
        swap = [(0, 1), (1, 0)]
        pieces = [column, lax.ppermute(column, "mp", swap)]
        which = jnp.stack([mine, 1 - mine]).astype(jnp.int32)
    else:
        columns = lax.all_gather(column, "mp", axis=0)
        pieces = [columns[k] for k in range(mp)]
        which = jnp.arange(mp, dtype=jnp.int32)
    which = jnp.concatenate([which, labels.reshape(1), (me >> 2).reshape(1).astype(jnp.int32)])
    frame_rows = (stem_len * n + STEM_SHIFT) // 128 + rows_stem + 16
    table_rows = (small_len * n + SMALL_SHIFT) // 128 + rows_small + 16
    frames = [pltpu.VMEM((frame_rows, 128), f32), pltpu.VMEM((table_rows, 128), f32)]
    w1, t1, t2, t3, t4, wp, bn, vec, pos = call(
        functools.partial(assemble_kernel, fast, len(pieces), mp, stem_len, small_len, rows_stem, rows_small),
        [
            ((32, 128), f32),
            ((192, W), bf16),
            ((3, W + C1, W), bf16),
            ((3, W + C2, W), bf16),
            ((3, W + C3, W), bf16),
            ((C4, D), bf16),
            ((8, W), f32),
            ((24, D), f32),
            ((T, D), f32),
        ],
        which,
        *pieces,
        smem=1,
        store=(1, 2, 3, 4, 5, 7, 8),
        scratch=frames
        + [
            pltpu.VMEM((9 * C1, 128), f32),
            pltpu.VMEM((9 * C2, 128), f32),
            pltpu.VMEM((9 * C2, 128), f32),
            pltpu.VMEM((192, W), f32),
            pltpu.VMEM((W + C1, W), f32),
            pltpu.VMEM((W + C2, W), f32),
        ],
        limit=20,
    )

    positions = SIDE * SIDE * n
    counts = [None, 64.0 * positions, 16.0 * positions, 4.0 * positions, 1.0 * positions]
    ax, conv, st = call(
        functools.partial(conv12_kernel, counts[1]),
        [((9, T, W + C1), bf16), ((4, T, W), f32), ((n, 2, W), f32)],
        xk,
        gram,
        w1,
        t1,
        bn,
        t2,
        load=(3, 5),
        limit=14,
    )
    convs = [None, None, conv]
    stats = [None, None, share(st)]
    inputs = [None, None, ax]
    kernels = [None, t1, t2, t3, t4]
    for level in (3, 4):
        r = 2 ** (4 - level)
        ax, conv, st = call(
            functools.partial(conv_kernel, level - 1, counts[level - 1]),
            [((2 * r + 1, T, W + CHANS[level - 1]), bf16), ((r, T, W), f32), ((n, 2, W), f32)],
            convs[level - 1],
            stats[level - 1],
            bn,
            kernels[level],
            load=(3,),
            store=(0, 1, 2) if level == 4 else (),
            limit=10,
        )
        inputs.append(ax)
        convs.append(conv)
        stats.append(share(st))

    a4, x0, n1 = call(
        functools.partial(embed_kernel, counts[4]),
        [((T, C4), bf16), ((T, D), f32), ((T, D), bf16)],
        stats[4],
        bn,
        convs[4],
        wp,
        pos,
        vec,
        load=(2, 3, 4, 5),
        store=(0, 1, 2),
        limit=12,
    )
    outs = call(
        functools.partial(block_kernel, counts[4]),
        [
            ((4, 2, 4, 48, FF), bf16),
            ((1, T, W), f32),
            ((n, 2, W), f32),
            ((32, D), f32),
            ((T, D), f32),
            ((C4, D), f32),
        ],
        stats[4],
        bn,
        n1,
        vec,
        x0,
        a4,
        wp,
        convs[4],
        gathered,
        hbm=(2, 3, 4, 5, 6, 7, 8),
        hbm_out=(0, 1, 2, 3, 4, 5),
        limit=44,
        scratch=[
            pltpu.VMEM((1, T, W), f32),
            pltpu.VMEM((C4, D), bf16),
            pltpu.VMEM((24, D), f32),
            pltpu.VMEM((1, T, W), f32),
            pltpu.VMEM((n, 2, W), f32),
            pltpu.VMEM((32, D), f32),
            pltpu.VMEM((T, D), f32),
            pltpu.VMEM((C4, D), f32),
            pltpu.VMEM((2, 16, 48, 1536), bf16),
            pltpu.VMEM((2, 16, 48, 1536), bf16),
            pltpu.VMEM((2, 16, 48, 1536), bf16),
            pltpu.VMEM((2, 16, 48, 512), bf16),
            pltpu.SemaphoreType.DMA((35,)),
            pltpu.VMEM((T, W), bf16),
            pltpu.VMEM((T, D), f32),
            pltpu.VMEM((T, D), bf16),
            pltpu.VMEM((T, 3 * D), bf16),
            pltpu.VMEM((HEADS, T, T), f32),
            pltpu.VMEM((T, D), bf16),
            pltpu.VMEM((D, T), bf16),
            pltpu.VMEM((2, T, 1536), f32),
            pltpu.VMEM((T, D), f32),
            pltpu.VMEM((T, 3 * D), bf16),
            pltpu.VMEM((T, D), f32),
            pltpu.VMEM((2, T, 1536), bf16),
            pltpu.VMEM((32, 1536), f32),
        ],
    )
    grads, back, tot, facts, gpos, dwp = outs
    tot = share(tot)
    if fast:
        planes = [[8 * z + k for k in range(8)] for z in range(4)]
        owned = lax.psum_scatter(
            grads.reshape(8 * 4 * 48, FF),
            everyone,
            scatter_dimension=0,
            tiled=True,
            axis_index_groups=planes,
        )
        owned = [owned]
    else:
        g = jnp.transpose(grads, (2, 0, 3, 1, 4)).reshape(D, 2, 2, FF // 2)
        g = jnp.transpose(g, (0, 2, 1, 3)).reshape(dp, D // dp, 2, mp, part)
        g = jnp.transpose(g, (0, 3, 1, 2, 4)).reshape(n * (D // dp), 2 * part)
        owned = [lax.psum_scatter(g, everyone, scatter_dimension=0, tiled=True)]

    rows_d = D // dp
    rows_vec = 48 if fast else 0

    def outer(bo_all, fin_all, hs_all, bl_all):
        return dot_tn(bo_all, hs_all), dot_tn(fin_all, bl_all)

    if not fast:
        bo, fin = facts[OUT_BACK : OUT_BACK + 1], facts[OUT_FINAL : OUT_FINAL + 1]
        hs, bl = facts[OUT_HIDDEN:OUT_HEAD].reshape(1, FF), facts[OUT_HEAD:OUT_SUMS, 0:512].reshape(1, 1024)
        head_line = jnp.concatenate([bl[:, :500], bl[:, 512:1012]], 1).reshape(1, mp, cls)
        line = jnp.concatenate(
            [
                jnp.broadcast_to(bo.reshape(dp, 1, rows_d), (dp, mp, rows_d)),
                jnp.broadcast_to(fin.reshape(dp, 1, rows_d), (dp, mp, rows_d)),
                jnp.broadcast_to(hs.reshape(1, mp, part), (dp, mp, part)),
                jnp.broadcast_to(head_line, (dp, mp, cls)),
            ],
            2,
        ).reshape(n, -1)
        width = -(-line.shape[1] // 1024) * 1024
        line = jnp.pad(line, ((0, 0), (0, width - line.shape[1]))).astype(bf16)
        line = share(line.reshape(n, width // 128, 128)).reshape(n, width)
        cuts = [0, rows_d, 2 * rows_d, 2 * rows_d + part, 2 * rows_d + part + cls]
        grad_down, grad_head = outer(*[line[:, a:b] for a, b in zip(cuts[:-1], cuts[1:])])

    sums = [None] * 5
    kernel_grads = [None] * 5
    for level in (4, 3):
        r = 2 ** (4 - level)
        chan_in = CHANS[level - 1]
        g, back, so, sums[level - 1] = call(
            functools.partial(conv_back_kernel, level, counts[level], counts[level - 1]),
            [
                ((r + 1, T, W), bf16),
                ((2 * r, T, W), f32),
                ((n, 2, W), f32),
                ((2, W), f32),
            ],
            back,
            tot,
            convs[level],
            stats[level],
            kernels[level],
            convs[level - 1],
            stats[level - 1],
            bn,
            load=(0, 2, 3, 4) if level == 4 else (4,),
            limit=12,
        )
        (kernel_grads[level],) = call(
            functools.partial(kernel_grad, level),
            [((-(-CHANS[level] // 128), 9 * chan_in, 128), f32)],
            inputs[level],
            g,
            load=(0,) if level == 4 else (),
            scratch=[pltpu.VMEM((3, W + chan_in, W), f32)],
            limit=12,
        )
        if level == 4:
            so, kernel_grads[4] = lax.optimization_barrier((so, kernel_grads[4]))
            tot = share(so)
    outs = call(
        functools.partial(early_kernel, len(pieces), mp, stem_len, small_len, rows_stem, rows_small),
        [((dp, rows + rows_vec, 128), bf16)] * len(pieces),
        which,
        kernel_grads[3],
        kernel_grads[4],
        dwp,
        facts,
        gpos,
        smem=1,
        load=(3, 4, 5),
        scratch=frames + [pltpu.VMEM((48, 128), f32)],
        limit=18,
    )
    if mp == 2:
        column = outs[0] + lax.ppermute(outs[1], "mp", swap)
    else:
        column = lax.psum_scatter(jnp.stack(outs, 0), "mp", scatter_dimension=0)
    so, column = lax.optimization_barrier((so, column))
    tot = share(so)
    tot, column = lax.optimization_barrier((tot, column))
    column = lax.all_to_all(column, "dp", 0, 0)
    each = -(-LATE_ROWS // n)
    (late,) = call(
        functools.partial(conv2_back_kernel, counts[2], counts[1]),
        [((n, each, 128), f32)],
        back,
        tot,
        convs[2],
        stats[2],
        inputs[2],
        t2,
        xk,
        gram,
        w1,
        t1,
        bn,
        *sums[2:4],
        facts,
        load=(0, 4, 5, 6, 9, 13),
        scratch=[
            pltpu.VMEM((1, 9 * C1, 128), f32),
            pltpu.VMEM((5, T, W), bf16),
            pltpu.VMEM((3, W + C1, W), f32),
            pltpu.VMEM((192, W), f32),
            pltpu.VMEM((n * each, 128), f32),
        ],
        limit=20,
    )
    if fast:
        owned[0] = lax.optimization_barrier((owned[0], late))[0]
        lines = [[8 * z + k for z in range(4)] for k in range(8)]
        owned[0] = lax.psum_scatter(
            owned[0], everyone, scatter_dimension=0, tiled=True, axis_index_groups=lines
        )
    late, column = lax.optimization_barrier((late, column))
    late = share(late)
    if fast:
        line = column[:, rows:].reshape(2 * dp, 24, 128)
        grad_down, grad_head = outer(
            line[:, 16, 0:48],
            line[:, 16, 64:112],
            line[:, 0:12].reshape(2 * dp, part),
            line[:, 12:16].reshape(2 * dp, 512)[:, :cls],
        )
    grad_stem, grad_small, squares = call(
        functools.partial(unpack_kernel, stem_len, small_len),
        [((rows_stem, 128), f32), ((rows_small, 128), f32), ((1, 128), f32)],
        at,
        column,
        smem=1,
        limit=8,
    )

    g0, g1, ends = call(
        functools.partial(norm_kernel, len(owned)),
        [((rows_d, part), f32), ((rows_d, part), f32), ((n, each + 1, 128), f32)],
        *owned,
        late,
        squares,
        grad_down,
        grad_head,
        facts,
        limit=8,
    )
    grad_stem, grad_small, ends = call(
        functools.partial(last_kernel, counts[1], stem_len, small_len),
        [((rows_stem, 128), f32), ((rows_small, 128), f32), ((8, 128), f32)],
        at,
        share(ends),
        gram,
        w1,
        bn,
        grad_stem,
        grad_small,
        smem=1,
        scratch=[
            pltpu.VMEM((n * each, 128), f32),
            pltpu.VMEM((ROW_W3 + rows_stem, 128), f32),
            pltpu.VMEM((16 + rows_small, 128), f32),
        ],
        limit=8,
    )
    loss_sum, grad_norm, factor = ends[0, 0], ends[1, 0], ends[2, 0]
    grad_stem = grad_stem.reshape(-1)[:stem_len]
    grad_small = grad_small.reshape(-1)[:small_len]
    grad_block = jnp.stack([g0, g1, grad_down], 0)
    stem_new = adam_step(stem, stem_first, stem_second, grad_stem, factor, rate_stem)
    small_new = adam_step(small, small_first, small_second, grad_small, factor, rate_small)
    block_new = adam_step(block, block_first, block_second, grad_block, factor, rate_block)
    head_new = adam_step(head, head_first, head_second, grad_head, factor, rate_head)
    return (*stem_new, *small_new, *block_new, *head_new, loss_sum, grad_norm)


def solution(mesh):
    flat = P(("dp", "mp"))
    matrix = P(None, "dp", "mp")
    head = P("dp", "mp")
    states = (flat,) * 6 + (matrix,) * 3 + (head,) * 3
    return jax.shard_map(
        local,
        mesh=mesh,
        in_specs=(P("mp", "dp", None), P("mp", "dp")) + states,
        out_specs=states + (P(), P()),
        check_vma=False,
    )
```

```python
import functools

import jax
import jax.numpy as jnp
from jax import lax
from jax.experimental import pallas as pl
from jax.experimental.pallas import tpu as pltpu
from jax.sharding import PartitionSpec as P

D = 768
HEADS = 12
HEAD_DIM = 64
FF = 3072
CLASSES = 1000
C1 = 48
C2 = 96
C3 = 192
C4 = 384
STEP = 10
TOK = 197
SIDE = 14
T = 16 * SIDE
W = 384
CHANS = (3, C1, C2, C3, C4)

beta_one = 0.9
beta_two = 0.999
adam_epsilon = 1e-08
decay_rate = 0.05
clip_norm = 1.0
rate_stem = 0.05
rate_small = 0.5
rate_block = 0.05
rate_head = 0.05
batch_epsilon = 1e-05
layer_epsilon = 1e-06
smoothing = 0.1

bf16 = jnp.bfloat16
f32 = jnp.float32

STEM_SHIFT = 112
SMALL_SHIFT = 96
ROW_W2 = 11
ROW_W3 = ROW_W2 + 9 * C1 * C2 // 128
ROW_W4 = ROW_W3 + 9 * C2 * C3 // 128
ROW_WP = ROW_W4 + 9 * C3 * C4 // 128
STEM_ROWS = ROW_WP + C4 * D // 128
SMALL_NAMES = (
    ("proj_bias", 6),
    ("class_token", 6),
    ("position", 6 * TOK),
    ("norm1_gain", 6),
    ("norm1_bias", 6),
    ("query_bias", 6),
    ("value_bias", 6),
    ("out_bias", 6),
    ("norm2_gain", 6),
    ("norm2_bias", 6),
    ("hidden_bias", 24),
    ("mlp_bias", 6),
    ("final_gain", 6),
    ("final_bias", 6),
    ("head_bias", 8),
)
SMALL_AT = {}
_row = 12
for _name, _rows in SMALL_NAMES:
    SMALL_AT[_name] = _row
    _row += _rows
SMALL_ROWS = _row
VEC_NAMES = (
    "proj_bias",
    "norm1_gain",
    "norm1_bias",
    "query_bias",
    "value_bias",
    "out_bias",
    "norm2_gain",
    "norm2_bias",
    "mlp_bias",
    "final_gain",
    "final_bias",
)
VEC = {name: index for index, name in enumerate(VEC_NAMES)}
VEC_HIDDEN = 12
VEC_HEAD = 16
VEC_AIM = 18
OUT_BACK = 16
OUT_FINAL = 17
OUT_HIDDEN = 18
OUT_HEAD = 22
OUT_SUMS = 24
OUT_LOSS = 25


def dot(a, b):
    return jnp.dot(a, b, preferred_element_type=f32)


def dot_nt(a, b):
    return lax.dot_general(a, b, (((1,), (1,)), ((), ())), preferred_element_type=f32)


def dot_tn(a, b):
    return lax.dot_general(a, b, (((0,), (0,)), ((), ())), preferred_element_type=f32)


GELU_A = 0.7978845608028654
GELU_B = 0.044715


def gelu(x):
    return 0.5 * x * (1.0 + jnp.tanh(GELU_A * (x + GELU_B * x * x * x)))


def gelu_slope(x):
    t = jnp.tanh(GELU_A * (x + GELU_B * x * x * x))
    return 0.5 * (1.0 + t) + 0.5 * x * (1.0 - t * t) * GELU_A * (1.0 + 3.0 * GELU_B * x * x)


def dot_f32(a, b):
    return jnp.dot(a, b, preferred_element_type=f32, precision=lax.Precision.HIGHEST)


def up16(n):
    return -(-n // 16) * 16


def colsum(x):
    return jnp.sum(x, 0, keepdims=True)


def slot_index():
    return lax.broadcasted_iota(jnp.int32, (T, 1), 0)


def patch_mask():
    return ((slot_index() & 15) < SIDE).astype(f32)


def token_mask():
    p = slot_index()
    return (((p & 15) < SIDE) | (p == SIDE)).astype(f32)


def fold_phases(x, chan):
    step = W // 2
    while step >= chan:
        x = x + jnp.concatenate([x[:, step:], x[:, :step]], 1)
        step //= 2
    return x


def bn_stats(st_ref, count, chan):
    tot = fold_phases(jnp.sum(st_ref[:, 0:2, :], 0), chan)
    mean = tot[0:1] / count
    inv = lax.rsqrt(tot[1:2] / count - mean * mean + batch_epsilon)
    return mean, inv


def shift_lanes(x, s):
    lane = lax.broadcasted_iota(jnp.int32, x.shape, 1)
    row = lax.broadcasted_iota(jnp.int32, x.shape, 0)
    moved = pltpu.roll(x, s, 1)
    before = jnp.where(row == 0, 0.0, pltpu.roll(moved, 1, 0))
    return jnp.where(lane >= s, moved, before)


def pack_kernel(at_ref, stem_ref, small_ref, out_ref):
    rows = stem_ref.shape[0]
    out_ref[0:rows, :] = shift_lanes(stem_ref[...], at_ref[0]).astype(bf16)
    out_ref[rows:, :] = shift_lanes(small_ref[...], at_ref[1]).astype(bf16)


def flat_lanes(ref, row, count):
    return jnp.concatenate([ref[row + k : row + k + 1, :] for k in range(count)], 1)


def assemble_kernel(by_plane, parts, mp, stem_len, small_len, rows_stem, rows_small, at_ref, *refs):
    pieces = refs[:parts]
    s1, t1_ref, t2_ref, t3_ref, t4_ref, wp_ref, bn_ref, vec_ref, pos_ref = refs[parts : parts + 9]
    frame, table, s2, s3a, s3b, u1, u2, u3 = refs[parts + 9 :]
    frame[...] = jnp.zeros_like(frame)
    table[...] = jnp.zeros_like(table)
    for index, ref in enumerate(pieces):
        mv = at_ref[index]

        def put(d, carry):
            owner = ((at_ref[parts + 1] ^ (d & 3)) * 4 + (d >> 2) if by_plane else d) * mp + mv
            a = (owner * stem_len + STEM_SHIFT) // 128
            frame[pl.ds(a, rows_stem), :] += ref[d, 0:rows_stem, :].astype(f32)
            b = (owner * small_len + SMALL_SHIFT) // 128
            table[pl.ds(b, rows_small), :] += ref[d, rows_stem : rows_stem + rows_small, :].astype(f32)
            return carry

        lax.fori_loop(0, ref.shape[0], put, 0)
    s1[...] = jnp.zeros_like(s1)
    flat = flat_lanes(frame, 0, ROW_W2)
    for k in range(27):
        s1[k : k + 1, 0:C1] = flat[:, STEM_SHIFT + 48 * k : STEM_SHIFT + 48 * k + 48]
    u1[...] = jnp.zeros_like(u1)
    for tap in range(3):
        for j in range(8):
            cols = slice(j * C1, (j + 1) * C1)
            if j == 0:
                u1[tap * 64 + 48 : tap * 64 + 51, cols] = s1[tap * 9 : tap * 9 + 3, 0:C1]
                u1[tap * 64 : tap * 64 + 6, cols] = s1[tap * 9 + 3 : tap * 9 + 9, 0:C1]
            else:
                at = tap * 64 + 6 * j - 3
                u1[at : at + 9, cols] = s1[tap * 9 : tap * 9 + 9, 0:C1]
    t1_ref[...] = u1[...].astype(bf16)
    q = 9 * C1 // 4
    wide = jnp.concatenate([frame[pl.ds(ROW_W2 + k, q, stride=3), :] for k in range(3)], 1)
    for k in range(4):
        s2[pl.ds(k, q, stride=4), 0:C2] = wide[:, k * C2 : (k + 1) * C2]
    q = 9 * C2 // 2
    wide = jnp.concatenate([frame[pl.ds(ROW_W3 + k, q, stride=3), :] for k in range(3)], 1)
    for k in range(2):
        part = wide[:, k * C3 : (k + 1) * C3]
        s3a[pl.ds(k, q, stride=2), :] = part[:, 0:128]
        s3b[pl.ds(k, q, stride=2), 0 : C3 - 128] = part[:, 128:C3]
    for ref, chan_in, chan_out, src, u in (
        (t2_ref, C1, C2, (s2,), u2),
        (t3_ref, C2, C3, (s3a, s3b), u3),
    ):
        for tap in range(3):
            u[...] = jnp.zeros_like(u)
            base = tap * 3 * chan_in
            for j in range(W // chan_out):
                for k, s in enumerate(src):
                    width = min(128, chan_out - 128 * k)
                    cols = slice(j * chan_out + 128 * k, j * chan_out + 128 * k + width)
                    if j == 0:
                        u[W : W + chan_in, cols] = s[base : base + chan_in, 0:width]
                        u[0 : 2 * chan_in, cols] = s[base + chan_in : base + 3 * chan_in, 0:width]
                    else:
                        at = (2 * j - 1) * chan_in
                        u[at : at + 3 * chan_in, cols] = s[base : base + 3 * chan_in, 0:width]
            ref[tap] = u[...].astype(bf16)
    for tap in range(3):
        rows = 3 * C3
        for k in range(3):
            lanes = slice(k * 128, (k + 1) * 128)
            at = ROW_W4 + k + 3 * tap * rows
            t4_ref[tap, 0 : 2 * C3, lanes] = frame[pl.ds(at + 3 * C3, 2 * C3, stride=3), :].astype(bf16)
            t4_ref[tap, 2 * C3 : 3 * C3, lanes] = frame[pl.ds(at, C3, stride=3), :].astype(bf16)
    for k in range(6):
        lanes = slice(k * 128, (k + 1) * 128)
        wp_ref[:, lanes] = frame[pl.ds(ROW_WP + k, C4, stride=6), :].astype(bf16)
    flat = flat_lanes(table, 0, 12)
    first = SMALL_SHIFT
    for level in range(4):
        chan = CHANS[level + 1]
        for which in range(2):
            at = first + which * (C1 + C2 + C3 + C4)
            part = flat[:, at : at + chan]
            row = 2 * level + which
            for j in range(W // chan):
                bn_ref[row : row + 1, j * chan : (j + 1) * chan] = part
        first += chan
    vec_ref[...] = jnp.zeros_like(vec_ref)
    for name, index in VEC.items():
        vec_ref[index : index + 1, :] = flat_lanes(table, SMALL_AT[name], 6)
    for k in range(4):
        row = VEC_HIDDEN + k
        vec_ref[row : row + 1, :] = flat_lanes(table, SMALL_AT["hidden_bias"] + 6 * k, 6)
    flat = flat_lanes(table, SMALL_AT["head_bias"], 8)
    lane = lax.broadcasted_iota(jnp.int32, (1, 512), 1)
    for m in range(2):
        vec_ref[VEC_HEAD + m : VEC_HEAD + m + 1, 0:500] = flat[:, 500 * m : 500 * m + 500]
        aim = jnp.where(lane + 500 * m == at_ref[parts], 1.0 - smoothing, 0.0) + smoothing / CLASSES
        vec_ref[VEC_AIM + m : VEC_AIM + m + 1, 0:512] = jnp.where(lane < 500, aim, 0.0)
    pos_ref[...] = jnp.zeros_like(pos_ref)
    at = SMALL_AT["position"]
    for k in range(6):
        lanes = slice(k * 128, (k + 1) * 128)
        for r in range(SIDE):
            rows = table[pl.ds(at + k + 6 * (1 + SIDE * r), SIDE, stride=6), :]
            pos_ref[16 * r : 16 * r + SIDE, lanes] = rows
        mark = SMALL_AT["class_token"] + k
        pos_ref[SIDE : SIDE + 1, lanes] = table[mark : mark + 1, :] + table[at + k : at + k + 1, :]


def image_kernel(own_ref, next_ref, xk_ref, gram_ref, flat, chunks, xe):
    half = own_ref.shape[0]
    flat[0:half, :] = own_ref[...].astype(f32)
    flat[half : 2 * half, :] = next_ref[...].astype(f32)
    n = 2 * half // 3
    wide = jnp.concatenate([flat[pl.ds(k, n, stride=3), :] for k in range(3)], 1)
    for j in range(8):
        chunks[pl.ds(j, n, stride=8), 0:48] = wide[:, 48 * j : 48 * j + 48]
    mask = patch_mask()
    lane = lax.broadcasted_iota(jnp.int32, (T, 64), 1)

    def spread(i, carry):
        rows = [chunks[pl.ds(16 * SIDE * r + SIDE * i, 16), 0:64] for r in range(SIDE)]
        x = jnp.where(lane < 48, jnp.concatenate(rows, 0), 0.0) * mask
        left = pltpu.roll(jnp.concatenate([x, x], 1), 3, 1)[:, 0:64]
        left = jnp.where((lane >= 48) & (lane < 51), pltpu.roll(left, 1, 0), 0.0)
        xe[i + 1] = ((x + left) * mask).astype(bf16)
        return carry

    chunks[pl.ds(n * 8, 16), :] = jnp.zeros((16, 128), f32)
    lax.fori_loop(0, 16, spread, 0)
    last = xe[16]
    xe[0] = jnp.concatenate([jnp.zeros((16, 64), bf16), last[: T - 16]], 0)

    def step(i, carry):
        gram, ones = carry
        x = jnp.concatenate([xe[2 * i], xe[2 * i + 1], xe[2 * i + 2]], 1)
        xk_ref[i] = x
        return gram + dot_tn(x, x), ones + colsum(x.astype(f32))

    gram, ones = lax.fori_loop(0, 8, step, (jnp.zeros((192, 192), f32), jnp.zeros((1, 192), f32)))
    row = lax.broadcasted_iota(jnp.int32, (192, 256), 0)
    col = lax.broadcasted_iota(jnp.int32, (192, 256), 1)
    j, k = col >> 5, col & 31
    tap = (k >= 9).astype(jnp.int32) + (k >= 18).astype(jnp.int32)
    u = k - 9 * tap
    at = 64 * tap + jnp.where(j == 0, jnp.where(u < 3, 48 + u, u - 3), 6 * j - 3 + u)
    pick = ((row == at) & (k < 27)).astype(f32)
    both = lax.dot_general(
        pick,
        dot_f32(gram, pick),
        (((0,), (0,)), ((), ())),
        preferred_element_type=f32,
        precision=lax.Precision.HIGHEST,
    )
    ones = dot_f32(jnp.broadcast_to(ones, (8, 192)), pick)[0:1]
    total = jnp.zeros((32, 32), f32)
    line = jnp.zeros((1, 32), f32)
    for q in range(8):
        lanes = slice(32 * q, 32 * q + 32)
        total = total + both[lanes, lanes]
        line = line + ones[:, lanes]
    r32 = lax.broadcasted_iota(jnp.int32, (32, 32), 0)
    c32 = lax.broadcasted_iota(jnp.int32, (32, 32), 1)
    total = total + jnp.where(r32 == 27, line, 0.0)
    column = jnp.sum(jnp.where(r32 == c32, line, 0.0), 1, keepdims=True)
    total = total + jnp.where(c32 == 27, column, 0.0)
    flat8 = jnp.concatenate([total[8 * q : 8 * q + 8] for q in range(4)], 1)
    gram_ref[...] = jnp.broadcast_to(flat8[None], gram_ref.shape)


def level1_stats(gram_ref, w1_ref, count):
    flat8 = jnp.sum(gram_ref[...], 0)
    gram = jnp.concatenate([flat8[:, 32 * q : 32 * q + 32] for q in range(4)], 0)
    cross = dot_f32(gram, w1_ref[...])
    mean = cross[27:28] / count
    squares = colsum(w1_ref[...] * cross) / count
    inv = lax.rsqrt(squares - mean * mean + batch_epsilon)
    return gram, cross, mean, inv


def tile_lanes(x, chan):
    return jnp.concatenate([x[:, 0:chan]] * (W // chan), 1)


def conv12_kernel(count, xk_ref, gram_ref, w1_ref, t1_ref, bn_ref, t_ref, ax_ref, out_ref, st_ref):
    gram, cross, mean, inv = level1_stats(gram_ref, w1_ref, count)
    mean, inv = tile_lanes(mean, C1), tile_lanes(inv, C1)
    gain, bias = bn_ref[0:1, :], bn_ref[1:2, :]
    mask = patch_mask()
    weights = t1_ref[...]

    def activate(i, carry):
        a = gelu((dot(xk_ref[i], weights) - mean) * inv * gain + bias) * mask
        put_input(ax_ref, i, a, C1)
        return carry

    lax.fori_loop(0, 8, activate, 0)
    convolve(8, ax_ref, t_ref, out_ref, st_ref, mask, C1)


def put_input(ax_ref, i, a, chan):
    left = pltpu.roll(a[:, W - chan :], 1, 0)
    ax_ref[i + 1, :, 0:W] = a.astype(bf16)
    ax_ref[i + 1, :, W:] = left.astype(bf16)


def convolve(rows, ax_ref, t_ref, out_ref, st_ref, mask, chan):
    last = ax_ref[rows]
    ax_ref[0] = jnp.concatenate([jnp.zeros((16, W + chan), bf16), last[: T - 16]], 0)

    def step(i, carry):
        first, second = carry
        y = dot(ax_ref[2 * i], t_ref[0])
        y = y + dot(ax_ref[2 * i + 1], t_ref[1])
        y = y + dot(ax_ref[2 * i + 2], t_ref[2])
        out_ref[i] = y
        ym = y * mask
        return first + colsum(ym), second + colsum(ym * y)

    zero = jnp.zeros((1, W), f32)
    first, second = lax.fori_loop(0, rows // 2, step, (zero, zero))
    st = jnp.concatenate([first, second], 0)
    st_ref[...] = jnp.broadcast_to(st[None], st_ref.shape)


def conv_kernel(level, count, c_ref, stin_ref, bn_ref, t_ref, ax_ref, out_ref, st_ref):
    chan = CHANS[level]
    rows = c_ref.shape[0]
    mean, inv = bn_stats(stin_ref, count, chan)
    gain = bn_ref[2 * level - 2 : 2 * level - 1, :]
    bias = bn_ref[2 * level - 1 : 2 * level, :]
    mask = patch_mask()

    def activate(i, carry):
        put_input(ax_ref, i, gelu((c_ref[i] - mean) * inv * gain + bias) * mask, chan)
        return carry

    lax.fori_loop(0, rows, activate, 0)
    convolve(rows, ax_ref, t_ref, out_ref, st_ref, mask, chan)


def layer_norm(x):
    centered = x - jnp.mean(x, -1, keepdims=True)
    inv = lax.rsqrt(jnp.mean(centered * centered, -1, keepdims=True) + layer_epsilon)
    return centered * inv, inv


def layer_norm_back(dy, s, inv, gain):
    scaled = dy * gain
    inner = scaled - jnp.mean(scaled, -1, keepdims=True)
    return inv * (inner - s * jnp.mean(scaled * s, -1, keepdims=True))


def normed4(count, st_ref, bn_ref, c_ref):
    mean, inv = bn_stats(st_ref, count, C4)
    s = (c_ref[0] - mean) * inv
    return s, s * bn_ref[6:7, :] + bn_ref[7:8, :]


def embed_kernel(count, st_ref, bn_ref, c_ref, wp_ref, pos_ref, vec_ref, a4_ref, x0_ref, n1_ref):
    def vec(name):
        return vec_ref[VEC[name] : VEC[name] + 1, :]

    mask = patch_mask()
    _, y4 = normed4(count, st_ref, bn_ref, c_ref)
    a4_ref[...] = (gelu(y4) * mask).astype(bf16)
    x0 = (dot(a4_ref[...], wp_ref[...]) + vec("proj_bias")) * mask + pos_ref[...]
    x0_ref[...] = x0
    s1, _ = layer_norm(x0)
    n1_ref[...] = (s1 * vec("norm1_gain") + vec("norm1_bias")).astype(bf16)


def block_kernel(
    count,
    st_ref,
    bn_ref,
    n1_hbm,
    vec_hbm,
    x0_hbm,
    a4_hbm,
    wp_hbm,
    c_hbm,
    g_ref,
    gr_ref,
    bn4_hbm,
    so_hbm,
    out_hbm,
    gpos_hbm,
    dwp_hbm,
    c_ref,
    wp_ref,
    vec_ref,
    bn4_ref,
    so_ref,
    out_ref,
    gpos_ref,
    dwp_ref,
    wa,
    wu,
    wd,
    wh,
    sems,
    a4,
    x0,
    n1,
    qkv,
    probs,
    mixed,
    n2t,
    pre,
    acc,
    bqkv,
    mixed_f,
    bpre,
    rowbuf,
):
    gr0, gr1 = wu, wd
    fetched = []
    for k, (source, ref) in enumerate(
        ((n1_hbm, n1), (vec_hbm, vec_ref), (x0_hbm, x0), (a4_hbm, a4), (wp_hbm, wp_ref), (c_hbm, c_ref))
    ):
        fetched.append(pltpu.make_async_copy(source, ref, sems.at[24 + k]))
        if k < 2:
            fetched[-1].start()
    copies = []
    for m in range(2):
        for h in range(2):
            lanes = slice(D * h, D * h + D)
            copy = pltpu.make_async_copy(
                g_ref.at[:, m, :, lanes], wa.at[m, :, :, lanes], sems.at[35 + 2 * m + h]
            )
            copy.start()
            copies.append(copy)
    for k, (ref, at, size) in enumerate(
        ((wu, 1536, 1536), (wd, 3072, 1536), (wh, 4608, 512))
    ):
        for m in range(2):
            copy = pltpu.make_async_copy(
                g_ref.at[:, m, :, at : at + size], ref.at[m], sems.at[2 * k + m]
            )
            copy.start()
            copies.append(copy)
        if k == 0:
            for copy in fetched[2:]:
                copy.start()

    def send_out(grad, slot):
        out = []
        lanes = slice(1536 * slot, 1536 * slot + 1536)
        for m in range(2):
            for z in range(4):
                copy = pltpu.make_async_copy(
                    grad.at[m, 4 * z : 4 * z + 4],
                    gr_ref.at[:, m, z, :, lanes],
                    sems.at[8 + 8 * slot + 4 * m + z],
                )
                copy.start()
                out.append(copy)
        return out

    def write(ref, target, k):
        copy = pltpu.make_async_copy(ref, target, sems.at[30 + k])
        copy.start()
        moving.append(copy)

    def vec(name):
        return vec_ref[VEC[name] : VEC[name] + 1, :]

    mask = patch_mask()
    valid = token_mask()
    out_row = lax.broadcasted_iota(jnp.int32, (32, 1), 0)
    out_ref[...] = jnp.zeros_like(out_ref)
    key = lax.broadcasted_iota(jnp.int32, (1, T), 1)
    key_bias = jnp.where(((key & 15) < SIDE) | (key == SIDE), 0.0, -1e30)

    for copy in fetched[:2]:
        copy.wait()

    def tile(ref, m, at, size=256):
        return ref[m, :, :, pl.ds(at, size)].reshape(D, size)

    for part in range(9):
        if part % 3 == 0:
            copies[part // 3].wait()
        y = dot(n1[...], tile(wa, part // 6, 256 * (part % 6)))
        lanes = slice(256 * (part % 3), 256 * (part % 3) + 256)
        if part < 3:
            y = y + vec("query_bias")[:, lanes]
        elif part >= 6:
            y = y + vec("value_bias")[:, lanes]
        qkv[:, 256 * part : 256 * part + 256] = y.astype(bf16)
    scale = HEAD_DIM**-0.5

    def attend(pair, carry):
        at = pl.multiple_of(pair * 128, 128)
        q = qkv[:, pl.ds(at, 128)] * bf16(scale)
        k = qkv[:, pl.ds(at + D, 128)]
        v = qkv[:, pl.ds(at + 2 * D, 128)]
        out = []
        for h in range(2):
            lanes = slice(64 * h, 64 * h + 64)
            scores = dot_nt(q[:, lanes], k[:, lanes]) + key_bias
            e = jnp.exp(scores - jnp.max(scores, -1, keepdims=True))
            p = e * (1.0 / jnp.sum(e, -1, keepdims=True))
            probs[2 * pair + h] = p
            out.append(dot(p.astype(bf16), v[:, lanes]))
        out = jnp.concatenate(out, 1)
        mixed[:, pl.ds(at, 128)] = out.astype(bf16)
        mixed_f[:, pl.ds(at, 128)] = out
        return carry

    lax.fori_loop(0, HEADS // 2, attend, 0, unroll=6)
    for copy in fetched[2:]:
        copy.wait()
    copies[3].wait()
    att = [dot_nt(mixed[...], wa[1, :, :, D : 2 * D].reshape(D, D))]
    x1 = x0[...] + att[0] + vec("out_bias")
    mean_x1 = colsum(x1 * valid) / TOK
    s2, i2 = layer_norm(x1)
    n2 = (s2 * vec("norm2_gain") + vec("norm2_bias")).astype(bf16)
    n2t[...] = n2.T
    copies[4].wait()
    copies[5].wait()
    bias = [jnp.concatenate([vec_ref[r : r + 1, :], vec_ref[r + 1 : r + 2, :]], 1) for r in (12, 14)]
    rowbuf[0:1, :] = bias[0]
    rowbuf[8:9, :] = bias[1]

    def place(k):
        m = (k >= 6).astype(jnp.int32)
        return m, pl.multiple_of(8 * m, 8), pl.multiple_of((k - 6 * m) * 256, 256)

    def up(k, carry):
        m, row, at = place(k)
        y = dot(n2, tile(wu, m, at)) + rowbuf[pl.ds(row, 8), pl.ds(at, 256)][0:1]
        t = jnp.tanh(GELU_A * (y + GELU_B * y * y * y))
        half = 0.5 + 0.5 * t
        h = (y * half).astype(bf16).astype(f32) * valid
        rowbuf[pl.ds(16 + row, 8), pl.ds(at, 256)] = jnp.broadcast_to(colsum(h), (8, 256))
        inner = GELU_A + (3.0 * GELU_A * GELU_B) * y * y
        pre[m, :, pl.ds(at, 256)] = (half + 0.5 * y * (1.0 - t * t) * inner) * valid
        return carry

    lax.fori_loop(0, 12, up, 0, unroll=4)
    for m in range(2):
        for k in range(2):
            row = OUT_HIDDEN + 2 * m + k
            out_ref[row : row + 1, :] = rowbuf[16 + 8 * m : 17 + 8 * m, D * k : D * k + D]
    copies[6].wait()
    copies[7].wait()
    hs = jnp.concatenate([out_ref[OUT_HIDDEN + k : OUT_HIDDEN + k + 1, :] for k in range(4)], 1) / TOK
    high = hs.astype(bf16)
    low = (hs - high.astype(f32)).astype(bf16)
    out = jnp.zeros((1, D), f32)
    for m in range(2):
        lanes = slice(1536 * m, 1536 * m + 1536)
        both = jnp.concatenate(
            [jnp.broadcast_to(high[:, lanes], (8, 1536)), jnp.broadcast_to(low[:, lanes], (8, 1536))], 0
        )
        y = dot_nt(both, wd[m].reshape(D, 1536))
        out = out + y[0:1] + y[8:9]
    pooled = mean_x1 + out + vec("mlp_bias")
    s3, i3 = layer_norm(pooled)
    final = (s3 * vec("final_gain") + vec("final_bias")).astype(bf16)
    copies[8].wait()
    copies[9].wait()
    wide = jnp.broadcast_to(final, (16, D))
    logits = jnp.concatenate([dot(wide, wh[m].reshape(D, 512))[0:1] for m in range(2)], 1)
    lane = lax.broadcasted_iota(jnp.int32, (1, 1024), 1)
    real = (lane & 511) < CLASSES // 2
    def pair(row):
        return jnp.concatenate([vec_ref[row : row + 1, 0:512], vec_ref[row + 1 : row + 2, 0:512]], 1)

    logits = jnp.where(real, logits + pair(VEC_HEAD), -1e30)
    top = jnp.max(logits, -1, keepdims=True)
    log_probs = logits - top - jnp.log(jnp.sum(jnp.exp(logits - top), -1, keepdims=True))
    aim = pair(VEC_AIM)
    loss = -jnp.sum(jnp.where(real, aim * log_probs, 0.0), keepdims=True)
    out_ref[...] = jnp.where(out_row >= OUT_LOSS, jnp.broadcast_to(loss, out_ref.shape), out_ref[...])
    back_logits = jnp.where(real, jnp.exp(log_probs) - aim, 0.0).astype(bf16)
    for m in range(2):
        row = OUT_HEAD + m
        out_ref[row : row + 1, 0:512] = back_logits[:, 512 * m : 512 * m + 512].astype(f32)
    out_ref[OUT_FINAL : OUT_FINAL + 1, :] = final.astype(f32)
    wide = jnp.broadcast_to(back_logits, (16, 1024))
    back_final = (
        dot_nt(wide[:, 0:512], wh[0].reshape(D, 512)) + dot_nt(wide[:, 512:], wh[1].reshape(D, 512))
    )[0:1]
    def put(name, value):
        out_ref[VEC[name] : VEC[name] + 1, :] = value

    put("final_gain", back_final * s3)
    put("final_bias", back_final)
    back2 = layer_norm_back(back_final, s3, i3, vec("final_gain")) / TOK
    back_out = back2.astype(bf16)
    out_ref[OUT_BACK : OUT_BACK + 1, :] = back_out.astype(f32)
    put("mlp_bias", back_out.astype(f32) * TOK)
    wide = jnp.broadcast_to(back_out, (16, D))
    for m in range(2):
        for k in range(6):
            at = 256 * k
            rowbuf[8 * m : 8 * m + 1, at : at + 256] = dot(wide, tile(wd, m, at))[0:1]

    def down(k, carry):
        m, row, at = place(k)
        back = rowbuf[pl.ds(row, 8), pl.ds(at, 256)][0:1]
        bp = (back * pre[m, :, pl.ds(at, 256)]).astype(bf16)
        rowbuf[pl.ds(16 + row, 8), pl.ds(at, 256)] = jnp.broadcast_to(
            colsum(bp.astype(f32)), (8, 256)
        )
        bpre[m, :, pl.ds(at, 256)] = bp
        grad = dot(n2t[...], bp)
        gr1[m, :, :, pl.ds(at, 256)] = grad.astype(bf16).reshape(16, 48, 256)
        return carry

    lax.fori_loop(0, 12, down, 0, unroll=4)
    for m in range(2):
        for k in range(2):
            row = VEC_HIDDEN + 2 * m + k
            out_ref[row : row + 1, :] = rowbuf[16 + 8 * m : 17 + 8 * m, D * k : D * k + D]
    moving = send_out(gr1, 1)
    back_n2 = dot_nt(bpre[0], wu[0].reshape(D, 1536)) + dot_nt(bpre[1], wu[1].reshape(D, 1536))
    put("norm2_gain", colsum(back_n2 * s2))
    put("norm2_bias", colsum(back_n2))
    back1 = back2 * valid + layer_norm_back(back_n2, s2, i2, vec("norm2_gain"))
    back_att = back1.astype(bf16)
    put("out_bias", colsum(back_att.astype(f32)))
    back_att_t = back_att.T
    for k in range(3):
        lanes = slice(256 * k, 256 * k + 256)
        grad = dot(back_att_t, mixed[:, lanes])
        gr0[1, :, :, D + 256 * k : D + 256 * k + 256] = grad.astype(bf16).reshape(16, 48, 256)
    acc[...] = dot(back_att, wa[1, :, :, D : 2 * D].reshape(D, D))

    def attend_back(pair, carry):
        at = pl.multiple_of(pair * 128, 128)
        q = qkv[:, pl.ds(at, 128)]
        k = qkv[:, pl.ds(at + D, 128)]
        v = qkv[:, pl.ds(at + 2 * D, 128)]
        bm = acc[:, pl.ds(at, 128)].astype(bf16)
        bm_mixed = bm.astype(f32) * mixed_f[:, pl.ds(at, 128)]
        bq, bk, bv = [], [], []
        for h in range(2):
            lanes = slice(64 * h, 64 * h + 64)
            p = probs[2 * pair + h]
            bp = dot_nt(bm[:, lanes], v[:, lanes])
            bv.append(dot_tn(p.astype(bf16), bm[:, lanes]))
            inner = jnp.sum(bm_mixed[:, lanes], -1, keepdims=True)
            bs = (p * (bp - inner)).astype(bf16)
            bq.append(dot(bs, k[:, lanes]) * scale)
            bk.append(dot_tn(bs, q[:, lanes]) * scale)
        bqkv[:, pl.ds(at, 128)] = jnp.concatenate(bq, 1).astype(bf16)
        bqkv[:, pl.ds(at + D, 128)] = jnp.concatenate(bk, 1).astype(bf16)
        bqkv[:, pl.ds(at + 2 * D, 128)] = jnp.concatenate(bv, 1).astype(bf16)
        return carry

    lax.fori_loop(0, HEADS // 2, attend_back, 0, unroll=6)
    put("query_bias", colsum(bqkv[:, 0:D].astype(f32)))
    put("value_bias", colsum(bqkv[:, 2 * D :].astype(f32)))
    n1t = n1[...].T
    for part in range(9):
        m, at = part // 6, 256 * (part % 6)
        b = bqkv[:, 256 * part : 256 * part + 256]
        gr0[m, :, :, at : at + 256] = dot(n1t, b).astype(bf16).reshape(16, 48, 256)
    moving += send_out(gr0, 0)
    back_n1 = dot_nt(bqkv[:, 0:1536], wa[0].reshape(D, 1536))
    back_n1 = back_n1 + dot_nt(bqkv[:, 1536:], wa[1, :, :, 0:D].reshape(D, D))
    s1, i1 = layer_norm(x0[...])
    put("norm1_gain", colsum(back_n1 * s1))
    put("norm1_bias", colsum(back_n1))
    back0 = back1 + layer_norm_back(back_n1, s1, i1, vec("norm1_gain"))
    gpos_ref[...] = back0
    write(gpos_ref, gpos_hbm, 0)
    back_patch = (back0 * mask).astype(bf16)
    put("proj_bias", colsum(back_patch.astype(f32)))
    dwp_ref[...] = dot_tn(a4[...], back_patch)
    write(dwp_ref, dwp_hbm, 1)
    s4, y4 = normed4(count, st_ref, bn_ref, c_ref)
    bn4 = dot_nt(back_patch, wp_ref[...]) * gelu_slope(y4) * mask
    bn4_ref[0] = bn4
    write(bn4_ref, bn4_hbm, 2)
    st = jnp.concatenate([colsum(bn4), colsum(bn4 * s4)], 0)
    so_ref[...] = jnp.broadcast_to(st[None], so_ref.shape)
    write(so_ref, so_hbm, 3)
    out_ref[OUT_SUMS : OUT_SUMS + 1, :] = jnp.concatenate([st[0:1], st[1:2]], 1)
    write(out_ref, out_hbm, 4)
    for copy in moving:
        copy.wait()


def conv_back_kernel(
    level,
    count,
    count_in,
    back_ref,
    tot_ref,
    c_ref,
    st_ref,
    t_ref,
    cin_ref,
    stin_ref,
    bn_ref,
    g,
    backin_ref,
    so_ref,
    ss_ref,
):
    finish_level(level, count, back_ref, tot_ref, c_ref, st_ref, bn_ref, g)
    mean, inv = bn_stats(stin_ref, count_in, CHANS[level - 1])

    def normed(q):
        return (cin_ref[q] - mean) * inv

    def keep(q, y):
        backin_ref[q] = y

    st = back_through(level, g, t_ref, bn_ref, normed, keep)
    ss_ref[...] = st
    so_ref[...] = jnp.broadcast_to(st[None], so_ref.shape)


def finish_level(level, count, back_ref, tot_ref, c_ref, st_ref, bn_ref, g):
    chan = CHANS[level]
    rows = back_ref.shape[0]
    mask = patch_mask()
    mean, inv = bn_stats(st_ref, count, chan)
    gain = bn_ref[2 * level - 2 : 2 * level - 1, :]
    tot = fold_phases(jnp.sum(tot_ref[:, 0:2, :], 0), chan) / count

    def finish(i, carry):
        s = (c_ref[i] - mean) * inv
        g[i] = (inv * gain * (back_ref[i] - tot[0:1] - s * tot[1:2]) * mask).astype(bf16)
        return carry

    lax.fori_loop(0, rows, finish, 0)
    head = g[0]
    g[rows] = jnp.concatenate([head[16:], jnp.zeros((16, W), bf16)], 0)


def kernel_grad(level, ax_ref, g, dw_ref, dt):
    chan, chan_in = CHANS[level], CHANS[level - 1]
    rows = g.shape[0] - 1
    dt[...] = jnp.zeros_like(dt)

    def weights(i, carry):
        for tap in range(3):
            dt[tap] += dot_tn(ax_ref[2 * i + tap], g[i])
        return carry

    lax.fori_loop(0, rows, weights, 0)
    for tap in range(3):
        base = tap * 3 * chan_in
        for j in range(W // chan):
            for k in range(dw_ref.shape[0]):
                width = min(128, chan - 128 * k)
                cols = slice(j * chan + 128 * k, j * chan + 128 * k + width)
                if j == 0:
                    dw_ref[k, base : base + chan_in, 0:width] = dt[tap, W : W + chan_in, cols]
                    dw_ref[k, base + chan_in : base + 3 * chan_in, 0:width] = dt[
                        tap, 0 : 2 * chan_in, cols
                    ]
                else:
                    at = (2 * j - 1) * chan_in
                    dw_ref[k, base : base + 3 * chan_in, 0:width] += dt[
                        tap, at : at + 3 * chan_in, cols
                    ]


def back_through(level, g, t_ref, bn_ref, normed, keep):
    chan_in = CHANS[level - 1]
    rows = g.shape[0] - 1
    mask = patch_mask()
    gain = bn_ref[2 * level - 4 : 2 * level - 3, :]
    bias = bn_ref[2 * level - 3 : 2 * level - 2, :]

    def through(q, p, carry):
        first, second = carry
        left = pltpu.roll(p[:, W:], T - 1, 0)
        p = jnp.concatenate([p[:, 0 : W - chan_in], p[:, W - chan_in : W] + left], 1)
        s = normed(q)
        y = p * gelu_slope(s * gain + bias) * mask
        keep(q, y)
        return first + colsum(y), second + colsum(y * s)

    def back(i, carry):
        carry = through(2 * i, dot_nt(g[i], t_ref[1]), carry)
        p = dot_nt(g[i], t_ref[2]) + dot_nt(g[i + 1], t_ref[0])
        return through(2 * i + 1, p, carry)

    zero = jnp.zeros((1, W), f32)
    first, second = lax.fori_loop(0, rows, back, (zero, zero))
    return jnp.concatenate([first, second], 0)


LATE_W2 = 9 * C1 * C2 // 128
LATE_SUMS = 32
LATE_F = LATE_SUMS + 4 * 6


def late_sizes(n):
    kernel, exact = -(-LATE_W2 // n), -(-LATE_F // n)
    return kernel, exact, up16(kernel + 2 * exact)


def late_rows(w, f, rows):
    high = f.astype(bf16).astype(f32)
    fill = jnp.zeros((rows - w.shape[0] - 2 * f.shape[0], 128), f32)
    return jnp.concatenate([w, high, f - high, fill], 0).astype(bf16)


def conv2_back_kernel(
    count,
    count_in,
    back_ref,
    tot_ref,
    c_ref,
    st_ref,
    ax_ref,
    t_ref,
    xk_ref,
    gram_ref,
    w1_ref,
    t1_ref,
    bn_ref,
    ss2_ref,
    ss3_ref,
    ss4_ref,
    late_ref,
    dw,
    g,
    dt,
    dt1,
    late,
    exact,
):
    finish_level(2, count, back_ref, tot_ref, c_ref, st_ref, bn_ref, g)
    kernel_grad(2, ax_ref, g, dw, dt)
    gram, cross, mean, inv = level1_stats(gram_ref, w1_ref, count_in)
    mean, inv = tile_lanes(mean, C1), tile_lanes(inv, C1)
    weights = t1_ref[...]
    dt1[...] = jnp.zeros_like(dt1)

    def normed(q):
        return (dot(xk_ref[q], weights) - mean) * inv

    def keep(q, y):
        dt1[...] += dot_tn(xk_ref[q], y.astype(bf16))

    st = back_through(2, g, t_ref, bn_ref, normed, keep)
    late[...] = jnp.zeros_like(late)
    exact[...] = jnp.zeros_like(exact)
    q = 9 * C1 // 4
    wide = jnp.concatenate([dw[0, pl.ds(k, q, stride=4), :][:, 0:C2] for k in range(4)], 1)
    for k in range(3):
        late[pl.ds(k, q, stride=3), :] = wide[:, 128 * k : 128 * k + 128]
    for tap in range(3):
        base = 9 * tap
        for j in range(8):
            cols = slice(j * C1, (j + 1) * C1)
            if j == 0:
                exact[base : base + 3, 0:C1] = dt1[tap * 64 + 48 : tap * 64 + 51, cols]
                exact[base + 3 : base + 9, 0:C1] = dt1[tap * 64 : tap * 64 + 6, cols]
            else:
                at = tap * 64 + 6 * j - 3
                exact[base : base + 9, 0:C1] += dt1[at : at + 9, cols]
    ss4 = jnp.concatenate(
        [ss4_ref[OUT_SUMS : OUT_SUMS + 1, 0:W], ss4_ref[OUT_SUMS : OUT_SUMS + 1, W:]], 0
    )
    for level, ss in enumerate((st, ss2_ref[...], ss3_ref[...], ss4)):
        for which in range(2):
            for k in range(3):
                row = LATE_SUMS + 6 * level + 3 * which + k
                exact[row : row + 1, :] = ss[which : which + 1, 128 * k : 128 * k + 128]
    kernel, share, rows = late_sizes(late_ref.shape[0])

    def emit(d, carry):
        w = late[pl.ds(kernel * d, kernel), :]
        late_ref[d] = late_rows(w, exact[pl.ds(share * d, share), :], rows)
        return carry

    lax.fori_loop(0, late_ref.shape[0], emit, 0)


def early_kernel(
    parts,
    mp,
    stem_len,
    small_len,
    rows_stem,
    rows_small,
    at_ref,
    dw3_ref,
    dw4_ref,
    dwp_ref,
    gv_ref,
    gpos_ref,
    *refs,
):
    outs = refs[:parts]
    frame, table, vecs = refs[parts:]
    if outs[0].shape[1] > rows_stem + rows_small:
        vecs[...] = jnp.zeros_like(vecs)
        base = pl.multiple_of(24 * at_ref[0], 8)
        for index, ref in enumerate(outs):
            first = at_ref[index] == 0
            hs = [gv_ref[OUT_HIDDEN + k : OUT_HIDDEN + k + 1, :] for k in range(4)]
            hs = jnp.concatenate([jnp.where(first, hs[0], hs[2]), jnp.where(first, hs[1], hs[3])], 1)
            bl = [gv_ref[OUT_HEAD + k : OUT_HEAD + k + 1, 0:512] for k in range(2)]
            bl = jnp.where(first, bl[0], bl[1])
            rows = [hs[:, 128 * k : 128 * k + 128] for k in range(12)]
            rows += [bl[:, 128 * k : 128 * k + 128] for k in range(4)]
            vecs[pl.ds(base, 16), :] = jnp.concatenate(rows, 0)
            for d in range(16):
                lanes = slice(48 * d, 48 * d + 48)
                fill = jnp.zeros((1, 16), f32)
                row = jnp.concatenate(
                    [
                        gv_ref[OUT_BACK : OUT_BACK + 1, lanes],
                        fill,
                        gv_ref[OUT_FINAL : OUT_FINAL + 1, lanes],
                        fill,
                    ],
                    1,
                )
                vecs[pl.ds(base + 16, 8), :] = jnp.broadcast_to(row, (8, 128))
                ref[d, rows_stem + rows_small :, :] = vecs[...].astype(bf16)
    frame[0:ROW_W3, :] = jnp.zeros((ROW_W3, 128), f32)
    frame[STEM_ROWS:, :] = jnp.zeros((frame.shape[0] - STEM_ROWS, 128), f32)
    q = 9 * C2 // 2
    wide = jnp.concatenate(
        [
            jnp.concatenate(
                [
                    dw3_ref[0, pl.ds(k, q, stride=2), :],
                    dw3_ref[1, pl.ds(k, q, stride=2), :][:, 0 : C3 - 128],
                ],
                1,
            )
            for k in range(2)
        ],
        1,
    )
    for k in range(3):
        frame[pl.ds(ROW_W3 + k, q, stride=3), :] = wide[:, 128 * k : 128 * k + 128]
    for k in range(3):
        frame[pl.ds(ROW_W4 + k, 9 * C3, stride=3), :] = dw4_ref[k]
    for k in range(6):
        frame[pl.ds(ROW_WP + k, C4, stride=6), :] = dwp_ref[:, 128 * k : 128 * k + 128]
    table[0:12, :] = jnp.zeros((12, 128), f32)
    table[SMALL_ROWS:, :] = jnp.zeros((table.shape[0] - SMALL_ROWS, 128), f32)
    for k in range(6):
        lanes = slice(128 * k, 128 * k + 128)
        for name, index in VEC.items():
            row = SMALL_AT[name] + k
            table[row : row + 1, :] = gv_ref[index : index + 1, lanes]
        for h in range(4):
            row = SMALL_AT["hidden_bias"] + 6 * h + k
            table[row : row + 1, :] = gv_ref[VEC_HIDDEN + h : VEC_HIDDEN + h + 1, lanes]
        at = SMALL_AT["position"] + k
        for r in range(SIDE):
            table[pl.ds(at + 6 * (1 + SIDE * r), SIDE, stride=6), :] = gpos_ref[
                16 * r : 16 * r + SIDE, lanes
            ]
        table[at : at + 1, :] = gpos_ref[SIDE : SIDE + 1, lanes]
        row = SMALL_AT["class_token"] + k
        table[row : row + 1, :] = gpos_ref[SIDE : SIDE + 1, lanes]
    line = jnp.concatenate(
        [
            gv_ref[OUT_HEAD : OUT_HEAD + 1, 0:500],
            gv_ref[OUT_HEAD + 1 : OUT_HEAD + 2, 0:500],
            jnp.zeros((1, 24), f32),
        ],
        1,
    )
    row = SMALL_AT["head_bias"]
    for k in range(8):
        table[row + k : row + k + 1, :] = line[:, 128 * k : 128 * k + 128]
    for index, ref in enumerate(outs):
        mv = at_ref[index]

        def take(d, carry):
            owner = d * mp + mv
            a = (owner * stem_len + STEM_SHIFT) // 128
            ref[d, 0:rows_stem, :] = frame[pl.ds(a, rows_stem), :].astype(bf16)
            b = (owner * small_len + SMALL_SHIFT) // 128
            ref[d, rows_stem : rows_stem + rows_small, :] = table[pl.ds(b, rows_small), :].astype(bf16)
            return carry

        lax.fori_loop(0, ref.shape[0], take, 0)


def unshift_lanes(x, s, length):
    lane = lax.broadcasted_iota(jnp.int32, x.shape, 1)
    row = lax.broadcasted_iota(jnp.int32, x.shape, 0)
    moved = pltpu.roll(x, 128 - s, 1)
    after = pltpu.roll(moved, x.shape[0] - 1, 0)
    y = jnp.where(lane < 128 - s, moved, after)
    return jnp.where(row * 128 + lane < length, y, 0.0)


def unpack_kernel(stem_len, small_len, at_ref, x_ref, stem_ref, small_ref, sq_ref):
    rows = stem_ref.shape[0]
    end = rows + small_ref.shape[0]
    total = jnp.sum(x_ref[:, 0:end, :].astype(f32), 0)
    stem = unshift_lanes(total[0:rows], at_ref[0], stem_len)
    small = unshift_lanes(total[rows:], at_ref[1], small_len)
    stem_ref[...] = stem
    small_ref[...] = small
    sq_ref[...] = colsum(stem * stem) + colsum(small * small)


def norm_kernel(parts, *refs):
    sq_ref, sq1_ref, down_ref, head_ref, loss_ref, g0_ref, g1_ref, out_ref = refs[parts:]
    total = sum(ref[...].astype(f32) for ref in refs[:parts])
    half = g0_ref.shape[1]
    g0, g1 = total[:, 0:half], total[:, half:]
    g0_ref[...] = g0
    g1_ref[...] = g1
    squares = jnp.sum(g0 * g0 + g1 * g1 + down_ref[...] * down_ref[...], keepdims=True)
    squares = squares + jnp.sum(head_ref[...] * head_ref[...], keepdims=True)
    squares = squares + jnp.sum(sq_ref[...], keepdims=True)
    squares = squares + sq1_ref[0:1, 0:1] * (1.0 / out_ref.shape[0])
    lane = lax.broadcasted_iota(jnp.int32, (1, 128), 1)
    line = jnp.where(lane == 0, squares, loss_ref[OUT_LOSS : OUT_LOSS + 1, 0:128])
    out_ref[...] = jnp.broadcast_to(line[None], out_ref.shape)


def factor_kernel(x_ref, out_ref):
    total = jnp.sum(x_ref[...], 0)
    lane = lax.broadcasted_iota(jnp.int32, (1, 128), 1)
    norm = jnp.sqrt(jnp.sum(jnp.where(lane == 0, total, 0.0), keepdims=True))
    loss = jnp.sum(jnp.where(lane == 1, total, 0.0), keepdims=True)
    row = lax.broadcasted_iota(jnp.int32, (8, 128), 0)
    factor = jnp.minimum(1.0, clip_norm / norm)
    out_ref[...] = jnp.where(row == 0, loss, jnp.where(row == 1, norm, factor))


def late_kernel(x_ref, out_ref):
    kernel, share, rows = late_sizes(x_ref.shape[0])
    total = jnp.sum(x_ref[...].astype(f32), 0)
    exact = total[kernel : kernel + share] + total[kernel + share : kernel + 2 * share]
    out_ref[...] = jnp.broadcast_to(late_rows(total[0:kernel], exact, rows)[None], out_ref.shape)


def last_kernel(
    counts,
    stem_len,
    small_len,
    at_ref,
    x_ref,
    gram_ref,
    w1_ref,
    bn_ref,
    stem_ref,
    small_ref,
    stem_out,
    small_out,
    sq_ref,
    late,
    frame,
    table,
):
    frame[...] = jnp.zeros_like(frame)
    table[...] = jnp.zeros_like(table)
    kernel, share, _ = late_sizes(x_ref.shape[0])

    def collect(d, carry):
        x = x_ref[d].astype(f32)
        frame[pl.ds(ROW_W2 + kernel * d, kernel), :] = x[0:kernel]
        exact = x[kernel : kernel + share] + x[kernel + share : kernel + 2 * share]
        late[pl.ds(share * d, share), :] = exact
        return carry

    lax.fori_loop(0, x_ref.shape[0], collect, 0)
    line = [[jnp.zeros((1, SMALL_SHIFT), f32)], []]
    for level in range(4):
        chan = CHANS[level + 1]
        rows = []
        for which in range(2):
            row = LATE_SUMS + 6 * level + 3 * which
            rows.append(jnp.concatenate([late[row + k : row + k + 1, :] for k in range(3)], 1))
        both = fold_phases(jnp.concatenate(rows, 0), chan)
        line[0].append(both[1:2, 0:chan])
        line[1].append(both[0:1, 0:chan])
        if level == 0:
            tot = both[:, 0:128] / counts
    line = jnp.concatenate(line[0] + line[1], 1)
    for k in range(12):
        table[k : k + 1, :] = line[:, 128 * k : 128 * k + 128]
    gram, cross, mean, inv = level1_stats(gram_ref, w1_ref, counts)
    ones = gram[:, 27:28]
    grad = late[0:LATE_SUMS, :] - ones * tot[0:1] - (cross - ones * mean) * inv * tot[1:2]
    grad = grad * (inv * bn_ref[0:1, 0:128])
    line = [jnp.zeros((1, STEM_SHIFT), f32)] + [grad[k : k + 1, 0:C1] for k in range(27)]
    line = jnp.concatenate(line, 1)
    for k in range(ROW_W2):
        frame[k : k + 1, :] = line[:, 128 * k : 128 * k + 128]
    squares = jnp.sum(frame[0:ROW_W3, :] * frame[0:ROW_W3, :], keepdims=True)
    squares = squares + jnp.sum(table[0:12, :] * table[0:12, :], keepdims=True)
    sq_ref[...] = jnp.broadcast_to(squares, sq_ref.shape)
    part = frame[pl.ds(at_ref[2], stem_ref.shape[0]), :]
    stem_out[...] = stem_ref[...] + unshift_lanes(part, at_ref[0], stem_len)
    part = table[pl.ds(at_ref[3], small_ref.shape[0]), :]
    small_out[...] = small_ref[...] + unshift_lanes(part, at_ref[1], small_len)


def call(kernel, outs, *args, scratch=(), smem=0, hbm=(), load=(), store=(), hbm_out=(), limit=32):
    def space(index, free):
        if index in free:
            return pl.BlockSpec(memory_space=pltpu.HBM)
        return pl.BlockSpec(memory_space=pltpu.VMEM)

    def shape(index):
        where = pltpu.HBM if index in (*hbm_out, *store) else jax.ShapeDtypeStruct
        return where(*outs[index])

    args = [
        pltpu.with_memory_space_constraint(arg, pltpu.HBM) if index in (*hbm, *load) else arg
        for index, arg in enumerate(args)
    ]
    count = len(args)
    moved = [jax.ShapeDtypeStruct(args[k].shape, args[k].dtype) for k in load]
    moved += [jax.ShapeDtypeStruct(*outs[k]) for k in store]

    def body(*refs):
        refs = list(refs)
        if not moved:
            return kernel(*refs)
        buffers, sems = refs[-1 - len(moved) : -1], refs[-1]
        refs = refs[: -1 - len(moved)]
        copies = []
        for k, index in enumerate(load):
            copies.append(pltpu.make_async_copy(refs[index], buffers[k], sems.at[k]))
            copies[-1].start()
            refs[index] = buffers[k]
        for copy in copies:
            copy.wait()
        targets = []
        for k, index in enumerate(store):
            targets.append((buffers[len(load) + k], refs[count + index], sems.at[len(load) + k]))
            refs[count + index] = buffers[len(load) + k]
        kernel(*refs)
        copies = [pltpu.make_async_copy(*target) for target in targets]
        for copy in copies:
            copy.start()
        for copy in copies:
            copy.wait()

    extra = [pltpu.VMEM(x.shape, x.dtype) for x in moved]
    if moved:
        extra.append(pltpu.SemaphoreType.DMA((len(moved),)))
    specs = [pl.BlockSpec(memory_space=pltpu.SMEM)] * smem
    specs += [space(index, (*hbm, *load)) for index in range(smem, count)]
    return pl.pallas_call(
        body,
        out_shape=[shape(index) for index in range(len(outs))],
        in_specs=specs,
        out_specs=[space(index, (*hbm_out, *store)) for index in range(len(outs))],
        scratch_shapes=[*scratch, *extra],
        compiler_params=pltpu.CompilerParams(vmem_limit_bytes=limit * 1024 * 1024),
    )(*args)


def adam_step(weight, first, second, grad, factor, rate):
    grad = grad * factor
    first = beta_one * first + (1.0 - beta_one) * grad
    second = beta_two * second + (1.0 - beta_two) * grad * grad
    first_fixed = first / (1.0 - beta_one**STEP)
    second_fixed = second / (1.0 - beta_two**STEP)
    return (
        weight
        - rate * (first_fixed / (jnp.sqrt(second_fixed) + adam_epsilon) + decay_rate * weight),
        first,
        second,
    )


def local(
    pixels,
    labels,
    stem,
    stem_first,
    stem_second,
    small,
    small_first,
    small_second,
    block,
    block_first,
    block_second,
    head,
    head_first,
    head_second,
):
    dp, mp = lax.axis_size("dp"), lax.axis_size("mp")
    n = dp * mp
    me, mine = lax.axis_index("dp"), lax.axis_index("mp")
    owner = me * mp + mine
    stem_len, small_len = stem.shape[0], small.shape[0]
    rows_stem = up16(-(-(stem_len + 127) // 128))
    rows_small = up16(-(-(small_len + 127) // 128))
    rows = rows_stem + rows_small
    everyone = ("dp", "mp")
    fast = (dp, mp) == (16, 2)

    def share(x):
        return lax.all_to_all(x, everyone, 0, 0)

    part = FF // mp
    cls = CLASSES // mp
    cls_pad = 512 // (mp // 2)
    packed = jnp.concatenate(
        [block[0], block[1], block[2], jnp.pad(head, ((0, 0), (0, cls_pad - cls)))], 1
    ).astype(bf16)
    packed, stem, small = lax.optimization_barrier((packed, stem, small))
    gathered = lax.all_gather(packed, everyone, axis=0)
    stem_at, small_at = owner * stem_len + STEM_SHIFT, owner * small_len + SMALL_SHIFT
    at = jnp.stack(
        [
            stem_at % 128,
            small_at % 128,
            jnp.minimum(stem_at // 128, ROW_W3),
            jnp.minimum(small_at // 128, 16),
        ]
    ).astype(jnp.int32)
    (piece,) = call(
        pack_kernel,
        [((rows, 128), bf16)],
        at,
        jnp.pad(stem, (0, rows_stem * 128 - stem_len)).reshape(rows_stem, 128),
        jnp.pad(small, (0, rows_small * 128 - small_len)).reshape(rows_small, 128),
        smem=1,
        limit=4,
    )

    strip = pixels.reshape(pixels.shape[1], 128)
    strip, piece, at = lax.optimization_barrier((strip, piece, at))
    half = strip.shape[0] // 2
    pairs = [(source, (source + dp - 1) % dp) for source in range(dp)]
    lower = lax.ppermute(strip[:half], "dp", pairs)

    if fast:
        gathered = gathered.reshape(16, 2, 48, packed.shape[1])
    else:
        g = gathered.reshape(dp, mp, D // dp, packed.shape[1])
        g = jnp.transpose(g, (0, 2, 1, 3)).reshape(D, mp, -1)
        slots = [g[:, :, k * part : (k + 1) * part].reshape(D, 2, FF // 2) for k in range(3)]
        top = g[:, :, 3 * part : 3 * part + cls].reshape(D, 2, CLASSES // 2)
        slots.append(jnp.pad(top, ((0, 0), (0, 0), (0, 12))))
        g = jnp.concatenate(slots, 2).reshape(16, 48, 2, -1)
        gathered = jnp.transpose(g, (0, 2, 1, 3))

    if fast:
        planes = [[4 * z + k for k in range(4)] for z in range(4)]
        column = [piece]
        for k in (1, 2, 3):
            pairs = [(source, source ^ (4 * k)) for source in range(dp)]
            column.append(lax.ppermute(piece, "dp", pairs))
        *column, lower = lax.optimization_barrier((*column, lower))
        column = jnp.stack(column, 0)
        column = jnp.broadcast_to(column[None], (4, 4, rows, 128))
        column = lax.all_to_all(column, "dp", 0, 0, axis_index_groups=planes)
        column = column.reshape(dp, rows, 128)
    else:
        column = lax.all_to_all(jnp.broadcast_to(piece[None], (dp, rows, 128)), "dp", 0, 0)
    xk, gram = call(
        image_kernel,
        [((8, T, 192), bf16), ((n, 8, 128), f32)],
        strip[half:],
        lower,
        scratch=[
            pltpu.VMEM((2 * half, 128), f32),
            pltpu.VMEM((16 * half // 3 + 16, 128), f32),
            pltpu.VMEM((17, T, 64), bf16),
        ],
        limit=12,
    )
    gram, xk, column = lax.optimization_barrier((gram, xk, column))
    gram = share(gram)
    if mp == 2:
        swap = [(0, 1), (1, 0)]
        pieces = [column, lax.ppermute(column, "mp", swap)]
        which = jnp.stack([mine, 1 - mine]).astype(jnp.int32)
    else:
        columns = lax.all_gather(column, "mp", axis=0)
        pieces = [columns[k] for k in range(mp)]
        which = jnp.arange(mp, dtype=jnp.int32)
    which = jnp.concatenate([which, labels.reshape(1), (me >> 2).reshape(1).astype(jnp.int32)])
    frame_rows = (stem_len * n + STEM_SHIFT) // 128 + rows_stem + 16
    table_rows = (small_len * n + SMALL_SHIFT) // 128 + rows_small + 16
    frames = [pltpu.VMEM((frame_rows, 128), f32), pltpu.VMEM((table_rows, 128), f32)]
    w1, t1, t2, t3, t4, wp, bn, vec, pos = call(
        functools.partial(assemble_kernel, fast, len(pieces), mp, stem_len, small_len, rows_stem, rows_small),
        [
            ((32, 128), f32),
            ((192, W), bf16),
            ((3, W + C1, W), bf16),
            ((3, W + C2, W), bf16),
            ((3, W + C3, W), bf16),
            ((C4, D), bf16),
            ((8, W), f32),
            ((24, D), f32),
            ((T, D), f32),
        ],
        which,
        *pieces,
        smem=1,
        store=(1, 2, 3, 4, 5, 7, 8),
        scratch=frames
        + [
            pltpu.VMEM((9 * C1, 128), f32),
            pltpu.VMEM((9 * C2, 128), f32),
            pltpu.VMEM((9 * C2, 128), f32),
            pltpu.VMEM((192, W), f32),
            pltpu.VMEM((W + C1, W), f32),
            pltpu.VMEM((W + C2, W), f32),
        ],
        limit=20,
    )

    positions = SIDE * SIDE * n
    counts = [None, 64.0 * positions, 16.0 * positions, 4.0 * positions, 1.0 * positions]
    ax, conv, st = call(
        functools.partial(conv12_kernel, counts[1]),
        [((9, T, W + C1), bf16), ((4, T, W), f32), ((n, 2, W), f32)],
        xk,
        gram,
        w1,
        t1,
        bn,
        t2,
        load=(3, 5),
        limit=14,
    )
    convs = [None, None, conv]
    stats = [None, None, share(st)]
    inputs = [None, None, ax]
    kernels = [None, t1, t2, t3, t4]
    for level in (3, 4):
        r = 2 ** (4 - level)
        ax, conv, st = call(
            functools.partial(conv_kernel, level - 1, counts[level - 1]),
            [((2 * r + 1, T, W + CHANS[level - 1]), bf16), ((r, T, W), f32), ((n, 2, W), f32)],
            convs[level - 1],
            stats[level - 1],
            bn,
            kernels[level],
            load=(3,),
            store=(0, 1, 2) if level == 4 else (),
            limit=10,
        )
        inputs.append(ax)
        convs.append(conv)
        stats.append(share(st))

    a4, x0, n1 = call(
        functools.partial(embed_kernel, counts[4]),
        [((T, C4), bf16), ((T, D), f32), ((T, D), bf16)],
        stats[4],
        bn,
        convs[4],
        wp,
        pos,
        vec,
        load=(2, 3, 4, 5),
        store=(0, 1, 2),
        limit=12,
    )
    outs = call(
        functools.partial(block_kernel, counts[4]),
        [
            ((4, 2, 4, 48, FF), bf16),
            ((1, T, W), f32),
            ((n, 2, W), f32),
            ((32, D), f32),
            ((T, D), f32),
            ((C4, D), f32),
        ],
        stats[4],
        bn,
        n1,
        vec,
        x0,
        a4,
        wp,
        convs[4],
        gathered,
        hbm=(2, 3, 4, 5, 6, 7, 8),
        hbm_out=(0, 1, 2, 3, 4, 5),
        limit=44,
        scratch=[
            pltpu.VMEM((1, T, W), f32),
            pltpu.VMEM((C4, D), bf16),
            pltpu.VMEM((24, D), f32),
            pltpu.VMEM((1, T, W), f32),
            pltpu.VMEM((n, 2, W), f32),
            pltpu.VMEM((32, D), f32),
            pltpu.VMEM((T, D), f32),
            pltpu.VMEM((C4, D), f32),
            pltpu.VMEM((2, 16, 48, 1536), bf16),
            pltpu.VMEM((2, 16, 48, 1536), bf16),
            pltpu.VMEM((2, 16, 48, 1536), bf16),
            pltpu.VMEM((2, 16, 48, 512), bf16),
            pltpu.SemaphoreType.DMA((39,)),
            pltpu.VMEM((T, W), bf16),
            pltpu.VMEM((T, D), f32),
            pltpu.VMEM((T, D), bf16),
            pltpu.VMEM((T, 3 * D), bf16),
            pltpu.VMEM((HEADS, T, T), f32),
            pltpu.VMEM((T, D), bf16),
            pltpu.VMEM((D, T), bf16),
            pltpu.VMEM((2, T, 1536), f32),
            pltpu.VMEM((T, D), f32),
            pltpu.VMEM((T, 3 * D), bf16),
            pltpu.VMEM((T, D), f32),
            pltpu.VMEM((2, T, 1536), bf16),
            pltpu.VMEM((32, 1536), f32),
        ],
    )
    grads, back, tot, facts, gpos, dwp = outs
    tot = share(tot)
    if fast:
        planes = [[8 * z + k for k in range(8)] for z in range(4)]
        owned = lax.psum_scatter(
            grads.reshape(8 * 4 * 48, FF),
            everyone,
            scatter_dimension=0,
            tiled=True,
            axis_index_groups=planes,
        )
        owned = [owned]
    else:
        g = jnp.transpose(grads, (2, 0, 3, 1, 4)).reshape(D, 2, 2, FF // 2)
        g = jnp.transpose(g, (0, 2, 1, 3)).reshape(dp, D // dp, 2, mp, part)
        g = jnp.transpose(g, (0, 3, 1, 2, 4)).reshape(n * (D // dp), 2 * part)
        owned = [lax.psum_scatter(g, everyone, scatter_dimension=0, tiled=True)]

    rows_d = D // dp
    rows_vec = 48 if fast else 0

    def outer(bo_all, fin_all, hs_all, bl_all):
        return dot_tn(bo_all, hs_all), dot_tn(fin_all, bl_all)

    if not fast:
        bo, fin = facts[OUT_BACK : OUT_BACK + 1], facts[OUT_FINAL : OUT_FINAL + 1]
        hs, bl = facts[OUT_HIDDEN:OUT_HEAD].reshape(1, FF), facts[OUT_HEAD:OUT_SUMS, 0:512].reshape(1, 1024)
        head_line = jnp.concatenate([bl[:, :500], bl[:, 512:1012]], 1).reshape(1, mp, cls)
        line = jnp.concatenate(
            [
                jnp.broadcast_to(bo.reshape(dp, 1, rows_d), (dp, mp, rows_d)),
                jnp.broadcast_to(fin.reshape(dp, 1, rows_d), (dp, mp, rows_d)),
                jnp.broadcast_to(hs.reshape(1, mp, part), (dp, mp, part)),
                jnp.broadcast_to(head_line, (dp, mp, cls)),
            ],
            2,
        ).reshape(n, -1)
        width = -(-line.shape[1] // 1024) * 1024
        line = jnp.pad(line, ((0, 0), (0, width - line.shape[1]))).astype(bf16)
        line = share(line.reshape(n, width // 128, 128)).reshape(n, width)
        cuts = [0, rows_d, 2 * rows_d, 2 * rows_d + part, 2 * rows_d + part + cls]
        grad_down, grad_head = outer(*[line[:, a:b] for a, b in zip(cuts[:-1], cuts[1:])])

    sums = [None] * 5
    kernel_grads = [None] * 5
    for level in (4, 3):
        r = 2 ** (4 - level)
        chan_in = CHANS[level - 1]
        g, back, so, sums[level - 1] = call(
            functools.partial(conv_back_kernel, level, counts[level], counts[level - 1]),
            [
                ((r + 1, T, W), bf16),
                ((2 * r, T, W), f32),
                ((n, 2, W), f32),
                ((2, W), f32),
            ],
            back,
            tot,
            convs[level],
            stats[level],
            kernels[level],
            convs[level - 1],
            stats[level - 1],
            bn,
            load=(0, 2, 3, 4) if level == 4 else (4,),
            limit=12,
        )
        (kernel_grads[level],) = call(
            functools.partial(kernel_grad, level),
            [((-(-CHANS[level] // 128), 9 * chan_in, 128), f32)],
            inputs[level],
            g,
            load=(0,) if level == 4 else (),
            scratch=[pltpu.VMEM((3, W + chan_in, W), f32)],
            limit=12,
        )
        if level == 4:
            so, kernel_grads[4] = lax.optimization_barrier((so, kernel_grads[4]))
            tot = share(so)
    outs = call(
        functools.partial(early_kernel, len(pieces), mp, stem_len, small_len, rows_stem, rows_small),
        [((dp, rows + rows_vec, 128), bf16)] * len(pieces),
        which,
        kernel_grads[3],
        kernel_grads[4],
        dwp,
        facts,
        gpos,
        smem=1,
        load=(3, 4, 5),
        scratch=frames + [pltpu.VMEM((48, 128), f32)],
        limit=18,
    )
    if mp == 2:
        column = outs[0] + lax.ppermute(outs[1], "mp", swap)
    else:
        column = lax.psum_scatter(jnp.stack(outs, 0), "mp", scatter_dimension=0)
    so, column = lax.optimization_barrier((so, column))
    tot = share(so)
    tot, column = lax.optimization_barrier((tot, column))
    column = lax.all_to_all(column, "dp", 0, 0)
    kernel_rows, exact_rows, each = late_sizes(n)
    (late,) = call(
        functools.partial(conv2_back_kernel, counts[2], counts[1]),
        [((n, each, 128), bf16)],
        back,
        tot,
        convs[2],
        stats[2],
        inputs[2],
        t2,
        xk,
        gram,
        w1,
        t1,
        bn,
        *sums[2:4],
        facts,
        load=(0, 4, 5, 6, 9, 13),
        scratch=[
            pltpu.VMEM((1, 9 * C1, 128), f32),
            pltpu.VMEM((5, T, W), bf16),
            pltpu.VMEM((3, W + C1, W), f32),
            pltpu.VMEM((192, W), f32),
            pltpu.VMEM((n * kernel_rows, 128), f32),
            pltpu.VMEM((n * exact_rows, 128), f32),
        ],
        limit=20,
    )
    if fast:
        owned[0] = lax.optimization_barrier((owned[0], late))[0]
        lines = [[8 * z + k for z in range(4)] for k in range(8)]
        owned[0] = lax.psum_scatter(
            owned[0], everyone, scatter_dimension=0, tiled=True, axis_index_groups=lines
        )
    late, column = lax.optimization_barrier((late, column))
    late = share(late)
    (late,) = call(late_kernel, [((n, each, 128), bf16)], late, limit=8)
    late = share(late)
    if fast:
        line = column[:, rows:].reshape(2 * dp, 24, 128)
        grad_down, grad_head = outer(
            line[:, 16, 0:48],
            line[:, 16, 64:112],
            line[:, 0:12].reshape(2 * dp, part),
            line[:, 12:16].reshape(2 * dp, 512)[:, :cls],
        )
    grad_stem, grad_small, squares = call(
        functools.partial(unpack_kernel, stem_len, small_len),
        [((rows_stem, 128), f32), ((rows_small, 128), f32), ((1, 128), f32)],
        at,
        column,
        smem=1,
        limit=8,
    )

    grad_stem, grad_small, squares1 = call(
        functools.partial(last_kernel, counts[1], stem_len, small_len),
        [((rows_stem, 128), f32), ((rows_small, 128), f32), ((1, 128), f32)],
        at,
        late,
        gram,
        w1,
        bn,
        grad_stem,
        grad_small,
        smem=1,
        scratch=[
            pltpu.VMEM((n * exact_rows, 128), f32),
            pltpu.VMEM((ROW_W2 + n * kernel_rows + rows_stem, 128), f32),
            pltpu.VMEM((16 + rows_small, 128), f32),
        ],
        limit=8,
    )

    g0, g1, ends = call(
        functools.partial(norm_kernel, len(owned)),
        [((rows_d, part), f32), ((rows_d, part), f32), ((n, 1, 128), f32)],
        *owned,
        squares,
        squares1,
        grad_down,
        grad_head,
        facts,
        limit=8,
    )
    (ends,) = call(factor_kernel, [((8, 128), f32)], share(ends), limit=4)
    loss_sum, grad_norm, factor = ends[0, 0], ends[1, 0], ends[2, 0]
    grad_stem = grad_stem.reshape(-1)[:stem_len]
    grad_small = grad_small.reshape(-1)[:small_len]
    grad_block = jnp.stack([g0, g1, grad_down], 0)
    stem_new = adam_step(stem, stem_first, stem_second, grad_stem, factor, rate_stem)
    small_new = adam_step(small, small_first, small_second, grad_small, factor, rate_small)
    block_new = adam_step(block, block_first, block_second, grad_block, factor, rate_block)
    head_new = adam_step(head, head_first, head_second, grad_head, factor, rate_head)
    return (*stem_new, *small_new, *block_new, *head_new, loss_sum, grad_norm)


def solution(mesh):
    flat = P(("dp", "mp"))
    matrix = P(None, "dp", "mp")
    head = P("dp", "mp")
    states = (flat,) * 6 + (matrix,) * 3 + (head,) * 3
    return jax.shard_map(
        local,
        mesh=mesh,
        in_specs=(P("mp", "dp", None), P("mp", "dp")) + states,
        out_specs=states + (P(), P()),
        check_vma=False,
    )
```

```python
import functools

import jax
import jax.numpy as jnp
from jax import lax
from jax.experimental import pallas as pl
from jax.experimental.pallas import tpu as pltpu
from jax.sharding import PartitionSpec as P

D = 768
HEADS = 12
HEAD_DIM = 64
FF = 3072
CLASSES = 1000
C1 = 48
C2 = 96
C3 = 192
C4 = 384
STEP = 10
TOK = 197
SIDE = 14
T = 16 * SIDE
W = 384
CHANS = (3, C1, C2, C3, C4)

beta_one = 0.9
beta_two = 0.999
adam_epsilon = 1e-08
decay_rate = 0.05
clip_norm = 1.0
rate_stem = 0.05
rate_small = 0.5
rate_block = 0.05
rate_head = 0.05
batch_epsilon = 1e-05
layer_epsilon = 1e-06
smoothing = 0.1

bf16 = jnp.bfloat16
f32 = jnp.float32

STEM_SHIFT = 112
SMALL_SHIFT = 96
ROW_W2 = 11
ROW_W3 = ROW_W2 + 9 * C1 * C2 // 128
ROW_W4 = ROW_W3 + 9 * C2 * C3 // 128
ROW_WP = ROW_W4 + 9 * C3 * C4 // 128
STEM_ROWS = ROW_WP + C4 * D // 128
SMALL_NAMES = (
    ("proj_bias", 6),
    ("class_token", 6),
    ("position", 6 * TOK),
    ("norm1_gain", 6),
    ("norm1_bias", 6),
    ("query_bias", 6),
    ("value_bias", 6),
    ("out_bias", 6),
    ("norm2_gain", 6),
    ("norm2_bias", 6),
    ("hidden_bias", 24),
    ("mlp_bias", 6),
    ("final_gain", 6),
    ("final_bias", 6),
    ("head_bias", 8),
)
SMALL_AT = {}
_row = 12
for _name, _rows in SMALL_NAMES:
    SMALL_AT[_name] = _row
    _row += _rows
SMALL_ROWS = _row
VEC_NAMES = (
    "proj_bias",
    "norm1_gain",
    "norm1_bias",
    "query_bias",
    "value_bias",
    "out_bias",
    "norm2_gain",
    "norm2_bias",
    "mlp_bias",
    "final_gain",
    "final_bias",
)
VEC = {name: index for index, name in enumerate(VEC_NAMES)}
VEC_HIDDEN = 12
VEC_HEAD = 16
VEC_AIM = 18
OUT_BACK = 16
OUT_FINAL = 17
OUT_HIDDEN = 18
OUT_HEAD = 22
OUT_SUMS = 24
OUT_LOSS = 25


def dot(a, b):
    return jnp.dot(a, b, preferred_element_type=f32)


def dot_nt(a, b):
    return lax.dot_general(a, b, (((1,), (1,)), ((), ())), preferred_element_type=f32)


def dot_tn(a, b):
    return lax.dot_general(a, b, (((0,), (0,)), ((), ())), preferred_element_type=f32)


GELU_A = 0.7978845608028654
GELU_B = 0.044715


def gelu(x):
    return 0.5 * x * (1.0 + jnp.tanh(GELU_A * (x + GELU_B * x * x * x)))


def gelu_slope(x):
    t = jnp.tanh(GELU_A * (x + GELU_B * x * x * x))
    return 0.5 * (1.0 + t) + 0.5 * x * (1.0 - t * t) * GELU_A * (1.0 + 3.0 * GELU_B * x * x)


def dot_f32(a, b):
    return jnp.dot(a, b, preferred_element_type=f32, precision=lax.Precision.HIGHEST)


def up16(n):
    return -(-n // 16) * 16


def colsum(x):
    return jnp.sum(x, 0, keepdims=True)


def slot_index():
    return lax.broadcasted_iota(jnp.int32, (T, 1), 0)


def patch_mask():
    return ((slot_index() & 15) < SIDE).astype(f32)


def token_mask():
    p = slot_index()
    return (((p & 15) < SIDE) | (p == SIDE)).astype(f32)


def fold_phases(x, chan):
    step = W // 2
    while step >= chan:
        x = x + jnp.concatenate([x[:, step:], x[:, :step]], 1)
        step //= 2
    return x


def bn_stats(st_ref, count, chan):
    tot = fold_phases(jnp.sum(st_ref[:, 0:2, :], 0), chan)
    mean = tot[0:1] / count
    inv = lax.rsqrt(tot[1:2] / count - mean * mean + batch_epsilon)
    return mean, inv


def shift_lanes(x, s):
    lane = lax.broadcasted_iota(jnp.int32, x.shape, 1)
    row = lax.broadcasted_iota(jnp.int32, x.shape, 0)
    moved = pltpu.roll(x, s, 1)
    before = jnp.where(row == 0, 0.0, pltpu.roll(moved, 1, 0))
    return jnp.where(lane >= s, moved, before)


def pack_kernel(at_ref, stem_ref, small_ref, out_ref):
    rows = stem_ref.shape[0]
    out_ref[0:rows, :] = shift_lanes(stem_ref[...], at_ref[0]).astype(bf16)
    out_ref[rows:, :] = shift_lanes(small_ref[...], at_ref[1]).astype(bf16)


def flat_lanes(ref, row, count):
    return jnp.concatenate([ref[row + k : row + k + 1, :] for k in range(count)], 1)


def assemble_kernel(by_plane, parts, mp, stem_len, small_len, rows_stem, rows_small, at_ref, *refs):
    pieces = refs[:parts]
    s1, t1_ref, t2_ref, t3_ref, t4_ref, wp_ref, bn_ref, vec_ref, pos_ref = refs[parts : parts + 9]
    frame, table, s2, s3a, s3b, u1, u2, u3 = refs[parts + 9 :]
    frame[...] = jnp.zeros_like(frame)
    table[...] = jnp.zeros_like(table)
    for index, ref in enumerate(pieces):
        mv = at_ref[index]

        def put(d, carry):
            owner = (at_ref[parts + 1] ^ ((d & 3) * 4 + (d >> 2)) if by_plane else d) * mp + mv
            a = (owner * stem_len + STEM_SHIFT) // 128
            frame[pl.ds(a, rows_stem), :] += ref[d, 0:rows_stem, :].astype(f32)
            b = (owner * small_len + SMALL_SHIFT) // 128
            table[pl.ds(b, rows_small), :] += ref[d, rows_stem : rows_stem + rows_small, :].astype(f32)
            return carry

        lax.fori_loop(0, ref.shape[0], put, 0)
    s1[...] = jnp.zeros_like(s1)
    flat = flat_lanes(frame, 0, ROW_W2)
    for k in range(27):
        s1[k : k + 1, 0:C1] = flat[:, STEM_SHIFT + 48 * k : STEM_SHIFT + 48 * k + 48]
    u1[...] = jnp.zeros_like(u1)
    for tap in range(3):
        for j in range(8):
            cols = slice(j * C1, (j + 1) * C1)
            if j == 0:
                u1[tap * 64 + 48 : tap * 64 + 51, cols] = s1[tap * 9 : tap * 9 + 3, 0:C1]
                u1[tap * 64 : tap * 64 + 6, cols] = s1[tap * 9 + 3 : tap * 9 + 9, 0:C1]
            else:
                at = tap * 64 + 6 * j - 3
                u1[at : at + 9, cols] = s1[tap * 9 : tap * 9 + 9, 0:C1]
    t1_ref[...] = u1[...].astype(bf16)
    q = 9 * C1 // 4
    wide = jnp.concatenate([frame[pl.ds(ROW_W2 + k, q, stride=3), :] for k in range(3)], 1)
    for k in range(4):
        s2[pl.ds(k, q, stride=4), 0:C2] = wide[:, k * C2 : (k + 1) * C2]
    q = 9 * C2 // 2
    wide = jnp.concatenate([frame[pl.ds(ROW_W3 + k, q, stride=3), :] for k in range(3)], 1)
    for k in range(2):
        part = wide[:, k * C3 : (k + 1) * C3]
        s3a[pl.ds(k, q, stride=2), :] = part[:, 0:128]
        s3b[pl.ds(k, q, stride=2), 0 : C3 - 128] = part[:, 128:C3]
    for ref, chan_in, chan_out, src, u in (
        (t2_ref, C1, C2, (s2,), u2),
        (t3_ref, C2, C3, (s3a, s3b), u3),
    ):
        for tap in range(3):
            u[...] = jnp.zeros_like(u)
            base = tap * 3 * chan_in
            for j in range(W // chan_out):
                for k, s in enumerate(src):
                    width = min(128, chan_out - 128 * k)
                    cols = slice(j * chan_out + 128 * k, j * chan_out + 128 * k + width)
                    if j == 0:
                        u[W : W + chan_in, cols] = s[base : base + chan_in, 0:width]
                        u[0 : 2 * chan_in, cols] = s[base + chan_in : base + 3 * chan_in, 0:width]
                    else:
                        at = (2 * j - 1) * chan_in
                        u[at : at + 3 * chan_in, cols] = s[base : base + 3 * chan_in, 0:width]
            ref[tap] = u[...].astype(bf16)
    for tap in range(3):
        rows = 3 * C3
        for k in range(3):
            lanes = slice(k * 128, (k + 1) * 128)
            at = ROW_W4 + k + 3 * tap * rows
            t4_ref[tap, 0 : 2 * C3, lanes] = frame[pl.ds(at + 3 * C3, 2 * C3, stride=3), :].astype(bf16)
            t4_ref[tap, 2 * C3 : 3 * C3, lanes] = frame[pl.ds(at, C3, stride=3), :].astype(bf16)
    for k in range(6):
        lanes = slice(k * 128, (k + 1) * 128)
        wp_ref[:, lanes] = frame[pl.ds(ROW_WP + k, C4, stride=6), :].astype(bf16)
    flat = flat_lanes(table, 0, 12)
    first = SMALL_SHIFT
    for level in range(4):
        chan = CHANS[level + 1]
        for which in range(2):
            at = first + which * (C1 + C2 + C3 + C4)
            part = flat[:, at : at + chan]
            row = 2 * level + which
            for j in range(W // chan):
                bn_ref[row : row + 1, j * chan : (j + 1) * chan] = part
        first += chan
    vec_ref[...] = jnp.zeros_like(vec_ref)
    for name, index in VEC.items():
        vec_ref[index : index + 1, :] = flat_lanes(table, SMALL_AT[name], 6)
    for k in range(4):
        row = VEC_HIDDEN + k
        vec_ref[row : row + 1, :] = flat_lanes(table, SMALL_AT["hidden_bias"] + 6 * k, 6)
    flat = flat_lanes(table, SMALL_AT["head_bias"], 8)
    lane = lax.broadcasted_iota(jnp.int32, (1, 512), 1)
    for m in range(2):
        vec_ref[VEC_HEAD + m : VEC_HEAD + m + 1, 0:500] = flat[:, 500 * m : 500 * m + 500]
        aim = jnp.where(lane + 500 * m == at_ref[parts], 1.0 - smoothing, 0.0) + smoothing / CLASSES
        vec_ref[VEC_AIM + m : VEC_AIM + m + 1, 0:512] = jnp.where(lane < 500, aim, 0.0)
    pos_ref[...] = jnp.zeros_like(pos_ref)
    at = SMALL_AT["position"]
    for k in range(6):
        lanes = slice(k * 128, (k + 1) * 128)
        for r in range(SIDE):
            rows = table[pl.ds(at + k + 6 * (1 + SIDE * r), SIDE, stride=6), :]
            pos_ref[16 * r : 16 * r + SIDE, lanes] = rows
        mark = SMALL_AT["class_token"] + k
        pos_ref[SIDE : SIDE + 1, lanes] = table[mark : mark + 1, :] + table[at + k : at + k + 1, :]


def image_kernel(own_ref, next_ref, xk_ref, gram_ref, flat, chunks, xe):
    half = own_ref.shape[0]
    flat[0:half, :] = own_ref[...].astype(f32)
    flat[half : 2 * half, :] = next_ref[...].astype(f32)
    n = 2 * half // 3
    wide = jnp.concatenate([flat[pl.ds(k, n, stride=3), :] for k in range(3)], 1)
    for j in range(8):
        chunks[pl.ds(j, n, stride=8), 0:48] = wide[:, 48 * j : 48 * j + 48]
    mask = patch_mask()
    lane = lax.broadcasted_iota(jnp.int32, (T, 64), 1)

    def spread(i, carry):
        rows = [chunks[pl.ds(16 * SIDE * r + SIDE * i, 16), 0:64] for r in range(SIDE)]
        x = jnp.where(lane < 48, jnp.concatenate(rows, 0), 0.0) * mask
        left = pltpu.roll(jnp.concatenate([x, x], 1), 3, 1)[:, 0:64]
        left = jnp.where((lane >= 48) & (lane < 51), pltpu.roll(left, 1, 0), 0.0)
        xe[i + 1] = ((x + left) * mask).astype(bf16)
        return carry

    chunks[pl.ds(n * 8, 16), :] = jnp.zeros((16, 128), f32)
    lax.fori_loop(0, 16, spread, 0)
    last = xe[16]
    xe[0] = jnp.concatenate([jnp.zeros((16, 64), bf16), last[: T - 16]], 0)

    def step(i, carry):
        gram, ones = carry
        x = jnp.concatenate([xe[2 * i], xe[2 * i + 1], xe[2 * i + 2]], 1)
        xk_ref[i] = x
        return gram + dot_tn(x, x), ones + colsum(x.astype(f32))

    gram, ones = lax.fori_loop(0, 8, step, (jnp.zeros((192, 192), f32), jnp.zeros((1, 192), f32)))
    row = lax.broadcasted_iota(jnp.int32, (192, 256), 0)
    col = lax.broadcasted_iota(jnp.int32, (192, 256), 1)
    j, k = col >> 5, col & 31
    tap = (k >= 9).astype(jnp.int32) + (k >= 18).astype(jnp.int32)
    u = k - 9 * tap
    at = 64 * tap + jnp.where(j == 0, jnp.where(u < 3, 48 + u, u - 3), 6 * j - 3 + u)
    pick = ((row == at) & (k < 27)).astype(f32)
    both = lax.dot_general(
        pick,
        dot_f32(gram, pick),
        (((0,), (0,)), ((), ())),
        preferred_element_type=f32,
        precision=lax.Precision.HIGHEST,
    )
    ones = dot_f32(jnp.broadcast_to(ones, (8, 192)), pick)[0:1]
    total = jnp.zeros((32, 32), f32)
    line = jnp.zeros((1, 32), f32)
    for q in range(8):
        lanes = slice(32 * q, 32 * q + 32)
        total = total + both[lanes, lanes]
        line = line + ones[:, lanes]
    r32 = lax.broadcasted_iota(jnp.int32, (32, 32), 0)
    c32 = lax.broadcasted_iota(jnp.int32, (32, 32), 1)
    total = total + jnp.where(r32 == 27, line, 0.0)
    column = jnp.sum(jnp.where(r32 == c32, line, 0.0), 1, keepdims=True)
    total = total + jnp.where(c32 == 27, column, 0.0)
    flat8 = jnp.concatenate([total[8 * q : 8 * q + 8] for q in range(4)], 1)
    gram_ref[...] = jnp.broadcast_to(flat8[None], gram_ref.shape)


def level1_stats(gram_ref, w1_ref, count):
    flat8 = jnp.sum(gram_ref[...], 0)
    gram = jnp.concatenate([flat8[:, 32 * q : 32 * q + 32] for q in range(4)], 0)
    cross = dot_f32(gram, w1_ref[...])
    mean = cross[27:28] / count
    squares = colsum(w1_ref[...] * cross) / count
    inv = lax.rsqrt(squares - mean * mean + batch_epsilon)
    return gram, cross, mean, inv


def tile_lanes(x, chan):
    return jnp.concatenate([x[:, 0:chan]] * (W // chan), 1)


def conv12_kernel(count, xk_ref, gram_ref, w1_ref, t1_ref, bn_ref, t_ref, ax_ref, out_ref, st_ref):
    gram, cross, mean, inv = level1_stats(gram_ref, w1_ref, count)
    mean, inv = tile_lanes(mean, C1), tile_lanes(inv, C1)
    gain, bias = bn_ref[0:1, :], bn_ref[1:2, :]
    mask = patch_mask()
    weights = t1_ref[...]

    def activate(i, carry):
        a = gelu((dot(xk_ref[i], weights) - mean) * inv * gain + bias) * mask
        put_input(ax_ref, i, a, C1)
        return carry

    lax.fori_loop(0, 8, activate, 0)
    convolve(8, ax_ref, t_ref, out_ref, st_ref, mask, C1)


def put_input(ax_ref, i, a, chan):
    left = pltpu.roll(a[:, W - chan :], 1, 0)
    ax_ref[i + 1, :, 0:W] = a.astype(bf16)
    ax_ref[i + 1, :, W:] = left.astype(bf16)


def convolve(rows, ax_ref, t_ref, out_ref, st_ref, mask, chan):
    last = ax_ref[rows]
    ax_ref[0] = jnp.concatenate([jnp.zeros((16, W + chan), bf16), last[: T - 16]], 0)

    def step(i, carry):
        first, second = carry
        y = dot(ax_ref[2 * i], t_ref[0])
        y = y + dot(ax_ref[2 * i + 1], t_ref[1])
        y = y + dot(ax_ref[2 * i + 2], t_ref[2])
        out_ref[i] = y
        ym = y * mask
        return first + colsum(ym), second + colsum(ym * y)

    zero = jnp.zeros((1, W), f32)
    first, second = lax.fori_loop(0, rows // 2, step, (zero, zero))
    st = jnp.concatenate([first, second], 0)
    st_ref[...] = jnp.broadcast_to(st[None], st_ref.shape)


def conv_kernel(level, count, c_ref, stin_ref, bn_ref, t_ref, ax_ref, out_ref, st_ref):
    chan = CHANS[level]
    rows = c_ref.shape[0]
    mean, inv = bn_stats(stin_ref, count, chan)
    gain = bn_ref[2 * level - 2 : 2 * level - 1, :]
    bias = bn_ref[2 * level - 1 : 2 * level, :]
    mask = patch_mask()

    def activate(i, carry):
        put_input(ax_ref, i, gelu((c_ref[i] - mean) * inv * gain + bias) * mask, chan)
        return carry

    lax.fori_loop(0, rows, activate, 0)
    convolve(rows, ax_ref, t_ref, out_ref, st_ref, mask, chan)


def layer_norm(x):
    centered = x - jnp.mean(x, -1, keepdims=True)
    inv = lax.rsqrt(jnp.mean(centered * centered, -1, keepdims=True) + layer_epsilon)
    return centered * inv, inv


def layer_norm_back(dy, s, inv, gain):
    scaled = dy * gain
    inner = scaled - jnp.mean(scaled, -1, keepdims=True)
    return inv * (inner - s * jnp.mean(scaled * s, -1, keepdims=True))


def normed4(count, st_ref, bn_ref, c_ref):
    mean, inv = bn_stats(st_ref, count, C4)
    s = (c_ref[0] - mean) * inv
    return s, s * bn_ref[6:7, :] + bn_ref[7:8, :]


def embed_kernel(count, st_ref, bn_ref, c_ref, wp_ref, pos_ref, vec_ref, a4_ref, x0_ref, n1_ref):
    def vec(name):
        return vec_ref[VEC[name] : VEC[name] + 1, :]

    mask = patch_mask()
    _, y4 = normed4(count, st_ref, bn_ref, c_ref)
    a4_ref[...] = (gelu(y4) * mask).astype(bf16)
    x0 = (dot(a4_ref[...], wp_ref[...]) + vec("proj_bias")) * mask + pos_ref[...]
    x0_ref[...] = x0
    s1, _ = layer_norm(x0)
    n1_ref[...] = (s1 * vec("norm1_gain") + vec("norm1_bias")).astype(bf16)


def block_kernel(
    count,
    st_ref,
    bn_ref,
    n1_hbm,
    vec_hbm,
    x0_hbm,
    a4_hbm,
    wp_hbm,
    c_hbm,
    g_ref,
    gr_ref,
    bn4_hbm,
    so_hbm,
    out_hbm,
    gpos_hbm,
    dwp_hbm,
    c_ref,
    wp_ref,
    vec_ref,
    bn4_ref,
    so_ref,
    out_ref,
    gpos_ref,
    dwp_ref,
    wa,
    wu,
    wd,
    wh,
    sems,
    a4,
    x0,
    n1,
    qkv,
    probs,
    mixed,
    n2t,
    pre,
    acc,
    bqkv,
    mixed_f,
    bpre,
    rowbuf,
):
    gr0, gr1 = wu, wd
    fetched = []
    for k, (source, ref) in enumerate(
        ((n1_hbm, n1), (vec_hbm, vec_ref), (x0_hbm, x0), (a4_hbm, a4), (wp_hbm, wp_ref), (c_hbm, c_ref))
    ):
        fetched.append(pltpu.make_async_copy(source, ref, sems.at[24 + k]))
        if k < 2:
            fetched[-1].start()
    copies = []
    for m in range(2):
        for h in range(2):
            lanes = slice(D * h, D * h + D)
            copy = pltpu.make_async_copy(
                g_ref.at[:, m, :, lanes], wa.at[m, :, :, lanes], sems.at[35 + 2 * m + h]
            )
            copy.start()
            copies.append(copy)
    for k, (ref, at, size) in enumerate(
        ((wu, 1536, 1536), (wd, 3072, 1536), (wh, 4608, 512))
    ):
        for m in range(2):
            copy = pltpu.make_async_copy(
                g_ref.at[:, m, :, at : at + size], ref.at[m], sems.at[2 * k + m]
            )
            copy.start()
            copies.append(copy)
        if k == 0:
            for copy in fetched[2:]:
                copy.start()

    def send_out(grad, slot):
        out = []
        lanes = slice(1536 * slot, 1536 * slot + 1536)
        for m in range(2):
            for z in range(4):
                copy = pltpu.make_async_copy(
                    grad.at[m, 4 * z : 4 * z + 4],
                    gr_ref.at[:, m, z, :, lanes],
                    sems.at[8 + 8 * slot + 4 * m + z],
                )
                copy.start()
                out.append(copy)
        return out

    def write(ref, target, k):
        copy = pltpu.make_async_copy(ref, target, sems.at[30 + k])
        copy.start()
        moving.append(copy)

    def vec(name):
        return vec_ref[VEC[name] : VEC[name] + 1, :]

    mask = patch_mask()
    valid = token_mask()
    out_row = lax.broadcasted_iota(jnp.int32, (32, 1), 0)
    out_ref[...] = jnp.zeros_like(out_ref)
    key = lax.broadcasted_iota(jnp.int32, (1, T), 1)
    key_bias = jnp.where(((key & 15) < SIDE) | (key == SIDE), 0.0, -1e30)

    for copy in fetched[:2]:
        copy.wait()

    def tile(ref, m, at, size=256):
        return ref[m, :, :, pl.ds(at, size)].reshape(D, size)

    for part in range(9):
        if part % 3 == 0:
            copies[part // 3].wait()
        y = dot(n1[...], tile(wa, part // 6, 256 * (part % 6)))
        lanes = slice(256 * (part % 3), 256 * (part % 3) + 256)
        if part < 3:
            y = y + vec("query_bias")[:, lanes]
        elif part >= 6:
            y = y + vec("value_bias")[:, lanes]
        qkv[:, 256 * part : 256 * part + 256] = y.astype(bf16)
    scale = HEAD_DIM**-0.5

    def attend(pair, carry):
        at = pl.multiple_of(pair * 128, 128)
        q = qkv[:, pl.ds(at, 128)] * bf16(scale)
        k = qkv[:, pl.ds(at + D, 128)]
        v = qkv[:, pl.ds(at + 2 * D, 128)]
        out = []
        for h in range(2):
            lanes = slice(64 * h, 64 * h + 64)
            scores = dot_nt(q[:, lanes], k[:, lanes]) + key_bias
            e = jnp.exp(scores - jnp.max(scores, -1, keepdims=True))
            p = e * (1.0 / jnp.sum(e, -1, keepdims=True))
            probs[2 * pair + h] = p
            out.append(dot(p.astype(bf16), v[:, lanes]))
        out = jnp.concatenate(out, 1)
        mixed[:, pl.ds(at, 128)] = out.astype(bf16)
        mixed_f[:, pl.ds(at, 128)] = out
        return carry

    lax.fori_loop(0, HEADS // 2, attend, 0, unroll=6)
    for copy in fetched[2:]:
        copy.wait()
    copies[3].wait()
    att = [dot_nt(mixed[...], wa[1, :, :, D : 2 * D].reshape(D, D))]
    x1 = x0[...] + att[0] + vec("out_bias")
    mean_x1 = colsum(x1 * valid) / TOK
    s2, i2 = layer_norm(x1)
    n2 = (s2 * vec("norm2_gain") + vec("norm2_bias")).astype(bf16)
    n2t[...] = n2.T
    copies[4].wait()
    copies[5].wait()
    bias = [jnp.concatenate([vec_ref[r : r + 1, :], vec_ref[r + 1 : r + 2, :]], 1) for r in (12, 14)]
    rowbuf[0:1, :] = bias[0]
    rowbuf[8:9, :] = bias[1]

    def place(k):
        m = (k >= 6).astype(jnp.int32)
        return m, pl.multiple_of(8 * m, 8), pl.multiple_of((k - 6 * m) * 256, 256)

    def up(k, carry):
        m, row, at = place(k)
        y = dot(n2, tile(wu, m, at)) + rowbuf[pl.ds(row, 8), pl.ds(at, 256)][0:1]
        t = jnp.tanh(GELU_A * (y + GELU_B * y * y * y))
        half = 0.5 + 0.5 * t
        h = (y * half).astype(bf16).astype(f32) * valid
        rowbuf[pl.ds(16 + row, 8), pl.ds(at, 256)] = jnp.broadcast_to(colsum(h), (8, 256))
        inner = GELU_A + (3.0 * GELU_A * GELU_B) * y * y
        pre[m, :, pl.ds(at, 256)] = (half + 0.5 * y * (1.0 - t * t) * inner) * valid
        return carry

    lax.fori_loop(0, 12, up, 0, unroll=4)
    for m in range(2):
        for k in range(2):
            row = OUT_HIDDEN + 2 * m + k
            out_ref[row : row + 1, :] = rowbuf[16 + 8 * m : 17 + 8 * m, D * k : D * k + D]
    copies[6].wait()
    copies[7].wait()
    hs = jnp.concatenate([out_ref[OUT_HIDDEN + k : OUT_HIDDEN + k + 1, :] for k in range(4)], 1) / TOK
    high = hs.astype(bf16)
    low = (hs - high.astype(f32)).astype(bf16)
    out = jnp.zeros((1, D), f32)
    for m in range(2):
        lanes = slice(1536 * m, 1536 * m + 1536)
        both = jnp.concatenate(
            [jnp.broadcast_to(high[:, lanes], (8, 1536)), jnp.broadcast_to(low[:, lanes], (8, 1536))], 0
        )
        y = dot_nt(both, wd[m].reshape(D, 1536))
        out = out + y[0:1] + y[8:9]
    pooled = mean_x1 + out + vec("mlp_bias")
    s3, i3 = layer_norm(pooled)
    final = (s3 * vec("final_gain") + vec("final_bias")).astype(bf16)
    copies[8].wait()
    copies[9].wait()
    wide = jnp.broadcast_to(final, (16, D))
    logits = jnp.concatenate([dot(wide, wh[m].reshape(D, 512))[0:1] for m in range(2)], 1)
    lane = lax.broadcasted_iota(jnp.int32, (1, 1024), 1)
    real = (lane & 511) < CLASSES // 2
    def pair(row):
        return jnp.concatenate([vec_ref[row : row + 1, 0:512], vec_ref[row + 1 : row + 2, 0:512]], 1)

    logits = jnp.where(real, logits + pair(VEC_HEAD), -1e30)
    top = jnp.max(logits, -1, keepdims=True)
    log_probs = logits - top - jnp.log(jnp.sum(jnp.exp(logits - top), -1, keepdims=True))
    aim = pair(VEC_AIM)
    loss = -jnp.sum(jnp.where(real, aim * log_probs, 0.0), keepdims=True)
    out_ref[...] = jnp.where(out_row >= OUT_LOSS, jnp.broadcast_to(loss, out_ref.shape), out_ref[...])
    back_logits = jnp.where(real, jnp.exp(log_probs) - aim, 0.0).astype(bf16)
    for m in range(2):
        row = OUT_HEAD + m
        out_ref[row : row + 1, 0:512] = back_logits[:, 512 * m : 512 * m + 512].astype(f32)
    out_ref[OUT_FINAL : OUT_FINAL + 1, :] = final.astype(f32)
    wide = jnp.broadcast_to(back_logits, (16, 1024))
    back_final = (
        dot_nt(wide[:, 0:512], wh[0].reshape(D, 512)) + dot_nt(wide[:, 512:], wh[1].reshape(D, 512))
    )[0:1]
    def put(name, value):
        out_ref[VEC[name] : VEC[name] + 1, :] = value

    put("final_gain", back_final * s3)
    put("final_bias", back_final)
    back2 = layer_norm_back(back_final, s3, i3, vec("final_gain")) / TOK
    back_out = back2.astype(bf16)
    out_ref[OUT_BACK : OUT_BACK + 1, :] = back_out.astype(f32)
    put("mlp_bias", back_out.astype(f32) * TOK)
    wide = jnp.broadcast_to(back_out, (16, D))
    for m in range(2):
        for k in range(6):
            at = 256 * k
            rowbuf[8 * m : 8 * m + 1, at : at + 256] = dot(wide, tile(wd, m, at))[0:1]

    def down(k, carry):
        m, row, at = place(k)
        back = rowbuf[pl.ds(row, 8), pl.ds(at, 256)][0:1]
        bp = (back * pre[m, :, pl.ds(at, 256)]).astype(bf16)
        rowbuf[pl.ds(16 + row, 8), pl.ds(at, 256)] = jnp.broadcast_to(
            colsum(bp.astype(f32)), (8, 256)
        )
        bpre[m, :, pl.ds(at, 256)] = bp
        grad = dot(n2t[...], bp)
        gr1[m, :, :, pl.ds(at, 256)] = grad.astype(bf16).reshape(16, 48, 256)
        return carry

    lax.fori_loop(0, 12, down, 0, unroll=4)
    for m in range(2):
        for k in range(2):
            row = VEC_HIDDEN + 2 * m + k
            out_ref[row : row + 1, :] = rowbuf[16 + 8 * m : 17 + 8 * m, D * k : D * k + D]
    moving = send_out(gr1, 1)
    back_n2 = dot_nt(bpre[0], wu[0].reshape(D, 1536)) + dot_nt(bpre[1], wu[1].reshape(D, 1536))
    put("norm2_gain", colsum(back_n2 * s2))
    put("norm2_bias", colsum(back_n2))
    back1 = back2 * valid + layer_norm_back(back_n2, s2, i2, vec("norm2_gain"))
    back_att = back1.astype(bf16)
    put("out_bias", colsum(back_att.astype(f32)))
    back_att_t = back_att.T
    for k in range(3):
        lanes = slice(256 * k, 256 * k + 256)
        grad = dot(back_att_t, mixed[:, lanes])
        gr0[1, :, :, D + 256 * k : D + 256 * k + 256] = grad.astype(bf16).reshape(16, 48, 256)
    acc[...] = dot(back_att, wa[1, :, :, D : 2 * D].reshape(D, D))

    def attend_back(pair, carry):
        at = pl.multiple_of(pair * 128, 128)
        q = qkv[:, pl.ds(at, 128)]
        k = qkv[:, pl.ds(at + D, 128)]
        v = qkv[:, pl.ds(at + 2 * D, 128)]
        bm = acc[:, pl.ds(at, 128)].astype(bf16)
        bm_mixed = bm.astype(f32) * mixed_f[:, pl.ds(at, 128)]
        bq, bk, bv = [], [], []
        for h in range(2):
            lanes = slice(64 * h, 64 * h + 64)
            p = probs[2 * pair + h]
            bp = dot_nt(bm[:, lanes], v[:, lanes])
            bv.append(dot_tn(p.astype(bf16), bm[:, lanes]))
            inner = jnp.sum(bm_mixed[:, lanes], -1, keepdims=True)
            bs = (p * (bp - inner)).astype(bf16)
            bq.append(dot(bs, k[:, lanes]) * scale)
            bk.append(dot_tn(bs, q[:, lanes]) * scale)
        bqkv[:, pl.ds(at, 128)] = jnp.concatenate(bq, 1).astype(bf16)
        bqkv[:, pl.ds(at + D, 128)] = jnp.concatenate(bk, 1).astype(bf16)
        bqkv[:, pl.ds(at + 2 * D, 128)] = jnp.concatenate(bv, 1).astype(bf16)
        return carry

    lax.fori_loop(0, HEADS // 2, attend_back, 0, unroll=6)
    put("query_bias", colsum(bqkv[:, 0:D].astype(f32)))
    put("value_bias", colsum(bqkv[:, 2 * D :].astype(f32)))
    n1t = n1[...].T
    for part in range(9):
        m, at = part // 6, 256 * (part % 6)
        b = bqkv[:, 256 * part : 256 * part + 256]
        gr0[m, :, :, at : at + 256] = dot(n1t, b).astype(bf16).reshape(16, 48, 256)
    moving += send_out(gr0, 0)
    back_n1 = dot_nt(bqkv[:, 0:1536], wa[0].reshape(D, 1536))
    back_n1 = back_n1 + dot_nt(bqkv[:, 1536:], wa[1, :, :, 0:D].reshape(D, D))
    s1, i1 = layer_norm(x0[...])
    put("norm1_gain", colsum(back_n1 * s1))
    put("norm1_bias", colsum(back_n1))
    back0 = back1 + layer_norm_back(back_n1, s1, i1, vec("norm1_gain"))
    gpos_ref[...] = back0
    write(gpos_ref, gpos_hbm, 0)
    back_patch = (back0 * mask).astype(bf16)
    put("proj_bias", colsum(back_patch.astype(f32)))
    dwp_ref[...] = dot_tn(a4[...], back_patch)
    write(dwp_ref, dwp_hbm, 1)
    s4, y4 = normed4(count, st_ref, bn_ref, c_ref)
    bn4 = dot_nt(back_patch, wp_ref[...]) * gelu_slope(y4) * mask
    bn4_ref[0] = bn4
    write(bn4_ref, bn4_hbm, 2)
    st = jnp.concatenate([colsum(bn4), colsum(bn4 * s4)], 0)
    so_ref[...] = jnp.broadcast_to(st[None], so_ref.shape)
    write(so_ref, so_hbm, 3)
    out_ref[OUT_SUMS : OUT_SUMS + 1, :] = jnp.concatenate([st[0:1], st[1:2]], 1)
    write(out_ref, out_hbm, 4)
    for copy in moving:
        copy.wait()


def conv_back_kernel(
    level,
    count,
    count_in,
    back_ref,
    tot_ref,
    c_ref,
    st_ref,
    t_ref,
    cin_ref,
    stin_ref,
    bn_ref,
    g,
    backin_ref,
    so_ref,
    ss_ref,
):
    finish_level(level, count, back_ref, tot_ref, c_ref, st_ref, bn_ref, g)
    mean, inv = bn_stats(stin_ref, count_in, CHANS[level - 1])

    def normed(q):
        return (cin_ref[q] - mean) * inv

    def keep(q, y):
        backin_ref[q] = y

    st = back_through(level, g, t_ref, bn_ref, normed, keep)
    ss_ref[...] = st
    so_ref[...] = jnp.broadcast_to(st[None], so_ref.shape)


def finish_level(level, count, back_ref, tot_ref, c_ref, st_ref, bn_ref, g):
    chan = CHANS[level]
    rows = back_ref.shape[0]
    mask = patch_mask()
    mean, inv = bn_stats(st_ref, count, chan)
    gain = bn_ref[2 * level - 2 : 2 * level - 1, :]
    tot = fold_phases(jnp.sum(tot_ref[:, 0:2, :], 0), chan) / count

    def finish(i, carry):
        s = (c_ref[i] - mean) * inv
        g[i] = (inv * gain * (back_ref[i] - tot[0:1] - s * tot[1:2]) * mask).astype(bf16)
        return carry

    lax.fori_loop(0, rows, finish, 0)
    head = g[0]
    g[rows] = jnp.concatenate([head[16:], jnp.zeros((16, W), bf16)], 0)


def kernel_grad(level, ax_ref, g, dw_ref, dt):
    chan, chan_in = CHANS[level], CHANS[level - 1]
    rows = g.shape[0] - 1
    dt[...] = jnp.zeros_like(dt)

    def weights(i, carry):
        for tap in range(3):
            dt[tap] += dot_tn(ax_ref[2 * i + tap], g[i])
        return carry

    lax.fori_loop(0, rows, weights, 0)
    for tap in range(3):
        base = tap * 3 * chan_in
        for j in range(W // chan):
            for k in range(dw_ref.shape[0]):
                width = min(128, chan - 128 * k)
                cols = slice(j * chan + 128 * k, j * chan + 128 * k + width)
                if j == 0:
                    dw_ref[k, base : base + chan_in, 0:width] = dt[tap, W : W + chan_in, cols]
                    dw_ref[k, base + chan_in : base + 3 * chan_in, 0:width] = dt[
                        tap, 0 : 2 * chan_in, cols
                    ]
                else:
                    at = (2 * j - 1) * chan_in
                    dw_ref[k, base : base + 3 * chan_in, 0:width] += dt[
                        tap, at : at + 3 * chan_in, cols
                    ]


def back_through(level, g, t_ref, bn_ref, normed, keep):
    chan_in = CHANS[level - 1]
    rows = g.shape[0] - 1
    mask = patch_mask()
    gain = bn_ref[2 * level - 4 : 2 * level - 3, :]
    bias = bn_ref[2 * level - 3 : 2 * level - 2, :]

    def through(q, p, carry):
        first, second = carry
        left = pltpu.roll(p[:, W:], T - 1, 0)
        p = jnp.concatenate([p[:, 0 : W - chan_in], p[:, W - chan_in : W] + left], 1)
        s = normed(q)
        y = p * gelu_slope(s * gain + bias) * mask
        keep(q, y)
        return first + colsum(y), second + colsum(y * s)

    def back(i, carry):
        carry = through(2 * i, dot_nt(g[i], t_ref[1]), carry)
        p = dot_nt(g[i], t_ref[2]) + dot_nt(g[i + 1], t_ref[0])
        return through(2 * i + 1, p, carry)

    zero = jnp.zeros((1, W), f32)
    first, second = lax.fori_loop(0, rows, back, (zero, zero))
    return jnp.concatenate([first, second], 0)


LATE_W2 = 9 * C1 * C2 // 128
LATE_SUMS = 32
LATE_F = LATE_SUMS + 4 * 6


def late_sizes(n):
    kernel, exact = -(-LATE_W2 // n), -(-LATE_F // n)
    return kernel, exact, up16(kernel + 2 * exact)


def late_rows(w, f, rows):
    high = f.astype(bf16).astype(f32)
    fill = jnp.zeros((rows - w.shape[0] - 2 * f.shape[0], 128), f32)
    return jnp.concatenate([w, high, f - high, fill], 0).astype(bf16)


def conv2_back_kernel(
    count,
    count_in,
    back_ref,
    tot_ref,
    c_ref,
    st_ref,
    ax_ref,
    t_ref,
    xk_ref,
    gram_ref,
    w1_ref,
    t1_ref,
    bn_ref,
    ss2_ref,
    ss3_ref,
    ss4_ref,
    late_ref,
    dw,
    g,
    dt,
    dt1,
    late,
    exact,
):
    finish_level(2, count, back_ref, tot_ref, c_ref, st_ref, bn_ref, g)
    kernel_grad(2, ax_ref, g, dw, dt)
    gram, cross, mean, inv = level1_stats(gram_ref, w1_ref, count_in)
    mean, inv = tile_lanes(mean, C1), tile_lanes(inv, C1)
    weights = t1_ref[...]
    dt1[...] = jnp.zeros_like(dt1)

    def normed(q):
        return (dot(xk_ref[q], weights) - mean) * inv

    def keep(q, y):
        dt1[...] += dot_tn(xk_ref[q], y.astype(bf16))

    st = back_through(2, g, t_ref, bn_ref, normed, keep)
    late[...] = jnp.zeros_like(late)
    exact[...] = jnp.zeros_like(exact)
    q = 9 * C1 // 4
    wide = jnp.concatenate([dw[0, pl.ds(k, q, stride=4), :][:, 0:C2] for k in range(4)], 1)
    for k in range(3):
        late[pl.ds(k, q, stride=3), :] = wide[:, 128 * k : 128 * k + 128]
    for tap in range(3):
        base = 9 * tap
        for j in range(8):
            cols = slice(j * C1, (j + 1) * C1)
            if j == 0:
                exact[base : base + 3, 0:C1] = dt1[tap * 64 + 48 : tap * 64 + 51, cols]
                exact[base + 3 : base + 9, 0:C1] = dt1[tap * 64 : tap * 64 + 6, cols]
            else:
                at = tap * 64 + 6 * j - 3
                exact[base : base + 9, 0:C1] += dt1[at : at + 9, cols]
    ss4 = jnp.concatenate(
        [ss4_ref[OUT_SUMS : OUT_SUMS + 1, 0:W], ss4_ref[OUT_SUMS : OUT_SUMS + 1, W:]], 0
    )
    for level, ss in enumerate((st, ss2_ref[...], ss3_ref[...], ss4)):
        for which in range(2):
            for k in range(3):
                row = LATE_SUMS + 6 * level + 3 * which + k
                exact[row : row + 1, :] = ss[which : which + 1, 128 * k : 128 * k + 128]
    kernel, share, rows = late_sizes(late_ref.shape[0])

    def emit(d, carry):
        w = late[pl.ds(kernel * d, kernel), :]
        late_ref[d] = late_rows(w, exact[pl.ds(share * d, share), :], rows)
        return carry

    lax.fori_loop(0, late_ref.shape[0], emit, 0)


def early_kernel(
    parts,
    mp,
    stem_len,
    small_len,
    rows_stem,
    rows_small,
    at_ref,
    dw3_ref,
    dw4_ref,
    dwp_ref,
    gv_ref,
    gpos_ref,
    *refs,
):
    outs = refs[:parts]
    frame, table, vecs = refs[parts:]
    if outs[0].shape[1] > rows_stem + rows_small:
        vecs[...] = jnp.zeros_like(vecs)
        base = pl.multiple_of(24 * at_ref[0], 8)
        for index, ref in enumerate(outs):
            first = at_ref[index] == 0
            hs = [gv_ref[OUT_HIDDEN + k : OUT_HIDDEN + k + 1, :] for k in range(4)]
            hs = jnp.concatenate([jnp.where(first, hs[0], hs[2]), jnp.where(first, hs[1], hs[3])], 1)
            bl = [gv_ref[OUT_HEAD + k : OUT_HEAD + k + 1, 0:512] for k in range(2)]
            bl = jnp.where(first, bl[0], bl[1])
            rows = [hs[:, 128 * k : 128 * k + 128] for k in range(12)]
            rows += [bl[:, 128 * k : 128 * k + 128] for k in range(4)]
            vecs[pl.ds(base, 16), :] = jnp.concatenate(rows, 0)
            for d in range(16):
                lanes = slice(48 * d, 48 * d + 48)
                fill = jnp.zeros((1, 16), f32)
                row = jnp.concatenate(
                    [
                        gv_ref[OUT_BACK : OUT_BACK + 1, lanes],
                        fill,
                        gv_ref[OUT_FINAL : OUT_FINAL + 1, lanes],
                        fill,
                    ],
                    1,
                )
                vecs[pl.ds(base + 16, 8), :] = jnp.broadcast_to(row, (8, 128))
                ref[d, rows_stem + rows_small :, :] = vecs[...].astype(bf16)
    frame[0:ROW_W3, :] = jnp.zeros((ROW_W3, 128), f32)
    frame[STEM_ROWS:, :] = jnp.zeros((frame.shape[0] - STEM_ROWS, 128), f32)
    q = 9 * C2 // 2
    wide = jnp.concatenate(
        [
            jnp.concatenate(
                [
                    dw3_ref[0, pl.ds(k, q, stride=2), :],
                    dw3_ref[1, pl.ds(k, q, stride=2), :][:, 0 : C3 - 128],
                ],
                1,
            )
            for k in range(2)
        ],
        1,
    )
    for k in range(3):
        frame[pl.ds(ROW_W3 + k, q, stride=3), :] = wide[:, 128 * k : 128 * k + 128]
    for k in range(3):
        frame[pl.ds(ROW_W4 + k, 9 * C3, stride=3), :] = dw4_ref[k]
    for k in range(6):
        frame[pl.ds(ROW_WP + k, C4, stride=6), :] = dwp_ref[:, 128 * k : 128 * k + 128]
    table[0:12, :] = jnp.zeros((12, 128), f32)
    table[SMALL_ROWS:, :] = jnp.zeros((table.shape[0] - SMALL_ROWS, 128), f32)
    for k in range(6):
        lanes = slice(128 * k, 128 * k + 128)
        for name, index in VEC.items():
            row = SMALL_AT[name] + k
            table[row : row + 1, :] = gv_ref[index : index + 1, lanes]
        for h in range(4):
            row = SMALL_AT["hidden_bias"] + 6 * h + k
            table[row : row + 1, :] = gv_ref[VEC_HIDDEN + h : VEC_HIDDEN + h + 1, lanes]
        at = SMALL_AT["position"] + k
        for r in range(SIDE):
            table[pl.ds(at + 6 * (1 + SIDE * r), SIDE, stride=6), :] = gpos_ref[
                16 * r : 16 * r + SIDE, lanes
            ]
        table[at : at + 1, :] = gpos_ref[SIDE : SIDE + 1, lanes]
        row = SMALL_AT["class_token"] + k
        table[row : row + 1, :] = gpos_ref[SIDE : SIDE + 1, lanes]
    line = jnp.concatenate(
        [
            gv_ref[OUT_HEAD : OUT_HEAD + 1, 0:500],
            gv_ref[OUT_HEAD + 1 : OUT_HEAD + 2, 0:500],
            jnp.zeros((1, 24), f32),
        ],
        1,
    )
    row = SMALL_AT["head_bias"]
    for k in range(8):
        table[row + k : row + k + 1, :] = line[:, 128 * k : 128 * k + 128]
    for index, ref in enumerate(outs):
        mv = at_ref[index]

        def take(d, carry):
            owner = d * mp + mv
            a = (owner * stem_len + STEM_SHIFT) // 128
            ref[d, 0:rows_stem, :] = frame[pl.ds(a, rows_stem), :].astype(bf16)
            b = (owner * small_len + SMALL_SHIFT) // 128
            ref[d, rows_stem : rows_stem + rows_small, :] = table[pl.ds(b, rows_small), :].astype(bf16)
            return carry

        lax.fori_loop(0, ref.shape[0], take, 0)


def unshift_lanes(x, s, length):
    lane = lax.broadcasted_iota(jnp.int32, x.shape, 1)
    row = lax.broadcasted_iota(jnp.int32, x.shape, 0)
    moved = pltpu.roll(x, 128 - s, 1)
    after = pltpu.roll(moved, x.shape[0] - 1, 0)
    y = jnp.where(lane < 128 - s, moved, after)
    return jnp.where(row * 128 + lane < length, y, 0.0)


def unpack_kernel(stem_len, small_len, at_ref, x_ref, stem_ref, small_ref, sq_ref):
    rows = stem_ref.shape[0]
    end = rows + small_ref.shape[0]
    total = jnp.sum(x_ref[:, 0:end, :].astype(f32), 0)
    stem = unshift_lanes(total[0:rows], at_ref[0], stem_len)
    small = unshift_lanes(total[rows:], at_ref[1], small_len)
    stem_ref[...] = stem
    small_ref[...] = small
    sq_ref[...] = colsum(stem * stem) + colsum(small * small)


def norm_kernel(parts, *refs):
    sq_ref, sq1_ref, down_ref, head_ref, loss_ref, g0_ref, g1_ref, out_ref = refs[parts:]
    total = sum(ref[...].astype(f32) for ref in refs[:parts])
    half = g0_ref.shape[1]
    g0, g1 = total[:, 0:half], total[:, half:]
    g0_ref[...] = g0
    g1_ref[...] = g1
    squares = jnp.sum(g0 * g0 + g1 * g1 + down_ref[...] * down_ref[...], keepdims=True)
    squares = squares + jnp.sum(head_ref[...] * head_ref[...], keepdims=True)
    squares = squares + jnp.sum(sq_ref[...], keepdims=True)
    squares = squares + sq1_ref[0:1, 0:1] * (1.0 / out_ref.shape[0])
    lane = lax.broadcasted_iota(jnp.int32, (1, 128), 1)
    line = jnp.where(lane == 0, squares, loss_ref[OUT_LOSS : OUT_LOSS + 1, 0:128])
    out_ref[...] = jnp.broadcast_to(line[None], out_ref.shape)


def factor_kernel(x_ref, out_ref):
    total = jnp.sum(x_ref[...], 0)
    lane = lax.broadcasted_iota(jnp.int32, (1, 128), 1)
    norm = jnp.sqrt(jnp.sum(jnp.where(lane == 0, total, 0.0), keepdims=True))
    loss = jnp.sum(jnp.where(lane == 1, total, 0.0), keepdims=True)
    row = lax.broadcasted_iota(jnp.int32, (8, 128), 0)
    factor = jnp.minimum(1.0, clip_norm / norm)
    out_ref[...] = jnp.where(row == 0, loss, jnp.where(row == 1, norm, factor))


def late_kernel(x_ref, out_ref):
    kernel, share, rows = late_sizes(x_ref.shape[0])
    total = jnp.sum(x_ref[...].astype(f32), 0)
    exact = total[kernel : kernel + share] + total[kernel + share : kernel + 2 * share]
    out_ref[...] = jnp.broadcast_to(late_rows(total[0:kernel], exact, rows)[None], out_ref.shape)


def last_kernel(
    counts,
    stem_len,
    small_len,
    at_ref,
    x_ref,
    gram_ref,
    w1_ref,
    bn_ref,
    stem_ref,
    small_ref,
    stem_out,
    small_out,
    sq_ref,
    late,
    frame,
    table,
):
    frame[...] = jnp.zeros_like(frame)
    table[...] = jnp.zeros_like(table)
    kernel, share, _ = late_sizes(x_ref.shape[0])

    def collect(d, carry):
        x = x_ref[d].astype(f32)
        frame[pl.ds(ROW_W2 + kernel * d, kernel), :] = x[0:kernel]
        exact = x[kernel : kernel + share] + x[kernel + share : kernel + 2 * share]
        late[pl.ds(share * d, share), :] = exact
        return carry

    lax.fori_loop(0, x_ref.shape[0], collect, 0)
    line = [[jnp.zeros((1, SMALL_SHIFT), f32)], []]
    for level in range(4):
        chan = CHANS[level + 1]
        rows = []
        for which in range(2):
            row = LATE_SUMS + 6 * level + 3 * which
            rows.append(jnp.concatenate([late[row + k : row + k + 1, :] for k in range(3)], 1))
        both = fold_phases(jnp.concatenate(rows, 0), chan)
        line[0].append(both[1:2, 0:chan])
        line[1].append(both[0:1, 0:chan])
        if level == 0:
            tot = both[:, 0:128] / counts
    line = jnp.concatenate(line[0] + line[1], 1)
    for k in range(12):
        table[k : k + 1, :] = line[:, 128 * k : 128 * k + 128]
    gram, cross, mean, inv = level1_stats(gram_ref, w1_ref, counts)
    ones = gram[:, 27:28]
    grad = late[0:LATE_SUMS, :] - ones * tot[0:1] - (cross - ones * mean) * inv * tot[1:2]
    grad = grad * (inv * bn_ref[0:1, 0:128])
    line = [jnp.zeros((1, STEM_SHIFT), f32)] + [grad[k : k + 1, 0:C1] for k in range(27)]
    line = jnp.concatenate(line, 1)
    for k in range(ROW_W2):
        frame[k : k + 1, :] = line[:, 128 * k : 128 * k + 128]
    squares = jnp.sum(frame[0:ROW_W3, :] * frame[0:ROW_W3, :], keepdims=True)
    squares = squares + jnp.sum(table[0:12, :] * table[0:12, :], keepdims=True)
    sq_ref[...] = jnp.broadcast_to(squares, sq_ref.shape)
    part = frame[pl.ds(at_ref[2], stem_ref.shape[0]), :]
    stem_out[...] = stem_ref[...] + unshift_lanes(part, at_ref[0], stem_len)
    part = table[pl.ds(at_ref[3], small_ref.shape[0]), :]
    small_out[...] = small_ref[...] + unshift_lanes(part, at_ref[1], small_len)


def call(kernel, outs, *args, scratch=(), smem=0, hbm=(), load=(), store=(), hbm_out=(), limit=32):
    def space(index, free):
        if index in free:
            return pl.BlockSpec(memory_space=pltpu.HBM)
        return pl.BlockSpec(memory_space=pltpu.VMEM)

    def shape(index):
        where = pltpu.HBM if index in (*hbm_out, *store) else jax.ShapeDtypeStruct
        return where(*outs[index])

    args = [
        pltpu.with_memory_space_constraint(arg, pltpu.HBM) if index in (*hbm, *load) else arg
        for index, arg in enumerate(args)
    ]
    count = len(args)
    moved = [jax.ShapeDtypeStruct(args[k].shape, args[k].dtype) for k in load]
    moved += [jax.ShapeDtypeStruct(*outs[k]) for k in store]

    def body(*refs):
        refs = list(refs)
        if not moved:
            return kernel(*refs)
        buffers, sems = refs[-1 - len(moved) : -1], refs[-1]
        refs = refs[: -1 - len(moved)]
        copies = []
        for k, index in enumerate(load):
            copies.append(pltpu.make_async_copy(refs[index], buffers[k], sems.at[k]))
            copies[-1].start()
            refs[index] = buffers[k]
        for copy in copies:
            copy.wait()
        targets = []
        for k, index in enumerate(store):
            targets.append((buffers[len(load) + k], refs[count + index], sems.at[len(load) + k]))
            refs[count + index] = buffers[len(load) + k]
        kernel(*refs)
        copies = [pltpu.make_async_copy(*target) for target in targets]
        for copy in copies:
            copy.start()
        for copy in copies:
            copy.wait()

    extra = [pltpu.VMEM(x.shape, x.dtype) for x in moved]
    if moved:
        extra.append(pltpu.SemaphoreType.DMA((len(moved),)))
    specs = [pl.BlockSpec(memory_space=pltpu.SMEM)] * smem
    specs += [space(index, (*hbm, *load)) for index in range(smem, count)]
    return pl.pallas_call(
        body,
        out_shape=[shape(index) for index in range(len(outs))],
        in_specs=specs,
        out_specs=[space(index, (*hbm_out, *store)) for index in range(len(outs))],
        scratch_shapes=[*scratch, *extra],
        compiler_params=pltpu.CompilerParams(vmem_limit_bytes=limit * 1024 * 1024),
    )(*args)


def adam_step(weight, first, second, grad, factor, rate):
    grad = grad * factor
    first = beta_one * first + (1.0 - beta_one) * grad
    second = beta_two * second + (1.0 - beta_two) * grad * grad
    first_fixed = first / (1.0 - beta_one**STEP)
    second_fixed = second / (1.0 - beta_two**STEP)
    return (
        weight
        - rate * (first_fixed / (jnp.sqrt(second_fixed) + adam_epsilon) + decay_rate * weight),
        first,
        second,
    )


def local(
    pixels,
    labels,
    stem,
    stem_first,
    stem_second,
    small,
    small_first,
    small_second,
    block,
    block_first,
    block_second,
    head,
    head_first,
    head_second,
):
    dp, mp = lax.axis_size("dp"), lax.axis_size("mp")
    n = dp * mp
    me, mine = lax.axis_index("dp"), lax.axis_index("mp")
    owner = me * mp + mine
    stem_len, small_len = stem.shape[0], small.shape[0]
    rows_stem = up16(-(-(stem_len + 127) // 128))
    rows_small = up16(-(-(small_len + 127) // 128))
    rows = rows_stem + rows_small
    everyone = ("dp", "mp")
    fast = (dp, mp) == (16, 2)

    def share(x):
        return lax.all_to_all(x, everyone, 0, 0)

    part = FF // mp
    cls = CLASSES // mp
    cls_pad = 512 // (mp // 2)
    packed = jnp.concatenate(
        [block[0], block[1], block[2], jnp.pad(head, ((0, 0), (0, cls_pad - cls)))], 1
    ).astype(bf16)
    packed, stem, small = lax.optimization_barrier((packed, stem, small))
    gathered = lax.all_gather(packed, everyone, axis=0)
    stem_at, small_at = owner * stem_len + STEM_SHIFT, owner * small_len + SMALL_SHIFT
    at = jnp.stack(
        [
            stem_at % 128,
            small_at % 128,
            jnp.minimum(stem_at // 128, ROW_W3),
            jnp.minimum(small_at // 128, 16),
        ]
    ).astype(jnp.int32)
    (piece,) = call(
        pack_kernel,
        [((rows, 128), bf16)],
        at,
        jnp.pad(stem, (0, rows_stem * 128 - stem_len)).reshape(rows_stem, 128),
        jnp.pad(small, (0, rows_small * 128 - small_len)).reshape(rows_small, 128),
        smem=1,
        limit=4,
    )

    strip = pixels.reshape(pixels.shape[1], 128)
    strip, piece, at = lax.optimization_barrier((strip, piece, at))
    half = strip.shape[0] // 2
    pairs = [(source, (source + dp - 1) % dp) for source in range(dp)]
    lower = lax.ppermute(strip[:half], "dp", pairs)

    if fast:
        gathered = gathered.reshape(16, 2, 48, packed.shape[1])
    else:
        g = gathered.reshape(dp, mp, D // dp, packed.shape[1])
        g = jnp.transpose(g, (0, 2, 1, 3)).reshape(D, mp, -1)
        slots = [g[:, :, k * part : (k + 1) * part].reshape(D, 2, FF // 2) for k in range(3)]
        top = g[:, :, 3 * part : 3 * part + cls].reshape(D, 2, CLASSES // 2)
        slots.append(jnp.pad(top, ((0, 0), (0, 0), (0, 12))))
        g = jnp.concatenate(slots, 2).reshape(16, 48, 2, -1)
        gathered = jnp.transpose(g, (0, 2, 1, 3))

    if fast:
        planes = [[4 * z + k for k in range(4)] for z in range(4)]
        column = [piece]
        for k in (1, 2, 3):
            pairs = [(source, source ^ (4 * k)) for source in range(dp)]
            column.append(lax.ppermute(piece, "dp", pairs))
        *column, lower = lax.optimization_barrier((*column, lower))
        column = jnp.stack(column, 0)
        column = [column]
        for k in (1, 2, 3):
            pairs = [(source, source ^ k) for source in range(dp)]
            column.append(lax.ppermute(column[0], "dp", pairs))
        column = jnp.stack(column, 0)
        column = column.reshape(dp, rows, 128)
    else:
        column = lax.all_to_all(jnp.broadcast_to(piece[None], (dp, rows, 128)), "dp", 0, 0)
    xk, gram = call(
        image_kernel,
        [((8, T, 192), bf16), ((n, 8, 128), f32)],
        strip[half:],
        lower,
        scratch=[
            pltpu.VMEM((2 * half, 128), f32),
            pltpu.VMEM((16 * half // 3 + 16, 128), f32),
            pltpu.VMEM((17, T, 64), bf16),
        ],
        limit=12,
    )
    gram = share(gram)
    gram, xk, column = lax.optimization_barrier((gram, xk, column))
    if mp == 2:
        swap = [(0, 1), (1, 0)]
        pieces = [column, lax.ppermute(column, "mp", swap)]
        which = jnp.stack([mine, 1 - mine]).astype(jnp.int32)
    else:
        columns = lax.all_gather(column, "mp", axis=0)
        pieces = [columns[k] for k in range(mp)]
        which = jnp.arange(mp, dtype=jnp.int32)
    which = jnp.concatenate([which, labels.reshape(1), me.reshape(1).astype(jnp.int32)])
    frame_rows = (stem_len * n + STEM_SHIFT) // 128 + rows_stem + 16
    table_rows = (small_len * n + SMALL_SHIFT) // 128 + rows_small + 16
    frames = [pltpu.VMEM((frame_rows, 128), f32), pltpu.VMEM((table_rows, 128), f32)]
    w1, t1, t2, t3, t4, wp, bn, vec, pos = call(
        functools.partial(assemble_kernel, fast, len(pieces), mp, stem_len, small_len, rows_stem, rows_small),
        [
            ((32, 128), f32),
            ((192, W), bf16),
            ((3, W + C1, W), bf16),
            ((3, W + C2, W), bf16),
            ((3, W + C3, W), bf16),
            ((C4, D), bf16),
            ((8, W), f32),
            ((24, D), f32),
            ((T, D), f32),
        ],
        which,
        *pieces,
        smem=1,
        store=(1, 2, 3, 4, 5, 7, 8),
        scratch=frames
        + [
            pltpu.VMEM((9 * C1, 128), f32),
            pltpu.VMEM((9 * C2, 128), f32),
            pltpu.VMEM((9 * C2, 128), f32),
            pltpu.VMEM((192, W), f32),
            pltpu.VMEM((W + C1, W), f32),
            pltpu.VMEM((W + C2, W), f32),
        ],
        limit=20,
    )

    positions = SIDE * SIDE * n
    counts = [None, 64.0 * positions, 16.0 * positions, 4.0 * positions, 1.0 * positions]
    ax, conv, st = call(
        functools.partial(conv12_kernel, counts[1]),
        [((9, T, W + C1), bf16), ((4, T, W), f32), ((n, 2, W), f32)],
        xk,
        gram,
        w1,
        t1,
        bn,
        t2,
        load=(3, 5),
        limit=14,
    )
    convs = [None, None, conv]
    stats = [None, None, share(st)]
    inputs = [None, None, ax]
    kernels = [None, t1, t2, t3, t4]
    for level in (3, 4):
        r = 2 ** (4 - level)
        ax, conv, st = call(
            functools.partial(conv_kernel, level - 1, counts[level - 1]),
            [((2 * r + 1, T, W + CHANS[level - 1]), bf16), ((r, T, W), f32), ((n, 2, W), f32)],
            convs[level - 1],
            stats[level - 1],
            bn,
            kernels[level],
            load=(3,),
            store=(0, 1, 2) if level == 4 else (),
            limit=10,
        )
        inputs.append(ax)
        convs.append(conv)
        stats.append(share(st))

    a4, x0, n1 = call(
        functools.partial(embed_kernel, counts[4]),
        [((T, C4), bf16), ((T, D), f32), ((T, D), bf16)],
        stats[4],
        bn,
        convs[4],
        wp,
        pos,
        vec,
        load=(2, 3, 4, 5),
        store=(0, 1, 2),
        limit=12,
    )
    outs = call(
        functools.partial(block_kernel, counts[4]),
        [
            ((4, 2, 4, 48, FF), bf16),
            ((1, T, W), f32),
            ((n, 2, W), f32),
            ((32, D), f32),
            ((T, D), f32),
            ((C4, D), f32),
        ],
        stats[4],
        bn,
        n1,
        vec,
        x0,
        a4,
        wp,
        convs[4],
        gathered,
        hbm=(2, 3, 4, 5, 6, 7, 8),
        hbm_out=(0, 1, 2, 3, 4, 5),
        limit=44,
        scratch=[
            pltpu.VMEM((1, T, W), f32),
            pltpu.VMEM((C4, D), bf16),
            pltpu.VMEM((24, D), f32),
            pltpu.VMEM((1, T, W), f32),
            pltpu.VMEM((n, 2, W), f32),
            pltpu.VMEM((32, D), f32),
            pltpu.VMEM((T, D), f32),
            pltpu.VMEM((C4, D), f32),
            pltpu.VMEM((2, 16, 48, 1536), bf16),
            pltpu.VMEM((2, 16, 48, 1536), bf16),
            pltpu.VMEM((2, 16, 48, 1536), bf16),
            pltpu.VMEM((2, 16, 48, 512), bf16),
            pltpu.SemaphoreType.DMA((39,)),
            pltpu.VMEM((T, W), bf16),
            pltpu.VMEM((T, D), f32),
            pltpu.VMEM((T, D), bf16),
            pltpu.VMEM((T, 3 * D), bf16),
            pltpu.VMEM((HEADS, T, T), f32),
            pltpu.VMEM((T, D), bf16),
            pltpu.VMEM((D, T), bf16),
            pltpu.VMEM((2, T, 1536), f32),
            pltpu.VMEM((T, D), f32),
            pltpu.VMEM((T, 3 * D), bf16),
            pltpu.VMEM((T, D), f32),
            pltpu.VMEM((2, T, 1536), bf16),
            pltpu.VMEM((32, 1536), f32),
        ],
    )
    grads, back, tot, facts, gpos, dwp = outs
    tot = share(tot)
    if fast:
        planes = [[8 * z + k for k in range(8)] for z in range(4)]
        owned = lax.psum_scatter(
            grads.reshape(8 * 4 * 48, FF),
            everyone,
            scatter_dimension=0,
            tiled=True,
            axis_index_groups=planes,
        )
        owned = [owned]
    else:
        g = jnp.transpose(grads, (2, 0, 3, 1, 4)).reshape(D, 2, 2, FF // 2)
        g = jnp.transpose(g, (0, 2, 1, 3)).reshape(dp, D // dp, 2, mp, part)
        g = jnp.transpose(g, (0, 3, 1, 2, 4)).reshape(n * (D // dp), 2 * part)
        owned = [lax.psum_scatter(g, everyone, scatter_dimension=0, tiled=True)]

    rows_d = D // dp
    rows_vec = 48 if fast else 0

    def outer(bo_all, fin_all, hs_all, bl_all):
        return dot_tn(bo_all, hs_all), dot_tn(fin_all, bl_all)

    if not fast:
        bo, fin = facts[OUT_BACK : OUT_BACK + 1], facts[OUT_FINAL : OUT_FINAL + 1]
        hs, bl = facts[OUT_HIDDEN:OUT_HEAD].reshape(1, FF), facts[OUT_HEAD:OUT_SUMS, 0:512].reshape(1, 1024)
        head_line = jnp.concatenate([bl[:, :500], bl[:, 512:1012]], 1).reshape(1, mp, cls)
        line = jnp.concatenate(
            [
                jnp.broadcast_to(bo.reshape(dp, 1, rows_d), (dp, mp, rows_d)),
                jnp.broadcast_to(fin.reshape(dp, 1, rows_d), (dp, mp, rows_d)),
                jnp.broadcast_to(hs.reshape(1, mp, part), (dp, mp, part)),
                jnp.broadcast_to(head_line, (dp, mp, cls)),
            ],
            2,
        ).reshape(n, -1)
        width = -(-line.shape[1] // 1024) * 1024
        line = jnp.pad(line, ((0, 0), (0, width - line.shape[1]))).astype(bf16)
        line = share(line.reshape(n, width // 128, 128)).reshape(n, width)
        cuts = [0, rows_d, 2 * rows_d, 2 * rows_d + part, 2 * rows_d + part + cls]
        grad_down, grad_head = outer(*[line[:, a:b] for a, b in zip(cuts[:-1], cuts[1:])])

    sums = [None] * 5
    kernel_grads = [None] * 5
    for level in (4, 3):
        r = 2 ** (4 - level)
        chan_in = CHANS[level - 1]
        g, back, so, sums[level - 1] = call(
            functools.partial(conv_back_kernel, level, counts[level], counts[level - 1]),
            [
                ((r + 1, T, W), bf16),
                ((2 * r, T, W), f32),
                ((n, 2, W), f32),
                ((2, W), f32),
            ],
            back,
            tot,
            convs[level],
            stats[level],
            kernels[level],
            convs[level - 1],
            stats[level - 1],
            bn,
            load=(0, 2, 3, 4) if level == 4 else (4,),
            limit=12,
        )
        (kernel_grads[level],) = call(
            functools.partial(kernel_grad, level),
            [((-(-CHANS[level] // 128), 9 * chan_in, 128), f32)],
            inputs[level],
            g,
            load=(0,) if level == 4 else (),
            scratch=[pltpu.VMEM((3, W + chan_in, W), f32)],
            limit=12,
        )
        if level == 4:
            so, kernel_grads[4] = lax.optimization_barrier((so, kernel_grads[4]))
            tot = share(so)
    outs = call(
        functools.partial(early_kernel, len(pieces), mp, stem_len, small_len, rows_stem, rows_small),
        [((dp, rows + rows_vec, 128), bf16)] * len(pieces),
        which,
        kernel_grads[3],
        kernel_grads[4],
        dwp,
        facts,
        gpos,
        smem=1,
        load=(3, 4, 5),
        scratch=frames + [pltpu.VMEM((48, 128), f32)],
        limit=18,
    )
    if mp == 2:
        column = outs[0] + lax.ppermute(outs[1], "mp", swap)
    else:
        column = lax.psum_scatter(jnp.stack(outs, 0), "mp", scatter_dimension=0)
    so, column = lax.optimization_barrier((so, column))
    tot = share(so)
    tot, column = lax.optimization_barrier((tot, column))
    column = lax.all_to_all(column, "dp", 0, 0)
    kernel_rows, exact_rows, each = late_sizes(n)
    (late,) = call(
        functools.partial(conv2_back_kernel, counts[2], counts[1]),
        [((n, each, 128), bf16)],
        back,
        tot,
        convs[2],
        stats[2],
        inputs[2],
        t2,
        xk,
        gram,
        w1,
        t1,
        bn,
        *sums[2:4],
        facts,
        load=(0, 4, 5, 6, 9, 13),
        scratch=[
            pltpu.VMEM((1, 9 * C1, 128), f32),
            pltpu.VMEM((5, T, W), bf16),
            pltpu.VMEM((3, W + C1, W), f32),
            pltpu.VMEM((192, W), f32),
            pltpu.VMEM((n * kernel_rows, 128), f32),
            pltpu.VMEM((n * exact_rows, 128), f32),
        ],
        limit=20,
    )
    if fast:
        owned[0] = lax.optimization_barrier((owned[0], late))[0]
        lines = [[8 * z + k for z in range(4)] for k in range(8)]
        owned[0] = lax.psum_scatter(
            owned[0], everyone, scatter_dimension=0, tiled=True, axis_index_groups=lines
        )
    late, column = lax.optimization_barrier((late, column))
    late = share(late)
    (late,) = call(late_kernel, [((n, each, 128), bf16)], late, limit=8)
    late = share(late)
    if fast:
        line = column[:, rows:].reshape(2 * dp, 24, 128)
        grad_down, grad_head = outer(
            line[:, 16, 0:48],
            line[:, 16, 64:112],
            line[:, 0:12].reshape(2 * dp, part),
            line[:, 12:16].reshape(2 * dp, 512)[:, :cls],
        )
    grad_stem, grad_small, squares = call(
        functools.partial(unpack_kernel, stem_len, small_len),
        [((rows_stem, 128), f32), ((rows_small, 128), f32), ((1, 128), f32)],
        at,
        column,
        smem=1,
        limit=8,
    )

    grad_stem, grad_small, squares1 = call(
        functools.partial(last_kernel, counts[1], stem_len, small_len),
        [((rows_stem, 128), f32), ((rows_small, 128), f32), ((1, 128), f32)],
        at,
        late,
        gram,
        w1,
        bn,
        grad_stem,
        grad_small,
        smem=1,
        scratch=[
            pltpu.VMEM((n * exact_rows, 128), f32),
            pltpu.VMEM((ROW_W2 + n * kernel_rows + rows_stem, 128), f32),
            pltpu.VMEM((16 + rows_small, 128), f32),
        ],
        limit=8,
    )

    g0, g1, ends = call(
        functools.partial(norm_kernel, len(owned)),
        [((rows_d, part), f32), ((rows_d, part), f32), ((n, 1, 128), f32)],
        *owned,
        squares,
        squares1,
        grad_down,
        grad_head,
        facts,
        limit=8,
    )
    (ends,) = call(factor_kernel, [((8, 128), f32)], share(ends), limit=4)
    loss_sum, grad_norm, factor = ends[0, 0], ends[1, 0], ends[2, 0]
    grad_stem = grad_stem.reshape(-1)[:stem_len]
    grad_small = grad_small.reshape(-1)[:small_len]
    grad_block = jnp.stack([g0, g1, grad_down], 0)
    stem_new = adam_step(stem, stem_first, stem_second, grad_stem, factor, rate_stem)
    small_new = adam_step(small, small_first, small_second, grad_small, factor, rate_small)
    block_new = adam_step(block, block_first, block_second, grad_block, factor, rate_block)
    head_new = adam_step(head, head_first, head_second, grad_head, factor, rate_head)
    return (*stem_new, *small_new, *block_new, *head_new, loss_sum, grad_norm)


def solution(mesh):
    flat = P(("dp", "mp"))
    matrix = P(None, "dp", "mp")
    head = P("dp", "mp")
    states = (flat,) * 6 + (matrix,) * 3 + (head,) * 3
    return jax.shard_map(
        local,
        mesh=mesh,
        in_specs=(P("mp", "dp", None), P("mp", "dp")) + states,
        out_specs=states + (P(), P()),
        check_vma=False,
    )
```

```python
import functools

import jax
import jax.numpy as jnp
from jax import lax
from jax.experimental import pallas as pl
from jax.experimental.pallas import tpu as pltpu
from jax.sharding import PartitionSpec as P

D = 768
HEADS = 12
HEAD_DIM = 64
FF = 3072
CLASSES = 1000
C1 = 48
C2 = 96
C3 = 192
C4 = 384
STEP = 10
TOK = 197
SIDE = 14
T = 16 * SIDE
W = 384
CHANS = (3, C1, C2, C3, C4)

beta_one = 0.9
beta_two = 0.999
adam_epsilon = 1e-08
decay_rate = 0.05
clip_norm = 1.0
rate_stem = 0.05
rate_small = 0.5
rate_block = 0.05
rate_head = 0.05
batch_epsilon = 1e-05
layer_epsilon = 1e-06
smoothing = 0.1

bf16 = jnp.bfloat16
f32 = jnp.float32

STEM_SHIFT = 112
SMALL_SHIFT = 96
ROW_W2 = 11
ROW_W3 = ROW_W2 + 9 * C1 * C2 // 128
ROW_W4 = ROW_W3 + 9 * C2 * C3 // 128
ROW_WP = ROW_W4 + 9 * C3 * C4 // 128
STEM_ROWS = ROW_WP + C4 * D // 128
SMALL_NAMES = (
    ("proj_bias", 6),
    ("class_token", 6),
    ("position", 6 * TOK),
    ("norm1_gain", 6),
    ("norm1_bias", 6),
    ("query_bias", 6),
    ("value_bias", 6),
    ("out_bias", 6),
    ("norm2_gain", 6),
    ("norm2_bias", 6),
    ("hidden_bias", 24),
    ("mlp_bias", 6),
    ("final_gain", 6),
    ("final_bias", 6),
    ("head_bias", 8),
)
SMALL_AT = {}
_row = 12
for _name, _rows in SMALL_NAMES:
    SMALL_AT[_name] = _row
    _row += _rows
SMALL_ROWS = _row
VEC_NAMES = (
    "proj_bias",
    "norm1_gain",
    "norm1_bias",
    "query_bias",
    "value_bias",
    "out_bias",
    "norm2_gain",
    "norm2_bias",
    "mlp_bias",
    "final_gain",
    "final_bias",
)
VEC = {name: index for index, name in enumerate(VEC_NAMES)}
VEC_HIDDEN = 12
VEC_HEAD = 16
VEC_AIM = 18
OUT_BACK = 16
OUT_FINAL = 17
OUT_HIDDEN = 18
OUT_HEAD = 22
OUT_SUMS = 24
OUT_LOSS = 25


def dot(a, b):
    return jnp.dot(a, b, preferred_element_type=f32)


def dot_nt(a, b):
    return lax.dot_general(a, b, (((1,), (1,)), ((), ())), preferred_element_type=f32)


def dot_tn(a, b):
    return lax.dot_general(a, b, (((0,), (0,)), ((), ())), preferred_element_type=f32)


GELU_A = 0.7978845608028654
GELU_B = 0.044715


def gelu(x):
    return 0.5 * x * (1.0 + jnp.tanh(GELU_A * (x + GELU_B * x * x * x)))


def gelu_slope(x):
    t = jnp.tanh(GELU_A * (x + GELU_B * x * x * x))
    return 0.5 * (1.0 + t) + 0.5 * x * (1.0 - t * t) * GELU_A * (1.0 + 3.0 * GELU_B * x * x)


def dot_f32(a, b):
    return jnp.dot(a, b, preferred_element_type=f32, precision=lax.Precision.HIGHEST)


def up16(n):
    return -(-n // 16) * 16


def colsum(x):
    return jnp.sum(x, 0, keepdims=True)


def slot_index():
    return lax.broadcasted_iota(jnp.int32, (T, 1), 0)


def patch_mask():
    return ((slot_index() & 15) < SIDE).astype(f32)


def token_mask():
    p = slot_index()
    return (((p & 15) < SIDE) | (p == SIDE)).astype(f32)


def fold_phases(x, chan):
    step = W // 2
    while step >= chan:
        x = x + jnp.concatenate([x[:, step:], x[:, :step]], 1)
        step //= 2
    return x


def sent_width(chan):
    return -(-chan // 128) * 128


def to_send(st, chan):
    return fold_phases(st, chan)[:, 0 : sent_width(chan)]


def channel_sums(ref, chan):
    x = jnp.sum(ref[...], 0)[:, 0:chan]
    return jnp.concatenate([x] * (W // chan), 1)


def bn_stats(st_ref, count, chan):
    tot = channel_sums(st_ref, chan)
    mean = tot[0:1] / count
    inv = lax.rsqrt(tot[1:2] / count - mean * mean + batch_epsilon)
    return mean, inv


def shift_lanes(x, s):
    lane = lax.broadcasted_iota(jnp.int32, x.shape, 1)
    row = lax.broadcasted_iota(jnp.int32, x.shape, 0)
    moved = pltpu.roll(x, s, 1)
    before = jnp.where(row == 0, 0.0, pltpu.roll(moved, 1, 0))
    return jnp.where(lane >= s, moved, before)


def pack_kernel(at_ref, stem_ref, small_ref, out_ref):
    rows = stem_ref.shape[0]
    out_ref[0:rows, :] = shift_lanes(stem_ref[...], at_ref[0]).astype(bf16)
    out_ref[rows:, :] = shift_lanes(small_ref[...], at_ref[1]).astype(bf16)


def flat_lanes(ref, row, count):
    return jnp.concatenate([ref[row + k : row + k + 1, :] for k in range(count)], 1)


def assemble_kernel(by_plane, parts, mp, stem_len, small_len, rows_stem, rows_small, at_ref, *refs):
    pieces = refs[:parts]
    s1, t1_ref, t2_ref, t3_ref, t4_ref, wp_ref, bn_ref, vec_ref, pos_ref = refs[parts : parts + 9]
    frame, table, s2, s3a, s3b, u1, u2, u3 = refs[parts + 9 :]
    frame[...] = jnp.zeros_like(frame)
    table[...] = jnp.zeros_like(table)
    for index, ref in enumerate(pieces):
        mv = at_ref[index]

        def put(d, carry):
            owner = (at_ref[parts + 1] ^ ((d & 3) * 4 + (d >> 2)) if by_plane else d) * mp + mv
            a = (owner * stem_len + STEM_SHIFT) // 128
            frame[pl.ds(a, rows_stem), :] += ref[d, 0:rows_stem, :].astype(f32)
            b = (owner * small_len + SMALL_SHIFT) // 128
            table[pl.ds(b, rows_small), :] += ref[d, rows_stem : rows_stem + rows_small, :].astype(f32)
            return carry

        lax.fori_loop(0, ref.shape[0], put, 0)
    s1[...] = jnp.zeros_like(s1)
    flat = flat_lanes(frame, 0, ROW_W2)
    for k in range(27):
        s1[k : k + 1, 0:C1] = flat[:, STEM_SHIFT + 48 * k : STEM_SHIFT + 48 * k + 48]
    u1[...] = jnp.zeros_like(u1)
    for tap in range(3):
        for j in range(8):
            cols = slice(j * C1, (j + 1) * C1)
            if j == 0:
                u1[tap * 64 + 48 : tap * 64 + 51, cols] = s1[tap * 9 : tap * 9 + 3, 0:C1]
                u1[tap * 64 : tap * 64 + 6, cols] = s1[tap * 9 + 3 : tap * 9 + 9, 0:C1]
            else:
                at = tap * 64 + 6 * j - 3
                u1[at : at + 9, cols] = s1[tap * 9 : tap * 9 + 9, 0:C1]
    t1_ref[...] = u1[...].astype(bf16)
    q = 9 * C1 // 4
    wide = jnp.concatenate([frame[pl.ds(ROW_W2 + k, q, stride=3), :] for k in range(3)], 1)
    for k in range(4):
        s2[pl.ds(k, q, stride=4), 0:C2] = wide[:, k * C2 : (k + 1) * C2]
    q = 9 * C2 // 2
    wide = jnp.concatenate([frame[pl.ds(ROW_W3 + k, q, stride=3), :] for k in range(3)], 1)
    for k in range(2):
        part = wide[:, k * C3 : (k + 1) * C3]
        s3a[pl.ds(k, q, stride=2), :] = part[:, 0:128]
        s3b[pl.ds(k, q, stride=2), 0 : C3 - 128] = part[:, 128:C3]
    for ref, chan_in, chan_out, src, u in (
        (t2_ref, C1, C2, (s2,), u2),
        (t3_ref, C2, C3, (s3a, s3b), u3),
    ):
        for tap in range(3):
            u[...] = jnp.zeros_like(u)
            base = tap * 3 * chan_in
            for j in range(W // chan_out):
                for k, s in enumerate(src):
                    width = min(128, chan_out - 128 * k)
                    cols = slice(j * chan_out + 128 * k, j * chan_out + 128 * k + width)
                    if j == 0:
                        u[W : W + chan_in, cols] = s[base : base + chan_in, 0:width]
                        u[0 : 2 * chan_in, cols] = s[base + chan_in : base + 3 * chan_in, 0:width]
                    else:
                        at = (2 * j - 1) * chan_in
                        u[at : at + 3 * chan_in, cols] = s[base : base + 3 * chan_in, 0:width]
            ref[tap] = u[...].astype(bf16)
    for tap in range(3):
        rows = 3 * C3
        for k in range(3):
            lanes = slice(k * 128, (k + 1) * 128)
            at = ROW_W4 + k + 3 * tap * rows
            t4_ref[tap, 0 : 2 * C3, lanes] = frame[pl.ds(at + 3 * C3, 2 * C3, stride=3), :].astype(bf16)
            t4_ref[tap, 2 * C3 : 3 * C3, lanes] = frame[pl.ds(at, C3, stride=3), :].astype(bf16)
    for k in range(6):
        lanes = slice(k * 128, (k + 1) * 128)
        wp_ref[:, lanes] = frame[pl.ds(ROW_WP + k, C4, stride=6), :].astype(bf16)
    flat = flat_lanes(table, 0, 12)
    first = SMALL_SHIFT
    for level in range(4):
        chan = CHANS[level + 1]
        for which in range(2):
            at = first + which * (C1 + C2 + C3 + C4)
            part = flat[:, at : at + chan]
            row = 2 * level + which
            for j in range(W // chan):
                bn_ref[row : row + 1, j * chan : (j + 1) * chan] = part
        first += chan
    vec_ref[...] = jnp.zeros_like(vec_ref)
    for name, index in VEC.items():
        vec_ref[index : index + 1, :] = flat_lanes(table, SMALL_AT[name], 6)
    for k in range(4):
        row = VEC_HIDDEN + k
        vec_ref[row : row + 1, :] = flat_lanes(table, SMALL_AT["hidden_bias"] + 6 * k, 6)
    flat = flat_lanes(table, SMALL_AT["head_bias"], 8)
    lane = lax.broadcasted_iota(jnp.int32, (1, 512), 1)
    for m in range(2):
        vec_ref[VEC_HEAD + m : VEC_HEAD + m + 1, 0:500] = flat[:, 500 * m : 500 * m + 500]
        aim = jnp.where(lane + 500 * m == at_ref[parts], 1.0 - smoothing, 0.0) + smoothing / CLASSES
        vec_ref[VEC_AIM + m : VEC_AIM + m + 1, 0:512] = jnp.where(lane < 500, aim, 0.0)
    pos_ref[...] = jnp.zeros_like(pos_ref)
    at = SMALL_AT["position"]
    for k in range(6):
        lanes = slice(k * 128, (k + 1) * 128)
        for r in range(SIDE):
            rows = table[pl.ds(at + k + 6 * (1 + SIDE * r), SIDE, stride=6), :]
            pos_ref[16 * r : 16 * r + SIDE, lanes] = rows
        mark = SMALL_AT["class_token"] + k
        pos_ref[SIDE : SIDE + 1, lanes] = table[mark : mark + 1, :] + table[at + k : at + k + 1, :]


def image_kernel(own_ref, next_ref, xk_ref, gram_ref, flat, chunks, xe):
    half = own_ref.shape[0]
    flat[0:half, :] = own_ref[...].astype(f32)
    flat[half : 2 * half, :] = next_ref[...].astype(f32)
    n = 2 * half // 3
    wide = jnp.concatenate([flat[pl.ds(k, n, stride=3), :] for k in range(3)], 1)
    for j in range(8):
        chunks[pl.ds(j, n, stride=8), 0:48] = wide[:, 48 * j : 48 * j + 48]
    mask = patch_mask()
    lane = lax.broadcasted_iota(jnp.int32, (T, 64), 1)

    def spread(i, carry):
        rows = [chunks[pl.ds(16 * SIDE * r + SIDE * i, 16), 0:64] for r in range(SIDE)]
        x = jnp.where(lane < 48, jnp.concatenate(rows, 0), 0.0) * mask
        left = pltpu.roll(jnp.concatenate([x, x], 1), 3, 1)[:, 0:64]
        left = jnp.where((lane >= 48) & (lane < 51), pltpu.roll(left, 1, 0), 0.0)
        xe[i + 1] = ((x + left) * mask).astype(bf16)
        return carry

    chunks[pl.ds(n * 8, 16), :] = jnp.zeros((16, 128), f32)
    lax.fori_loop(0, 16, spread, 0)
    last = xe[16]
    xe[0] = jnp.concatenate([jnp.zeros((16, 64), bf16), last[: T - 16]], 0)

    def step(i, carry):
        gram, ones = carry
        x = jnp.concatenate([xe[2 * i], xe[2 * i + 1], xe[2 * i + 2]], 1)
        xk_ref[i] = x
        return gram + dot_tn(x, x), ones + colsum(x.astype(f32))

    gram, ones = lax.fori_loop(0, 8, step, (jnp.zeros((192, 192), f32), jnp.zeros((1, 192), f32)))
    row = lax.broadcasted_iota(jnp.int32, (192, 256), 0)
    col = lax.broadcasted_iota(jnp.int32, (192, 256), 1)
    j, k = col >> 5, col & 31
    tap = (k >= 9).astype(jnp.int32) + (k >= 18).astype(jnp.int32)
    u = k - 9 * tap
    at = 64 * tap + jnp.where(j == 0, jnp.where(u < 3, 48 + u, u - 3), 6 * j - 3 + u)
    pick = ((row == at) & (k < 27)).astype(f32)
    both = lax.dot_general(
        pick,
        dot_f32(gram, pick),
        (((0,), (0,)), ((), ())),
        preferred_element_type=f32,
        precision=lax.Precision.HIGHEST,
    )
    ones = dot_f32(jnp.broadcast_to(ones, (8, 192)), pick)[0:1]
    total = jnp.zeros((32, 32), f32)
    line = jnp.zeros((1, 32), f32)
    for q in range(8):
        lanes = slice(32 * q, 32 * q + 32)
        total = total + both[lanes, lanes]
        line = line + ones[:, lanes]
    r32 = lax.broadcasted_iota(jnp.int32, (32, 32), 0)
    c32 = lax.broadcasted_iota(jnp.int32, (32, 32), 1)
    total = total + jnp.where(r32 == 27, line, 0.0)
    column = jnp.sum(jnp.where(r32 == c32, line, 0.0), 1, keepdims=True)
    total = total + jnp.where(c32 == 27, column, 0.0)
    flat8 = jnp.concatenate([total[8 * q : 8 * q + 8] for q in range(4)], 1)
    gram_ref[...] = jnp.broadcast_to(flat8[None], gram_ref.shape)


def level1_stats(gram_ref, w1_ref, count):
    flat8 = jnp.sum(gram_ref[...], 0)
    gram = jnp.concatenate([flat8[:, 32 * q : 32 * q + 32] for q in range(4)], 0)
    cross = dot_f32(gram, w1_ref[...])
    mean = cross[27:28] / count
    squares = colsum(w1_ref[...] * cross) / count
    inv = lax.rsqrt(squares - mean * mean + batch_epsilon)
    return gram, cross, mean, inv


def tile_lanes(x, chan):
    return jnp.concatenate([x[:, 0:chan]] * (W // chan), 1)


def conv12_kernel(count, xk_ref, gram_ref, w1_ref, t1_ref, bn_ref, t_ref, ax_ref, out_ref, st_ref):
    gram, cross, mean, inv = level1_stats(gram_ref, w1_ref, count)
    mean, inv = tile_lanes(mean, C1), tile_lanes(inv, C1)
    gain, bias = bn_ref[0:1, :], bn_ref[1:2, :]
    mask = patch_mask()
    weights = t1_ref[...]

    def activate(i, carry):
        a = gelu((dot(xk_ref[i], weights) - mean) * inv * gain + bias) * mask
        put_input(ax_ref, i, a, C1)
        return carry

    lax.fori_loop(0, 8, activate, 0)
    convolve(8, ax_ref, t_ref, out_ref, st_ref, mask, C1)


def put_input(ax_ref, i, a, chan):
    left = pltpu.roll(a[:, W - chan :], 1, 0)
    ax_ref[i + 1, :, 0:W] = a.astype(bf16)
    ax_ref[i + 1, :, W:] = left.astype(bf16)


def convolve(rows, ax_ref, t_ref, out_ref, st_ref, mask, chan):
    last = ax_ref[rows]
    ax_ref[0] = jnp.concatenate([jnp.zeros((16, W + chan), bf16), last[: T - 16]], 0)

    def step(i, carry):
        first, second = carry
        y = dot(ax_ref[2 * i], t_ref[0])
        y = y + dot(ax_ref[2 * i + 1], t_ref[1])
        y = y + dot(ax_ref[2 * i + 2], t_ref[2])
        out_ref[i] = y
        ym = y * mask
        return first + colsum(ym), second + colsum(ym * y)

    zero = jnp.zeros((1, W), f32)
    first, second = lax.fori_loop(0, rows // 2, step, (zero, zero))
    st = jnp.concatenate([first, second], 0)
    st_ref[...] = jnp.broadcast_to(to_send(st, 2 * chan)[None], st_ref.shape)


def conv_kernel(level, count, c_ref, stin_ref, bn_ref, t_ref, ax_ref, out_ref, st_ref):
    chan = CHANS[level]
    rows = c_ref.shape[0]
    mean, inv = bn_stats(stin_ref, count, chan)
    gain = bn_ref[2 * level - 2 : 2 * level - 1, :]
    bias = bn_ref[2 * level - 1 : 2 * level, :]
    mask = patch_mask()

    def activate(i, carry):
        put_input(ax_ref, i, gelu((c_ref[i] - mean) * inv * gain + bias) * mask, chan)
        return carry

    lax.fori_loop(0, rows, activate, 0)
    convolve(rows, ax_ref, t_ref, out_ref, st_ref, mask, chan)


def layer_norm(x):
    centered = x - jnp.mean(x, -1, keepdims=True)
    inv = lax.rsqrt(jnp.mean(centered * centered, -1, keepdims=True) + layer_epsilon)
    return centered * inv, inv


def layer_norm_back(dy, s, inv, gain):
    scaled = dy * gain
    inner = scaled - jnp.mean(scaled, -1, keepdims=True)
    return inv * (inner - s * jnp.mean(scaled * s, -1, keepdims=True))


def normed4(count, st_ref, bn_ref, c_ref):
    mean, inv = bn_stats(st_ref, count, C4)
    s = (c_ref[0] - mean) * inv
    return s, s * bn_ref[6:7, :] + bn_ref[7:8, :]


def embed_kernel(count, st_ref, bn_ref, c_ref, wp_ref, pos_ref, vec_ref, a4_ref, x0_ref, n1_ref):
    def vec(name):
        return vec_ref[VEC[name] : VEC[name] + 1, :]

    mask = patch_mask()
    _, y4 = normed4(count, st_ref, bn_ref, c_ref)
    a4_ref[...] = (gelu(y4) * mask).astype(bf16)
    x0 = (dot(a4_ref[...], wp_ref[...]) + vec("proj_bias")) * mask + pos_ref[...]
    x0_ref[...] = x0
    s1, _ = layer_norm(x0)
    n1_ref[...] = (s1 * vec("norm1_gain") + vec("norm1_bias")).astype(bf16)


def block_kernel(
    count,
    st_ref,
    bn_ref,
    n1_hbm,
    vec_hbm,
    x0_hbm,
    a4_hbm,
    wp_hbm,
    c_hbm,
    g_ref,
    gr_ref,
    bn4_hbm,
    so_hbm,
    out_hbm,
    gpos_hbm,
    dwp_hbm,
    c_ref,
    wp_ref,
    vec_ref,
    bn4_ref,
    so_ref,
    out_ref,
    gpos_ref,
    dwp_ref,
    wa,
    wu,
    wd,
    wh,
    sems,
    a4,
    x0,
    n1,
    qkv,
    probs,
    mixed,
    n2t,
    pre,
    acc,
    bqkv,
    mixed_f,
    bpre,
    rowbuf,
):
    gr0, gr1 = wu, wd
    fetched = []
    for k, (source, ref) in enumerate(
        ((n1_hbm, n1), (vec_hbm, vec_ref), (x0_hbm, x0), (a4_hbm, a4), (wp_hbm, wp_ref), (c_hbm, c_ref))
    ):
        fetched.append(pltpu.make_async_copy(source, ref, sems.at[24 + k]))
        if k < 2:
            fetched[-1].start()
    copies = []
    for m in range(2):
        for h in range(2):
            lanes = slice(D * h, D * h + D)
            copy = pltpu.make_async_copy(
                g_ref.at[:, m, :, lanes], wa.at[m, :, :, lanes], sems.at[35 + 2 * m + h]
            )
            copy.start()
            copies.append(copy)
    for k, (ref, at, size) in enumerate(
        ((wu, 1536, 1536), (wd, 3072, 1536), (wh, 4608, 512))
    ):
        for m in range(2):
            copy = pltpu.make_async_copy(
                g_ref.at[:, m, :, at : at + size], ref.at[m], sems.at[2 * k + m]
            )
            copy.start()
            copies.append(copy)
        if k == 0:
            for copy in fetched[2:]:
                copy.start()

    def send_out(grad, slot):
        out = []
        lanes = slice(1536 * slot, 1536 * slot + 1536)
        for m in range(2):
            for z in range(4):
                copy = pltpu.make_async_copy(
                    grad.at[m, 4 * z : 4 * z + 4],
                    gr_ref.at[:, m, z, :, lanes],
                    sems.at[8 + 8 * slot + 4 * m + z],
                )
                copy.start()
                out.append(copy)
        return out

    def write(ref, target, k):
        copy = pltpu.make_async_copy(ref, target, sems.at[30 + k])
        copy.start()
        moving.append(copy)

    def vec(name):
        return vec_ref[VEC[name] : VEC[name] + 1, :]

    mask = patch_mask()
    valid = token_mask()
    out_row = lax.broadcasted_iota(jnp.int32, (32, 1), 0)
    out_ref[...] = jnp.zeros_like(out_ref)
    key = lax.broadcasted_iota(jnp.int32, (1, T), 1)
    key_bias = jnp.where(((key & 15) < SIDE) | (key == SIDE), 0.0, -1e30)

    for copy in fetched[:2]:
        copy.wait()

    def tile(ref, m, at, size=256):
        return ref[m, :, :, pl.ds(at, size)].reshape(D, size)

    for part in range(9):
        if part % 3 == 0:
            copies[part // 3].wait()
        y = dot(n1[...], tile(wa, part // 6, 256 * (part % 6)))
        lanes = slice(256 * (part % 3), 256 * (part % 3) + 256)
        if part < 3:
            y = y + vec("query_bias")[:, lanes]
        elif part >= 6:
            y = y + vec("value_bias")[:, lanes]
        qkv[:, 256 * part : 256 * part + 256] = y.astype(bf16)
    scale = HEAD_DIM**-0.5

    def attend(pair, carry):
        at = pl.multiple_of(pair * 128, 128)
        q = qkv[:, pl.ds(at, 128)] * bf16(scale)
        k = qkv[:, pl.ds(at + D, 128)]
        v = qkv[:, pl.ds(at + 2 * D, 128)]
        out = []
        for h in range(2):
            lanes = slice(64 * h, 64 * h + 64)
            scores = dot_nt(q[:, lanes], k[:, lanes]) + key_bias
            e = jnp.exp(scores - jnp.max(scores, -1, keepdims=True))
            p = e * (1.0 / jnp.sum(e, -1, keepdims=True))
            probs[2 * pair + h] = p
            out.append(dot(p.astype(bf16), v[:, lanes]))
        out = jnp.concatenate(out, 1)
        mixed[:, pl.ds(at, 128)] = out.astype(bf16)
        mixed_f[:, pl.ds(at, 128)] = out
        return carry

    lax.fori_loop(0, HEADS // 2, attend, 0, unroll=6)
    for copy in fetched[2:]:
        copy.wait()
    copies[3].wait()
    att = [dot_nt(mixed[...], wa[1, :, :, D : 2 * D].reshape(D, D))]
    x1 = x0[...] + att[0] + vec("out_bias")
    mean_x1 = colsum(x1 * valid) / TOK
    s2, i2 = layer_norm(x1)
    n2 = (s2 * vec("norm2_gain") + vec("norm2_bias")).astype(bf16)
    n2t[...] = n2.T
    copies[4].wait()
    copies[5].wait()
    bias = [jnp.concatenate([vec_ref[r : r + 1, :], vec_ref[r + 1 : r + 2, :]], 1) for r in (12, 14)]
    rowbuf[0:1, :] = bias[0]
    rowbuf[8:9, :] = bias[1]

    def place(k):
        m = (k >= 6).astype(jnp.int32)
        return m, pl.multiple_of(8 * m, 8), pl.multiple_of((k - 6 * m) * 256, 256)

    def up(k, carry):
        m, row, at = place(k)
        y = dot(n2, tile(wu, m, at)) + rowbuf[pl.ds(row, 8), pl.ds(at, 256)][0:1]
        t = jnp.tanh(GELU_A * (y + GELU_B * y * y * y))
        half = 0.5 + 0.5 * t
        h = (y * half).astype(bf16).astype(f32) * valid
        rowbuf[pl.ds(16 + row, 8), pl.ds(at, 256)] = jnp.broadcast_to(colsum(h), (8, 256))
        inner = GELU_A + (3.0 * GELU_A * GELU_B) * y * y
        pre[m, :, pl.ds(at, 256)] = (half + 0.5 * y * (1.0 - t * t) * inner) * valid
        return carry

    lax.fori_loop(0, 12, up, 0, unroll=4)
    for m in range(2):
        for k in range(2):
            row = OUT_HIDDEN + 2 * m + k
            out_ref[row : row + 1, :] = rowbuf[16 + 8 * m : 17 + 8 * m, D * k : D * k + D]
    copies[6].wait()
    copies[7].wait()
    hs = jnp.concatenate([out_ref[OUT_HIDDEN + k : OUT_HIDDEN + k + 1, :] for k in range(4)], 1) / TOK
    high = hs.astype(bf16)
    low = (hs - high.astype(f32)).astype(bf16)
    out = jnp.zeros((1, D), f32)
    for m in range(2):
        lanes = slice(1536 * m, 1536 * m + 1536)
        both = jnp.concatenate(
            [jnp.broadcast_to(high[:, lanes], (8, 1536)), jnp.broadcast_to(low[:, lanes], (8, 1536))], 0
        )
        y = dot_nt(both, wd[m].reshape(D, 1536))
        out = out + y[0:1] + y[8:9]
    pooled = mean_x1 + out + vec("mlp_bias")
    s3, i3 = layer_norm(pooled)
    final = (s3 * vec("final_gain") + vec("final_bias")).astype(bf16)
    copies[8].wait()
    copies[9].wait()
    wide = jnp.broadcast_to(final, (16, D))
    logits = jnp.concatenate([dot(wide, wh[m].reshape(D, 512))[0:1] for m in range(2)], 1)
    lane = lax.broadcasted_iota(jnp.int32, (1, 1024), 1)
    real = (lane & 511) < CLASSES // 2
    def pair(row):
        return jnp.concatenate([vec_ref[row : row + 1, 0:512], vec_ref[row + 1 : row + 2, 0:512]], 1)

    logits = jnp.where(real, logits + pair(VEC_HEAD), -1e30)
    top = jnp.max(logits, -1, keepdims=True)
    log_probs = logits - top - jnp.log(jnp.sum(jnp.exp(logits - top), -1, keepdims=True))
    aim = pair(VEC_AIM)
    loss = -jnp.sum(jnp.where(real, aim * log_probs, 0.0), keepdims=True)
    out_ref[...] = jnp.where(out_row >= OUT_LOSS, jnp.broadcast_to(loss, out_ref.shape), out_ref[...])
    back_logits = jnp.where(real, jnp.exp(log_probs) - aim, 0.0).astype(bf16)
    for m in range(2):
        row = OUT_HEAD + m
        out_ref[row : row + 1, 0:512] = back_logits[:, 512 * m : 512 * m + 512].astype(f32)
    out_ref[OUT_FINAL : OUT_FINAL + 1, :] = final.astype(f32)
    wide = jnp.broadcast_to(back_logits, (16, 1024))
    back_final = (
        dot_nt(wide[:, 0:512], wh[0].reshape(D, 512)) + dot_nt(wide[:, 512:], wh[1].reshape(D, 512))
    )[0:1]
    def put(name, value):
        out_ref[VEC[name] : VEC[name] + 1, :] = value

    put("final_gain", back_final * s3)
    put("final_bias", back_final)
    back2 = layer_norm_back(back_final, s3, i3, vec("final_gain")) / TOK
    back_out = back2.astype(bf16)
    out_ref[OUT_BACK : OUT_BACK + 1, :] = back_out.astype(f32)
    put("mlp_bias", back_out.astype(f32) * TOK)
    wide = jnp.broadcast_to(back_out, (16, D))
    for m in range(2):
        for k in range(6):
            at = 256 * k
            rowbuf[8 * m : 8 * m + 1, at : at + 256] = dot(wide, tile(wd, m, at))[0:1]

    def down(k, carry):
        m, row, at = place(k)
        back = rowbuf[pl.ds(row, 8), pl.ds(at, 256)][0:1]
        bp = (back * pre[m, :, pl.ds(at, 256)]).astype(bf16)
        rowbuf[pl.ds(16 + row, 8), pl.ds(at, 256)] = jnp.broadcast_to(
            colsum(bp.astype(f32)), (8, 256)
        )
        bpre[m, :, pl.ds(at, 256)] = bp
        grad = dot(n2t[...], bp)
        gr1[m, :, :, pl.ds(at, 256)] = grad.astype(bf16).reshape(16, 48, 256)
        return carry

    lax.fori_loop(0, 12, down, 0, unroll=4)
    for m in range(2):
        for k in range(2):
            row = VEC_HIDDEN + 2 * m + k
            out_ref[row : row + 1, :] = rowbuf[16 + 8 * m : 17 + 8 * m, D * k : D * k + D]
    moving = send_out(gr1, 1)
    back_n2 = dot_nt(bpre[0], wu[0].reshape(D, 1536)) + dot_nt(bpre[1], wu[1].reshape(D, 1536))
    put("norm2_gain", colsum(back_n2 * s2))
    put("norm2_bias", colsum(back_n2))
    back1 = back2 * valid + layer_norm_back(back_n2, s2, i2, vec("norm2_gain"))
    back_att = back1.astype(bf16)
    put("out_bias", colsum(back_att.astype(f32)))
    back_att_t = back_att.T
    for k in range(3):
        lanes = slice(256 * k, 256 * k + 256)
        grad = dot(back_att_t, mixed[:, lanes])
        gr0[1, :, :, D + 256 * k : D + 256 * k + 256] = grad.astype(bf16).reshape(16, 48, 256)
    acc[...] = dot(back_att, wa[1, :, :, D : 2 * D].reshape(D, D))

    def attend_back(pair, carry):
        at = pl.multiple_of(pair * 128, 128)
        q = qkv[:, pl.ds(at, 128)]
        k = qkv[:, pl.ds(at + D, 128)]
        v = qkv[:, pl.ds(at + 2 * D, 128)]
        bm = acc[:, pl.ds(at, 128)].astype(bf16)
        bm_mixed = bm.astype(f32) * mixed_f[:, pl.ds(at, 128)]
        bq, bk, bv = [], [], []
        for h in range(2):
            lanes = slice(64 * h, 64 * h + 64)
            p = probs[2 * pair + h]
            bp = dot_nt(bm[:, lanes], v[:, lanes])
            bv.append(dot_tn(p.astype(bf16), bm[:, lanes]))
            inner = jnp.sum(bm_mixed[:, lanes], -1, keepdims=True)
            bs = (p * (bp - inner)).astype(bf16)
            bq.append(dot(bs, k[:, lanes]) * scale)
            bk.append(dot_tn(bs, q[:, lanes]) * scale)
        bqkv[:, pl.ds(at, 128)] = jnp.concatenate(bq, 1).astype(bf16)
        bqkv[:, pl.ds(at + D, 128)] = jnp.concatenate(bk, 1).astype(bf16)
        bqkv[:, pl.ds(at + 2 * D, 128)] = jnp.concatenate(bv, 1).astype(bf16)
        return carry

    lax.fori_loop(0, HEADS // 2, attend_back, 0, unroll=6)
    put("query_bias", colsum(bqkv[:, 0:D].astype(f32)))
    put("value_bias", colsum(bqkv[:, 2 * D :].astype(f32)))
    n1t = n1[...].T
    for part in range(9):
        m, at = part // 6, 256 * (part % 6)
        b = bqkv[:, 256 * part : 256 * part + 256]
        gr0[m, :, :, at : at + 256] = dot(n1t, b).astype(bf16).reshape(16, 48, 256)
    moving += send_out(gr0, 0)
    back_n1 = dot_nt(bqkv[:, 0:1536], wa[0].reshape(D, 1536))
    back_n1 = back_n1 + dot_nt(bqkv[:, 1536:], wa[1, :, :, 0:D].reshape(D, D))
    s1, i1 = layer_norm(x0[...])
    put("norm1_gain", colsum(back_n1 * s1))
    put("norm1_bias", colsum(back_n1))
    back0 = back1 + layer_norm_back(back_n1, s1, i1, vec("norm1_gain"))
    gpos_ref[...] = back0
    write(gpos_ref, gpos_hbm, 0)
    back_patch = (back0 * mask).astype(bf16)
    put("proj_bias", colsum(back_patch.astype(f32)))
    dwp_ref[...] = dot_tn(a4[...], back_patch)
    write(dwp_ref, dwp_hbm, 1)
    s4, y4 = normed4(count, st_ref, bn_ref, c_ref)
    bn4 = dot_nt(back_patch, wp_ref[...]) * gelu_slope(y4) * mask
    bn4_ref[0] = bn4
    write(bn4_ref, bn4_hbm, 2)
    st = jnp.concatenate([colsum(bn4), colsum(bn4 * s4)], 0)
    so_ref[...] = jnp.broadcast_to(st[None], so_ref.shape)
    write(so_ref, so_hbm, 3)
    out_ref[OUT_SUMS : OUT_SUMS + 1, :] = jnp.concatenate([st[0:1], st[1:2]], 1)
    write(out_ref, out_hbm, 4)
    for copy in moving:
        copy.wait()


def conv_back_kernel(
    level,
    count,
    count_in,
    back_ref,
    tot_ref,
    c_ref,
    st_ref,
    t_ref,
    cin_ref,
    stin_ref,
    bn_ref,
    g,
    backin_ref,
    so_ref,
    ss_ref,
):
    finish_level(level, count, back_ref, tot_ref, c_ref, st_ref, bn_ref, g)
    mean, inv = bn_stats(stin_ref, count_in, CHANS[level - 1])

    def normed(q):
        return (cin_ref[q] - mean) * inv

    def keep(q, y):
        backin_ref[q] = y

    st = back_through(level, g, t_ref, bn_ref, normed, keep)
    ss_ref[...] = st
    so_ref[...] = jnp.broadcast_to(to_send(st, CHANS[level - 1])[None], so_ref.shape)


def finish_level(level, count, back_ref, tot_ref, c_ref, st_ref, bn_ref, g):
    chan = CHANS[level]
    rows = back_ref.shape[0]
    mask = patch_mask()
    mean, inv = bn_stats(st_ref, count, chan)
    gain = bn_ref[2 * level - 2 : 2 * level - 1, :]
    tot = channel_sums(tot_ref, chan) / count

    def finish(i, carry):
        s = (c_ref[i] - mean) * inv
        g[i] = (inv * gain * (back_ref[i] - tot[0:1] - s * tot[1:2]) * mask).astype(bf16)
        return carry

    lax.fori_loop(0, rows, finish, 0)
    head = g[0]
    g[rows] = jnp.concatenate([head[16:], jnp.zeros((16, W), bf16)], 0)


def kernel_grad(level, ax_ref, g, dw_ref, dt):
    chan, chan_in = CHANS[level], CHANS[level - 1]
    rows = g.shape[0] - 1
    dt[...] = jnp.zeros_like(dt)

    def weights(i, carry):
        for tap in range(3):
            dt[tap] += dot_tn(ax_ref[2 * i + tap], g[i])
        return carry

    lax.fori_loop(0, rows, weights, 0)
    for tap in range(3):
        base = tap * 3 * chan_in
        for j in range(W // chan):
            for k in range(dw_ref.shape[0]):
                width = min(128, chan - 128 * k)
                cols = slice(j * chan + 128 * k, j * chan + 128 * k + width)
                if j == 0:
                    dw_ref[k, base : base + chan_in, 0:width] = dt[tap, W : W + chan_in, cols]
                    dw_ref[k, base + chan_in : base + 3 * chan_in, 0:width] = dt[
                        tap, 0 : 2 * chan_in, cols
                    ]
                else:
                    at = (2 * j - 1) * chan_in
                    dw_ref[k, base : base + 3 * chan_in, 0:width] += dt[
                        tap, at : at + 3 * chan_in, cols
                    ]


def back_through(level, g, t_ref, bn_ref, normed, keep):
    chan_in = CHANS[level - 1]
    rows = g.shape[0] - 1
    mask = patch_mask()
    gain = bn_ref[2 * level - 4 : 2 * level - 3, :]
    bias = bn_ref[2 * level - 3 : 2 * level - 2, :]

    def through(q, p, carry):
        first, second = carry
        left = pltpu.roll(p[:, W:], T - 1, 0)
        p = jnp.concatenate([p[:, 0 : W - chan_in], p[:, W - chan_in : W] + left], 1)
        s = normed(q)
        y = p * gelu_slope(s * gain + bias) * mask
        keep(q, y)
        return first + colsum(y), second + colsum(y * s)

    def back(i, carry):
        carry = through(2 * i, dot_nt(g[i], t_ref[1]), carry)
        p = dot_nt(g[i], t_ref[2]) + dot_nt(g[i + 1], t_ref[0])
        return through(2 * i + 1, p, carry)

    zero = jnp.zeros((1, W), f32)
    first, second = lax.fori_loop(0, rows, back, (zero, zero))
    return jnp.concatenate([first, second], 0)


LATE_W2 = 9 * C1 * C2 // 128
LATE_SUMS = 32
LATE_F = LATE_SUMS + 4 * 6


def late_sizes(n):
    kernel, exact = -(-LATE_W2 // n), -(-LATE_F // n)
    return kernel, exact, up16(kernel + 2 * exact)


def late_rows(w, f, rows):
    high = f.astype(bf16).astype(f32)
    fill = jnp.zeros((rows - w.shape[0] - 2 * f.shape[0], 128), f32)
    return jnp.concatenate([w, high, f - high, fill], 0).astype(bf16)


def conv2_back_kernel(
    count,
    count_in,
    back_ref,
    tot_ref,
    c_ref,
    st_ref,
    ax_ref,
    t_ref,
    xk_ref,
    gram_ref,
    w1_ref,
    t1_ref,
    bn_ref,
    ss2_ref,
    ss3_ref,
    ss4_ref,
    late_ref,
    dw,
    g,
    dt,
    dt1,
    late,
    exact,
):
    finish_level(2, count, back_ref, tot_ref, c_ref, st_ref, bn_ref, g)
    kernel_grad(2, ax_ref, g, dw, dt)
    gram, cross, mean, inv = level1_stats(gram_ref, w1_ref, count_in)
    mean, inv = tile_lanes(mean, C1), tile_lanes(inv, C1)
    weights = t1_ref[...]
    dt1[...] = jnp.zeros_like(dt1)

    def normed(q):
        return (dot(xk_ref[q], weights) - mean) * inv

    def keep(q, y):
        dt1[...] += dot_tn(xk_ref[q], y.astype(bf16))

    st = back_through(2, g, t_ref, bn_ref, normed, keep)
    late[...] = jnp.zeros_like(late)
    exact[...] = jnp.zeros_like(exact)
    q = 9 * C1 // 4
    wide = jnp.concatenate([dw[0, pl.ds(k, q, stride=4), :][:, 0:C2] for k in range(4)], 1)
    for k in range(3):
        late[pl.ds(k, q, stride=3), :] = wide[:, 128 * k : 128 * k + 128]
    for tap in range(3):
        base = 9 * tap
        for j in range(8):
            cols = slice(j * C1, (j + 1) * C1)
            if j == 0:
                exact[base : base + 3, 0:C1] = dt1[tap * 64 + 48 : tap * 64 + 51, cols]
                exact[base + 3 : base + 9, 0:C1] = dt1[tap * 64 : tap * 64 + 6, cols]
            else:
                at = tap * 64 + 6 * j - 3
                exact[base : base + 9, 0:C1] += dt1[at : at + 9, cols]
    ss4 = jnp.concatenate(
        [ss4_ref[OUT_SUMS : OUT_SUMS + 1, 0:W], ss4_ref[OUT_SUMS : OUT_SUMS + 1, W:]], 0
    )
    for level, ss in enumerate((st, ss2_ref[...], ss3_ref[...], ss4)):
        for which in range(2):
            for k in range(3):
                row = LATE_SUMS + 6 * level + 3 * which + k
                exact[row : row + 1, :] = ss[which : which + 1, 128 * k : 128 * k + 128]
    kernel, share, rows = late_sizes(late_ref.shape[0])

    def emit(d, carry):
        w = late[pl.ds(kernel * d, kernel), :]
        late_ref[d] = late_rows(w, exact[pl.ds(share * d, share), :], rows)
        return carry

    lax.fori_loop(0, late_ref.shape[0], emit, 0)


def early_kernel(
    parts,
    mp,
    stem_len,
    small_len,
    rows_stem,
    rows_small,
    at_ref,
    dw3_ref,
    dw4_ref,
    dwp_ref,
    gv_ref,
    gpos_ref,
    *refs,
):
    outs = refs[:parts]
    frame, table, vecs = refs[parts:]
    if outs[0].shape[1] > rows_stem + rows_small:
        vecs[...] = jnp.zeros_like(vecs)
        base = pl.multiple_of(24 * at_ref[0], 8)
        for index, ref in enumerate(outs):
            first = at_ref[index] == 0
            hs = [gv_ref[OUT_HIDDEN + k : OUT_HIDDEN + k + 1, :] for k in range(4)]
            hs = jnp.concatenate([jnp.where(first, hs[0], hs[2]), jnp.where(first, hs[1], hs[3])], 1)
            bl = [gv_ref[OUT_HEAD + k : OUT_HEAD + k + 1, 0:512] for k in range(2)]
            bl = jnp.where(first, bl[0], bl[1])
            rows = [hs[:, 128 * k : 128 * k + 128] for k in range(12)]
            rows += [bl[:, 128 * k : 128 * k + 128] for k in range(4)]
            vecs[pl.ds(base, 16), :] = jnp.concatenate(rows, 0)
            for d in range(16):
                lanes = slice(48 * d, 48 * d + 48)
                fill = jnp.zeros((1, 16), f32)
                row = jnp.concatenate(
                    [
                        gv_ref[OUT_BACK : OUT_BACK + 1, lanes],
                        fill,
                        gv_ref[OUT_FINAL : OUT_FINAL + 1, lanes],
                        fill,
                    ],
                    1,
                )
                vecs[pl.ds(base + 16, 8), :] = jnp.broadcast_to(row, (8, 128))
                ref[d, rows_stem + rows_small :, :] = vecs[...].astype(bf16)
    frame[0:ROW_W3, :] = jnp.zeros((ROW_W3, 128), f32)
    frame[STEM_ROWS:, :] = jnp.zeros((frame.shape[0] - STEM_ROWS, 128), f32)
    q = 9 * C2 // 2
    wide = jnp.concatenate(
        [
            jnp.concatenate(
                [
                    dw3_ref[0, pl.ds(k, q, stride=2), :],
                    dw3_ref[1, pl.ds(k, q, stride=2), :][:, 0 : C3 - 128],
                ],
                1,
            )
            for k in range(2)
        ],
        1,
    )
    for k in range(3):
        frame[pl.ds(ROW_W3 + k, q, stride=3), :] = wide[:, 128 * k : 128 * k + 128]
    for k in range(3):
        frame[pl.ds(ROW_W4 + k, 9 * C3, stride=3), :] = dw4_ref[k]
    for k in range(6):
        frame[pl.ds(ROW_WP + k, C4, stride=6), :] = dwp_ref[:, 128 * k : 128 * k + 128]
    table[0:12, :] = jnp.zeros((12, 128), f32)
    table[SMALL_ROWS:, :] = jnp.zeros((table.shape[0] - SMALL_ROWS, 128), f32)
    for k in range(6):
        lanes = slice(128 * k, 128 * k + 128)
        for name, index in VEC.items():
            row = SMALL_AT[name] + k
            table[row : row + 1, :] = gv_ref[index : index + 1, lanes]
        for h in range(4):
            row = SMALL_AT["hidden_bias"] + 6 * h + k
            table[row : row + 1, :] = gv_ref[VEC_HIDDEN + h : VEC_HIDDEN + h + 1, lanes]
        at = SMALL_AT["position"] + k
        for r in range(SIDE):
            table[pl.ds(at + 6 * (1 + SIDE * r), SIDE, stride=6), :] = gpos_ref[
                16 * r : 16 * r + SIDE, lanes
            ]
        table[at : at + 1, :] = gpos_ref[SIDE : SIDE + 1, lanes]
        row = SMALL_AT["class_token"] + k
        table[row : row + 1, :] = gpos_ref[SIDE : SIDE + 1, lanes]
    line = jnp.concatenate(
        [
            gv_ref[OUT_HEAD : OUT_HEAD + 1, 0:500],
            gv_ref[OUT_HEAD + 1 : OUT_HEAD + 2, 0:500],
            jnp.zeros((1, 24), f32),
        ],
        1,
    )
    row = SMALL_AT["head_bias"]
    for k in range(8):
        table[row + k : row + k + 1, :] = line[:, 128 * k : 128 * k + 128]
    for index, ref in enumerate(outs):
        mv = at_ref[index]

        def take(d, carry):
            owner = d * mp + mv
            a = (owner * stem_len + STEM_SHIFT) // 128
            ref[d, 0:rows_stem, :] = frame[pl.ds(a, rows_stem), :].astype(bf16)
            b = (owner * small_len + SMALL_SHIFT) // 128
            ref[d, rows_stem : rows_stem + rows_small, :] = table[pl.ds(b, rows_small), :].astype(bf16)
            return carry

        lax.fori_loop(0, ref.shape[0], take, 0)


def unshift_lanes(x, s, length):
    lane = lax.broadcasted_iota(jnp.int32, x.shape, 1)
    row = lax.broadcasted_iota(jnp.int32, x.shape, 0)
    moved = pltpu.roll(x, 128 - s, 1)
    after = pltpu.roll(moved, x.shape[0] - 1, 0)
    y = jnp.where(lane < 128 - s, moved, after)
    return jnp.where(row * 128 + lane < length, y, 0.0)


def unpack_kernel(stem_len, small_len, at_ref, x_ref, stem_ref, small_ref, sq_ref):
    rows = stem_ref.shape[0]
    end = rows + small_ref.shape[0]
    total = jnp.sum(x_ref[:, 0:end, :].astype(f32), 0)
    stem = unshift_lanes(total[0:rows], at_ref[0], stem_len)
    small = unshift_lanes(total[rows:], at_ref[1], small_len)
    stem_ref[...] = stem
    small_ref[...] = small
    sq_ref[...] = colsum(stem * stem) + colsum(small * small)


def norm_kernel(parts, *refs):
    sq_ref, sq1_ref, down_ref, head_ref, loss_ref, g0_ref, g1_ref, out_ref = refs[parts:]
    total = sum(ref[...].astype(f32) for ref in refs[:parts])
    half = g0_ref.shape[1]
    g0, g1 = total[:, 0:half], total[:, half:]
    g0_ref[...] = g0
    g1_ref[...] = g1
    squares = jnp.sum(g0 * g0 + g1 * g1 + down_ref[...] * down_ref[...], keepdims=True)
    squares = squares + jnp.sum(head_ref[...] * head_ref[...], keepdims=True)
    squares = squares + jnp.sum(sq_ref[...], keepdims=True)
    squares = squares + sq1_ref[0:1, 0:1] * (1.0 / out_ref.shape[0])
    lane = lax.broadcasted_iota(jnp.int32, (1, 128), 1)
    line = jnp.where(lane == 0, squares, loss_ref[OUT_LOSS : OUT_LOSS + 1, 0:128])
    out_ref[...] = jnp.broadcast_to(line[None], out_ref.shape)


def factor_kernel(x_ref, out_ref):
    total = jnp.sum(x_ref[...], 0)
    lane = lax.broadcasted_iota(jnp.int32, (1, 128), 1)
    norm = jnp.sqrt(jnp.sum(jnp.where(lane == 0, total, 0.0), keepdims=True))
    loss = jnp.sum(jnp.where(lane == 1, total, 0.0), keepdims=True)
    row = lax.broadcasted_iota(jnp.int32, (8, 128), 0)
    factor = jnp.minimum(1.0, clip_norm / norm)
    out_ref[...] = jnp.where(row == 0, loss, jnp.where(row == 1, norm, factor))


def late_kernel(x_ref, out_ref):
    kernel, share, rows = late_sizes(x_ref.shape[0])
    total = jnp.sum(x_ref[...].astype(f32), 0)
    exact = total[kernel : kernel + share] + total[kernel + share : kernel + 2 * share]
    out_ref[...] = jnp.broadcast_to(late_rows(total[0:kernel], exact, rows)[None], out_ref.shape)


def last_kernel(
    counts,
    stem_len,
    small_len,
    at_ref,
    x_ref,
    gram_ref,
    w1_ref,
    bn_ref,
    stem_ref,
    small_ref,
    stem_out,
    small_out,
    sq_ref,
    late,
    frame,
    table,
):
    frame[...] = jnp.zeros_like(frame)
    table[...] = jnp.zeros_like(table)
    kernel, share, _ = late_sizes(x_ref.shape[0])

    def collect(d, carry):
        x = x_ref[d].astype(f32)
        frame[pl.ds(ROW_W2 + kernel * d, kernel), :] = x[0:kernel]
        exact = x[kernel : kernel + share] + x[kernel + share : kernel + 2 * share]
        late[pl.ds(share * d, share), :] = exact
        return carry

    lax.fori_loop(0, x_ref.shape[0], collect, 0)
    line = [[jnp.zeros((1, SMALL_SHIFT), f32)], []]
    for level in range(4):
        chan = CHANS[level + 1]
        rows = []
        for which in range(2):
            row = LATE_SUMS + 6 * level + 3 * which
            rows.append(jnp.concatenate([late[row + k : row + k + 1, :] for k in range(3)], 1))
        both = fold_phases(jnp.concatenate(rows, 0), chan)
        line[0].append(both[1:2, 0:chan])
        line[1].append(both[0:1, 0:chan])
        if level == 0:
            tot = both[:, 0:128] / counts
    line = jnp.concatenate(line[0] + line[1], 1)
    for k in range(12):
        table[k : k + 1, :] = line[:, 128 * k : 128 * k + 128]
    gram, cross, mean, inv = level1_stats(gram_ref, w1_ref, counts)
    ones = gram[:, 27:28]
    grad = late[0:LATE_SUMS, :] - ones * tot[0:1] - (cross - ones * mean) * inv * tot[1:2]
    grad = grad * (inv * bn_ref[0:1, 0:128])
    line = [jnp.zeros((1, STEM_SHIFT), f32)] + [grad[k : k + 1, 0:C1] for k in range(27)]
    line = jnp.concatenate(line, 1)
    for k in range(ROW_W2):
        frame[k : k + 1, :] = line[:, 128 * k : 128 * k + 128]
    squares = jnp.sum(frame[0:ROW_W3, :] * frame[0:ROW_W3, :], keepdims=True)
    squares = squares + jnp.sum(table[0:12, :] * table[0:12, :], keepdims=True)
    sq_ref[...] = jnp.broadcast_to(squares, sq_ref.shape)
    part = frame[pl.ds(at_ref[2], stem_ref.shape[0]), :]
    stem_out[...] = stem_ref[...] + unshift_lanes(part, at_ref[0], stem_len)
    part = table[pl.ds(at_ref[3], small_ref.shape[0]), :]
    small_out[...] = small_ref[...] + unshift_lanes(part, at_ref[1], small_len)


def call(kernel, outs, *args, scratch=(), smem=0, hbm=(), load=(), store=(), hbm_out=(), limit=32):
    def space(index, free):
        if index in free:
            return pl.BlockSpec(memory_space=pltpu.HBM)
        return pl.BlockSpec(memory_space=pltpu.VMEM)

    def shape(index):
        where = pltpu.HBM if index in (*hbm_out, *store) else jax.ShapeDtypeStruct
        return where(*outs[index])

    args = [
        pltpu.with_memory_space_constraint(arg, pltpu.HBM) if index in (*hbm, *load) else arg
        for index, arg in enumerate(args)
    ]
    count = len(args)
    moved = [jax.ShapeDtypeStruct(args[k].shape, args[k].dtype) for k in load]
    moved += [jax.ShapeDtypeStruct(*outs[k]) for k in store]

    def body(*refs):
        refs = list(refs)
        if not moved:
            return kernel(*refs)
        buffers, sems = refs[-1 - len(moved) : -1], refs[-1]
        refs = refs[: -1 - len(moved)]
        copies = []
        for k, index in enumerate(load):
            copies.append(pltpu.make_async_copy(refs[index], buffers[k], sems.at[k]))
            copies[-1].start()
            refs[index] = buffers[k]
        for copy in copies:
            copy.wait()
        targets = []
        for k, index in enumerate(store):
            targets.append((buffers[len(load) + k], refs[count + index], sems.at[len(load) + k]))
            refs[count + index] = buffers[len(load) + k]
        kernel(*refs)
        copies = [pltpu.make_async_copy(*target) for target in targets]
        for copy in copies:
            copy.start()
        for copy in copies:
            copy.wait()

    extra = [pltpu.VMEM(x.shape, x.dtype) for x in moved]
    if moved:
        extra.append(pltpu.SemaphoreType.DMA((len(moved),)))
    specs = [pl.BlockSpec(memory_space=pltpu.SMEM)] * smem
    specs += [space(index, (*hbm, *load)) for index in range(smem, count)]
    return pl.pallas_call(
        body,
        out_shape=[shape(index) for index in range(len(outs))],
        in_specs=specs,
        out_specs=[space(index, (*hbm_out, *store)) for index in range(len(outs))],
        scratch_shapes=[*scratch, *extra],
        compiler_params=pltpu.CompilerParams(vmem_limit_bytes=limit * 1024 * 1024),
    )(*args)


def adam_step(weight, first, second, grad, factor, rate):
    grad = grad * factor
    first = beta_one * first + (1.0 - beta_one) * grad
    second = beta_two * second + (1.0 - beta_two) * grad * grad
    first_fixed = first / (1.0 - beta_one**STEP)
    second_fixed = second / (1.0 - beta_two**STEP)
    return (
        weight
        - rate * (first_fixed / (jnp.sqrt(second_fixed) + adam_epsilon) + decay_rate * weight),
        first,
        second,
    )


def local(
    pixels,
    labels,
    stem,
    stem_first,
    stem_second,
    small,
    small_first,
    small_second,
    block,
    block_first,
    block_second,
    head,
    head_first,
    head_second,
):
    dp, mp = lax.axis_size("dp"), lax.axis_size("mp")
    n = dp * mp
    me, mine = lax.axis_index("dp"), lax.axis_index("mp")
    owner = me * mp + mine
    stem_len, small_len = stem.shape[0], small.shape[0]
    rows_stem = up16(-(-(stem_len + 127) // 128))
    rows_small = up16(-(-(small_len + 127) // 128))
    rows = rows_stem + rows_small
    everyone = ("dp", "mp")
    fast = (dp, mp) == (16, 2)

    def share(x):
        return lax.all_to_all(x, everyone, 0, 0)

    part = FF // mp
    cls = CLASSES // mp
    cls_pad = 512 // (mp // 2)
    packed = jnp.concatenate(
        [block[0], block[1], block[2], jnp.pad(head, ((0, 0), (0, cls_pad - cls)))], 1
    ).astype(bf16)
    packed, stem, small = lax.optimization_barrier((packed, stem, small))
    gathered = lax.all_gather(packed, everyone, axis=0)
    stem_at, small_at = owner * stem_len + STEM_SHIFT, owner * small_len + SMALL_SHIFT
    at = jnp.stack(
        [
            stem_at % 128,
            small_at % 128,
            jnp.minimum(stem_at // 128, ROW_W3),
            jnp.minimum(small_at // 128, 16),
        ]
    ).astype(jnp.int32)
    (piece,) = call(
        pack_kernel,
        [((rows, 128), bf16)],
        at,
        jnp.pad(stem, (0, rows_stem * 128 - stem_len)).reshape(rows_stem, 128),
        jnp.pad(small, (0, rows_small * 128 - small_len)).reshape(rows_small, 128),
        smem=1,
        limit=4,
    )

    strip = pixels.reshape(pixels.shape[1], 128)
    strip, piece, at = lax.optimization_barrier((strip, piece, at))
    half = strip.shape[0] // 2
    pairs = [(source, (source + dp - 1) % dp) for source in range(dp)]
    lower = lax.ppermute(strip[:half], "dp", pairs)

    if fast:
        gathered = gathered.reshape(16, 2, 48, packed.shape[1])
    else:
        g = gathered.reshape(dp, mp, D // dp, packed.shape[1])
        g = jnp.transpose(g, (0, 2, 1, 3)).reshape(D, mp, -1)
        slots = [g[:, :, k * part : (k + 1) * part].reshape(D, 2, FF // 2) for k in range(3)]
        top = g[:, :, 3 * part : 3 * part + cls].reshape(D, 2, CLASSES // 2)
        slots.append(jnp.pad(top, ((0, 0), (0, 0), (0, 12))))
        g = jnp.concatenate(slots, 2).reshape(16, 48, 2, -1)
        gathered = jnp.transpose(g, (0, 2, 1, 3))

    if fast:
        planes = [[4 * z + k for k in range(4)] for z in range(4)]
        column = [piece]
        for k in (1, 2, 3):
            pairs = [(source, source ^ (4 * k)) for source in range(dp)]
            column.append(lax.ppermute(piece, "dp", pairs))
        *column, lower = lax.optimization_barrier((*column, lower))
        column = jnp.stack(column, 0)
        column = [column]
        for k in (1, 2, 3):
            pairs = [(source, source ^ k) for source in range(dp)]
            column.append(lax.ppermute(column[0], "dp", pairs))
        column = jnp.stack(column, 0)
        column = column.reshape(dp, rows, 128)
    else:
        column = lax.all_to_all(jnp.broadcast_to(piece[None], (dp, rows, 128)), "dp", 0, 0)
    xk, gram = call(
        image_kernel,
        [((8, T, 192), bf16), ((n, 8, 128), f32)],
        strip[half:],
        lower,
        scratch=[
            pltpu.VMEM((2 * half, 128), f32),
            pltpu.VMEM((16 * half // 3 + 16, 128), f32),
            pltpu.VMEM((17, T, 64), bf16),
        ],
        limit=12,
    )
    gram = share(gram)
    gram, xk, column = lax.optimization_barrier((gram, xk, column))
    if mp == 2:
        swap = [(0, 1), (1, 0)]
        pieces = [column, lax.ppermute(column, "mp", swap)]
        which = jnp.stack([mine, 1 - mine]).astype(jnp.int32)
    else:
        columns = lax.all_gather(column, "mp", axis=0)
        pieces = [columns[k] for k in range(mp)]
        which = jnp.arange(mp, dtype=jnp.int32)
    which = jnp.concatenate([which, labels.reshape(1), me.reshape(1).astype(jnp.int32)])
    frame_rows = (stem_len * n + STEM_SHIFT) // 128 + rows_stem + 16
    table_rows = (small_len * n + SMALL_SHIFT) // 128 + rows_small + 16
    frames = [pltpu.VMEM((frame_rows, 128), f32), pltpu.VMEM((table_rows, 128), f32)]
    w1, t1, t2, t3, t4, wp, bn, vec, pos = call(
        functools.partial(assemble_kernel, fast, len(pieces), mp, stem_len, small_len, rows_stem, rows_small),
        [
            ((32, 128), f32),
            ((192, W), bf16),
            ((3, W + C1, W), bf16),
            ((3, W + C2, W), bf16),
            ((3, W + C3, W), bf16),
            ((C4, D), bf16),
            ((8, W), f32),
            ((24, D), f32),
            ((T, D), f32),
        ],
        which,
        *pieces,
        smem=1,
        store=(1, 2, 3, 4, 5, 7, 8),
        scratch=frames
        + [
            pltpu.VMEM((9 * C1, 128), f32),
            pltpu.VMEM((9 * C2, 128), f32),
            pltpu.VMEM((9 * C2, 128), f32),
            pltpu.VMEM((192, W), f32),
            pltpu.VMEM((W + C1, W), f32),
            pltpu.VMEM((W + C2, W), f32),
        ],
        limit=20,
    )

    positions = SIDE * SIDE * n
    counts = [None, 64.0 * positions, 16.0 * positions, 4.0 * positions, 1.0 * positions]
    ax, conv, st = call(
        functools.partial(conv12_kernel, counts[1]),
        [((9, T, W + C1), bf16), ((4, T, W), f32), ((n, 2, sent_width(C2)), f32)],
        xk,
        gram,
        w1,
        t1,
        bn,
        t2,
        load=(3, 5),
        limit=14,
    )
    convs = [None, None, conv]
    stats = [None, None, share(st)]
    inputs = [None, None, ax]
    kernels = [None, t1, t2, t3, t4]
    for level in (3, 4):
        r = 2 ** (4 - level)
        ax, conv, st = call(
            functools.partial(conv_kernel, level - 1, counts[level - 1]),
            [((2 * r + 1, T, W + CHANS[level - 1]), bf16), ((r, T, W), f32), ((n, 2, sent_width(CHANS[level])), f32)],
            convs[level - 1],
            stats[level - 1],
            bn,
            kernels[level],
            load=(3,),
            store=(0, 1, 2) if level == 4 else (),
            limit=10,
        )
        inputs.append(ax)
        convs.append(conv)
        stats.append(share(st))

    a4, x0, n1 = call(
        functools.partial(embed_kernel, counts[4]),
        [((T, C4), bf16), ((T, D), f32), ((T, D), bf16)],
        stats[4],
        bn,
        convs[4],
        wp,
        pos,
        vec,
        load=(2, 3, 4, 5),
        store=(0, 1, 2),
        limit=12,
    )
    outs = call(
        functools.partial(block_kernel, counts[4]),
        [
            ((4, 2, 4, 48, FF), bf16),
            ((1, T, W), f32),
            ((n, 2, W), f32),
            ((32, D), f32),
            ((T, D), f32),
            ((C4, D), f32),
        ],
        stats[4],
        bn,
        n1,
        vec,
        x0,
        a4,
        wp,
        convs[4],
        gathered,
        hbm=(2, 3, 4, 5, 6, 7, 8),
        hbm_out=(0, 1, 2, 3, 4, 5),
        limit=44,
        scratch=[
            pltpu.VMEM((1, T, W), f32),
            pltpu.VMEM((C4, D), bf16),
            pltpu.VMEM((24, D), f32),
            pltpu.VMEM((1, T, W), f32),
            pltpu.VMEM((n, 2, W), f32),
            pltpu.VMEM((32, D), f32),
            pltpu.VMEM((T, D), f32),
            pltpu.VMEM((C4, D), f32),
            pltpu.VMEM((2, 16, 48, 1536), bf16),
            pltpu.VMEM((2, 16, 48, 1536), bf16),
            pltpu.VMEM((2, 16, 48, 1536), bf16),
            pltpu.VMEM((2, 16, 48, 512), bf16),
            pltpu.SemaphoreType.DMA((39,)),
            pltpu.VMEM((T, W), bf16),
            pltpu.VMEM((T, D), f32),
            pltpu.VMEM((T, D), bf16),
            pltpu.VMEM((T, 3 * D), bf16),
            pltpu.VMEM((HEADS, T, T), f32),
            pltpu.VMEM((T, D), bf16),
            pltpu.VMEM((D, T), bf16),
            pltpu.VMEM((2, T, 1536), f32),
            pltpu.VMEM((T, D), f32),
            pltpu.VMEM((T, 3 * D), bf16),
            pltpu.VMEM((T, D), f32),
            pltpu.VMEM((2, T, 1536), bf16),
            pltpu.VMEM((32, 1536), f32),
        ],
    )
    grads, back, tot, facts, gpos, dwp = outs
    tot = share(tot)
    if fast:
        planes = [[8 * z + k for k in range(8)] for z in range(4)]
        owned = lax.psum_scatter(
            grads.reshape(8 * 4 * 48, FF),
            everyone,
            scatter_dimension=0,
            tiled=True,
            axis_index_groups=planes,
        )
        owned = [owned]
    else:
        g = jnp.transpose(grads, (2, 0, 3, 1, 4)).reshape(D, 2, 2, FF // 2)
        g = jnp.transpose(g, (0, 2, 1, 3)).reshape(dp, D // dp, 2, mp, part)
        g = jnp.transpose(g, (0, 3, 1, 2, 4)).reshape(n * (D // dp), 2 * part)
        owned = [lax.psum_scatter(g, everyone, scatter_dimension=0, tiled=True)]

    rows_d = D // dp
    rows_vec = 48 if fast else 0

    def outer(bo_all, fin_all, hs_all, bl_all):
        return dot_tn(bo_all, hs_all), dot_tn(fin_all, bl_all)

    if not fast:
        bo, fin = facts[OUT_BACK : OUT_BACK + 1], facts[OUT_FINAL : OUT_FINAL + 1]
        hs, bl = facts[OUT_HIDDEN:OUT_HEAD].reshape(1, FF), facts[OUT_HEAD:OUT_SUMS, 0:512].reshape(1, 1024)
        head_line = jnp.concatenate([bl[:, :500], bl[:, 512:1012]], 1).reshape(1, mp, cls)
        line = jnp.concatenate(
            [
                jnp.broadcast_to(bo.reshape(dp, 1, rows_d), (dp, mp, rows_d)),
                jnp.broadcast_to(fin.reshape(dp, 1, rows_d), (dp, mp, rows_d)),
                jnp.broadcast_to(hs.reshape(1, mp, part), (dp, mp, part)),
                jnp.broadcast_to(head_line, (dp, mp, cls)),
            ],
            2,
        ).reshape(n, -1)
        width = -(-line.shape[1] // 1024) * 1024
        line = jnp.pad(line, ((0, 0), (0, width - line.shape[1]))).astype(bf16)
        line = share(line.reshape(n, width // 128, 128)).reshape(n, width)
        cuts = [0, rows_d, 2 * rows_d, 2 * rows_d + part, 2 * rows_d + part + cls]
        grad_down, grad_head = outer(*[line[:, a:b] for a, b in zip(cuts[:-1], cuts[1:])])

    sums = [None] * 5
    kernel_grads = [None] * 5
    for level in (4, 3):
        r = 2 ** (4 - level)
        chan_in = CHANS[level - 1]
        g, back, so, sums[level - 1] = call(
            functools.partial(conv_back_kernel, level, counts[level], counts[level - 1]),
            [
                ((r + 1, T, W), bf16),
                ((2 * r, T, W), f32),
                ((n, 2, sent_width(chan_in)), f32),
                ((2, W), f32),
            ],
            back,
            tot,
            convs[level],
            stats[level],
            kernels[level],
            convs[level - 1],
            stats[level - 1],
            bn,
            load=(0, 2, 3, 4) if level == 4 else (4,),
            limit=12,
        )
        (kernel_grads[level],) = call(
            functools.partial(kernel_grad, level),
            [((-(-CHANS[level] // 128), 9 * chan_in, 128), f32)],
            inputs[level],
            g,
            load=(0,) if level == 4 else (),
            scratch=[pltpu.VMEM((3, W + chan_in, W), f32)],
            limit=12,
        )
        if level == 4:
            so, kernel_grads[4] = lax.optimization_barrier((so, kernel_grads[4]))
            tot = share(so)
    outs = call(
        functools.partial(early_kernel, len(pieces), mp, stem_len, small_len, rows_stem, rows_small),
        [((dp, rows + rows_vec, 128), bf16)] * len(pieces),
        which,
        kernel_grads[3],
        kernel_grads[4],
        dwp,
        facts,
        gpos,
        smem=1,
        load=(3, 4, 5),
        scratch=frames + [pltpu.VMEM((48, 128), f32)],
        limit=18,
    )
    if mp == 2:
        column = outs[0] + lax.ppermute(outs[1], "mp", swap)
    else:
        column = lax.psum_scatter(jnp.stack(outs, 0), "mp", scatter_dimension=0)
    so, column = lax.optimization_barrier((so, column))
    tot = share(so)
    tot, column = lax.optimization_barrier((tot, column))
    column = lax.all_to_all(column, "dp", 0, 0)
    kernel_rows, exact_rows, each = late_sizes(n)
    (late,) = call(
        functools.partial(conv2_back_kernel, counts[2], counts[1]),
        [((n, each, 128), bf16)],
        back,
        tot,
        convs[2],
        stats[2],
        inputs[2],
        t2,
        xk,
        gram,
        w1,
        t1,
        bn,
        *sums[2:4],
        facts,
        load=(0, 4, 5, 6, 9, 13),
        scratch=[
            pltpu.VMEM((1, 9 * C1, 128), f32),
            pltpu.VMEM((5, T, W), bf16),
            pltpu.VMEM((3, W + C1, W), f32),
            pltpu.VMEM((192, W), f32),
            pltpu.VMEM((n * kernel_rows, 128), f32),
            pltpu.VMEM((n * exact_rows, 128), f32),
        ],
        limit=20,
    )
    if fast:
        owned[0] = lax.optimization_barrier((owned[0], late))[0]
        lines = [[8 * z + k for z in range(4)] for k in range(8)]
        owned[0] = lax.psum_scatter(
            owned[0], everyone, scatter_dimension=0, tiled=True, axis_index_groups=lines
        )
    late, column = lax.optimization_barrier((late, column))
    late = share(late)
    (late,) = call(late_kernel, [((n, each, 128), bf16)], late, limit=8)
    late = share(late)
    if fast:
        line = column[:, rows:].reshape(2 * dp, 24, 128)
        grad_down, grad_head = outer(
            line[:, 16, 0:48],
            line[:, 16, 64:112],
            line[:, 0:12].reshape(2 * dp, part),
            line[:, 12:16].reshape(2 * dp, 512)[:, :cls],
        )
    grad_stem, grad_small, squares = call(
        functools.partial(unpack_kernel, stem_len, small_len),
        [((rows_stem, 128), f32), ((rows_small, 128), f32), ((1, 128), f32)],
        at,
        column,
        smem=1,
        limit=8,
    )

    grad_stem, grad_small, squares1 = call(
        functools.partial(last_kernel, counts[1], stem_len, small_len),
        [((rows_stem, 128), f32), ((rows_small, 128), f32), ((1, 128), f32)],
        at,
        late,
        gram,
        w1,
        bn,
        grad_stem,
        grad_small,
        smem=1,
        scratch=[
            pltpu.VMEM((n * exact_rows, 128), f32),
            pltpu.VMEM((ROW_W2 + n * kernel_rows + rows_stem, 128), f32),
            pltpu.VMEM((16 + rows_small, 128), f32),
        ],
        limit=8,
    )

    g0, g1, ends = call(
        functools.partial(norm_kernel, len(owned)),
        [((rows_d, part), f32), ((rows_d, part), f32), ((n, 1, 128), f32)],
        *owned,
        squares,
        squares1,
        grad_down,
        grad_head,
        facts,
        limit=8,
    )
    (ends,) = call(factor_kernel, [((8, 128), f32)], share(ends), limit=4)
    loss_sum, grad_norm, factor = ends[0, 0], ends[1, 0], ends[2, 0]
    grad_stem = grad_stem.reshape(-1)[:stem_len]
    grad_small = grad_small.reshape(-1)[:small_len]
    grad_block = jnp.stack([g0, g1, grad_down], 0)
    stem_new = adam_step(stem, stem_first, stem_second, grad_stem, factor, rate_stem)
    small_new = adam_step(small, small_first, small_second, grad_small, factor, rate_small)
    block_new = adam_step(block, block_first, block_second, grad_block, factor, rate_block)
    head_new = adam_step(head, head_first, head_second, grad_head, factor, rate_head)
    return (*stem_new, *small_new, *block_new, *head_new, loss_sum, grad_norm)


def solution(mesh):
    flat = P(("dp", "mp"))
    matrix = P(None, "dp", "mp")
    head = P("dp", "mp")
    states = (flat,) * 6 + (matrix,) * 3 + (head,) * 3
    return jax.shard_map(
        local,
        mesh=mesh,
        in_specs=(P("mp", "dp", None), P("mp", "dp")) + states,
        out_specs=states + (P(), P()),
        check_vma=False,
    )
```
